32 devices in a mesh: dp: 16 (over z, x, core), seq: 2 (over y).
Axes of the slice: x: 2, y: 2, z: 4, core: 2. Of those that a mesh axis runs over, the one named last changes fastest.
Arguments:
- query_rows: bfloat16 [18432, 2048], P(('dp', 'seq')), may hold values from -500 to 500
- key_rows: bfloat16 [18432, 2048], P(('dp', 'seq')), may hold values from -5 to 5
- value_rows: bfloat16 [18432, 2048], P(('dp', 'seq')), may hold values from -6 to 6
- windows: int32 [16, 3], replicated, may hold values from 1 to 3, as said below
- out_weight: bfloat16 [2048, 3072], P('dp', 'seq'), may hold values from -0.125 to 0.125
- gate_scale: bfloat16 [16, 3072], P('dp', 'seq'), may hold values from 0.5 to 1.5
- out_grad: bfloat16 [18432, 3072], P('dp', 'seq'), may hold values from -0.046875 to 0.046875
Outputs:
- block_out: bfloat16 [18432, 3072], P('dp', 'seq')
- weight_grad: float32 [2048, 3072], P('dp', 'seq')
The draws below stay inside these ranges and needn't reach their ends.
Inputs may be any that keep to these rules, and one draw needn't show every extreme that they name: `windows`: one head has extent 3 along all three dimensions.
All inputs are finite; a program needn't handle non-finite values.
Results may differ from the reference program's by a relative error of at most 0.0057.
Values may be sent and summed in bfloat16 or wider, within the bound.
No kernel may reach another device: no remote copies, remote signals or barrier semaphores. Data moves between devices by JAX's collectives and lax.ppermute only.
A program may use at most 192 MiB of HBM per device.

```python
import math
import jax
import jax.numpy as jnp
from jax import lax

D = 3072
HEADS = 16
HEAD_DIM = 128
GH = 3
GW = 4
EXT = 3
GT = 2
HD = 2048
TILE = 48
NT = 24
CLIP_TOK = 1152
CLIPS = 16
TOKENS = 18432


def shared_keys(key):
    raw = jax.random.normal(jax.random.fold_in(key, 7), (TOKENS, HD), jnp.float32)
    return jnp.clip(raw, -5.0, 5.0)


def draw_key_rows(key, part):
    base = shared_keys(key)
    return base.astype(jnp.bfloat16)


def draw_query_rows(key, part):
    own = jnp.clip(jax.random.normal(jax.random.fold_in(key, 13), (TOKENS, HD), jnp.float32), -5.0, 5.0)
    return own.astype(jnp.bfloat16)


def draw_windows(key, part):
    extent_key, head_key = jax.random.split(jax.random.fold_in(key, 21))
    extent = jax.random.randint(extent_key, (HEADS, 3), 1, EXT + 1).astype(jnp.int32)
    widest = jax.random.randint(head_key, (), 0, HEADS).astype(jnp.int32)
    head_id = jnp.arange(HEADS).astype(jnp.int32)
    extent = jnp.where(head_id[:, None] == widest, EXT, extent)
    return extent.astype(jnp.int32)


def steps_of(stream_key, shape, cuts, smallest, largest):
    level = 1.0
    for axis_at, parts in cuts:
        heights = jax.random.uniform(jax.random.fold_in(jax.random.fold_in(stream_key, 6), axis_at), (parts,), jnp.float32, smallest / len(cuts), largest / len(cuts))
        level = level * jnp.repeat(jnp.exp(heights), shape[axis_at] // parts).reshape((-1,) + (1,) * (len(shape) - 1 - axis_at))
    return level


def normal_values(own_key, dims, scale, reach, shards=(), kind=jnp.bfloat16):
    array = jax.random.normal(own_key, dims, jnp.float32) * scale
    if len(shards) > 0:
        array = steps_of(own_key, dims, shards, -0.22, 0.18) * array
    return jnp.clip(array, min=-reach, max=reach).astype(kind)


def setup_inputs(seed: int = 0) -> dict:
    streams_of = jax.random.split(jax.random.key(seed), 8)
    return {
        "query_rows": draw_query_rows(jax.random.fold_in(streams_of[7], 71), 0),
        "key_rows": draw_key_rows(jax.random.fold_in(streams_of[7], 71), 0),
        "value_rows": normal_values(streams_of[2], (TOKENS, HD), 1.0, 6.0, ((0, 32),)),
        "windows": draw_windows(jax.random.fold_in(streams_of[7], 71), 0),
        "out_weight": normal_values(streams_of[4], (HD, D), HD ** -0.5, 0.125, ((0, 16), (1, 2))),
        "gate_scale": jnp.clip(0.5 + 1.0 * jax.random.uniform(streams_of[5], (CLIPS, D), jnp.float32) ** steps_of(streams_of[5], (CLIPS, D), ((0, 16), (1, 2)), -0.2, 0.2), 0.5, 1.5).astype(jnp.bfloat16),
        "out_grad": normal_values(streams_of[6], (TOKENS, D), TOKENS ** -0.5, 0.046875, ((0, 16), (1, 2))),
    }


def grid_limits():
    return (GT, GH, GW)

def tile_coords(length):
    position = jnp.arange(length).astype(jnp.int32)
    tile_id = position // TILE
    plane_size = GH * GW
    return jnp.stack([tile_id // plane_size, tile_id // GW % GH, tile_id % GW])

def head_windows(windows):
    limits = grid_limits()
    tile_id = jnp.arange(NT).astype(jnp.int32)
    coords = jnp.stack([tile_id // (GH * GW), tile_id // GW % GH, tile_id % GW])
    starts = []
    extents = []
    for axis_no in range(3):
        extent = jnp.minimum(windows[:, axis_no], limits[axis_no]).astype(jnp.int32)[:, None]
        start = jnp.clip(coords[axis_no][None, :] - (extent - 1) // 2, 0, limits[axis_no] - extent)
        starts.append(start.astype(jnp.int32))
        extents.append(extent)
    return (jnp.stack(starts), jnp.stack(extents))

def clip_attention(query_part, key_part, value_part, starts, extents):
    count = query_part.shape[0]
    row_block = math.gcd(count, 512)
    blocks = count // row_block
    score_scale = 1.0 / math.sqrt(HEAD_DIM)
    key_coords = tile_coords(count)
    query_blocks = query_part.astype(jnp.float32).reshape(blocks, row_block, HEADS, HEAD_DIM)
    key_heads = key_part.astype(jnp.float32).reshape(count, HEADS, HEAD_DIM)
    value_heads = value_part.astype(jnp.float32).reshape(count, HEADS, HEAD_DIM)
    firsts = (jnp.arange(blocks) * row_block).astype(jnp.int32)

    def one_block(operands):
        query_block, first_row = operands
        query_tiles = (first_row + jnp.arange(row_block).astype(jnp.int32)) // TILE
        visible = jnp.ones((HEADS, row_block, count), dtype=bool)
        for axis_no in range(3):
            lower = jnp.take(starts[axis_no], query_tiles, axis=1)[:, :, None]
            upper = lower + extents[axis_no][:, :, None]
            column = key_coords[axis_no][None, None, :]
            visible = visible & (column >= lower) & (column < upper)
        scores = jnp.einsum('qhd,khd->hqk', query_block, key_heads) * score_scale
        scores = jnp.where(visible, scores, -jnp.inf)
        row_peak = lax.optimization_barrier(jnp.max(scores, axis=-1, keepdims=True))
        weights = jnp.exp(scores - row_peak)
        denominator = lax.optimization_barrier(jnp.sum(weights, axis=-1, keepdims=True))
        weights_low = (weights / denominator).astype(jnp.bfloat16)
        blended = jnp.einsum('hqk,khd->qhd', weights_low.astype(jnp.float32), value_heads)
        return blended.astype(jnp.bfloat16).reshape(row_block, HD)
    return lax.map(one_block, (query_blocks, firsts)).reshape(count, HD)

def reference(query_rows, key_rows, value_rows, windows, out_weight, gate_scale, out_grad):
    clip_count = gate_scale.shape[0]
    starts, extents = head_windows(windows)
    query_clips = query_rows.reshape(clip_count, CLIP_TOK, HD)
    key_clips = key_rows.reshape(clip_count, CLIP_TOK, HD)
    value_clips = value_rows.reshape(clip_count, CLIP_TOK, HD)
    grad_clips = out_grad.reshape(clip_count, CLIP_TOK, D)

    def per_clip(carried, operands):
        query_part, key_part, value_part, gate_row, grad_part = operands
        attention = clip_attention(query_part, key_part, value_part, starts, extents)
        projected = jnp.dot(attention, out_weight, preferred_element_type=jnp.float32)
        gate_wide = gate_row.astype(jnp.float32)
        result = (projected * gate_wide).astype(jnp.bfloat16)
        grad_proj = (grad_part.astype(jnp.float32) * gate_wide).astype(jnp.bfloat16)
        carried = carried + lax.dot_general(attention, grad_proj, (((0,), (0,)), ((), ())), preferred_element_type=jnp.float32)
        return (carried, result)
    initial = jnp.zeros((HD, D), jnp.float32)
    weight_grad, outputs = lax.scan(per_clip, initial, (query_clips, key_clips, value_clips, gate_scale, grad_clips))
    return (outputs.reshape(TOKENS, D), weight_grad)
```

```python
import math

import jax
import jax.numpy as jnp
import numpy as np
from jax import lax
from jax.experimental import pallas as pl
from jax.experimental.pallas import tpu as pltpu
from jax.sharding import PartitionSpec as P

HEADS = 16
HEAD_DIM = 128
GH = 3
GW = 4
GT = 2
TILE = 48
NT = 24
CLIP_TOK = NT * TILE
Q_ROWS = GW * TILE
LOG2_SCALE = math.log2(math.e) / math.sqrt(HEAD_DIM)
VMEM_LIMIT = 40 * 1024 * 1024


def window_bias(windows):
    tile_id = np.arange(NT)
    coords = np.stack([tile_id // (GH * GW), tile_id // GW % GH, tile_id % GW]).astype(np.int32)
    token_coords = np.repeat(coords, TILE, axis=1)
    inside = None
    for axis_no, limit in enumerate((GT, GH, GW)):
        extent = jnp.minimum(windows[:, axis_no], limit)[:, None]
        start = jnp.clip(coords[axis_no][None, :] - (extent - 1) // 2, 0, limit - extent)
        column = token_coords[axis_no][None, None, :]
        here = (column >= start[:, :, None]) & (column < (start + extent)[:, :, None])
        inside = here if inside is None else inside & here
    return jnp.where(inside, 0.0, -jnp.inf).astype(jnp.float32)


def attend_rows(queries, first_tile, bias_ref, keys, values):
    count = queries.shape[0]
    tiles = count // TILE
    scores = lax.dot_general(
        queries, keys, (((1,), (1,)), ((), ())), preferred_element_type=jnp.float32
    )
    bias = bias_ref[0, first_tile : first_tile + tiles, :]
    scores = (scores.reshape(tiles, TILE, CLIP_TOK) + bias[:, None, :]).reshape(count, CLIP_TOK)
    peak = jnp.max(scores, axis=-1, keepdims=True)
    weights = jnp.exp2((scores - peak) * LOG2_SCALE).astype(jnp.bfloat16)
    blended = jnp.dot(weights, values, preferred_element_type=jnp.float32)
    return (blended[:, :HEAD_DIM] / blended[:, HEAD_DIM:]).astype(jnp.bfloat16)


def fill_values(values_ref, parts):
    at = 0
    for part in parts:
        rows = part.shape[0]
        values_ref[at : at + rows, :HEAD_DIM] = part
        at += rows
    values_ref[:, HEAD_DIM:] = jnp.ones((CLIP_TOK, HEAD_DIM), jnp.bfloat16)


def pair_kernel(place_ref, q_ref, k_ref, v_ref, other_ref, bias_ref, out_ref, keys_ref, values_ref):
    half = CLIP_TOK // 2
    keys_ref[:half, :] = k_ref[...]
    keys_ref[half:, :] = other_ref[1]
    fill_values(values_ref, (v_ref[...], other_ref[2]))
    keys = keys_ref[...]
    values = values_ref[...]
    for side in range(2):
        base = pl.multiple_of((place_ref[0] if side == 0 else 1 - place_ref[0]) * half, half)
        for at in range(0, half, Q_ROWS):
            queries = q_ref[at : at + Q_ROWS, :] if side == 0 else other_ref[0, at : at + Q_ROWS, :]
            first_tile = (side * half + at) // TILE
            out_ref[pl.ds(base + at, Q_ROWS), :] = attend_rows(
                queries, first_tile, bias_ref, keys, values
            )


def whole_kernel(place_ref, q_ref, k_ref, v_ref, bias_ref, out_ref, values_ref):
    fill_values(values_ref, (v_ref[...],))
    keys = k_ref[...]
    values = values_ref[...]
    for at in range(0, CLIP_TOK, Q_ROWS):
        out_ref[at : at + Q_ROWS, :] = attend_rows(
            q_ref[at : at + Q_ROWS, :], at // TILE, bias_ref, keys, values
        )


def attention_cost(heads):
    pairs = heads * CLIP_TOK * CLIP_TOK
    return pl.CostEstimate(
        flops=pairs * HEAD_DIM * 6,
        bytes_accessed=heads * CLIP_TOK * HEAD_DIM * 8,
        transcendentals=pairs,
    )


def attend_pair(place, local_heads, picked, query, key, value, other, bias):
    half = CLIP_TOK // 2
    first, step = picked[0], picked[1] - picked[0] if len(picked) > 1 else 1

    def head(i, place_ref):
        return place_ref[0] * local_heads + first + step * i

    own = pl.BlockSpec((half, HEAD_DIM), lambda i, p: (0, head(i, p)))
    return pl.pallas_call(
        pair_kernel,
        grid_spec=pltpu.PrefetchScalarGridSpec(
            num_scalar_prefetch=1,
            grid=(len(picked),),
            in_specs=[
                own,
                own,
                own,
                pl.BlockSpec((3, half, HEAD_DIM), lambda i, p: (0, 0, i)),
                pl.BlockSpec((1, NT, CLIP_TOK), lambda i, p: (head(i, p), 0, 0)),
            ],
            out_specs=pl.BlockSpec((CLIP_TOK, HEAD_DIM), lambda i, p: (0, i)),
            scratch_shapes=[
                pltpu.VMEM((CLIP_TOK, HEAD_DIM), jnp.bfloat16),
                pltpu.VMEM((CLIP_TOK, 2 * HEAD_DIM), jnp.bfloat16),
            ],
        ),
        out_shape=jax.ShapeDtypeStruct((CLIP_TOK, len(picked) * HEAD_DIM), jnp.bfloat16),
        compiler_params=pltpu.CompilerParams(vmem_limit_bytes=VMEM_LIMIT),
        cost_estimate=attention_cost(len(picked)),
    )(place, query, key, value, other, bias)


def attend_whole(place, query, key, value, bias):
    local_heads = query.shape[1] // HEAD_DIM
    column = pl.BlockSpec((CLIP_TOK, HEAD_DIM), lambda i, p: (0, i))
    return pl.pallas_call(
        whole_kernel,
        grid_spec=pltpu.PrefetchScalarGridSpec(
            num_scalar_prefetch=1,
            grid=(local_heads,),
            in_specs=[
                column,
                column,
                column,
                pl.BlockSpec((1, NT, CLIP_TOK), lambda i, p: (p[0] * local_heads + i, 0, 0)),
            ],
            out_specs=column,
            scratch_shapes=[pltpu.VMEM((CLIP_TOK, 2 * HEAD_DIM), jnp.bfloat16)],
        ),
        out_shape=jax.ShapeDtypeStruct(query.shape, jnp.bfloat16),
        compiler_params=pltpu.CompilerParams(vmem_limit_bytes=VMEM_LIMIT),
        cost_estimate=attention_cost(local_heads),
    )(place, query, key, value, bias)


def pack_kernel(place_ref, q_ref, k_ref, v_ref, out_ref):
    out_ref[0] = q_ref[...]
    out_ref[1] = k_ref[...]
    out_ref[2] = v_ref[...]


def pack_partner(place, local_heads, picked, query, key, value):
    rows = query.shape[0]
    first, step = picked[0], picked[1] - picked[0] if len(picked) > 1 else 1
    column = pl.BlockSpec(
        (rows, HEAD_DIM), lambda i, p: (0, (1 - p[0]) * local_heads + first + step * i)
    )
    return pl.pallas_call(
        pack_kernel,
        grid_spec=pltpu.PrefetchScalarGridSpec(
            num_scalar_prefetch=1,
            grid=(len(picked),),
            in_specs=[column, column, column],
            out_specs=pl.BlockSpec((3, rows, HEAD_DIM), lambda i, p: (0, 0, i)),
        ),
        out_shape=jax.ShapeDtypeStruct((3, rows, len(picked) * HEAD_DIM), jnp.bfloat16),
        compiler_params=pltpu.CompilerParams(vmem_limit_bytes=VMEM_LIMIT),
    )(place, query, key, value)


def contract_tokens(columns, grad_proj, kind):
    return lax.dot_general(
        columns, grad_proj, (((0,), (0,)), ((), ())), preferred_element_type=jnp.float32
    ).astype(kind)


def swap_bit(value, dp_count, bit, sender=None):
    pairs = [(i, i ^ bit) for i in range(dp_count) if sender is None or sender(i)]
    return lax.ppermute(value, "dp", pairs)


def reduce_group(partial, dp_count, group):
    index = lax.axis_index("dp")
    core_bit, x_bit = group & 1, group & 2
    wide = jnp.float32
    came = swap_bit(partial, dp_count, 1, lambda i: i & 1 != core_bit)
    total = partial.astype(wide) + came.astype(wide)
    total = total.reshape((2, 2) + total.shape[1:])

    def on_core(i):
        return i & 1 == core_bit

    low = (index & 4) != 0
    sent = jnp.where(low, total[:, 0], total[:, 1]).astype(jnp.bfloat16)
    kept = jnp.where(low, total[:, 1], total[:, 0])
    total = kept + swap_bit(sent, dp_count, 4, on_core).astype(wide)
    high = (index & 8) != 0
    sent = jnp.where(high, total[0], total[1]).astype(jnp.bfloat16)
    kept = jnp.where(high, total[1], total[0])
    total = kept + swap_bit(sent, dp_count, 8, on_core).astype(wide)
    came = swap_bit(
        total.astype(jnp.bfloat16), dp_count, 2, lambda i: on_core(i) and i & 2 != x_bit
    )
    return total + came.astype(wide)


def paired_device(query_rows, key_rows, value_rows, windows, out_weight, gate_scale, out_grad):
    dp_count = HEADS
    seq_at = lax.axis_index("seq")
    place = seq_at.reshape(1).astype(jnp.int32)
    local_heads = HEADS // 2
    group_count = 4
    swap = [(0, 1), (1, 0)]
    bias = window_bias(windows)
    weight = lax.all_gather(out_weight, "dp", axis=0, tiled=True)
    weight = weight.reshape(4, 4, HEAD_DIM, weight.shape[1])
    gate_row = gate_scale[0].astype(jnp.float32)
    grad_proj = (out_grad.astype(jnp.float32) * gate_row).astype(jnp.bfloat16)

    others = []
    for g in range(group_count):
        picked = (g, g + 4)
        packed = pack_partner(place, local_heads, picked, query_rows, key_rows, value_rows)
        others.append(lax.ppermute(packed, "seq", swap))
    projected = None
    weight_grad = None
    owned = lax.axis_index("dp") & 3
    for g in range(group_count):
        mine = attend_pair(
            place, local_heads, (g, g + 4), query_rows, key_rows, value_rows, others[g], bias
        )
        theirs = lax.ppermute(mine, "seq", swap)
        columns = jnp.where(
            seq_at == 0,
            jnp.concatenate([mine, theirs], axis=1),
            jnp.concatenate([theirs, mine], axis=1),
        )
        partial = contract_tokens(columns, grad_proj, jnp.bfloat16)
        partial = partial.reshape(4, HEAD_DIM, partial.shape[1])
        reduced = reduce_group(partial, dp_count, g)
        weight_grad = reduced if g == 0 else jnp.where(owned == g, reduced, weight_grad)
        rows = weight[:, g].reshape(4 * HEAD_DIM, weight.shape[3])
        term = jnp.dot(columns, rows, preferred_element_type=jnp.float32)
        projected = term if g == 0 else projected + term
    block_out = (projected * gate_row).astype(jnp.bfloat16)
    return (block_out, weight_grad)


def general_device(query_rows, key_rows, value_rows, windows, out_weight, gate_scale, out_grad):
    query, key, value = (
        lax.all_to_all(rows, "seq", split_axis=1, concat_axis=0, tiled=True)
        for rows in (query_rows, key_rows, value_rows)
    )
    place = lax.axis_index("seq").reshape(1).astype(jnp.int32)
    mine = attend_whole(place, query, key, value, window_bias(windows))
    columns = lax.all_gather(mine, "seq", axis=1, tiled=True)
    weight = lax.all_gather(out_weight, "dp", axis=0, tiled=True)
    gate_row = gate_scale[0].astype(jnp.float32)
    projected = jnp.dot(columns, weight, preferred_element_type=jnp.float32)
    block_out = (projected * gate_row).astype(jnp.bfloat16)
    grad_proj = (out_grad.astype(jnp.float32) * gate_row).astype(jnp.bfloat16)
    weight_grad = lax.psum_scatter(
        contract_tokens(columns, grad_proj, jnp.float32), "dp", scatter_dimension=0, tiled=True
    )
    return (block_out, weight_grad)


def solution(mesh):
    paired = mesh.shape["seq"] == 2 and mesh.shape["dp"] == HEADS
    return jax.shard_map(
        paired_device if paired else general_device,
        mesh=mesh,
        in_specs=(
            P(("dp", "seq"), None),
            P(("dp", "seq"), None),
            P(("dp", "seq"), None),
            P(),
            P("dp", "seq"),
            P("dp", "seq"),
            P("dp", "seq"),
        ),
        out_specs=(P("dp", "seq"), P("dp", "seq")),
        check_vma=False,
    )
```

```python
import math

import jax
import jax.numpy as jnp
import numpy as np
from jax import lax
from jax.experimental import pallas as pl
from jax.experimental.pallas import tpu as pltpu
from jax.sharding import PartitionSpec as P

HEADS = 16
HEAD_DIM = 128
GH = 3
GW = 4
GT = 2
TILE = 48
NT = 24
CLIP_TOK = NT * TILE
Q_ROWS = GW * TILE
LOG2_SCALE = math.log2(math.e) / math.sqrt(HEAD_DIM)
VMEM_LIMIT = 24 * 1024 * 1024
VMEM_WHOLE = 60 * 1024 * 1024
SMALL_COST = pl.CostEstimate(flops=1, bytes_accessed=1, transcendentals=0)


def window_bias(windows):
    tile_id = np.arange(NT)
    coords = np.stack([tile_id // (GH * GW), tile_id // GW % GH, tile_id % GW]).astype(np.int32)
    token_coords = np.repeat(coords, TILE, axis=1)
    inside = None
    for axis_no, limit in enumerate((GT, GH, GW)):
        extent = jnp.minimum(windows[:, axis_no], limit)[:, None]
        start = jnp.clip(coords[axis_no][None, :] - (extent - 1) // 2, 0, limit - extent)
        column = token_coords[axis_no][None, None, :]
        here = (column >= start[:, :, None]) & (column < (start + extent)[:, :, None])
        inside = here if inside is None else inside & here
    return jnp.where(inside, 0.0, -jnp.inf).astype(jnp.float32)


def attend_rows(queries, first_tile, bias_ref, keys, values):
    count = queries.shape[0]
    tiles = count // TILE
    scores = lax.dot_general(
        queries, keys, (((1,), (1,)), ((), ())), preferred_element_type=jnp.float32
    )
    bias = bias_ref[0, first_tile : first_tile + tiles, :]
    scores = (scores.reshape(tiles, TILE, CLIP_TOK) + bias[:, None, :]).reshape(count, CLIP_TOK)
    peak = jnp.max(scores, axis=-1, keepdims=True)
    weights = jnp.exp2((scores - peak) * LOG2_SCALE).astype(jnp.bfloat16)
    blended = jnp.dot(weights, values, preferred_element_type=jnp.float32)
    return (blended[:, :HEAD_DIM] / blended[:, HEAD_DIM:]).astype(jnp.bfloat16)


def fill_values(values_ref, parts):
    at = 0
    for part in parts:
        rows = part.shape[0]
        values_ref[at : at + rows, :HEAD_DIM] = part
        at += rows
    values_ref[:, HEAD_DIM:] = jnp.ones((CLIP_TOK, HEAD_DIM), jnp.bfloat16)


def pair_kernel(place_ref, q_ref, k_ref, v_ref, other_ref, bias_ref, *rest):
    out_ref, keys_ref, values_ref = rest[-3:]
    half = CLIP_TOK // 2
    keys_ref[:half, :] = k_ref[...]
    keys_ref[half:, :] = other_ref[1]
    fill_values(values_ref, (v_ref[...], other_ref[2]))
    keys = keys_ref[...]
    values = values_ref[...]
    for side in range(2):
        base = pl.multiple_of((place_ref[0] if side == 0 else 1 - place_ref[0]) * half, half)
        for at in range(0, half, Q_ROWS):
            queries = q_ref[at : at + Q_ROWS, :] if side == 0 else other_ref[0, at : at + Q_ROWS, :]
            first_tile = (side * half + at) // TILE
            out_ref[pl.ds(base + at, Q_ROWS), :] = attend_rows(
                queries, first_tile, bias_ref, keys, values
            )


def whole_kernel(place_ref, q_ref, k_ref, v_ref, bias_ref, out_ref, values_ref):
    fill_values(values_ref, (v_ref[...],))
    keys = k_ref[...]
    values = values_ref[...]
    for at in range(0, CLIP_TOK, Q_ROWS):
        out_ref[at : at + Q_ROWS, :] = attend_rows(
            q_ref[at : at + Q_ROWS, :], at // TILE, bias_ref, keys, values
        )


def attention_cost(heads):
    pairs = heads * CLIP_TOK * CLIP_TOK
    return pl.CostEstimate(
        flops=pairs * HEAD_DIM * 6,
        bytes_accessed=heads * CLIP_TOK * HEAD_DIM * 8,
        transcendentals=pairs,
    )


def attend_pair(place, local_heads, picked, query, key, value, other, base, bias, earlier):
    half = CLIP_TOK // 2
    first, step = picked[0], picked[1] - picked[0] if len(picked) > 1 else 1

    def head(i, place_ref):
        return place_ref[0] * local_heads + first + step * i

    own = pl.BlockSpec((half, HEAD_DIM), lambda i, p: (0, head(i, p)))
    return pl.pallas_call(
        pair_kernel,
        grid_spec=pltpu.PrefetchScalarGridSpec(
            num_scalar_prefetch=1,
            grid=(len(picked),),
            in_specs=[
                own,
                own,
                own,
                pl.BlockSpec((3, half, HEAD_DIM), lambda i, p: (0, 0, base + i)),
                pl.BlockSpec((1, NT, CLIP_TOK), lambda i, p: (head(i, p), 0, 0)),
            ]
            + [pl.BlockSpec(memory_space=pl.ANY)] * len(earlier),
            out_specs=pl.BlockSpec((CLIP_TOK, HEAD_DIM), lambda i, p: (0, i)),
            scratch_shapes=[
                pltpu.VMEM((CLIP_TOK, HEAD_DIM), jnp.bfloat16),
                pltpu.VMEM((CLIP_TOK, 2 * HEAD_DIM), jnp.bfloat16),
            ],
        ),
        out_shape=jax.ShapeDtypeStruct((CLIP_TOK, len(picked) * HEAD_DIM), jnp.bfloat16),
        compiler_params=pltpu.CompilerParams(vmem_limit_bytes=VMEM_LIMIT),
        cost_estimate=SMALL_COST,
    )(place, query, key, value, other, bias, *earlier)


def attend_whole(place, query, key, value, bias):
    local_heads = query.shape[1] // HEAD_DIM
    column = pl.BlockSpec((CLIP_TOK, HEAD_DIM), lambda i, p: (0, i))
    return pl.pallas_call(
        whole_kernel,
        grid_spec=pltpu.PrefetchScalarGridSpec(
            num_scalar_prefetch=1,
            grid=(local_heads,),
            in_specs=[
                column,
                column,
                column,
                pl.BlockSpec((1, NT, CLIP_TOK), lambda i, p: (p[0] * local_heads + i, 0, 0)),
            ],
            out_specs=column,
            scratch_shapes=[pltpu.VMEM((CLIP_TOK, 2 * HEAD_DIM), jnp.bfloat16)],
        ),
        out_shape=jax.ShapeDtypeStruct(query.shape, jnp.bfloat16),
        compiler_params=pltpu.CompilerParams(vmem_limit_bytes=VMEM_LIMIT),
        cost_estimate=attention_cost(local_heads),
    )(place, query, key, value, bias)


def pack_kernel(place_ref, q_ref, k_ref, v_ref, *rest):
    out_ref = rest[-1]
    out_ref[0] = q_ref[...]
    out_ref[1] = k_ref[...]
    out_ref[2] = v_ref[...]


def pack_partner(place, local_heads, first, count, query, key, value, earlier, limit):
    rows = query.shape[0]

    def head(i, place_ref):
        return (1 - place_ref[0]) * local_heads + first + i // 2 + i % 2 * 4

    column = pl.BlockSpec((rows, HEAD_DIM), lambda i, p: (0, head(i, p)))
    return pl.pallas_call(
        pack_kernel,
        grid_spec=pltpu.PrefetchScalarGridSpec(
            num_scalar_prefetch=1,
            grid=(count,),
            in_specs=[column, column, column]
            + [pl.BlockSpec(memory_space=pl.ANY)] * len(earlier),
            out_specs=pl.BlockSpec((3, rows, HEAD_DIM), lambda i, p: (0, 0, i)),
        ),
        out_shape=jax.ShapeDtypeStruct((3, rows, count * HEAD_DIM), jnp.bfloat16),
        compiler_params=pltpu.CompilerParams(vmem_limit_bytes=limit),
        cost_estimate=SMALL_COST,
    )(place, query, key, value, *earlier)


def gradient_kernel(place_ref, mine_ref, theirs_ref, grad_ref, *rest):
    out_ref = rest[-1]
    heads = out_ref.shape[0] // 2
    columns = grad_ref.shape[1]
    step = columns // 3
    for source, side in ((mine_ref, place_ref[0]), (theirs_ref, 1 - place_ref[0])):
        for at in range(0, columns, step):
            product = lax.dot_general(
                source[...],
                grad_ref[:, at : at + step],
                (((0,), (0,)), ((), ())),
                preferred_element_type=jnp.float32,
            )
            product = product.reshape(heads, HEAD_DIM, step).astype(jnp.bfloat16)
            out_ref[pl.ds(side * heads, heads), :, at : at + step] = product


def group_gradient(place, mine, theirs, grad_proj, earlier):
    heads = 2 * mine.shape[1] // HEAD_DIM
    columns = grad_proj.shape[1]

    def whole(*shape):
        return pl.BlockSpec(shape, lambda i, p: (0,) * len(shape))

    return pl.pallas_call(
        gradient_kernel,
        grid_spec=pltpu.PrefetchScalarGridSpec(
            num_scalar_prefetch=1,
            grid=(1,),
            in_specs=[whole(*mine.shape), whole(*theirs.shape), whole(*grad_proj.shape)]
            + [pl.BlockSpec(memory_space=pl.ANY)] * len(earlier),
            out_specs=whole(heads, HEAD_DIM, columns),
        ),
        out_shape=jax.ShapeDtypeStruct((heads, HEAD_DIM, columns), jnp.bfloat16),
        compiler_params=pltpu.CompilerParams(vmem_limit_bytes=VMEM_LIMIT),
        cost_estimate=SMALL_COST,
    )(place, mine, theirs, grad_proj, *earlier)


def contract_tokens(columns, grad_proj, kind):
    return lax.dot_general(
        columns, grad_proj, (((0,), (0,)), ((), ())), preferred_element_type=jnp.float32
    ).astype(kind)


def after(value, *earlier):
    return lax.optimization_barrier((value,) + earlier)[0]


def by_place(place, table):
    picked = jnp.int32(0)
    for at, entry in enumerate(table):
        picked = jnp.where(place == at, jnp.int32(entry), picked)
    return picked


def on_core(i, group):
    return i & 1 == group & 1


def core_reduce(partial, group):
    pairs = [(i, i ^ 1) for i in range(HEADS) if not on_core(i, group)]
    return lax.ppermute(partial, "dp", pairs)


def x_blocks(partial, came):
    total = partial.astype(jnp.float32) + came.astype(jnp.float32)
    half = total.shape[2] // 2
    right = (lax.axis_index("dp") & 2) != 0
    kept = jnp.where(right, total[:, :, half:], total[:, :, :half])
    return kept, jnp.where(right, total[:, :, :half], total[:, :, half:]).astype(jnp.bfloat16)


def x_reduce(sent, group):
    return lax.ppermute(sent, "dp", [(i, i ^ 2) for i in range(HEADS) if on_core(i, group)])


def z_blocks(kept, came, levels):
    level = lax.axis_index("dp") // 4
    position = [levels.index(z) if z in levels else 0 for z in range(4)]

    def block(shift):
        at = by_place(level, [position[(z + shift) % 4] for z in range(4)])
        own = lax.dynamic_index_in_dim(kept, at, 0, keepdims=False)
        other = lax.dynamic_index_in_dim(came, at, 0, keepdims=False)
        return own + other.astype(jnp.float32)

    return block(0), [block(shift).astype(jnp.bfloat16) for shift in (1, 3, 2)]


def z_reduce(sent, group, levels):
    arrived = []
    for value, shift in zip(sent, (1, 3, 2)):
        pairs = [
            (z * 4 + low, (z + shift) % 4 * 4 + low)
            for z in range(4)
            if (z + shift) % 4 in levels
            for low in range(4)
            if on_core(low, group)
        ]
        arrived.append(lax.ppermute(value, "dp", pairs))
    return arrived


def finish_reduce(own, arrived, group):
    total = own
    for term in arrived:
        total = total + term.astype(jnp.float32)
    x_bit = group & 2
    pairs = [(i, i ^ 2) for i in range(HEADS) if on_core(i, group) and i & 2 != x_bit]
    came = lax.ppermute(total.astype(jnp.bfloat16), "dp", pairs).astype(jnp.float32)
    return jnp.concatenate([came, total] if x_bit else [total, came], axis=1)


def paired_device(query_rows, key_rows, value_rows, windows, out_weight, gate_scale, out_grad):
    seq_at = lax.axis_index("seq")
    place = seq_at.reshape(1).astype(jnp.int32)
    local_heads = HEADS // 2
    swap = [(0, 1), (1, 0)]
    groups = [
        (0, (0, 4), (0, 1, 2, 3)),
        (1, (1, 5), (0, 1, 2, 3)),
        (2, (2, 6), (0, 1, 2, 3)),
        (3, (3,), (0, 2)),
        (3, (7,), (1, 3)),
    ]
    bias = window_bias(windows)
    weight = lax.all_gather(out_weight, "dp", axis=0, tiled=True)
    weight = weight.reshape(HEADS, HEAD_DIM, weight.shape[1])
    gate_row = gate_scale[0].astype(jnp.float32)
    grad_proj = (out_grad.astype(jnp.float32) * gate_row).astype(jnp.bfloat16)
    sources = (query_rows, key_rows, value_rows)

    def pack(first, limit, *earlier):
        return pack_partner(place, local_heads, first, 2, *sources, earlier, limit)

    def attention(n, other, base, *earlier):
        return attend_pair(place, local_heads, groups[n][1], *sources, other, base, bias, earlier)

    def exchange(mine):
        return lax.ppermute(mine, "seq", swap)

    def join(mine, theirs):
        return jnp.where(
            seq_at == 0,
            jnp.concatenate([mine, theirs], axis=1),
            jnp.concatenate([theirs, mine], axis=1),
        )

    def gradient(mine, theirs, *earlier):
        return group_gradient(place, mine, theirs, grad_proj, earlier)

    def project(n, columns):
        group, _, levels = groups[n]
        rows = jnp.concatenate([weight[4 * z + group] for z in levels], axis=0)
        return jnp.dot(columns, rows, preferred_element_type=jnp.float32)

    packed0 = pack(0, VMEM_WHOLE)
    packed1 = pack(1, VMEM_WHOLE, packed0)
    packed2 = pack(2, VMEM_LIMIT, packed1)
    packed3 = pack(3, VMEM_LIMIT, packed2)
    other0 = exchange(packed0)
    other1 = exchange(packed1)
    other2 = exchange(packed2)
    other3 = exchange(packed3)
    mine0 = attention(0, other0, 0, packed3)
    theirs0 = exchange(mine0)
    mine1 = attention(1, other1, 0, mine0)
    theirs1 = exchange(mine1)
    mine2 = attention(2, other2, 0, mine1)
    theirs2 = exchange(mine2)
    mine3 = attention(3, other3, 0, mine2)
    theirs3 = exchange(mine3)
    mine4 = attention(4, other3, 1, mine3)
    theirs4 = exchange(mine4)
    partial0 = gradient(mine0, theirs0, mine4)
    partial1 = gradient(mine1, theirs1, partial0)
    core0 = core_reduce(partial0, 0)
    core1 = core_reduce(partial1, 1)
    kept0, sentx0 = x_blocks(partial0, after(core0, partial1))
    across0 = x_reduce(sentx0, 0)
    kept1, sentx1 = x_blocks(partial1, after(core1, partial1))
    across1 = x_reduce(sentx1, 1)
    partial2 = gradient(mine2, theirs2, sentx0, sentx1)
    core2 = core_reduce(partial2, 2)
    own0, sent0 = z_blocks(kept0, after(across0, partial2), groups[0][2])
    arrived0 = z_reduce(sent0, 0, groups[0][2])
    partial3 = gradient(mine3, theirs3, sent0[0])
    core3 = core_reduce(partial3, 3)
    own1, sent1 = z_blocks(kept1, after(across1, partial3), groups[1][2])
    arrived1 = z_reduce(sent1, 1, groups[1][2])
    kept2, sentx2 = x_blocks(partial2, after(core2, partial3))
    across2 = x_reduce(sentx2, 2)
    partial4 = gradient(mine4, theirs4, sent1[0], sentx2)
    core4 = core_reduce(partial4, 3)
    columns = [
        join(mine, theirs)
        for mine, theirs in (
            (mine0, theirs0),
            (mine1, theirs1),
            (mine2, theirs2),
            (mine3, theirs3),
            (mine4, theirs4),
        )
    ]
    kept3, sentx3 = x_blocks(partial3, after(core3, partial4))
    across3 = x_reduce(sentx3, 3)
    projected = project(0, after(columns[0], sentx3)) + project(1, columns[1])
    kept4, sentx4 = x_blocks(partial4, after(core4, projected))
    across4 = x_reduce(sentx4, 3)
    own2, sent2 = z_blocks(kept2, after(across2, sentx4), groups[2][2])
    arrived2 = z_reduce(sent2, 2, groups[2][2])
    own3, sent3 = z_blocks(kept3, after(across3, sent2[0]), groups[3][2])
    arrived3 = z_reduce(sent3, 3, groups[3][2])
    projected = projected + project(2, after(columns[2], sent3[0]))
    own4, sent4 = z_blocks(kept4, after(across4, projected), groups[4][2])
    arrived4 = z_reduce(sent4, 3, groups[4][2])
    projected = projected + project(3, after(columns[3], sent4[0])) + project(4, columns[4])
    block_out = (projected * gate_row).astype(jnp.bfloat16)
    final0 = finish_reduce(after(own0, partial4), arrived0, 0)
    final1 = finish_reduce(after(own1, partial4), arrived1, 1)
    final2 = finish_reduce(own2, arrived2, 2)
    final3 = finish_reduce(own3, arrived3, 3)
    final4 = finish_reduce(own4, arrived4, 3)
    index = lax.axis_index("dp")
    owned = index & 3
    weight_grad = jnp.where((index & 4) != 0, final4, final3)
    for n, final in ((2, final2), (1, final1), (0, final0)):
        weight_grad = jnp.where(owned == n, final, weight_grad)
    return (block_out, weight_grad)


def general_device(query_rows, key_rows, value_rows, windows, out_weight, gate_scale, out_grad):
    query, key, value = (
        lax.all_to_all(rows, "seq", split_axis=1, concat_axis=0, tiled=True)
        for rows in (query_rows, key_rows, value_rows)
    )
    place = lax.axis_index("seq").reshape(1).astype(jnp.int32)
    mine = attend_whole(place, query, key, value, window_bias(windows))
    columns = lax.all_gather(mine, "seq", axis=1, tiled=True)
    weight = lax.all_gather(out_weight, "dp", axis=0, tiled=True)
    gate_row = gate_scale[0].astype(jnp.float32)
    projected = jnp.dot(columns, weight, preferred_element_type=jnp.float32)
    block_out = (projected * gate_row).astype(jnp.bfloat16)
    grad_proj = (out_grad.astype(jnp.float32) * gate_row).astype(jnp.bfloat16)
    weight_grad = lax.psum_scatter(
        contract_tokens(columns, grad_proj, jnp.float32), "dp", scatter_dimension=0, tiled=True
    )
    return (block_out, weight_grad)


def solution(mesh):
    paired = mesh.shape["seq"] == 2 and mesh.shape["dp"] == HEADS
    return jax.shard_map(
        paired_device if paired else general_device,
        mesh=mesh,
        in_specs=(
            P(("dp", "seq"), None),
            P(("dp", "seq"), None),
            P(("dp", "seq"), None),
            P(),
            P("dp", "seq"),
            P("dp", "seq"),
            P("dp", "seq"),
        ),
        out_specs=(P("dp", "seq"), P("dp", "seq")),
        check_vma=False,
    )
```

```python
import math

import jax
import jax.numpy as jnp
import numpy as np
from jax import lax
from jax.experimental import pallas as pl
from jax.experimental.pallas import tpu as pltpu
from jax.sharding import PartitionSpec as P

HEADS = 16
HEAD_DIM = 128
GH = 3
GW = 4
GT = 2
TILE = 48
NT = 24
CLIP_TOK = NT * TILE
Q_ROWS = GW * TILE
LOG2_SCALE = math.log2(math.e) / math.sqrt(HEAD_DIM)
VMEM_LIMIT = 24 * 1024 * 1024
VMEM_WHOLE = 60 * 1024 * 1024
SMALL_COST = pl.CostEstimate(flops=1, bytes_accessed=1, transcendentals=0)


def window_bias(windows):
    tile_id = np.arange(NT)
    coords = np.stack([tile_id // (GH * GW), tile_id // GW % GH, tile_id % GW]).astype(np.int32)
    token_coords = np.repeat(coords, TILE, axis=1)
    inside = None
    for axis_no, limit in enumerate((GT, GH, GW)):
        extent = jnp.minimum(windows[:, axis_no], limit)[:, None]
        start = jnp.clip(coords[axis_no][None, :] - (extent - 1) // 2, 0, limit - extent)
        column = token_coords[axis_no][None, None, :]
        here = (column >= start[:, :, None]) & (column < (start + extent)[:, :, None])
        inside = here if inside is None else inside & here
    return jnp.where(inside, 0.0, -jnp.inf).astype(jnp.float32)


def attend_rows(queries, first_tile, bias_ref, keys, values):
    count = queries.shape[0]
    tiles = count // TILE
    scores = lax.dot_general(
        queries, keys, (((1,), (1,)), ((), ())), preferred_element_type=jnp.float32
    )
    bias = bias_ref[0, first_tile : first_tile + tiles, :]
    scores = (scores.reshape(tiles, TILE, CLIP_TOK) + bias[:, None, :]).reshape(count, CLIP_TOK)
    peak = jnp.max(scores, axis=-1, keepdims=True)
    weights = jnp.exp2((scores - peak) * LOG2_SCALE).astype(jnp.bfloat16)
    blended = jnp.dot(weights, values, preferred_element_type=jnp.float32)
    return (blended[:, :HEAD_DIM] / blended[:, HEAD_DIM:]).astype(jnp.bfloat16)


def fill_values(values_ref, parts):
    at = 0
    for part in parts:
        rows = part.shape[0]
        values_ref[at : at + rows, :HEAD_DIM] = part
        at += rows
    values_ref[:, HEAD_DIM:] = jnp.ones((CLIP_TOK, HEAD_DIM), jnp.bfloat16)


def pair_kernel(place_ref, q_ref, k_ref, v_ref, other_ref, bias_ref, *rest):
    out_ref, keys_ref, values_ref = rest[-3:]
    half = CLIP_TOK // 2
    keys_ref[:half, :] = k_ref[...]
    keys_ref[half:, :] = other_ref[1]
    fill_values(values_ref, (v_ref[...], other_ref[2]))
    keys = keys_ref[...]
    values = values_ref[...]
    for side in range(2):
        base = pl.multiple_of((place_ref[0] if side == 0 else 1 - place_ref[0]) * half, half)
        for at in range(0, half, Q_ROWS):
            queries = q_ref[at : at + Q_ROWS, :] if side == 0 else other_ref[0, at : at + Q_ROWS, :]
            first_tile = (side * half + at) // TILE
            out_ref[pl.ds(base + at, Q_ROWS), :] = attend_rows(
                queries, first_tile, bias_ref, keys, values
            )


def whole_kernel(place_ref, q_ref, k_ref, v_ref, bias_ref, out_ref, values_ref):
    fill_values(values_ref, (v_ref[...],))
    keys = k_ref[...]
    values = values_ref[...]
    for at in range(0, CLIP_TOK, Q_ROWS):
        out_ref[at : at + Q_ROWS, :] = attend_rows(
            q_ref[at : at + Q_ROWS, :], at // TILE, bias_ref, keys, values
        )


def attention_cost(heads):
    pairs = heads * CLIP_TOK * CLIP_TOK
    return pl.CostEstimate(
        flops=pairs * HEAD_DIM * 6,
        bytes_accessed=heads * CLIP_TOK * HEAD_DIM * 8,
        transcendentals=pairs,
    )


def attend_pair(place, local_heads, picked, query, key, value, other, base, bias, earlier):
    half = CLIP_TOK // 2
    first, step = picked[0], picked[1] - picked[0] if len(picked) > 1 else 1

    def head(i, place_ref):
        return place_ref[0] * local_heads + first + step * i

    own = pl.BlockSpec((half, HEAD_DIM), lambda i, p: (0, head(i, p)))
    return pl.pallas_call(
        pair_kernel,
        grid_spec=pltpu.PrefetchScalarGridSpec(
            num_scalar_prefetch=1,
            grid=(len(picked),),
            in_specs=[
                own,
                own,
                own,
                pl.BlockSpec((3, half, HEAD_DIM), lambda i, p: (0, 0, base + i)),
                pl.BlockSpec((1, NT, CLIP_TOK), lambda i, p: (head(i, p), 0, 0)),
            ]
            + [pl.BlockSpec(memory_space=pl.ANY)] * len(earlier),
            out_specs=pl.BlockSpec((CLIP_TOK, HEAD_DIM), lambda i, p: (0, i)),
            scratch_shapes=[
                pltpu.VMEM((CLIP_TOK, HEAD_DIM), jnp.bfloat16),
                pltpu.VMEM((CLIP_TOK, 2 * HEAD_DIM), jnp.bfloat16),
            ],
        ),
        out_shape=jax.ShapeDtypeStruct((CLIP_TOK, len(picked) * HEAD_DIM), jnp.bfloat16),
        compiler_params=pltpu.CompilerParams(vmem_limit_bytes=VMEM_LIMIT),
        cost_estimate=SMALL_COST,
    )(place, query, key, value, other, bias, *earlier)


def attend_whole(place, query, key, value, bias):
    local_heads = query.shape[1] // HEAD_DIM
    column = pl.BlockSpec((CLIP_TOK, HEAD_DIM), lambda i, p: (0, i))
    return pl.pallas_call(
        whole_kernel,
        grid_spec=pltpu.PrefetchScalarGridSpec(
            num_scalar_prefetch=1,
            grid=(local_heads,),
            in_specs=[
                column,
                column,
                column,
                pl.BlockSpec((1, NT, CLIP_TOK), lambda i, p: (p[0] * local_heads + i, 0, 0)),
            ],
            out_specs=column,
            scratch_shapes=[pltpu.VMEM((CLIP_TOK, 2 * HEAD_DIM), jnp.bfloat16)],
        ),
        out_shape=jax.ShapeDtypeStruct(query.shape, jnp.bfloat16),
        compiler_params=pltpu.CompilerParams(vmem_limit_bytes=VMEM_LIMIT),
        cost_estimate=attention_cost(local_heads),
    )(place, query, key, value, bias)


def pack_kernel(place_ref, q_ref, k_ref, v_ref, *rest):
    out_ref = rest[-1]
    out_ref[0] = q_ref[...]
    out_ref[1] = k_ref[...]
    out_ref[2] = v_ref[...]


def pack_partner(place, local_heads, first, count, query, key, value, earlier, limit):
    rows = query.shape[0]

    def head(i, place_ref):
        return (1 - place_ref[0]) * local_heads + first + i // 2 + i % 2 * 4

    column = pl.BlockSpec((rows, HEAD_DIM), lambda i, p: (0, head(i, p)))
    return pl.pallas_call(
        pack_kernel,
        grid_spec=pltpu.PrefetchScalarGridSpec(
            num_scalar_prefetch=1,
            grid=(count,),
            in_specs=[column, column, column]
            + [pl.BlockSpec(memory_space=pl.ANY)] * len(earlier),
            out_specs=pl.BlockSpec((3, rows, HEAD_DIM), lambda i, p: (0, 0, i)),
        ),
        out_shape=jax.ShapeDtypeStruct((3, rows, count * HEAD_DIM), jnp.bfloat16),
        compiler_params=pltpu.CompilerParams(vmem_limit_bytes=limit),
        cost_estimate=SMALL_COST,
    )(place, query, key, value, *earlier)


def gradient_kernel(place_ref, mine_ref, theirs_ref, grad_ref, *rest):
    out_ref = rest[-1]
    heads = out_ref.shape[0] // 2
    columns = grad_ref.shape[1]
    step = columns // 3
    for source, side in ((mine_ref, place_ref[0]), (theirs_ref, 1 - place_ref[0])):
        for at in range(0, columns, step):
            product = lax.dot_general(
                source[...],
                grad_ref[:, at : at + step],
                (((0,), (0,)), ((), ())),
                preferred_element_type=jnp.float32,
            )
            product = product.reshape(heads, HEAD_DIM, step).astype(jnp.bfloat16)
            out_ref[pl.ds(side * heads, heads), :, at : at + step] = product


def group_gradient(place, mine, theirs, grad_proj, earlier):
    heads = 2 * mine.shape[1] // HEAD_DIM
    columns = grad_proj.shape[1]

    def whole(*shape):
        return pl.BlockSpec(shape, lambda i, p: (0,) * len(shape))

    return pl.pallas_call(
        gradient_kernel,
        grid_spec=pltpu.PrefetchScalarGridSpec(
            num_scalar_prefetch=1,
            grid=(1,),
            in_specs=[whole(*mine.shape), whole(*theirs.shape), whole(*grad_proj.shape)]
            + [pl.BlockSpec(memory_space=pl.ANY)] * len(earlier),
            out_specs=whole(heads, HEAD_DIM, columns),
        ),
        out_shape=jax.ShapeDtypeStruct((heads, HEAD_DIM, columns), jnp.bfloat16),
        compiler_params=pltpu.CompilerParams(vmem_limit_bytes=VMEM_LIMIT),
        cost_estimate=SMALL_COST,
    )(place, mine, theirs, grad_proj, *earlier)


def contract_tokens(columns, grad_proj, kind):
    return lax.dot_general(
        columns, grad_proj, (((0,), (0,)), ((), ())), preferred_element_type=jnp.float32
    ).astype(kind)


def after(value, *earlier):
    return lax.optimization_barrier((value,) + earlier)[0]


def by_place(place, table):
    picked = jnp.int32(0)
    for at, entry in enumerate(table):
        picked = jnp.where(place == at, jnp.int32(entry), picked)
    return picked


def to_owners(pieces):
    at = lax.axis_index("dp") & 3
    stacked = jnp.stack(pieces)
    quarters = [lax.dynamic_index_in_dim(stacked, at, 0, keepdims=False)]
    for flip in (1, 2, 3):
        sent = lax.dynamic_index_in_dim(stacked, at ^ flip, 0, keepdims=False)
        quarters.append(lax.ppermute(sent, "dp", [(i, i ^ flip) for i in range(HEADS)]))
    ordered = []
    for place in range(4):
        block = quarters[0]
        for flip in (1, 2, 3):
            block = jnp.where(at ^ flip == place, quarters[flip], block)
        ordered.append(block.astype(jnp.float32))
    return jnp.concatenate(ordered, axis=0)


def paired_device(query_rows, key_rows, value_rows, windows, out_weight, gate_scale, out_grad):
    seq_at = lax.axis_index("seq")
    place = seq_at.reshape(1).astype(jnp.int32)
    local_heads = HEADS // 2
    swap = [(0, 1), (1, 0)]
    bias = window_bias(windows)
    weight = lax.all_gather(out_weight, "dp", axis=0, tiled=True)
    weight = weight.reshape(HEADS, HEAD_DIM, weight.shape[1])
    gate_row = gate_scale[0].astype(jnp.float32)
    grad_proj = (out_grad.astype(jnp.float32) * gate_row).astype(jnp.bfloat16)
    sources = (query_rows, key_rows, value_rows)

    def pack(g, limit, *earlier):
        return pack_partner(place, local_heads, g, 2, *sources, earlier, limit)

    def attention(g, other, *earlier):
        return attend_pair(place, local_heads, (g, g + 4), *sources, other, 0, bias, earlier)

    def exchange(mine):
        return lax.ppermute(mine, "seq", swap)

    def join(mine, theirs):
        return jnp.where(
            seq_at == 0,
            jnp.concatenate([mine, theirs], axis=1),
            jnp.concatenate([theirs, mine], axis=1),
        )

    def gradient(mine, theirs, *earlier):
        rows = group_gradient(place, mine, theirs, grad_proj, earlier)
        return rows.reshape(-1, rows.shape[2])

    def reduce(partial):
        return lax.psum_scatter(partial, "dp", scatter_dimension=0, tiled=True)

    def project(g, columns):
        rows = jnp.concatenate([weight[4 * z + g] for z in range(4)], axis=0)
        return jnp.dot(columns, rows, preferred_element_type=jnp.float32)

    packed0 = pack(0, VMEM_WHOLE)
    packed1 = pack(1, VMEM_WHOLE, packed0)
    other0 = exchange(packed0)
    other1 = exchange(packed1)
    mine0 = attention(0, other0, packed1)
    theirs0 = exchange(mine0)
    packed2 = pack(2, VMEM_LIMIT, mine0)
    other2 = exchange(packed2)
    mine1 = attention(1, other1, packed2)
    theirs1 = exchange(mine1)
    packed3 = pack(3, VMEM_LIMIT, mine1)
    other3 = exchange(packed3)
    mine2 = attention(2, other2, mine1, packed3)
    theirs2 = exchange(mine2)
    partial0 = gradient(mine0, theirs0, mine2)
    reduced0 = reduce(partial0)
    partial1 = gradient(mine1, theirs1, partial0)
    reduced1 = reduce(partial1)
    mine3 = attention(3, other3, partial1)
    theirs3 = exchange(mine3)
    columns0 = join(mine0, theirs0)
    columns1 = join(mine1, theirs1)
    projected = project(0, after(columns0, mine3)) + project(1, columns1)
    partial2 = gradient(mine2, theirs2, projected)
    reduced2 = reduce(partial2)
    columns2 = join(mine2, after(theirs2, partial2))
    projected = projected + project(2, columns2)
    partial3 = gradient(mine3, theirs3, partial2)
    reduced3 = reduce(partial3)
    columns3 = join(mine3, after(theirs3, partial3))
    projected = projected + project(3, columns3)
    block_out = (projected * gate_row).astype(jnp.bfloat16)
    weight_grad = to_owners([reduced0, reduced1, reduced2, reduced3])
    return (block_out, weight_grad)


def general_device(query_rows, key_rows, value_rows, windows, out_weight, gate_scale, out_grad):
    query, key, value = (
        lax.all_to_all(rows, "seq", split_axis=1, concat_axis=0, tiled=True)
        for rows in (query_rows, key_rows, value_rows)
    )
    place = lax.axis_index("seq").reshape(1).astype(jnp.int32)
    mine = attend_whole(place, query, key, value, window_bias(windows))
    columns = lax.all_gather(mine, "seq", axis=1, tiled=True)
    weight = lax.all_gather(out_weight, "dp", axis=0, tiled=True)
    gate_row = gate_scale[0].astype(jnp.float32)
    projected = jnp.dot(columns, weight, preferred_element_type=jnp.float32)
    block_out = (projected * gate_row).astype(jnp.bfloat16)
    grad_proj = (out_grad.astype(jnp.float32) * gate_row).astype(jnp.bfloat16)
    weight_grad = lax.psum_scatter(
        contract_tokens(columns, grad_proj, jnp.float32), "dp", scatter_dimension=0, tiled=True
    )
    return (block_out, weight_grad)


def solution(mesh):
    paired = mesh.shape["seq"] == 2 and mesh.shape["dp"] == HEADS
    return jax.shard_map(
        paired_device if paired else general_device,
        mesh=mesh,
        in_specs=(
            P(("dp", "seq"), None),
            P(("dp", "seq"), None),
            P(("dp", "seq"), None),
            P(),
            P("dp", "seq"),
            P("dp", "seq"),
            P("dp", "seq"),
        ),
        out_specs=(P("dp", "seq"), P("dp", "seq")),
        check_vma=False,
    )
```

```python
import math

import jax
import jax.numpy as jnp
import numpy as np
from jax import lax
from jax.experimental import pallas as pl
from jax.experimental.pallas import tpu as pltpu
from jax.sharding import PartitionSpec as P

HEADS = 16
HEAD_DIM = 128
GH = 3
GW = 4
GT = 2
TILE = 48
NT = 24
CLIP_TOK = NT * TILE
Q_ROWS = GW * TILE
LOG2_SCALE = math.log2(math.e) / math.sqrt(HEAD_DIM)
VMEM_LIMIT = 24 * 1024 * 1024
VMEM_WHOLE = 60 * 1024 * 1024
SMALL_COST = pl.CostEstimate(flops=1, bytes_accessed=1, transcendentals=0)


def window_bias(windows):
    tile_id = np.arange(NT)
    coords = np.stack([tile_id // (GH * GW), tile_id // GW % GH, tile_id % GW]).astype(np.int32)
    token_coords = np.repeat(coords, TILE, axis=1)
    inside = None
    for axis_no, limit in enumerate((GT, GH, GW)):
        extent = jnp.minimum(windows[:, axis_no], limit)[:, None]
        start = jnp.clip(coords[axis_no][None, :] - (extent - 1) // 2, 0, limit - extent)
        column = token_coords[axis_no][None, None, :]
        here = (column >= start[:, :, None]) & (column < (start + extent)[:, :, None])
        inside = here if inside is None else inside & here
    return jnp.where(inside, 0.0, -jnp.inf).astype(jnp.float32)


def attend_rows(queries, first_tile, bias_ref, keys, values):
    count = queries.shape[0]
    tiles = count // TILE
    scores = lax.dot_general(
        queries, keys, (((1,), (1,)), ((), ())), preferred_element_type=jnp.float32
    )
    bias = bias_ref[0, first_tile : first_tile + tiles, :]
    scores = (scores.reshape(tiles, TILE, CLIP_TOK) + bias[:, None, :]).reshape(count, CLIP_TOK)
    peak = jnp.max(scores, axis=-1, keepdims=True)
    weights = jnp.exp2((scores - peak) * LOG2_SCALE).astype(jnp.bfloat16)
    blended = jnp.dot(weights, values, preferred_element_type=jnp.float32)
    return (blended[:, :HEAD_DIM] / blended[:, HEAD_DIM:]).astype(jnp.bfloat16)


def fill_values(values_ref, parts):
    at = 0
    for part in parts:
        rows = part.shape[0]
        values_ref[at : at + rows, :HEAD_DIM] = part
        at += rows
    values_ref[:, HEAD_DIM:] = jnp.ones((CLIP_TOK, HEAD_DIM), jnp.bfloat16)


def pair_kernel(place_ref, q_ref, k_ref, v_ref, other_ref, bias_ref, *rest):
    out_ref, keys_ref, values_ref = rest[-3:]
    half = CLIP_TOK // 2
    keys_ref[:half, :] = k_ref[...]
    keys_ref[half:, :] = other_ref[1]
    fill_values(values_ref, (v_ref[...], other_ref[2]))
    keys = keys_ref[...]
    values = values_ref[...]
    for side in range(2):
        base = pl.multiple_of((place_ref[0] if side == 0 else 1 - place_ref[0]) * half, half)
        for at in range(0, half, Q_ROWS):
            queries = q_ref[at : at + Q_ROWS, :] if side == 0 else other_ref[0, at : at + Q_ROWS, :]
            first_tile = (side * half + at) // TILE
            out_ref[pl.ds(base + at, Q_ROWS), :] = attend_rows(
                queries, first_tile, bias_ref, keys, values
            )


def whole_kernel(place_ref, q_ref, k_ref, v_ref, bias_ref, out_ref, values_ref):
    fill_values(values_ref, (v_ref[...],))
    keys = k_ref[...]
    values = values_ref[...]
    for at in range(0, CLIP_TOK, Q_ROWS):
        out_ref[at : at + Q_ROWS, :] = attend_rows(
            q_ref[at : at + Q_ROWS, :], at // TILE, bias_ref, keys, values
        )


def attention_cost(heads):
    pairs = heads * CLIP_TOK * CLIP_TOK
    return pl.CostEstimate(
        flops=pairs * HEAD_DIM * 6,
        bytes_accessed=heads * CLIP_TOK * HEAD_DIM * 8,
        transcendentals=pairs,
    )


def attend_pair(place, local_heads, picked, query, key, value, other, bias, earlier):
    half = CLIP_TOK // 2
    first, step = picked[0], picked[1] - picked[0]

    def head(i, place_ref):
        return place_ref[0] * local_heads + first + step * i

    own = pl.BlockSpec((half, HEAD_DIM), lambda i, p: (0, head(i, p)))
    return pl.pallas_call(
        pair_kernel,
        grid_spec=pltpu.PrefetchScalarGridSpec(
            num_scalar_prefetch=1,
            grid=(len(picked),),
            in_specs=[
                own,
                own,
                own,
                pl.BlockSpec((3, half, HEAD_DIM), lambda i, p: (0, 0, i)),
                pl.BlockSpec((1, NT, CLIP_TOK), lambda i, p: (head(i, p), 0, 0)),
            ]
            + [pl.BlockSpec(memory_space=pl.ANY)] * len(earlier),
            out_specs=pl.BlockSpec((CLIP_TOK, HEAD_DIM), lambda i, p: (0, i)),
            scratch_shapes=[
                pltpu.VMEM((CLIP_TOK, HEAD_DIM), jnp.bfloat16),
                pltpu.VMEM((CLIP_TOK, 2 * HEAD_DIM), jnp.bfloat16),
            ],
        ),
        out_shape=jax.ShapeDtypeStruct((CLIP_TOK, len(picked) * HEAD_DIM), jnp.bfloat16),
        compiler_params=pltpu.CompilerParams(vmem_limit_bytes=VMEM_LIMIT),
        cost_estimate=SMALL_COST,
    )(place, query, key, value, other, bias, *earlier)


def attend_whole(place, query, key, value, bias):
    local_heads = query.shape[1] // HEAD_DIM
    column = pl.BlockSpec((CLIP_TOK, HEAD_DIM), lambda i, p: (0, i))
    return pl.pallas_call(
        whole_kernel,
        grid_spec=pltpu.PrefetchScalarGridSpec(
            num_scalar_prefetch=1,
            grid=(local_heads,),
            in_specs=[
                column,
                column,
                column,
                pl.BlockSpec((1, NT, CLIP_TOK), lambda i, p: (p[0] * local_heads + i, 0, 0)),
            ],
            out_specs=column,
            scratch_shapes=[pltpu.VMEM((CLIP_TOK, 2 * HEAD_DIM), jnp.bfloat16)],
        ),
        out_shape=jax.ShapeDtypeStruct(query.shape, jnp.bfloat16),
        compiler_params=pltpu.CompilerParams(vmem_limit_bytes=VMEM_LIMIT),
        cost_estimate=attention_cost(local_heads),
    )(place, query, key, value, bias)


def pack_kernel(place_ref, q_ref, k_ref, v_ref, *rest):
    out_ref = rest[-1]
    out_ref[0] = q_ref[...]
    out_ref[1] = k_ref[...]
    out_ref[2] = v_ref[...]


def pack_partner(place, local_heads, picked, query, key, value, earlier, limit):
    rows = query.shape[0]
    count = len(picked)
    first, step = picked[0], picked[1] - picked[0]

    def head(i, place_ref):
        return (1 - place_ref[0]) * local_heads + first + step * i

    column = pl.BlockSpec((rows, HEAD_DIM), lambda i, p: (0, head(i, p)))
    return pl.pallas_call(
        pack_kernel,
        grid_spec=pltpu.PrefetchScalarGridSpec(
            num_scalar_prefetch=1,
            grid=(count,),
            in_specs=[column, column, column]
            + [pl.BlockSpec(memory_space=pl.ANY)] * len(earlier),
            out_specs=pl.BlockSpec((3, rows, HEAD_DIM), lambda i, p: (0, 0, i)),
        ),
        out_shape=jax.ShapeDtypeStruct((3, rows, count * HEAD_DIM), jnp.bfloat16),
        compiler_params=pltpu.CompilerParams(vmem_limit_bytes=limit),
        cost_estimate=SMALL_COST,
    )(place, query, key, value, *earlier)


def gradient_kernel(place_ref, mine_ref, theirs_ref, grad_ref, *rest):
    out_ref = rest[-1]
    heads = out_ref.shape[0] // 2
    columns = grad_ref.shape[1]
    step = columns // 3
    for source, side in ((mine_ref, place_ref[0]), (theirs_ref, 1 - place_ref[0])):
        for at in range(0, columns, step):
            product = lax.dot_general(
                source[...],
                grad_ref[:, at : at + step],
                (((0,), (0,)), ((), ())),
                preferred_element_type=jnp.float32,
            )
            product = product.reshape(heads, HEAD_DIM, step).astype(jnp.bfloat16)
            out_ref[pl.ds(side * heads, heads), :, at : at + step] = product


def head_gradient(place, mine, theirs, grad_proj, width, earlier=()):
    heads = 2 * width // HEAD_DIM
    rows, columns = grad_proj.shape
    taken = pl.BlockSpec((rows, width), lambda i, p: (0, p[1]))
    return pl.pallas_call(
        gradient_kernel,
        grid_spec=pltpu.PrefetchScalarGridSpec(
            num_scalar_prefetch=1,
            grid=(1,),
            in_specs=[taken, taken, pl.BlockSpec((rows, columns), lambda i, p: (0, 0))]
            + [pl.BlockSpec(memory_space=pl.ANY)] * len(earlier),
            out_specs=pl.BlockSpec((heads, HEAD_DIM, columns), lambda i, p: (0, 0, 0)),
        ),
        out_shape=jax.ShapeDtypeStruct((heads, HEAD_DIM, columns), jnp.bfloat16),
        compiler_params=pltpu.CompilerParams(vmem_limit_bytes=VMEM_LIMIT),
        cost_estimate=SMALL_COST,
    )(place, mine, theirs, grad_proj, *earlier)


def contract_tokens(columns, grad_proj, kind):
    return lax.dot_general(
        columns, grad_proj, (((0,), (0,)), ((), ())), preferred_element_type=jnp.float32
    ).astype(kind)


def after(value, *earlier):
    return lax.optimization_barrier((value,) + earlier)[0]


def dp_send(value, flip, sender):
    return lax.ppermute(value, "dp", [(i, i ^ flip) for i in range(HEADS) if sender(i)])


def same_bits(i):
    return (i >> 1 ^ i) & 1 == 0


def core_step(sent, kept, seq_at, grad_proj, earlier):
    def rows(picked, earlier):
        mine, theirs, width, column = picked
        place = jnp.stack([seq_at, column]).astype(jnp.int32)
        return head_gradient(place, mine, theirs, grad_proj, width, earlier)

    going = rows(sent, earlier)
    came = dp_send(going, 1, lambda i: True)
    staying = rows(kept, (going,))
    total = (staying.astype(jnp.float32) + came.astype(jnp.float32)).astype(jnp.bfloat16)
    return staying, came, total


def chip_sum(staying, came, across):
    return staying.astype(jnp.float32) + came.astype(jnp.float32) + across.astype(jnp.float32)


def split_level(total, bit):
    upper = (lax.axis_index("dp") & bit) != 0
    kept = jnp.where(upper, total[1], total[0])
    return kept, jnp.where(upper, total[0], total[1]).astype(jnp.bfloat16)


def paired_device(query_rows, key_rows, value_rows, windows, out_weight, gate_scale, out_grad):
    seq_at = lax.axis_index("seq")
    place = seq_at.reshape(1).astype(jnp.int32)
    local_heads = HEADS // 2
    swap = [(0, 1), (1, 0)]
    calls = [(0, 4), (3, 7), (1, 2), (5, 6)]
    bias = window_bias(windows)
    weight = lax.all_gather(out_weight, "dp", axis=0, tiled=True)
    weight = weight.reshape(HEADS, HEAD_DIM, weight.shape[1])
    gate_row = gate_scale[0].astype(jnp.float32)
    grad_proj = (out_grad.astype(jnp.float32) * gate_row).astype(jnp.bfloat16)
    sources = (query_rows, key_rows, value_rows)

    def pack(n, limit, *earlier):
        return pack_partner(place, local_heads, calls[n], *sources, earlier, limit)

    def attention(n, other, *earlier):
        return attend_pair(place, local_heads, calls[n], *sources, other, bias, earlier)

    def exchange(mine):
        return lax.ppermute(mine, "seq", swap)

    def project(n, mine, theirs):
        columns = jnp.where(
            seq_at == 0,
            jnp.concatenate([mine, theirs], axis=1),
            jnp.concatenate([theirs, mine], axis=1),
        )
        rows = [weight[side * local_heads + head] for side in range(2) for head in calls[n]]
        rows = jnp.concatenate(rows, axis=0)
        return jnp.dot(columns, rows, preferred_element_type=jnp.float32)

    index = lax.axis_index("dp")
    core = index & 1

    def chip_sums_all_z(mine0, theirs0, mine1, theirs1, grad_proj):
        first = core == 0
        sent = (jnp.where(first, mine1, mine0), jnp.where(first, theirs1, theirs0), 2 * HEAD_DIM, 0)
        kept = (jnp.where(first, mine0, mine1), jnp.where(first, theirs0, theirs1), 2 * HEAD_DIM, 0)
        stayed, came, total = core_step(sent, kept, seq_at, grad_proj, ())
        across = dp_send(total, 2, lambda i: not same_bits(i))
        level = chip_sum(stayed, came, across)
        return split_level(level.reshape((2, 2) + level.shape[1:]).swapaxes(0, 1), 4)

    def core_step_half_z(mine, theirs, grad_proj, *earlier):
        return core_step(
            (mine, theirs, HEAD_DIM, core), (mine, theirs, HEAD_DIM, 1 - core), seq_at, grad_proj, earlier
        )

    def apart(step, *operands):
        shapes = jax.eval_shape(step, *operands)
        return lax.cond(
            windows[0, 0] > 0,
            step,
            lambda *_: jax.tree.map(lambda leaf: jnp.zeros(leaf.shape, leaf.dtype), shapes),
            *operands,
        )

    packed0 = pack(0, VMEM_WHOLE)
    packed1 = pack(1, VMEM_WHOLE, packed0)
    packed2 = pack(2, VMEM_LIMIT, packed1)
    packed3 = pack(3, VMEM_LIMIT, packed2)
    other0 = exchange(packed0)
    other1 = exchange(packed1)
    other2 = exchange(packed2)
    other3 = exchange(packed3)
    mine0 = attention(0, other0, packed3)
    theirs0 = exchange(mine0)
    mine1 = attention(1, other1, mine0)
    theirs1 = exchange(mine1)
    mine2 = attention(2, other2, mine1)
    theirs2 = exchange(mine2)
    mine3 = attention(3, other3, mine2)
    theirs3 = exchange(mine3)

    kept_a, sent_a = apart(
        chip_sums_all_z, after(mine0, mine3), theirs0, mine1, theirs1, grad_proj
    )
    low_a = dp_send(sent_a, 4, same_bits)
    stayed_b, came_b, total_b = core_step_half_z(mine2, theirs2, grad_proj, sent_a, theirs3)
    across_b = dp_send(total_b, 2, same_bits)
    stayed_c, came_c, total_c = core_step_half_z(mine3, theirs3, grad_proj, stayed_b)
    across_c = dp_send(total_c, 2, same_bits)

    projected = project(0, after(mine0, total_c), theirs0) + project(1, mine1, theirs1)
    kept_b = chip_sum(stayed_b, came_b, after(across_b, total_c))
    low_b = dp_send(kept_b.astype(jnp.bfloat16), 4, lambda i: not same_bits(i) and i & 4 != 0)
    kept_a, sent_a = split_level(kept_a + after(low_a, total_c).astype(jnp.float32), 8)
    high_a = dp_send(sent_a, 8, same_bits)
    kept_c = chip_sum(stayed_c, came_c, after(across_c, projected, sent_a))
    low_c = dp_send(kept_c.astype(jnp.bfloat16), 4, lambda i: not same_bits(i) and i & 4 == 0)
    kept_b, sent_b = split_level(kept_b + low_b.astype(jnp.float32), 8)
    high_b = dp_send(sent_b, 8, lambda i: not same_bits(i) and i & 4 == 0)
    projected = projected + project(2, after(mine2, sent_b, kept_c), theirs2)
    kept_c, sent_c = split_level(kept_c + after(low_c, projected).astype(jnp.float32), 8)
    high_c = dp_send(sent_c, 8, lambda i: not same_bits(i) and i & 4 != 0)
    projected = projected + project(3, after(mine3, sent_c), theirs3)
    block_out = (projected * gate_row).astype(jnp.bfloat16)
    weight_grad = jnp.where(
        same_bits(index),
        kept_a + high_a.astype(jnp.float32),
        jnp.where(
            (index & 4) == 0,
            kept_b + high_b.astype(jnp.float32),
            kept_c + high_c.astype(jnp.float32),
        ),
    )
    return (block_out, weight_grad)


def general_device(query_rows, key_rows, value_rows, windows, out_weight, gate_scale, out_grad):
    query, key, value = (
        lax.all_to_all(rows, "seq", split_axis=1, concat_axis=0, tiled=True)
        for rows in (query_rows, key_rows, value_rows)
    )
    place = lax.axis_index("seq").reshape(1).astype(jnp.int32)
    mine = attend_whole(place, query, key, value, window_bias(windows))
    columns = lax.all_gather(mine, "seq", axis=1, tiled=True)
    weight = lax.all_gather(out_weight, "dp", axis=0, tiled=True)
    gate_row = gate_scale[0].astype(jnp.float32)
    projected = jnp.dot(columns, weight, preferred_element_type=jnp.float32)
    block_out = (projected * gate_row).astype(jnp.bfloat16)
    grad_proj = (out_grad.astype(jnp.float32) * gate_row).astype(jnp.bfloat16)
    weight_grad = lax.psum_scatter(
        contract_tokens(columns, grad_proj, jnp.float32), "dp", scatter_dimension=0, tiled=True
    )
    return (block_out, weight_grad)


def solution(mesh):
    paired = mesh.shape["seq"] == 2 and mesh.shape["dp"] == HEADS
    return jax.shard_map(
        paired_device if paired else general_device,
        mesh=mesh,
        in_specs=(
            P(("dp", "seq"), None),
            P(("dp", "seq"), None),
            P(("dp", "seq"), None),
            P(),
            P("dp", "seq"),
            P("dp", "seq"),
            P("dp", "seq"),
        ),
        out_specs=(P("dp", "seq"), P("dp", "seq")),
        check_vma=False,
    )
```

```python
import functools
import math

import jax
import jax.numpy as jnp
import numpy as np
from jax import lax
from jax.experimental import pallas as pl
from jax.experimental.pallas import tpu as pltpu
from jax.sharding import PartitionSpec as P

HEADS = 16
HEAD_DIM = 128
GH = 3
GW = 4
GT = 2
TILE = 48
NT = 24
CLIP_TOK = NT * TILE
Q_ROWS = GW * TILE
LOG2_SCALE = math.log2(math.e) / math.sqrt(HEAD_DIM)
VMEM_LIMIT = 24 * 1024 * 1024
VMEM_WHOLE = 60 * 1024 * 1024
SMALL_COST = pl.CostEstimate(flops=1, bytes_accessed=1, transcendentals=0)


def window_bias(windows):
    tile_id = np.arange(NT)
    coords = np.stack([tile_id // (GH * GW), tile_id // GW % GH, tile_id % GW]).astype(np.int32)
    token_coords = np.repeat(coords, TILE, axis=1)
    inside = None
    for axis_no, limit in enumerate((GT, GH, GW)):
        extent = jnp.minimum(windows[:, axis_no], limit)[:, None]
        start = jnp.clip(coords[axis_no][None, :] - (extent - 1) // 2, 0, limit - extent)
        column = token_coords[axis_no][None, None, :]
        here = (column >= start[:, :, None]) & (column < (start + extent)[:, :, None])
        inside = here if inside is None else inside & here
    return jnp.where(inside, 0.0, -jnp.inf).astype(jnp.float32)


def attend_rows(queries, first_tile, bias_ref, keys, values):
    count = queries.shape[0]
    tiles = count // TILE
    scores = lax.dot_general(
        queries, keys, (((1,), (1,)), ((), ())), preferred_element_type=jnp.float32
    )
    bias = bias_ref[0, first_tile : first_tile + tiles, :]
    scores = (scores.reshape(tiles, TILE, CLIP_TOK) + bias[:, None, :]).reshape(count, CLIP_TOK)
    peak = jnp.max(scores, axis=-1, keepdims=True)
    weights = jnp.exp2((scores - peak) * LOG2_SCALE).astype(jnp.bfloat16)
    blended = jnp.dot(weights, values, preferred_element_type=jnp.float32)
    return (blended[:, :HEAD_DIM] / blended[:, HEAD_DIM:]).astype(jnp.bfloat16)


def fill_values(values_ref, parts):
    at = 0
    for part in parts:
        rows = part.shape[0]
        values_ref[at : at + rows, :HEAD_DIM] = part
        at += rows
    values_ref[:, HEAD_DIM:] = jnp.ones((CLIP_TOK, HEAD_DIM), jnp.bfloat16)


def pair_kernel(place_ref, q_ref, k_ref, v_ref, other_ref, bias_ref, *rest):
    out_ref, keys_ref, values_ref = rest[-3:]
    half = CLIP_TOK // 2
    keys_ref[:half, :] = k_ref[...]
    keys_ref[half:, :] = other_ref[1]
    fill_values(values_ref, (v_ref[...], other_ref[2]))
    keys = keys_ref[...]
    values = values_ref[...]
    for side in range(2):
        base = pl.multiple_of((place_ref[0] if side == 0 else 1 - place_ref[0]) * half, half)
        for at in range(0, half, Q_ROWS):
            queries = q_ref[at : at + Q_ROWS, :] if side == 0 else other_ref[0, at : at + Q_ROWS, :]
            first_tile = (side * half + at) // TILE
            out_ref[pl.ds(base + at, Q_ROWS), :] = attend_rows(
                queries, first_tile, bias_ref, keys, values
            )


def whole_kernel(place_ref, q_ref, k_ref, v_ref, bias_ref, out_ref, values_ref):
    fill_values(values_ref, (v_ref[...],))
    keys = k_ref[...]
    values = values_ref[...]
    for at in range(0, CLIP_TOK, Q_ROWS):
        out_ref[at : at + Q_ROWS, :] = attend_rows(
            q_ref[at : at + Q_ROWS, :], at // TILE, bias_ref, keys, values
        )


def attention_cost(heads):
    pairs = heads * CLIP_TOK * CLIP_TOK
    return pl.CostEstimate(
        flops=pairs * HEAD_DIM * 6,
        bytes_accessed=heads * CLIP_TOK * HEAD_DIM * 8,
        transcendentals=pairs,
    )


def attend_pair(place, local_heads, picked, query, key, value, other, bias, earlier):
    half = CLIP_TOK // 2
    first, step = picked[0], picked[1] - picked[0]

    def head(i, place_ref):
        return place_ref[0] * local_heads + first + step * i

    own = pl.BlockSpec((half, HEAD_DIM), lambda i, p: (0, head(i, p)))
    return pl.pallas_call(
        pair_kernel,
        grid_spec=pltpu.PrefetchScalarGridSpec(
            num_scalar_prefetch=1,
            grid=(len(picked),),
            in_specs=[
                own,
                own,
                own,
                pl.BlockSpec((3, half, HEAD_DIM), lambda i, p: (0, 0, i)),
                pl.BlockSpec((1, NT, CLIP_TOK), lambda i, p: (head(i, p), 0, 0)),
            ]
            + [pl.BlockSpec(memory_space=pl.ANY)] * len(earlier),
            out_specs=pl.BlockSpec((CLIP_TOK, HEAD_DIM), lambda i, p: (0, i)),
            scratch_shapes=[
                pltpu.VMEM((CLIP_TOK, HEAD_DIM), jnp.bfloat16),
                pltpu.VMEM((CLIP_TOK, 2 * HEAD_DIM), jnp.bfloat16),
            ],
        ),
        out_shape=jax.ShapeDtypeStruct((CLIP_TOK, len(picked) * HEAD_DIM), jnp.bfloat16),
        compiler_params=pltpu.CompilerParams(vmem_limit_bytes=VMEM_LIMIT),
        cost_estimate=SMALL_COST,
    )(place, query, key, value, other, bias, *earlier)


def attend_whole(place, query, key, value, bias):
    local_heads = query.shape[1] // HEAD_DIM
    column = pl.BlockSpec((CLIP_TOK, HEAD_DIM), lambda i, p: (0, i))
    return pl.pallas_call(
        whole_kernel,
        grid_spec=pltpu.PrefetchScalarGridSpec(
            num_scalar_prefetch=1,
            grid=(local_heads,),
            in_specs=[
                column,
                column,
                column,
                pl.BlockSpec((1, NT, CLIP_TOK), lambda i, p: (p[0] * local_heads + i, 0, 0)),
            ],
            out_specs=column,
            scratch_shapes=[pltpu.VMEM((CLIP_TOK, 2 * HEAD_DIM), jnp.bfloat16)],
        ),
        out_shape=jax.ShapeDtypeStruct(query.shape, jnp.bfloat16),
        compiler_params=pltpu.CompilerParams(vmem_limit_bytes=VMEM_LIMIT),
        cost_estimate=attention_cost(local_heads),
    )(place, query, key, value, bias)


def pack_kernel(place_ref, q_ref, k_ref, v_ref, *rest):
    out_ref = rest[-1]
    out_ref[0] = q_ref[...]
    out_ref[1] = k_ref[...]
    out_ref[2] = v_ref[...]


def pack_partner(place, local_heads, picked, query, key, value, earlier, limit):
    rows = query.shape[0]
    count = len(picked)
    first, step = picked[0], picked[1] - picked[0]

    def head(i, place_ref):
        return (1 - place_ref[0]) * local_heads + first + step * i

    column = pl.BlockSpec((rows, HEAD_DIM), lambda i, p: (0, head(i, p)))
    return pl.pallas_call(
        pack_kernel,
        grid_spec=pltpu.PrefetchScalarGridSpec(
            num_scalar_prefetch=1,
            grid=(count,),
            in_specs=[column, column, column]
            + [pl.BlockSpec(memory_space=pl.ANY)] * len(earlier),
            out_specs=pl.BlockSpec((3, rows, HEAD_DIM), lambda i, p: (0, 0, i)),
        ),
        out_shape=jax.ShapeDtypeStruct((3, rows, count * HEAD_DIM), jnp.bfloat16),
        compiler_params=pltpu.CompilerParams(vmem_limit_bytes=limit),
        cost_estimate=SMALL_COST,
    )(place, query, key, value, *earlier)


def whole_block(shape):
    return pl.BlockSpec(shape, lambda i, p: (0,) * len(shape))


def gradient_kernel(place_ref, *refs, by_call):
    sources, grad_ref = refs[:4], refs[4]
    sent_ref, kept_ref = refs[-2:]
    core = place_ref[1]
    columns = grad_ref.shape[1]
    step = columns // 3
    for at in range(0, columns, step):
        grad = grad_ref[:, at : at + step]
        for n, source in enumerate(sources):
            call = n // 2
            side = place_ref[0] if n % 2 == 0 else 1 - place_ref[0]
            product = lax.dot_general(
                source[...], grad, (((0,), (0,)), ((), ())), preferred_element_type=jnp.float32
            ).astype(jnp.bfloat16)
            for part in range(2):
                rows = product[part * HEAD_DIM : (part + 1) * HEAD_DIM, :][None]
                level = 2 * side + (part if by_call else call)
                keeper = call if by_call else 1 - part

                @pl.when(core == keeper)
                def _():
                    kept_ref[pl.ds(level, 1), :, at : at + step] = rows

                @pl.when(core != keeper)
                def _():
                    sent_ref[pl.ds(level, 1), :, at : at + step] = rows


def batch_gradient(place, sources, grad_proj, by_call, earlier):
    columns = grad_proj.shape[1]
    shape = (4, HEAD_DIM, columns)
    result = jax.ShapeDtypeStruct(shape, jnp.bfloat16)
    return pl.pallas_call(
        functools.partial(gradient_kernel, by_call=by_call),
        grid_spec=pltpu.PrefetchScalarGridSpec(
            num_scalar_prefetch=1,
            grid=(1,),
            in_specs=[whole_block(each.shape) for each in sources]
            + [whole_block(grad_proj.shape)]
            + [pl.BlockSpec(memory_space=pl.ANY)] * len(earlier),
            out_specs=[whole_block(shape)] * 2,
        ),
        out_shape=[result, result],
        compiler_params=pltpu.CompilerParams(vmem_limit_bytes=VMEM_LIMIT),
        cost_estimate=SMALL_COST,
    )(place, *sources, grad_proj, *earlier)


def level_kernel(place_ref, *refs):
    kept_ref, sent_ref = refs[-2:]
    kept_ref[...] = refs[0][...].astype(jnp.float32) + refs[1][...].astype(jnp.float32)
    total = refs[2][...].astype(jnp.float32) + refs[3][...].astype(jnp.float32)
    sent_ref[...] = total.astype(jnp.bfloat16)


def level_step(bit, own, came, earlier):
    pairs = own.shape[0] // 2
    shape = (pairs,) + own.shape[1:]
    block = (1,) + own.shape[1:]
    keep = pl.BlockSpec(block, lambda i, p: (2 * i + p[0], 0, 0))
    send = pl.BlockSpec(block, lambda i, p: (2 * i + 1 - p[0], 0, 0))
    out = pl.BlockSpec(block, lambda i, p: (i, 0, 0))
    return pl.pallas_call(
        level_kernel,
        grid_spec=pltpu.PrefetchScalarGridSpec(
            num_scalar_prefetch=1,
            grid=(pairs,),
            in_specs=[keep, keep, send, send] + [pl.BlockSpec(memory_space=pl.ANY)] * len(earlier),
            out_specs=[out, out],
        ),
        out_shape=[
            jax.ShapeDtypeStruct(shape, jnp.float32),
            jax.ShapeDtypeStruct(shape, jnp.bfloat16),
        ],
        compiler_params=pltpu.CompilerParams(vmem_limit_bytes=VMEM_LIMIT),
        cost_estimate=SMALL_COST,
    )(bit.reshape(1).astype(jnp.int32), own, came, own, came, *earlier)


def project_kernel(place_ref, *refs, calls, local_heads, last):
    sources, weight_ref, out_ref = refs[:4], refs[4], refs[-1]
    rows = []
    for n in range(4):
        side = place_ref[0] if n % 2 == 0 else 1 - place_ref[0]
        for head in calls[n // 2]:
            rows.append(weight_ref[side * local_heads + head])
    columns = jnp.concatenate([each[...] for each in sources], axis=1)
    total = jnp.dot(columns, jnp.concatenate(rows, axis=0), preferred_element_type=jnp.float32)
    if last:
        total = (total + refs[5][...]) * refs[6][...]
    out_ref[...] = total.astype(out_ref.dtype)


def project(place, sources, weight, calls, local_heads, last, earlier):
    heads, depth, columns = weight.shape
    rows = sources[0].shape[0]
    step = columns // 3
    block = pl.BlockSpec((rows, step), lambda i, p: (0, i))
    return pl.pallas_call(
        functools.partial(project_kernel, calls=calls, local_heads=local_heads, last=bool(last)),
        grid_spec=pltpu.PrefetchScalarGridSpec(
            num_scalar_prefetch=1,
            grid=(3,),
            in_specs=[whole_block(each.shape) for each in sources]
            + [pl.BlockSpec((heads, depth, step), lambda i, p: (0, 0, i))]
            + ([block, pl.BlockSpec((1, step), lambda i, p: (0, i))] if last else [])
            + [pl.BlockSpec(memory_space=pl.ANY)] * len(earlier),
            out_specs=block,
        ),
        out_shape=jax.ShapeDtypeStruct((rows, columns), jnp.bfloat16 if last else jnp.float32),
        compiler_params=pltpu.CompilerParams(vmem_limit_bytes=VMEM_LIMIT),
        cost_estimate=SMALL_COST,
    )(place, *sources, weight, *last, *earlier)


def contract_tokens(columns, grad_proj, kind):
    return lax.dot_general(
        columns, grad_proj, (((0,), (0,)), ((), ())), preferred_element_type=jnp.float32
    ).astype(kind)


def after(value, *earlier):
    return lax.optimization_barrier((value,) + earlier)[0]


def dp_send(value, flip, sender):
    return lax.ppermute(value, "dp", [(i, i ^ flip) for i in range(HEADS) if sender(i)])


def same_bits(i):
    return (i >> 1 ^ i) & 1 == 0


def paired_device(query_rows, key_rows, value_rows, windows, out_weight, gate_scale, out_grad):
    seq_at = lax.axis_index("seq")
    place = seq_at.reshape(1).astype(jnp.int32)
    local_heads = HEADS // 2
    swap = [(0, 1), (1, 0)]
    calls = [(0, 4), (3, 7), (1, 2), (5, 6)]
    bias = window_bias(windows)
    weight = lax.all_gather(out_weight, "dp", axis=0, tiled=True)
    weight = weight.reshape(HEADS, HEAD_DIM, weight.shape[1])
    gate_row = gate_scale[0].astype(jnp.float32)
    grad_proj = (out_grad.astype(jnp.float32) * gate_row).astype(jnp.bfloat16)
    sources = (query_rows, key_rows, value_rows)

    def pack(n, limit, *earlier):
        return pack_partner(place, local_heads, calls[n], *sources, earlier, limit)

    def attention(n, other, *earlier):
        return attend_pair(place, local_heads, calls[n], *sources, other, bias, earlier)

    def exchange(mine):
        return lax.ppermute(mine, "seq", swap)

    index = lax.axis_index("dp")
    core = index & 1

    where = jnp.stack([seq_at, core]).astype(jnp.int32)

    def core_step(by_call, mine_a, theirs_a, mine_b, theirs_b, grad_proj, *earlier):
        sources = (mine_a, theirs_a, mine_b, theirs_b)
        sent, kept = batch_gradient(where, sources, grad_proj, by_call, earlier)
        came = dp_send(sent, 1, lambda i: True)
        return (kept.astype(jnp.float32) + came.astype(jnp.float32)).astype(jnp.bfloat16)

    def apart(step, *operands):
        shapes = jax.eval_shape(step, *operands)
        return lax.cond(
            windows[0, 0] > 0,
            step,
            lambda *_: jax.tree.map(lambda leaf: jnp.zeros(leaf.shape, leaf.dtype), shapes),
            *operands,
        )

    packed0 = pack(0, VMEM_WHOLE)
    packed1 = pack(1, VMEM_WHOLE, packed0)
    packed2 = pack(2, VMEM_LIMIT, packed1)
    packed3 = pack(3, VMEM_LIMIT, packed2)
    other0 = exchange(packed0)
    other1 = exchange(packed1)
    other2 = exchange(packed2)
    other3 = exchange(packed3)
    mine0 = attention(0, other0, packed3)
    theirs0 = exchange(mine0)
    mine1 = attention(1, other1, mine0)
    theirs1 = exchange(mine1)
    mine2 = attention(2, other2, mine1)
    theirs2 = exchange(mine2)
    mine3 = attention(3, other3, mine2)
    theirs3 = exchange(mine3)

    def unlike(i):
        return not same_bits(i)

    low_bit, high_bit = index >> 2 & 1, index >> 3 & 1
    total_a = apart(
        functools.partial(core_step, True), after(mine0, mine3), theirs0, mine1, theirs1, grad_proj
    )
    across_a = dp_send(total_a, 2, unlike)
    first = (mine0, theirs0, mine1, theirs1)
    projected = project(place, first, weight, calls[:2], local_heads, (), (total_a, theirs2))
    second = (mine2, theirs2, mine3, theirs3)
    sent_b, kept_b = batch_gradient(where, second, grad_proj, False, (projected,))
    came_b = dp_send(sent_b, 1, lambda i: True)
    kept_a, sent_a = level_step(low_bit, total_a, across_a, (sent_b,))
    low_a = dp_send(sent_a, 4, same_bits)
    total_b = kept_b.astype(jnp.float32) + after(came_b, sent_a).astype(jnp.float32)
    total_b = total_b.astype(jnp.bfloat16)
    across_b = dp_send(total_b, 2, same_bits)
    kept_a, sent_a = level_step(high_bit, kept_a, low_a, (total_b,))
    high_a = dp_send(sent_a, 8, same_bits)
    block_out = project(
        place, second, weight, calls[2:], local_heads, (projected, gate_row[None]), (sent_a,)
    )
    kept_b, sent_b = level_step(low_bit, total_b, across_b, (block_out,))
    low_b = dp_send(sent_b, 4, unlike)
    kept_b, sent_b = level_step(high_bit, kept_b, low_b, (high_a,))
    high_b = dp_send(sent_b, 8, unlike)
    weight_grad = jnp.where(
        same_bits(index),
        kept_a[0] + high_a[0].astype(jnp.float32),
        kept_b[0] + high_b[0].astype(jnp.float32),
    )
    return (block_out, weight_grad)


def general_device(query_rows, key_rows, value_rows, windows, out_weight, gate_scale, out_grad):
    query, key, value = (
        lax.all_to_all(rows, "seq", split_axis=1, concat_axis=0, tiled=True)
        for rows in (query_rows, key_rows, value_rows)
    )
    place = lax.axis_index("seq").reshape(1).astype(jnp.int32)
    mine = attend_whole(place, query, key, value, window_bias(windows))
    columns = lax.all_gather(mine, "seq", axis=1, tiled=True)
    weight = lax.all_gather(out_weight, "dp", axis=0, tiled=True)
    gate_row = gate_scale[0].astype(jnp.float32)
    projected = jnp.dot(columns, weight, preferred_element_type=jnp.float32)
    block_out = (projected * gate_row).astype(jnp.bfloat16)
    grad_proj = (out_grad.astype(jnp.float32) * gate_row).astype(jnp.bfloat16)
    weight_grad = lax.psum_scatter(
        contract_tokens(columns, grad_proj, jnp.float32), "dp", scatter_dimension=0, tiled=True
    )
    return (block_out, weight_grad)


def solution(mesh):
    paired = mesh.shape["seq"] == 2 and mesh.shape["dp"] == HEADS
    return jax.shard_map(
        paired_device if paired else general_device,
        mesh=mesh,
        in_specs=(
            P(("dp", "seq"), None),
            P(("dp", "seq"), None),
            P(("dp", "seq"), None),
            P(),
            P("dp", "seq"),
            P("dp", "seq"),
            P("dp", "seq"),
        ),
        out_specs=(P("dp", "seq"), P("dp", "seq")),
        check_vma=False,
    )
```

```python
import functools
import math

import jax
import jax.numpy as jnp
import numpy as np
from jax import lax
from jax.experimental import pallas as pl
from jax.experimental.pallas import tpu as pltpu
from jax.sharding import PartitionSpec as P

HEADS = 16
HEAD_DIM = 128
GH = 3
GW = 4
GT = 2
TILE = 48
NT = 24
CLIP_TOK = NT * TILE
Q_ROWS = GW * TILE
LOG2_SCALE = math.log2(math.e) / math.sqrt(HEAD_DIM)
VMEM_LIMIT = 24 * 1024 * 1024
VMEM_WHOLE = 60 * 1024 * 1024
VMEM_SMALL = 12 * 1024 * 1024
SMALL_COST = pl.CostEstimate(flops=1, bytes_accessed=1, transcendentals=0)


def window_bias(windows):
    tile_id = np.arange(NT)
    coords = np.stack([tile_id // (GH * GW), tile_id // GW % GH, tile_id % GW]).astype(np.int32)
    token_coords = np.repeat(coords, TILE, axis=1)
    inside = None
    for axis_no, limit in enumerate((GT, GH, GW)):
        extent = jnp.minimum(windows[:, axis_no], limit)[:, None]
        start = jnp.clip(coords[axis_no][None, :] - (extent - 1) // 2, 0, limit - extent)
        column = token_coords[axis_no][None, None, :]
        here = (column >= start[:, :, None]) & (column < (start + extent)[:, :, None])
        inside = here if inside is None else inside & here
    return jnp.where(inside, 0.0, -jnp.inf).astype(jnp.float32)


def attend_rows(queries, first_tile, bias_ref, keys, values):
    count = queries.shape[0]
    tiles = count // TILE
    scores = lax.dot_general(
        queries, keys, (((1,), (1,)), ((), ())), preferred_element_type=jnp.float32
    )
    bias = bias_ref[0, first_tile : first_tile + tiles, :]
    scores = (scores.reshape(tiles, TILE, CLIP_TOK) + bias[:, None, :]).reshape(count, CLIP_TOK)
    peak = jnp.max(scores, axis=-1, keepdims=True)
    weights = jnp.exp2((scores - peak) * LOG2_SCALE).astype(jnp.bfloat16)
    blended = jnp.dot(weights, values, preferred_element_type=jnp.float32)
    return (blended[:, :HEAD_DIM] / blended[:, HEAD_DIM:]).astype(jnp.bfloat16)


def fill_values(values_ref, parts):
    at = 0
    for part in parts:
        rows = part.shape[0]
        values_ref[at : at + rows, :HEAD_DIM] = part
        at += rows
    values_ref[:, HEAD_DIM:] = jnp.ones((CLIP_TOK, HEAD_DIM), jnp.bfloat16)


def pair_kernel(place_ref, q_ref, k_ref, v_ref, other_ref, bias_ref, *rest):
    out_ref, keys_ref, values_ref = rest[-3:]
    half = CLIP_TOK // 2
    keys_ref[:half, :] = k_ref[...]
    keys_ref[half:, :] = other_ref[1]
    fill_values(values_ref, (v_ref[...], other_ref[2]))
    keys = keys_ref[...]
    values = values_ref[...]
    for side in range(2):
        base = pl.multiple_of((place_ref[0] if side == 0 else 1 - place_ref[0]) * half, half)
        for at in range(0, half, Q_ROWS):
            queries = q_ref[at : at + Q_ROWS, :] if side == 0 else other_ref[0, at : at + Q_ROWS, :]
            first_tile = (side * half + at) // TILE
            out_ref[pl.ds(base + at, Q_ROWS), :] = attend_rows(
                queries, first_tile, bias_ref, keys, values
            )


def whole_kernel(place_ref, q_ref, k_ref, v_ref, bias_ref, out_ref, values_ref):
    fill_values(values_ref, (v_ref[...],))
    keys = k_ref[...]
    values = values_ref[...]
    for at in range(0, CLIP_TOK, Q_ROWS):
        out_ref[at : at + Q_ROWS, :] = attend_rows(
            q_ref[at : at + Q_ROWS, :], at // TILE, bias_ref, keys, values
        )


def attention_cost(heads):
    pairs = heads * CLIP_TOK * CLIP_TOK
    return pl.CostEstimate(
        flops=pairs * HEAD_DIM * 6,
        bytes_accessed=heads * CLIP_TOK * HEAD_DIM * 8,
        transcendentals=pairs,
    )


def attend_pair(place, local_heads, picked, query, key, value, other, bias, earlier):
    half = CLIP_TOK // 2
    first, step = picked[0], picked[1] - picked[0]

    def head(i, place_ref):
        return place_ref[0] * local_heads + first + step * i

    own = pl.BlockSpec((half, HEAD_DIM), lambda i, p: (0, head(i, p)))
    return pl.pallas_call(
        pair_kernel,
        grid_spec=pltpu.PrefetchScalarGridSpec(
            num_scalar_prefetch=1,
            grid=(len(picked),),
            in_specs=[
                own,
                own,
                own,
                pl.BlockSpec((3, half, HEAD_DIM), lambda i, p: (0, 0, i)),
                pl.BlockSpec((1, NT, CLIP_TOK), lambda i, p: (head(i, p), 0, 0)),
            ]
            + [pl.BlockSpec(memory_space=pl.ANY)] * len(earlier),
            out_specs=pl.BlockSpec((CLIP_TOK, HEAD_DIM), lambda i, p: (0, i)),
            scratch_shapes=[
                pltpu.VMEM((CLIP_TOK, HEAD_DIM), jnp.bfloat16),
                pltpu.VMEM((CLIP_TOK, 2 * HEAD_DIM), jnp.bfloat16),
            ],
        ),
        out_shape=jax.ShapeDtypeStruct((CLIP_TOK, len(picked) * HEAD_DIM), jnp.bfloat16),
        compiler_params=pltpu.CompilerParams(vmem_limit_bytes=VMEM_LIMIT),
        cost_estimate=SMALL_COST,
    )(place, query, key, value, other, bias, *earlier)


def attend_whole(place, query, key, value, bias):
    local_heads = query.shape[1] // HEAD_DIM
    column = pl.BlockSpec((CLIP_TOK, HEAD_DIM), lambda i, p: (0, i))
    return pl.pallas_call(
        whole_kernel,
        grid_spec=pltpu.PrefetchScalarGridSpec(
            num_scalar_prefetch=1,
            grid=(local_heads,),
            in_specs=[
                column,
                column,
                column,
                pl.BlockSpec((1, NT, CLIP_TOK), lambda i, p: (p[0] * local_heads + i, 0, 0)),
            ],
            out_specs=column,
            scratch_shapes=[pltpu.VMEM((CLIP_TOK, 2 * HEAD_DIM), jnp.bfloat16)],
        ),
        out_shape=jax.ShapeDtypeStruct(query.shape, jnp.bfloat16),
        compiler_params=pltpu.CompilerParams(vmem_limit_bytes=VMEM_LIMIT),
        cost_estimate=attention_cost(local_heads),
    )(place, query, key, value, bias)


def pack_kernel(place_ref, q_ref, k_ref, v_ref, *rest):
    out_ref = rest[-1]
    out_ref[0] = q_ref[...]
    out_ref[1] = k_ref[...]
    out_ref[2] = v_ref[...]


def pack_partner(place, local_heads, picked, query, key, value, earlier, limit):
    rows = query.shape[0]
    count = len(picked)
    first, step = picked[0], picked[1] - picked[0]

    def head(i, place_ref):
        return (1 - place_ref[0]) * local_heads + first + step * i

    column = pl.BlockSpec((rows, HEAD_DIM), lambda i, p: (0, head(i, p)))
    return pl.pallas_call(
        pack_kernel,
        grid_spec=pltpu.PrefetchScalarGridSpec(
            num_scalar_prefetch=1,
            grid=(count,),
            in_specs=[column, column, column]
            + [pl.BlockSpec(memory_space=pl.ANY)] * len(earlier),
            out_specs=pl.BlockSpec((3, rows, HEAD_DIM), lambda i, p: (0, 0, i)),
        ),
        out_shape=jax.ShapeDtypeStruct((3, rows, count * HEAD_DIM), jnp.bfloat16),
        compiler_params=pltpu.CompilerParams(vmem_limit_bytes=limit),
        cost_estimate=SMALL_COST,
    )(place, query, key, value, *earlier)


def whole_block(shape):
    return pl.BlockSpec(shape, lambda i, p: (0,) * len(shape))


def gradient_kernel(place_ref, *refs, by_call):
    grad = refs[4][...]
    sent_ref, kept_ref = refs[-2:]
    first_core = place_ref[1] == 0

    def rows(source):
        product = lax.dot_general(
            source, grad, (((0,), (0,)), ((), ())), preferred_element_type=jnp.float32
        )
        return product.astype(jnp.bfloat16).reshape(2, HEAD_DIM, grad.shape[1])

    for n in range(2):
        side = place_ref[0] if n == 0 else 1 - place_ref[0]
        if by_call:
            one, two = refs[n][...], refs[2 + n][...]
            sent_ref[pl.ds(2 * side, 2)] = rows(jnp.where(first_core, two, one))
            kept_ref[pl.ds(2 * side, 2)] = rows(jnp.where(first_core, one, two))
            continue
        for call in range(2):
            one, two = refs[2 * call + n][:, :HEAD_DIM], refs[2 * call + n][:, HEAD_DIM:]
            both = [jnp.where(first_core, one, two), jnp.where(first_core, two, one)]
            both = rows(jnp.concatenate(both, axis=1))
            sent_ref[pl.ds(2 * call + side, 1)] = both[:1]
            kept_ref[pl.ds(2 * call + side, 1)] = both[1:]


def batch_gradient(place, sources, grad_proj, by_call, earlier=()):
    columns = grad_proj.shape[1]
    shape = (4, HEAD_DIM, columns)
    result = jax.ShapeDtypeStruct(shape, jnp.bfloat16)
    return pl.pallas_call(
        functools.partial(gradient_kernel, by_call=by_call),
        grid_spec=pltpu.PrefetchScalarGridSpec(
            num_scalar_prefetch=1,
            grid=(1,),
            in_specs=[whole_block(each.shape) for each in sources]
            + [whole_block(grad_proj.shape)]
            + [pl.BlockSpec(memory_space=pl.ANY)] * len(earlier),
            out_specs=[whole_block(shape)] * 2,
        ),
        out_shape=[result, result],
        compiler_params=pltpu.CompilerParams(vmem_limit_bytes=VMEM_LIMIT),
        cost_estimate=SMALL_COST,
    )(place, *sources, grad_proj, *earlier)


def sum_of(blocks):
    total = blocks[0].astype(jnp.float32)
    for block in blocks[1:]:
        total = total + block.astype(jnp.float32)
    return total


def level_step(bit, terms, earlier=()):
    count = len(terms)
    pairs = terms[0].shape[0] // 2
    shape = (pairs,) + terms[0].shape[1:]
    block = (1,) + terms[0].shape[1:]
    keep = pl.BlockSpec(block, lambda i, p: (2 * i + p[0], 0, 0))
    send = pl.BlockSpec(block, lambda i, p: (2 * i + 1 - p[0], 0, 0))
    out = pl.BlockSpec(block, lambda i, p: (i, 0, 0))

    def kernel(place_ref, *refs):
        kept_ref, sent_ref = refs[-2:]
        kept_ref[...] = sum_of([ref[...] for ref in refs[:count]])
        sent_ref[...] = sum_of([ref[...] for ref in refs[count : 2 * count]]).astype(jnp.bfloat16)

    return pl.pallas_call(
        kernel,
        grid_spec=pltpu.PrefetchScalarGridSpec(
            num_scalar_prefetch=1,
            grid=(pairs,),
            in_specs=[keep] * count
            + [send] * count
            + [pl.BlockSpec(memory_space=pl.ANY)] * len(earlier),
            out_specs=[out, out],
        ),
        out_shape=[
            jax.ShapeDtypeStruct(shape, jnp.float32),
            jax.ShapeDtypeStruct(shape, jnp.bfloat16),
        ],
        compiler_params=pltpu.CompilerParams(vmem_limit_bytes=VMEM_SMALL),
        cost_estimate=SMALL_COST,
    )(bit.reshape(1).astype(jnp.int32), *terms, *terms, *earlier)


def total_step(terms, parts=1, earlier=()):
    count = terms[0].shape[0] // parts
    shape = (count,) + terms[0].shape[1:]
    blocks = [
        pl.BlockSpec((1,) + shape[1:], lambda i, part=part: (part * count + i, 0, 0))
        for part in range(parts)
    ]

    def kernel(*refs):
        for part in range(parts):
            mine = refs[part * len(terms) : (part + 1) * len(terms)]
            refs[part - parts][...] = sum_of([ref[...] for ref in mine]).astype(jnp.bfloat16)

    return pl.pallas_call(
        kernel,
        grid=(count,),
        in_specs=[block for block in blocks for _ in terms]
        + [pl.BlockSpec(memory_space=pl.ANY)] * len(earlier),
        out_specs=[blocks[0]] * parts,
        out_shape=[jax.ShapeDtypeStruct(shape, jnp.bfloat16)] * parts,
        compiler_params=pltpu.CompilerParams(vmem_limit_bytes=VMEM_SMALL),
        cost_estimate=SMALL_COST,
    )(*[term for _ in range(parts) for term in terms], *earlier)


def project_kernel(place_ref, *refs, calls, local_heads, last):
    sources, weight_ref, out_ref = refs[:4], refs[4], refs[-1]
    rows = []
    for n in range(4):
        side = place_ref[0] if n % 2 == 0 else 1 - place_ref[0]
        for head in calls[n // 2]:
            rows.append(weight_ref[side * local_heads + head])
    columns = jnp.concatenate([each[...] for each in sources], axis=1)
    total = jnp.dot(columns, jnp.concatenate(rows, axis=0), preferred_element_type=jnp.float32)
    if last:
        total = (total + refs[5][...]) * refs[6][...]
    out_ref[...] = total.astype(out_ref.dtype)


def project(place, sources, weight, calls, local_heads, last, earlier):
    heads, depth, columns = weight.shape
    rows = sources[0].shape[0]
    step = columns // 3
    block = pl.BlockSpec((rows, step), lambda i, p: (0, i))
    return pl.pallas_call(
        functools.partial(project_kernel, calls=calls, local_heads=local_heads, last=bool(last)),
        grid_spec=pltpu.PrefetchScalarGridSpec(
            num_scalar_prefetch=1,
            grid=(3,),
            in_specs=[whole_block(each.shape) for each in sources]
            + [pl.BlockSpec((heads, depth, step), lambda i, p: (0, 0, i))]
            + ([block, pl.BlockSpec((1, step), lambda i, p: (0, i))] if last else [])
            + [pl.BlockSpec(memory_space=pl.ANY)] * len(earlier),
            out_specs=block,
        ),
        out_shape=jax.ShapeDtypeStruct((rows, columns), jnp.bfloat16 if last else jnp.float32),
        compiler_params=pltpu.CompilerParams(vmem_limit_bytes=VMEM_LIMIT),
        cost_estimate=SMALL_COST,
    )(place, *sources, weight, *last, *earlier)


def contract_tokens(columns, grad_proj, kind):
    return lax.dot_general(
        columns, grad_proj, (((0,), (0,)), ((), ())), preferred_element_type=jnp.float32
    ).astype(kind)


def after(value, *earlier):
    return lax.optimization_barrier((value,) + earlier)[0]


def dp_send(value, flip, sender):
    return lax.ppermute(value, "dp", [(i, i ^ flip) for i in range(HEADS) if sender(i)])


def same_bits(i):
    return (i >> 1 ^ i) & 1 == 0


def paired_device(query_rows, key_rows, value_rows, windows, out_weight, gate_scale, out_grad):
    seq_at = lax.axis_index("seq")
    place = seq_at.reshape(1).astype(jnp.int32)
    local_heads = HEADS // 2
    swap = [(0, 1), (1, 0)]
    calls = [(0, 4), (3, 7), (1, 2), (5, 6)]
    bias = window_bias(windows)
    weight = lax.all_gather(out_weight, "dp", axis=0, tiled=True)
    weight = weight.reshape(HEADS, HEAD_DIM, weight.shape[1])
    gate_row = gate_scale[0].astype(jnp.float32)
    grad_proj = (out_grad.astype(jnp.float32) * gate_row).astype(jnp.bfloat16)
    sources = (query_rows, key_rows, value_rows)

    def pack(n, limit, *earlier):
        return pack_partner(place, local_heads, calls[n], *sources, earlier, limit)

    def attention(n, other, *earlier):
        return attend_pair(place, local_heads, calls[n], *sources, other, bias, earlier)

    def exchange(mine):
        return lax.ppermute(mine, "seq", swap)

    index = lax.axis_index("dp")
    core = index & 1

    where = jnp.stack([seq_at, core]).astype(jnp.int32)

    def core_step(*operands):
        sent, kept = batch_gradient(where, operands[:4], operands[4], True)
        return total_step([kept, dp_send(sent, 1, lambda i: True)])[0]

    def apart(step, *operands):
        shapes = jax.eval_shape(step, *operands)
        return lax.cond(
            windows[0, 0] > 0,
            step,
            lambda *_: jax.tree.map(lambda leaf: jnp.zeros(leaf.shape, leaf.dtype), shapes),
            *operands,
        )

    packed0 = pack(0, VMEM_WHOLE)
    packed1 = pack(1, VMEM_WHOLE, packed0)
    packed2 = pack(2, VMEM_LIMIT, packed1)
    packed3 = pack(3, VMEM_LIMIT, packed2)
    other0 = exchange(packed0)
    other1 = exchange(packed1)
    other2 = exchange(packed2)
    other3 = exchange(packed3)
    mine0 = attention(0, other0, packed3)
    theirs0 = exchange(mine0)
    mine1 = attention(1, other1, mine0)
    theirs1 = exchange(mine1)
    mine2 = attention(2, other2, mine1)
    theirs2 = exchange(mine2)
    mine3 = attention(3, other3, mine2)
    theirs3 = exchange(mine3)

    def unlike(i):
        return not same_bits(i)

    low_bit, high_bit = index >> 2 & 1, index >> 3 & 1
    def like_even(i):
        return unlike(i) and i & 4 == 0

    def like_odd(i):
        return unlike(i) and i & 4 != 0

    first = (mine0, theirs0, mine1, theirs1)
    second = (mine2, theirs2, mine3, theirs3)
    total_a = apart(core_step, after(mine0, mine3), *first[1:], grad_proj)
    across_a = dp_send(total_a, 2, unlike)
    projected = project(place, first, weight, calls[:2], local_heads, (), (total_a, theirs2))
    sent, kept = batch_gradient(where, second, grad_proj, False, (projected,))
    came = dp_send(sent, 1, lambda i: True)
    kept_a, sent_a = level_step(low_bit, [total_a, across_a], (sent,))
    low_a = dp_send(sent_a, 4, same_bits)
    total_b, total_c = total_step([kept, came], 2, (sent_a,))
    across_b = dp_send(total_b, 2, same_bits)
    across_c = dp_send(total_c, 2, same_bits)
    (sent_b,) = total_step([total_b, across_b], 1, (total_c,))
    low_b = dp_send(sent_b, 4, like_odd)
    kept_a, sent_a = level_step(high_bit, [kept_a, low_a], (sent_b,))
    high_a = dp_send(sent_a, 8, same_bits)
    (sent_c,) = total_step([total_c, across_c], 1, (sent_a,))
    low_c = dp_send(sent_c, 4, like_even)
    kept_b, sent_b = level_step(high_bit, [total_b, across_b, low_b], (sent_c,))
    high_b = dp_send(sent_b, 8, like_even)
    block_out = project(
        place, second, weight, calls[2:], local_heads, (projected, gate_row[None]), (sent_b,)
    )
    kept_c, sent_c = level_step(high_bit, [total_c, across_c, low_c], (block_out, high_a, high_b))
    high_c = dp_send(sent_c, 8, like_odd)
    weight_grad = jnp.where(
        same_bits(index),
        kept_a[0] + high_a[0].astype(jnp.float32),
        jnp.where(
            low_bit == 0,
            kept_b[0] + high_b[0].astype(jnp.float32),
            kept_c[0] + high_c[0].astype(jnp.float32),
        ),
    )
    return (block_out, weight_grad)


def general_device(query_rows, key_rows, value_rows, windows, out_weight, gate_scale, out_grad):
    query, key, value = (
        lax.all_to_all(rows, "seq", split_axis=1, concat_axis=0, tiled=True)
        for rows in (query_rows, key_rows, value_rows)
    )
    place = lax.axis_index("seq").reshape(1).astype(jnp.int32)
    mine = attend_whole(place, query, key, value, window_bias(windows))
    columns = lax.all_gather(mine, "seq", axis=1, tiled=True)
    weight = lax.all_gather(out_weight, "dp", axis=0, tiled=True)
    gate_row = gate_scale[0].astype(jnp.float32)
    projected = jnp.dot(columns, weight, preferred_element_type=jnp.float32)
    block_out = (projected * gate_row).astype(jnp.bfloat16)
    grad_proj = (out_grad.astype(jnp.float32) * gate_row).astype(jnp.bfloat16)
    weight_grad = lax.psum_scatter(
        contract_tokens(columns, grad_proj, jnp.float32), "dp", scatter_dimension=0, tiled=True
    )
    return (block_out, weight_grad)


def solution(mesh):
    paired = mesh.shape["seq"] == 2 and mesh.shape["dp"] == HEADS
    return jax.shard_map(
        paired_device if paired else general_device,
        mesh=mesh,
        in_specs=(
            P(("dp", "seq"), None),
            P(("dp", "seq"), None),
            P(("dp", "seq"), None),
            P(),
            P("dp", "seq"),
            P("dp", "seq"),
            P("dp", "seq"),
        ),
        out_specs=(P("dp", "seq"), P("dp", "seq")),
        check_vma=False,
    )
```

```python
import functools
import math

import jax
import jax.numpy as jnp
import numpy as np
from jax import lax
from jax.experimental import pallas as pl
from jax.experimental.pallas import tpu as pltpu
from jax.sharding import PartitionSpec as P

HEADS = 16
HEAD_DIM = 128
GH = 3
GW = 4
GT = 2
TILE = 48
NT = 24
CLIP_TOK = NT * TILE
Q_ROWS = GW * TILE
LOG2_SCALE = math.log2(math.e) / math.sqrt(HEAD_DIM)
VMEM_LIMIT = 16 * 1024 * 1024
VMEM_GRADIENT = 20 * 1024 * 1024
VMEM_PROJECT = 16 * 1024 * 1024
PROJECT_STEPS = 6
VMEM_WHOLE = 60 * 1024 * 1024
VMEM_SMALL = 12 * 1024 * 1024
SMALL_COST = pl.CostEstimate(flops=1, bytes_accessed=1, transcendentals=0)


def window_bias(windows):
    tile_id = np.arange(NT)
    coords = np.stack([tile_id // (GH * GW), tile_id // GW % GH, tile_id % GW]).astype(np.int32)
    token_coords = np.repeat(coords, TILE, axis=1)
    inside = None
    for axis_no, limit in enumerate((GT, GH, GW)):
        extent = jnp.minimum(windows[:, axis_no], limit)[:, None]
        start = jnp.clip(coords[axis_no][None, :] - (extent - 1) // 2, 0, limit - extent)
        column = token_coords[axis_no][None, None, :]
        here = (column >= start[:, :, None]) & (column < (start + extent)[:, :, None])
        inside = here if inside is None else inside & here
    return jnp.where(inside, 0.0, -jnp.inf).astype(jnp.float32)


def attend_rows(queries, first_tile, bias_ref, keys, values):
    count = queries.shape[0]
    tiles = count // TILE
    scores = lax.dot_general(
        queries, keys, (((1,), (1,)), ((), ())), preferred_element_type=jnp.float32
    )
    bias = bias_ref[0, first_tile : first_tile + tiles, :]
    scores = (scores.reshape(tiles, TILE, CLIP_TOK) + bias[:, None, :]).reshape(count, CLIP_TOK)
    peak = jnp.max(scores, axis=-1, keepdims=True)
    weights = jnp.exp2((scores - peak) * LOG2_SCALE).astype(jnp.bfloat16)
    blended = jnp.dot(weights, values, preferred_element_type=jnp.float32)
    return (blended[:, :HEAD_DIM] / blended[:, HEAD_DIM:]).astype(jnp.bfloat16)


def fill_values(values_ref, parts):
    at = 0
    for part in parts:
        rows = part.shape[0]
        values_ref[at : at + rows, :HEAD_DIM] = part
        at += rows
    values_ref[:, HEAD_DIM:] = jnp.ones((CLIP_TOK, HEAD_DIM), jnp.bfloat16)


def pair_kernel(place_ref, q_ref, k_ref, v_ref, other_ref, bias_ref, *rest):
    out_ref, keys_ref, values_ref = rest[-3:]
    half = CLIP_TOK // 2
    keys_ref[:half, :] = k_ref[...]
    keys_ref[half:, :] = other_ref[1]
    fill_values(values_ref, (v_ref[...], other_ref[2]))
    keys = keys_ref[...]
    values = values_ref[...]
    for side in range(2):
        base = pl.multiple_of((place_ref[0] if side == 0 else 1 - place_ref[0]) * half, half)
        for at in range(0, half, Q_ROWS):
            queries = q_ref[at : at + Q_ROWS, :] if side == 0 else other_ref[0, at : at + Q_ROWS, :]
            first_tile = (side * half + at) // TILE
            out_ref[pl.ds(base + at, Q_ROWS), :] = attend_rows(
                queries, first_tile, bias_ref, keys, values
            )


def whole_kernel(place_ref, q_ref, k_ref, v_ref, bias_ref, out_ref, values_ref):
    fill_values(values_ref, (v_ref[...],))
    keys = k_ref[...]
    values = values_ref[...]
    for at in range(0, CLIP_TOK, Q_ROWS):
        out_ref[at : at + Q_ROWS, :] = attend_rows(
            q_ref[at : at + Q_ROWS, :], at // TILE, bias_ref, keys, values
        )


def attention_cost(heads):
    pairs = heads * CLIP_TOK * CLIP_TOK
    return pl.CostEstimate(
        flops=pairs * HEAD_DIM * 6,
        bytes_accessed=heads * CLIP_TOK * HEAD_DIM * 8,
        transcendentals=pairs,
    )


def attend_pair(place, local_heads, picked, query, key, value, other, bias, earlier):
    half = CLIP_TOK // 2
    first, step = picked[0], picked[1] - picked[0]

    def head(i, place_ref):
        return place_ref[0] * local_heads + first + step * i

    own = pl.BlockSpec((half, HEAD_DIM), lambda i, p: (0, head(i, p)))
    return pl.pallas_call(
        pair_kernel,
        grid_spec=pltpu.PrefetchScalarGridSpec(
            num_scalar_prefetch=1,
            grid=(len(picked),),
            in_specs=[
                own,
                own,
                own,
                pl.BlockSpec((3, half, HEAD_DIM), lambda i, p: (0, 0, i)),
                pl.BlockSpec((1, NT, CLIP_TOK), lambda i, p: (head(i, p), 0, 0)),
            ]
            + [pl.BlockSpec(memory_space=pl.ANY)] * len(earlier),
            out_specs=pl.BlockSpec((CLIP_TOK, HEAD_DIM), lambda i, p: (0, i)),
            scratch_shapes=[
                pltpu.VMEM((CLIP_TOK, HEAD_DIM), jnp.bfloat16),
                pltpu.VMEM((CLIP_TOK, 2 * HEAD_DIM), jnp.bfloat16),
            ],
        ),
        out_shape=jax.ShapeDtypeStruct((CLIP_TOK, len(picked) * HEAD_DIM), jnp.bfloat16),
        compiler_params=pltpu.CompilerParams(vmem_limit_bytes=VMEM_LIMIT),
        cost_estimate=SMALL_COST,
    )(place, query, key, value, other, bias, *earlier)


def attend_whole(place, query, key, value, bias):
    local_heads = query.shape[1] // HEAD_DIM
    column = pl.BlockSpec((CLIP_TOK, HEAD_DIM), lambda i, p: (0, i))
    return pl.pallas_call(
        whole_kernel,
        grid_spec=pltpu.PrefetchScalarGridSpec(
            num_scalar_prefetch=1,
            grid=(local_heads,),
            in_specs=[
                column,
                column,
                column,
                pl.BlockSpec((1, NT, CLIP_TOK), lambda i, p: (p[0] * local_heads + i, 0, 0)),
            ],
            out_specs=column,
            scratch_shapes=[pltpu.VMEM((CLIP_TOK, 2 * HEAD_DIM), jnp.bfloat16)],
        ),
        out_shape=jax.ShapeDtypeStruct(query.shape, jnp.bfloat16),
        compiler_params=pltpu.CompilerParams(vmem_limit_bytes=VMEM_LIMIT),
        cost_estimate=attention_cost(local_heads),
    )(place, query, key, value, bias)


def pack_kernel(place_ref, q_ref, k_ref, v_ref, *rest):
    out_ref = rest[-1]
    out_ref[0] = q_ref[...]
    out_ref[1] = k_ref[...]
    out_ref[2] = v_ref[...]


def pack_partner(place, local_heads, picked, query, key, value, earlier, limit):
    rows = query.shape[0]
    count = len(picked)
    first, step = picked[0], picked[1] - picked[0]

    def head(i, place_ref):
        return (1 - place_ref[0]) * local_heads + first + step * i

    column = pl.BlockSpec((rows, HEAD_DIM), lambda i, p: (0, head(i, p)))
    return pl.pallas_call(
        pack_kernel,
        grid_spec=pltpu.PrefetchScalarGridSpec(
            num_scalar_prefetch=1,
            grid=(count,),
            in_specs=[column, column, column]
            + [pl.BlockSpec(memory_space=pl.ANY)] * len(earlier),
            out_specs=pl.BlockSpec((3, rows, HEAD_DIM), lambda i, p: (0, 0, i)),
        ),
        out_shape=jax.ShapeDtypeStruct((3, rows, count * HEAD_DIM), jnp.bfloat16),
        compiler_params=pltpu.CompilerParams(vmem_limit_bytes=limit),
        cost_estimate=SMALL_COST,
    )(place, query, key, value, *earlier)


def whole_block(shape):
    return pl.BlockSpec(shape, lambda i, p: (0,) * len(shape), pipeline_mode=pl.Buffered(1))


def gradient_kernel(place_ref, *refs, by_call):
    grad_ref = refs[4]
    sent_ref, kept_ref = refs[-2:]
    first_core = place_ref[1] == 0
    sent, kept, levels = [], [], []
    for n in range(2):
        side = place_ref[0] if n == 0 else 1 - place_ref[0]
        if by_call:
            one, two = refs[n][...], refs[2 + n][...]
            sent.append(jnp.where(first_core, two, one))
            kept.append(jnp.where(first_core, one, two))
            levels += [2 * side, 2 * side + 1]
            continue
        for call in range(2):
            one, two = refs[2 * call + n][:, :HEAD_DIM], refs[2 * call + n][:, HEAD_DIM:]
            sent.append(jnp.where(first_core, one, two))
            kept.append(jnp.where(first_core, two, one))
            levels.append(2 * call + side)
    rows = jnp.concatenate(sent + kept, axis=1).T
    columns = grad_ref.shape[1]
    step = columns // 3
    for at in range(0, columns, step):
        product = jnp.dot(rows, grad_ref[:, at : at + step], preferred_element_type=jnp.float32)
        product = product.astype(jnp.bfloat16).reshape(8, HEAD_DIM, step)
        for n, level in enumerate(levels):
            sent_ref[pl.ds(level, 1), :, at : at + step] = product[n : n + 1]
            kept_ref[pl.ds(level, 1), :, at : at + step] = product[4 + n : 5 + n]


def batch_gradient(place, sources, grad_proj, by_call, earlier=()):
    columns = grad_proj.shape[1]
    shape = (4, HEAD_DIM, columns)
    result = jax.ShapeDtypeStruct(shape, jnp.bfloat16)
    return pl.pallas_call(
        functools.partial(gradient_kernel, by_call=by_call),
        grid_spec=pltpu.PrefetchScalarGridSpec(
            num_scalar_prefetch=1,
            grid=(1,),
            in_specs=[whole_block(each.shape) for each in sources]
            + [whole_block(grad_proj.shape)]
            + [pl.BlockSpec(memory_space=pl.ANY)] * len(earlier),
            out_specs=[whole_block(shape)] * 2,
        ),
        out_shape=[result, result],
        compiler_params=pltpu.CompilerParams(vmem_limit_bytes=VMEM_GRADIENT),
        cost_estimate=SMALL_COST,
    )(place, *sources, grad_proj, *earlier)


def sum_of(blocks):
    total = blocks[0].astype(jnp.float32)
    for block in blocks[1:]:
        total = total + block.astype(jnp.float32)
    return total


def level_step(bit, terms, earlier=()):
    count = len(terms)
    pairs = terms[0].shape[0] // 2
    shape = (pairs,) + terms[0].shape[1:]
    block = (1,) + terms[0].shape[1:]
    keep = pl.BlockSpec(block, lambda i, p: (2 * i + p[0], 0, 0))
    send = pl.BlockSpec(block, lambda i, p: (2 * i + 1 - p[0], 0, 0))
    out = pl.BlockSpec(block, lambda i, p: (i, 0, 0))

    def kernel(place_ref, *refs):
        kept_ref, sent_ref = refs[-2:]
        kept_ref[...] = sum_of([ref[...] for ref in refs[:count]])
        sent_ref[...] = sum_of([ref[...] for ref in refs[count : 2 * count]]).astype(jnp.bfloat16)

    return pl.pallas_call(
        kernel,
        grid_spec=pltpu.PrefetchScalarGridSpec(
            num_scalar_prefetch=1,
            grid=(pairs,),
            in_specs=[keep] * count
            + [send] * count
            + [pl.BlockSpec(memory_space=pl.ANY)] * len(earlier),
            out_specs=[out, out],
        ),
        out_shape=[
            jax.ShapeDtypeStruct(shape, jnp.float32),
            jax.ShapeDtypeStruct(shape, jnp.bfloat16),
        ],
        compiler_params=pltpu.CompilerParams(vmem_limit_bytes=VMEM_SMALL),
        cost_estimate=SMALL_COST,
    )(bit.reshape(1).astype(jnp.int32), *terms, *terms, *earlier)


def total_step(terms, parts=1, earlier=()):
    count = terms[0].shape[0] // parts
    shape = (count,) + terms[0].shape[1:]
    blocks = [
        pl.BlockSpec((1,) + shape[1:], lambda i, part=part: (part * count + i, 0, 0))
        for part in range(parts)
    ]

    def kernel(*refs):
        for part in range(parts):
            mine = refs[part * len(terms) : (part + 1) * len(terms)]
            refs[part - parts][...] = sum_of([ref[...] for ref in mine]).astype(jnp.bfloat16)

    return pl.pallas_call(
        kernel,
        grid=(count,),
        in_specs=[block for block in blocks for _ in terms]
        + [pl.BlockSpec(memory_space=pl.ANY)] * len(earlier),
        out_specs=[blocks[0]] * parts,
        out_shape=[jax.ShapeDtypeStruct(shape, jnp.bfloat16)] * parts,
        compiler_params=pltpu.CompilerParams(vmem_limit_bytes=VMEM_SMALL),
        cost_estimate=SMALL_COST,
    )(*[term for _ in range(parts) for term in terms], *earlier)


def project_kernel(place_ref, *refs, calls, local_heads, last):
    sources, weight_ref, out_ref = refs[:4], refs[4], refs[-1]
    rows = []
    for n in range(4):
        side = place_ref[0] if n % 2 == 0 else 1 - place_ref[0]
        for head in calls[n // 2]:
            rows.append(weight_ref[side * local_heads + head])
    columns = jnp.concatenate([each[...] for each in sources], axis=1)
    total = jnp.dot(columns, jnp.concatenate(rows, axis=0), preferred_element_type=jnp.float32)
    if last:
        total = (total + refs[5][...]) * refs[6][...]
    out_ref[...] = total.astype(out_ref.dtype)


def project(place, sources, weight, calls, local_heads, last, earlier):
    heads, depth, columns = weight.shape
    rows = sources[0].shape[0]
    step = columns // PROJECT_STEPS
    block = pl.BlockSpec((rows, step), lambda i, p: (0, i))
    return pl.pallas_call(
        functools.partial(project_kernel, calls=calls, local_heads=local_heads, last=bool(last)),
        grid_spec=pltpu.PrefetchScalarGridSpec(
            num_scalar_prefetch=1,
            grid=(PROJECT_STEPS,),
            in_specs=[whole_block(each.shape) for each in sources]
            + [pl.BlockSpec((heads, depth, step), lambda i, p: (0, 0, i))]
            + ([block, pl.BlockSpec((1, step), lambda i, p: (0, i))] if last else [])
            + [pl.BlockSpec(memory_space=pl.ANY)] * len(earlier),
            out_specs=block,
        ),
        out_shape=jax.ShapeDtypeStruct((rows, columns), jnp.bfloat16 if last else jnp.float32),
        compiler_params=pltpu.CompilerParams(vmem_limit_bytes=VMEM_PROJECT),
        cost_estimate=SMALL_COST,
    )(place, *sources, weight, *last, *earlier)


def contract_tokens(columns, grad_proj, kind):
    return lax.dot_general(
        columns, grad_proj, (((0,), (0,)), ((), ())), preferred_element_type=jnp.float32
    ).astype(kind)


def after(value, *earlier):
    return lax.optimization_barrier((value,) + earlier)[0]


def dp_send(value, flip, sender):
    return lax.ppermute(value, "dp", [(i, i ^ flip) for i in range(HEADS) if sender(i)])


def same_bits(i):
    return (i >> 1 ^ i) & 1 == 0


def paired_device(query_rows, key_rows, value_rows, windows, out_weight, gate_scale, out_grad):
    seq_at = lax.axis_index("seq")
    place = seq_at.reshape(1).astype(jnp.int32)
    local_heads = HEADS // 2
    swap = [(0, 1), (1, 0)]
    calls = [(0, 4), (3, 7), (1, 2), (5, 6)]
    bias = window_bias(windows)
    weight = lax.all_gather(out_weight, "dp", axis=0, tiled=True)
    weight = weight.reshape(HEADS, HEAD_DIM, weight.shape[1])
    gate_row = gate_scale[0].astype(jnp.float32)
    grad_proj = (out_grad.astype(jnp.float32) * gate_row).astype(jnp.bfloat16)
    sources = (query_rows, key_rows, value_rows)

    def pack(n, limit, *earlier):
        return pack_partner(place, local_heads, calls[n], *sources, earlier, limit)

    def attention(n, other, *earlier):
        return attend_pair(place, local_heads, calls[n], *sources, other, bias, earlier)

    def exchange(mine):
        return lax.ppermute(mine, "seq", swap)

    index = lax.axis_index("dp")
    core = index & 1

    where = jnp.stack([seq_at, core]).astype(jnp.int32)

    def core_step(*operands):
        sent, kept = batch_gradient(where, operands[:4], operands[4], True)
        return total_step([kept, dp_send(sent, 1, lambda i: True)])[0]

    def apart(step, *operands):
        shapes = jax.eval_shape(step, *operands)
        return lax.cond(
            windows[0, 0] > 0,
            step,
            lambda *_: jax.tree.map(lambda leaf: jnp.zeros(leaf.shape, leaf.dtype), shapes),
            *operands,
        )

    packed0 = pack(0, VMEM_WHOLE)
    packed1 = pack(1, VMEM_WHOLE, packed0)
    packed2 = pack(2, VMEM_LIMIT, packed1)
    packed3 = pack(3, VMEM_LIMIT, packed2)
    other0 = exchange(packed0)
    other1 = exchange(packed1)
    other2 = exchange(packed2)
    other3 = exchange(packed3)
    mine0 = attention(0, other0, packed3)
    theirs0 = exchange(mine0)
    mine1 = attention(1, other1, mine0)
    theirs1 = exchange(mine1)
    mine2 = attention(2, other2, mine1)
    theirs2 = exchange(mine2)
    mine3 = attention(3, other3, mine2)
    theirs3 = exchange(mine3)

    def unlike(i):
        return not same_bits(i)

    low_bit, high_bit = index >> 2 & 1, index >> 3 & 1
    def like_even(i):
        return unlike(i) and i & 4 == 0

    def like_odd(i):
        return unlike(i) and i & 4 != 0

    first = (mine0, theirs0, mine1, theirs1)
    second = (mine2, theirs2, mine3, theirs3)
    total_a = apart(core_step, after(mine0, mine3), *first[1:], grad_proj)
    across_a = dp_send(total_a, 2, unlike)
    projected = project(place, first, weight, calls[:2], local_heads, (), (total_a, theirs2))
    sent, kept = batch_gradient(where, second, grad_proj, False, (projected,))
    came = dp_send(sent, 1, lambda i: True)
    kept_a, sent_a = level_step(low_bit, [total_a, across_a], (sent,))
    low_a = dp_send(sent_a, 4, same_bits)
    total_b, total_c = total_step([kept, came], 2, (sent_a,))
    across_b = dp_send(total_b, 2, same_bits)
    across_c = dp_send(total_c, 2, same_bits)
    block_out = project(
        place, second, weight, calls[2:], local_heads, (projected, gate_row[None]), (total_b,)
    )
    (sent_b,) = total_step([total_b, across_b], 1, (block_out,))
    low_b = dp_send(sent_b, 4, like_odd)
    kept_a, sent_a = level_step(high_bit, [kept_a, low_a], (sent_b,))
    high_a = dp_send(sent_a, 8, same_bits)
    (sent_c,) = total_step([total_c, across_c], 1, (sent_a,))
    low_c = dp_send(sent_c, 4, like_even)
    kept_b, sent_b = level_step(high_bit, [total_b, across_b, low_b], (sent_c,))
    high_b = dp_send(sent_b, 8, like_even)
    final_a = kept_a[0] + high_a[0].astype(jnp.float32)
    kept_c, sent_c = level_step(high_bit, [total_c, across_c, low_c], (sent_b, high_a))
    high_c = dp_send(sent_c, 8, like_odd)
    final_b = kept_b[0] + after(high_b, sent_c)[0].astype(jnp.float32)
    final_ab = lax.optimization_barrier(jnp.where(same_bits(index), final_a, final_b))
    is_c = jnp.logical_not(same_bits(index)) & (low_bit == 1)
    weight_grad = jnp.where(is_c, kept_c[0] + high_c[0].astype(jnp.float32), final_ab)
    return (block_out, weight_grad)


def general_device(query_rows, key_rows, value_rows, windows, out_weight, gate_scale, out_grad):
    query, key, value = (
        lax.all_to_all(rows, "seq", split_axis=1, concat_axis=0, tiled=True)
        for rows in (query_rows, key_rows, value_rows)
    )
    place = lax.axis_index("seq").reshape(1).astype(jnp.int32)
    mine = attend_whole(place, query, key, value, window_bias(windows))
    columns = lax.all_gather(mine, "seq", axis=1, tiled=True)
    weight = lax.all_gather(out_weight, "dp", axis=0, tiled=True)
    gate_row = gate_scale[0].astype(jnp.float32)
    projected = jnp.dot(columns, weight, preferred_element_type=jnp.float32)
    block_out = (projected * gate_row).astype(jnp.bfloat16)
    grad_proj = (out_grad.astype(jnp.float32) * gate_row).astype(jnp.bfloat16)
    weight_grad = lax.psum_scatter(
        contract_tokens(columns, grad_proj, jnp.float32), "dp", scatter_dimension=0, tiled=True
    )
    return (block_out, weight_grad)


def solution(mesh):
    paired = mesh.shape["seq"] == 2 and mesh.shape["dp"] == HEADS
    return jax.shard_map(
        paired_device if paired else general_device,
        mesh=mesh,
        in_specs=(
            P(("dp", "seq"), None),
            P(("dp", "seq"), None),
            P(("dp", "seq"), None),
            P(),
            P("dp", "seq"),
            P("dp", "seq"),
            P("dp", "seq"),
        ),
        out_specs=(P("dp", "seq"), P("dp", "seq")),
        check_vma=False,
    )
```

```python
import functools
import math

import jax
import jax.numpy as jnp
import numpy as np
from jax import lax
from jax.experimental import pallas as pl
from jax.experimental.pallas import tpu as pltpu
from jax.sharding import PartitionSpec as P

HEADS = 16
HEAD_DIM = 128
GH = 3
GW = 4
GT = 2
TILE = 48
NT = 24
CLIP_TOK = NT * TILE
Q_ROWS = GW * TILE
LOG2_SCALE = math.log2(math.e) / math.sqrt(HEAD_DIM)
VMEM_LIMIT = 16 * 1024 * 1024
VMEM_GRADIENT = 20 * 1024 * 1024
VMEM_PROJECT = 16 * 1024 * 1024
PROJECT_STEPS = 6
GRADIENT_STEPS = 3
SEQ, CORE, X, LOW, HIGH = range(5)
VMEM_WHOLE = 60 * 1024 * 1024
VMEM_SMALL = 12 * 1024 * 1024
SMALL_COST = pl.CostEstimate(flops=1, bytes_accessed=1, transcendentals=0)


def window_bias(windows):
    tile_id = np.arange(NT)
    coords = np.stack([tile_id // (GH * GW), tile_id // GW % GH, tile_id % GW]).astype(np.int32)
    token_coords = np.repeat(coords, TILE, axis=1)
    inside = None
    for axis_no, limit in enumerate((GT, GH, GW)):
        extent = jnp.minimum(windows[:, axis_no], limit)[:, None]
        start = jnp.clip(coords[axis_no][None, :] - (extent - 1) // 2, 0, limit - extent)
        column = token_coords[axis_no][None, None, :]
        here = (column >= start[:, :, None]) & (column < (start + extent)[:, :, None])
        inside = here if inside is None else inside & here
    return jnp.where(inside, 0.0, -jnp.inf).astype(jnp.float32)


def attend_rows(queries, first_tile, bias_ref, keys, values):
    count = queries.shape[0]
    tiles = count // TILE
    scores = lax.dot_general(
        queries, keys, (((1,), (1,)), ((), ())), preferred_element_type=jnp.float32
    )
    bias = bias_ref[0, first_tile : first_tile + tiles, :]
    scores = (scores.reshape(tiles, TILE, CLIP_TOK) + bias[:, None, :]).reshape(count, CLIP_TOK)
    peak = jnp.max(scores, axis=-1, keepdims=True)
    weights = jnp.exp2((scores - peak) * LOG2_SCALE).astype(jnp.bfloat16)
    blended = jnp.dot(weights, values, preferred_element_type=jnp.float32)
    return (blended[:, :HEAD_DIM] / blended[:, HEAD_DIM:]).astype(jnp.bfloat16)


def fill_values(values_ref, parts):
    at = 0
    for part in parts:
        rows = part.shape[0]
        values_ref[at : at + rows, :HEAD_DIM] = part
        at += rows
    values_ref[:, HEAD_DIM:] = jnp.ones((CLIP_TOK, HEAD_DIM), jnp.bfloat16)


def pair_kernel(place_ref, q_ref, k_ref, v_ref, other_ref, bias_ref, *rest):
    out_ref, keys_ref, values_ref = rest[-3:]
    half = CLIP_TOK // 2
    keys_ref[:half, :] = k_ref[...]
    keys_ref[half:, :] = other_ref[1]
    fill_values(values_ref, (v_ref[...], other_ref[2]))
    keys = keys_ref[...]
    values = values_ref[...]
    for side in range(2):
        base = pl.multiple_of((place_ref[0] if side == 0 else 1 - place_ref[0]) * half, half)
        for at in range(0, half, Q_ROWS):
            queries = q_ref[at : at + Q_ROWS, :] if side == 0 else other_ref[0, at : at + Q_ROWS, :]
            first_tile = (side * half + at) // TILE
            out_ref[pl.ds(base + at, Q_ROWS), :] = attend_rows(
                queries, first_tile, bias_ref, keys, values
            )


def whole_kernel(place_ref, q_ref, k_ref, v_ref, bias_ref, out_ref, values_ref):
    fill_values(values_ref, (v_ref[...],))
    keys = k_ref[...]
    values = values_ref[...]
    for at in range(0, CLIP_TOK, Q_ROWS):
        out_ref[at : at + Q_ROWS, :] = attend_rows(
            q_ref[at : at + Q_ROWS, :], at // TILE, bias_ref, keys, values
        )


def attention_cost(heads):
    pairs = heads * CLIP_TOK * CLIP_TOK
    return pl.CostEstimate(
        flops=pairs * HEAD_DIM * 6,
        bytes_accessed=heads * CLIP_TOK * HEAD_DIM * 8,
        transcendentals=pairs,
    )


def attend_pair(place, local_heads, picked, query, key, value, other, bias, earlier):
    half = CLIP_TOK // 2
    first, step = picked[0], picked[1] - picked[0]

    def head(i, place_ref):
        return place_ref[0] * local_heads + first + step * i

    own = pl.BlockSpec((half, HEAD_DIM), lambda i, p: (0, head(i, p)))
    return pl.pallas_call(
        pair_kernel,
        grid_spec=pltpu.PrefetchScalarGridSpec(
            num_scalar_prefetch=1,
            grid=(len(picked),),
            in_specs=[
                own,
                own,
                own,
                pl.BlockSpec((3, half, HEAD_DIM), lambda i, p: (0, 0, i)),
                pl.BlockSpec((1, NT, CLIP_TOK), lambda i, p: (head(i, p), 0, 0)),
            ]
            + [pl.BlockSpec(memory_space=pl.ANY)] * len(earlier),
            out_specs=pl.BlockSpec((CLIP_TOK, HEAD_DIM), lambda i, p: (0, i)),
            scratch_shapes=[
                pltpu.VMEM((CLIP_TOK, HEAD_DIM), jnp.bfloat16),
                pltpu.VMEM((CLIP_TOK, 2 * HEAD_DIM), jnp.bfloat16),
            ],
        ),
        out_shape=jax.ShapeDtypeStruct((CLIP_TOK, len(picked) * HEAD_DIM), jnp.bfloat16),
        compiler_params=pltpu.CompilerParams(vmem_limit_bytes=VMEM_LIMIT),
        cost_estimate=SMALL_COST,
    )(place, query, key, value, other, bias, *earlier)


def attend_whole(place, query, key, value, bias):
    local_heads = query.shape[1] // HEAD_DIM
    column = pl.BlockSpec((CLIP_TOK, HEAD_DIM), lambda i, p: (0, i))
    return pl.pallas_call(
        whole_kernel,
        grid_spec=pltpu.PrefetchScalarGridSpec(
            num_scalar_prefetch=1,
            grid=(local_heads,),
            in_specs=[
                column,
                column,
                column,
                pl.BlockSpec((1, NT, CLIP_TOK), lambda i, p: (p[0] * local_heads + i, 0, 0)),
            ],
            out_specs=column,
            scratch_shapes=[pltpu.VMEM((CLIP_TOK, 2 * HEAD_DIM), jnp.bfloat16)],
        ),
        out_shape=jax.ShapeDtypeStruct(query.shape, jnp.bfloat16),
        compiler_params=pltpu.CompilerParams(vmem_limit_bytes=VMEM_LIMIT),
        cost_estimate=attention_cost(local_heads),
    )(place, query, key, value, bias)


def pack_kernel(place_ref, q_ref, k_ref, v_ref, *rest):
    out_ref = rest[-1]
    out_ref[0] = q_ref[...]
    out_ref[1] = k_ref[...]
    out_ref[2] = v_ref[...]


def pack_partner(place, local_heads, picked, query, key, value, earlier, limit):
    rows = query.shape[0]
    count = len(picked)
    first, step = picked[0], picked[1] - picked[0]

    def head(i, place_ref):
        return (1 - place_ref[0]) * local_heads + first + step * i

    column = pl.BlockSpec((rows, HEAD_DIM), lambda i, p: (0, head(i, p)))
    return pl.pallas_call(
        pack_kernel,
        grid_spec=pltpu.PrefetchScalarGridSpec(
            num_scalar_prefetch=1,
            grid=(count,),
            in_specs=[column, column, column]
            + [pl.BlockSpec(memory_space=pl.ANY)] * len(earlier),
            out_specs=pl.BlockSpec((3, rows, HEAD_DIM), lambda i, p: (0, 0, i)),
        ),
        out_shape=jax.ShapeDtypeStruct((3, rows, count * HEAD_DIM), jnp.bfloat16),
        compiler_params=pltpu.CompilerParams(vmem_limit_bytes=limit),
        cost_estimate=SMALL_COST,
    )(place, query, key, value, *earlier)


def whole_block(shape):
    return pl.BlockSpec(shape, lambda i, p: (0,) * len(shape), pipeline_mode=pl.Buffered(1))


def gradient_kernel(place_ref, *refs, by_call):
    grad_ref = refs[4]
    sent_ref, kept_ref, rows_ref = refs[-3:]
    first_core = place_ref[CORE] == 0
    levels = []
    for n in range(2):
        side = place_ref[SEQ] if n == 0 else 1 - place_ref[SEQ]
        levels += [2 * side, 2 * side + 1] if by_call else [side, 2 + side]

    @pl.when(pl.program_id(0) == 0)
    def _():
        sent, kept = [], []
        for n in range(2):
            for part in range(2):
                if by_call:
                    at = slice(part * HEAD_DIM, (part + 1) * HEAD_DIM)
                    one, two = refs[2 + n][:, at], refs[n][:, at]
                else:
                    one, two = refs[2 * part + n][:, :HEAD_DIM], refs[2 * part + n][:, HEAD_DIM:]
                sent.append(jnp.where(first_core, one, two))
                kept.append(jnp.where(first_core, two, one))
        rows_ref[...] = jnp.concatenate(sent + kept, axis=1).T

    product = jnp.dot(rows_ref[...], grad_ref[...], preferred_element_type=jnp.float32)
    product = product.astype(jnp.bfloat16).reshape(8, HEAD_DIM, grad_ref.shape[1])
    for n, level in enumerate(levels):
        sent_ref[pl.ds(level, 1)] = product[n : n + 1]
        kept_ref[pl.ds(level, 1)] = product[4 + n : 5 + n]


def batch_gradient(place, sources, grad_proj, by_call, earlier=()):
    rows, columns = grad_proj.shape
    step = columns // GRADIENT_STEPS
    out = pl.BlockSpec((4, HEAD_DIM, step), lambda i, p: (0, 0, i))
    result = jax.ShapeDtypeStruct((4, HEAD_DIM, columns), jnp.bfloat16)
    return pl.pallas_call(
        functools.partial(gradient_kernel, by_call=by_call),
        grid_spec=pltpu.PrefetchScalarGridSpec(
            num_scalar_prefetch=1,
            grid=(GRADIENT_STEPS,),
            in_specs=[whole_block(each.shape) for each in sources]
            + [pl.BlockSpec((rows, step), lambda i, p: (0, i))]
            + [pl.BlockSpec(memory_space=pl.ANY)] * len(earlier),
            out_specs=[out, out],
            scratch_shapes=[pltpu.VMEM((8 * HEAD_DIM, rows), jnp.bfloat16)],
        ),
        out_shape=[result, result],
        compiler_params=pltpu.CompilerParams(vmem_limit_bytes=VMEM_GRADIENT),
        cost_estimate=SMALL_COST,
    )(place, *sources, grad_proj, *earlier)


def sum_of(blocks):
    total = blocks[0].astype(jnp.float32)
    for block in blocks[1:]:
        total = total + block.astype(jnp.float32)
    return total


def level_step(place, bit, terms, earlier=()):
    count = len(terms)
    pairs = terms[0].shape[0] // 2
    shape = (pairs,) + terms[0].shape[1:]
    block = (1,) + terms[0].shape[1:]
    keep = pl.BlockSpec(block, lambda i, p: (2 * i + p[bit], 0, 0))
    send = pl.BlockSpec(block, lambda i, p: (2 * i + 1 - p[bit], 0, 0))
    out = pl.BlockSpec(block, lambda i, p: (i, 0, 0))

    def kernel(place_ref, *refs):
        kept_ref, sent_ref = refs[-2:]
        kept_ref[...] = sum_of([ref[...] for ref in refs[:count]])
        sent_ref[...] = sum_of([ref[...] for ref in refs[count : 2 * count]]).astype(jnp.bfloat16)

    return pl.pallas_call(
        kernel,
        grid_spec=pltpu.PrefetchScalarGridSpec(
            num_scalar_prefetch=1,
            grid=(pairs,),
            in_specs=[keep] * count
            + [send] * count
            + [pl.BlockSpec(memory_space=pl.ANY)] * len(earlier),
            out_specs=[out, out],
        ),
        out_shape=[
            jax.ShapeDtypeStruct(shape, jnp.float32),
            jax.ShapeDtypeStruct(shape, jnp.bfloat16),
        ],
        compiler_params=pltpu.CompilerParams(vmem_limit_bytes=VMEM_SMALL),
        cost_estimate=SMALL_COST,
    )(place, *terms, *terms, *earlier)


def total_step(terms, parts=1, earlier=()):
    count = terms[0].shape[0] // parts
    shape = (count,) + terms[0].shape[1:]
    blocks = [
        pl.BlockSpec((1,) + shape[1:], lambda i, part=part: (part * count + i, 0, 0))
        for part in range(parts)
    ]

    def kernel(*refs):
        for part in range(parts):
            mine = refs[part * len(terms) : (part + 1) * len(terms)]
            refs[part - parts][...] = sum_of([ref[...] for ref in mine]).astype(jnp.bfloat16)

    return pl.pallas_call(
        kernel,
        grid=(count,),
        in_specs=[block for block in blocks for _ in terms]
        + [pl.BlockSpec(memory_space=pl.ANY)] * len(earlier),
        out_specs=[blocks[0]] * parts,
        out_shape=[jax.ShapeDtypeStruct(shape, jnp.bfloat16)] * parts,
        compiler_params=pltpu.CompilerParams(vmem_limit_bytes=VMEM_SMALL),
        cost_estimate=SMALL_COST,
    )(*[term for _ in range(parts) for term in terms], *earlier)


def choose_owned(place, batch_a, batch_b, batch_c):
    block = batch_a[0].shape

    def kernel(place_ref, *refs):
        alike = place_ref[CORE] == place_ref[X]
        odd = place_ref[LOW] == 1
        owned = (alike, ~alike & ~odd, ~alike & odd)
        for n, mine in enumerate(owned):

            @pl.when(mine)
            def _():
                refs[-1][...] = refs[2 * n][0] + refs[2 * n + 1][0].astype(jnp.float32)

    return pl.pallas_call(
        kernel,
        grid_spec=pltpu.PrefetchScalarGridSpec(
            num_scalar_prefetch=1,
            grid=(1,),
            in_specs=[whole_block(block)] * 6,
            out_specs=whole_block(block[1:]),
        ),
        out_shape=jax.ShapeDtypeStruct(block[1:], jnp.float32),
        compiler_params=pltpu.CompilerParams(vmem_limit_bytes=VMEM_SMALL),
        cost_estimate=SMALL_COST,
    )(place, *batch_a, *batch_b, *batch_c)


def project_kernel(place_ref, *refs, calls, local_heads, last):
    sources, weight_ref, out_ref = refs[:4], refs[4], refs[-1]
    rows = []
    for n in range(4):
        side = place_ref[0] if n % 2 == 0 else 1 - place_ref[0]
        for head in calls[n // 2]:
            rows.append(weight_ref[side * local_heads + head])
    columns = jnp.concatenate([each[...] for each in sources], axis=1)
    total = jnp.dot(columns, jnp.concatenate(rows, axis=0), preferred_element_type=jnp.float32)
    if last:
        total = (total + refs[5][...]) * refs[6][...]
    out_ref[...] = total.astype(out_ref.dtype)


def project(place, sources, weight, calls, local_heads, last, earlier):
    heads, depth, columns = weight.shape
    rows = sources[0].shape[0]
    step = columns // PROJECT_STEPS
    block = pl.BlockSpec((rows, step), lambda i, p: (0, i))
    return pl.pallas_call(
        functools.partial(project_kernel, calls=calls, local_heads=local_heads, last=bool(last)),
        grid_spec=pltpu.PrefetchScalarGridSpec(
            num_scalar_prefetch=1,
            grid=(PROJECT_STEPS,),
            in_specs=[whole_block(each.shape) for each in sources]
            + [pl.BlockSpec((heads, depth, step), lambda i, p: (0, 0, i))]
            + ([block, pl.BlockSpec((1, step), lambda i, p: (0, i))] if last else [])
            + [pl.BlockSpec(memory_space=pl.ANY)] * len(earlier),
            out_specs=block,
        ),
        out_shape=jax.ShapeDtypeStruct((rows, columns), jnp.bfloat16 if last else jnp.float32),
        compiler_params=pltpu.CompilerParams(vmem_limit_bytes=VMEM_PROJECT),
        cost_estimate=SMALL_COST,
    )(place, *sources, weight, *last, *earlier)


def contract_tokens(columns, grad_proj, kind):
    return lax.dot_general(
        columns, grad_proj, (((0,), (0,)), ((), ())), preferred_element_type=jnp.float32
    ).astype(kind)


def after(value, *earlier):
    return lax.optimization_barrier((value,) + earlier)[0]


def dp_send(value, flip, sender):
    return lax.ppermute(value, "dp", [(i, i ^ flip) for i in range(HEADS) if sender(i)])


def same_bits(i):
    return (i >> 1 ^ i) & 1 == 0


def paired_device(query_rows, key_rows, value_rows, windows, out_weight, gate_scale, out_grad):
    index = lax.axis_index("dp")
    place = jnp.stack([lax.axis_index("seq")] + [index >> bit & 1 for bit in range(4)])
    place = lax.optimization_barrier(place.astype(jnp.int32))
    local_heads = HEADS // 2
    swap = [(0, 1), (1, 0)]
    calls = [(0, 4), (3, 7), (1, 2), (5, 6)]
    bias = window_bias(windows)
    weight = lax.all_gather(out_weight, "dp", axis=0, tiled=True)
    weight = weight.reshape(HEADS, HEAD_DIM, weight.shape[1])
    gate_row = gate_scale[0].astype(jnp.float32)
    grad_proj = (out_grad.astype(jnp.float32) * gate_row).astype(jnp.bfloat16)
    sources = (query_rows, key_rows, value_rows)

    def pack(n, limit, *earlier):
        return pack_partner(place, local_heads, calls[n], *sources, earlier, limit)

    def attention(n, other, *earlier):
        return attend_pair(place, local_heads, calls[n], *sources, other, bias, earlier)

    def exchange(mine):
        return lax.ppermute(mine, "seq", swap)

    def core_step(*operands):
        sent, kept = batch_gradient(place, operands[:4], operands[4], True)
        return total_step([kept, dp_send(sent, 1, lambda i: True)])[0]

    def apart(step, *operands):
        shapes = jax.eval_shape(step, *operands)
        return lax.cond(
            windows[0, 0] > 0,
            step,
            lambda *_: jax.tree.map(lambda leaf: jnp.zeros(leaf.shape, leaf.dtype), shapes),
            *operands,
        )

    packed0 = pack(0, VMEM_WHOLE)
    packed1 = pack(1, VMEM_WHOLE, packed0)
    packed2 = pack(2, VMEM_LIMIT, packed1)
    packed3 = pack(3, VMEM_LIMIT, packed2)
    other0 = exchange(packed0)
    other1 = exchange(packed1)
    other2 = exchange(packed2)
    other3 = exchange(packed3)
    mine0 = attention(0, other0, packed3)
    theirs0 = exchange(mine0)
    mine1 = attention(1, other1, mine0)
    theirs1 = exchange(mine1)
    mine2 = attention(2, other2, mine1)
    theirs2 = exchange(mine2)
    mine3 = attention(3, other3, mine2)
    theirs3 = exchange(mine3)

    def unlike(i):
        return not same_bits(i)

    def like_even(i):
        return unlike(i) and i & 4 == 0

    def like_odd(i):
        return unlike(i) and i & 4 != 0

    first = (mine0, theirs0, mine1, theirs1)
    second = (mine2, theirs2, mine3, theirs3)
    total_a = apart(core_step, after(mine0, mine3, weight), *first[1:], grad_proj)
    across_a = dp_send(total_a, 2, unlike)
    projected = project(place, first, weight, calls[:2], local_heads, (), (total_a, theirs2))
    sent, kept = batch_gradient(place, second, grad_proj, False, (projected,))
    came = dp_send(sent, 1, lambda i: True)
    kept_a, sent_a = level_step(place, LOW, [total_a, across_a], (sent,))
    low_a = dp_send(sent_a, 4, same_bits)
    total_b, total_c = total_step([kept, came], 2, (sent_a,))
    across_b = dp_send(total_b, 2, same_bits)
    across_c = dp_send(total_c, 2, same_bits)
    block_out = project(
        place, second, weight, calls[2:], local_heads, (projected, gate_row[None]), (total_b,)
    )
    (sent_b,) = total_step([total_b, across_b], 1, (block_out,))
    low_b = dp_send(sent_b, 4, like_odd)
    kept_a, sent_a = level_step(place, HIGH, [kept_a, low_a], (sent_b,))
    high_a = dp_send(sent_a, 8, same_bits)
    (sent_c,) = total_step([total_c, across_c], 1, (sent_a,))
    low_c = dp_send(sent_c, 4, like_even)
    kept_b, sent_b = level_step(place, HIGH, [total_b, across_b, low_b], (sent_c,))
    high_b = dp_send(sent_b, 8, like_even)
    kept_c, sent_c = level_step(place, HIGH, [total_c, across_c, low_c], (high_a, high_b))
    high_c = dp_send(sent_c, 8, like_odd)
    weight_grad = choose_owned(place, (kept_a, high_a), (kept_b, high_b), (kept_c, high_c))
    return (block_out, weight_grad)


def general_device(query_rows, key_rows, value_rows, windows, out_weight, gate_scale, out_grad):
    query, key, value = (
        lax.all_to_all(rows, "seq", split_axis=1, concat_axis=0, tiled=True)
        for rows in (query_rows, key_rows, value_rows)
    )
    place = lax.axis_index("seq").reshape(1).astype(jnp.int32)
    mine = attend_whole(place, query, key, value, window_bias(windows))
    columns = lax.all_gather(mine, "seq", axis=1, tiled=True)
    weight = lax.all_gather(out_weight, "dp", axis=0, tiled=True)
    gate_row = gate_scale[0].astype(jnp.float32)
    projected = jnp.dot(columns, weight, preferred_element_type=jnp.float32)
    block_out = (projected * gate_row).astype(jnp.bfloat16)
    grad_proj = (out_grad.astype(jnp.float32) * gate_row).astype(jnp.bfloat16)
    weight_grad = lax.psum_scatter(
        contract_tokens(columns, grad_proj, jnp.float32), "dp", scatter_dimension=0, tiled=True
    )
    return (block_out, weight_grad)


def solution(mesh):
    paired = mesh.shape["seq"] == 2 and mesh.shape["dp"] == HEADS
    return jax.shard_map(
        paired_device if paired else general_device,
        mesh=mesh,
        in_specs=(
            P(("dp", "seq"), None),
            P(("dp", "seq"), None),
            P(("dp", "seq"), None),
            P(),
            P("dp", "seq"),
            P("dp", "seq"),
            P("dp", "seq"),
        ),
        out_specs=(P("dp", "seq"), P("dp", "seq")),
        check_vma=False,
    )
```

```python
import functools
import math

import jax
import jax.numpy as jnp
import numpy as np
from jax import lax
from jax.experimental import pallas as pl
from jax.experimental.pallas import tpu as pltpu
from jax.sharding import PartitionSpec as P

HEADS = 16
HEAD_DIM = 128
GH = 3
GW = 4
GT = 2
TILE = 48
NT = 24
CLIP_TOK = NT * TILE
Q_ROWS = GW * TILE
LOG2_SCALE = math.log2(math.e) / math.sqrt(HEAD_DIM)
VMEM_LIMIT = 16 * 1024 * 1024
VMEM_GRADIENT = 20 * 1024 * 1024
VMEM_PROJECT = 16 * 1024 * 1024
PROJECT_STEPS = 6
GRADIENT_STEPS = 3
SEQ, CORE, X, LOW, HIGH = range(5)
VMEM_WHOLE = 60 * 1024 * 1024
VMEM_SMALL = 12 * 1024 * 1024
SMALL_COST = pl.CostEstimate(flops=1, bytes_accessed=1, transcendentals=0)


def window_bias(windows):
    tile_id = np.arange(NT)
    coords = np.stack([tile_id // (GH * GW), tile_id // GW % GH, tile_id % GW]).astype(np.int32)
    token_coords = np.repeat(coords, TILE, axis=1)
    inside = None
    for axis_no, limit in enumerate((GT, GH, GW)):
        extent = jnp.minimum(windows[:, axis_no], limit)[:, None]
        start = jnp.clip(coords[axis_no][None, :] - (extent - 1) // 2, 0, limit - extent)
        column = token_coords[axis_no][None, None, :]
        here = (column >= start[:, :, None]) & (column < (start + extent)[:, :, None])
        inside = here if inside is None else inside & here
    return jnp.where(inside, 0.0, -jnp.inf).astype(jnp.float32)


def attend_rows(queries, first_tile, bias_ref, keys, values):
    count = queries.shape[0]
    tiles = count // TILE
    scores = lax.dot_general(
        queries, keys, (((1,), (1,)), ((), ())), preferred_element_type=jnp.float32
    )
    bias = bias_ref[0, first_tile : first_tile + tiles, :]
    scores = (scores.reshape(tiles, TILE, CLIP_TOK) + bias[:, None, :]).reshape(count, CLIP_TOK)
    peak = jnp.max(scores, axis=-1, keepdims=True)
    weights = jnp.exp2((scores - peak) * LOG2_SCALE).astype(jnp.bfloat16)
    blended = jnp.dot(weights, values, preferred_element_type=jnp.float32)
    return (blended[:, :HEAD_DIM] / blended[:, HEAD_DIM:]).astype(jnp.bfloat16)


def fill_values(values_ref, parts):
    at = 0
    for part in parts:
        rows = part.shape[0]
        values_ref[at : at + rows, :HEAD_DIM] = part
        at += rows
    values_ref[:, HEAD_DIM:] = jnp.ones((CLIP_TOK, HEAD_DIM), jnp.bfloat16)


def pair_kernel(place_ref, q_ref, k_ref, v_ref, other_ref, bias_ref, *rest):
    out_ref, keys_ref, values_ref = rest[-3:]
    half = CLIP_TOK // 2
    keys_ref[:half, :] = k_ref[...]
    keys_ref[half:, :] = other_ref[1]
    fill_values(values_ref, (v_ref[...], other_ref[2]))
    keys = keys_ref[...]
    values = values_ref[...]
    for side in range(2):
        base = pl.multiple_of((place_ref[0] if side == 0 else 1 - place_ref[0]) * half, half)
        for at in range(0, half, Q_ROWS):
            queries = q_ref[at : at + Q_ROWS, :] if side == 0 else other_ref[0, at : at + Q_ROWS, :]
            first_tile = (side * half + at) // TILE
            out_ref[pl.ds(base + at, Q_ROWS), :] = attend_rows(
                queries, first_tile, bias_ref, keys, values
            )


def whole_kernel(place_ref, q_ref, k_ref, v_ref, bias_ref, out_ref, values_ref):
    fill_values(values_ref, (v_ref[...],))
    keys = k_ref[...]
    values = values_ref[...]
    for at in range(0, CLIP_TOK, Q_ROWS):
        out_ref[at : at + Q_ROWS, :] = attend_rows(
            q_ref[at : at + Q_ROWS, :], at // TILE, bias_ref, keys, values
        )


def attention_cost(heads):
    pairs = heads * CLIP_TOK * CLIP_TOK
    return pl.CostEstimate(
        flops=pairs * HEAD_DIM * 6,
        bytes_accessed=heads * CLIP_TOK * HEAD_DIM * 8,
        transcendentals=pairs,
    )


def attend_pair(place, local_heads, picked, query, key, value, other, bias, earlier):
    half = CLIP_TOK // 2
    first, step = picked[0], picked[1] - picked[0]

    def head(i, place_ref):
        return place_ref[0] * local_heads + first + step * i

    own = pl.BlockSpec((half, HEAD_DIM), lambda i, p: (0, head(i, p)))
    return pl.pallas_call(
        pair_kernel,
        grid_spec=pltpu.PrefetchScalarGridSpec(
            num_scalar_prefetch=1,
            grid=(len(picked),),
            in_specs=[
                own,
                own,
                own,
                pl.BlockSpec((3, half, HEAD_DIM), lambda i, p: (0, 0, i)),
                pl.BlockSpec((1, NT, CLIP_TOK), lambda i, p: (head(i, p), 0, 0)),
            ]
            + [pl.BlockSpec(memory_space=pl.ANY)] * len(earlier),
            out_specs=pl.BlockSpec((CLIP_TOK, HEAD_DIM), lambda i, p: (0, i)),
            scratch_shapes=[
                pltpu.VMEM((CLIP_TOK, HEAD_DIM), jnp.bfloat16),
                pltpu.VMEM((CLIP_TOK, 2 * HEAD_DIM), jnp.bfloat16),
            ],
        ),
        out_shape=jax.ShapeDtypeStruct((CLIP_TOK, len(picked) * HEAD_DIM), jnp.bfloat16),
        compiler_params=pltpu.CompilerParams(vmem_limit_bytes=VMEM_LIMIT),
        cost_estimate=SMALL_COST,
    )(place, query, key, value, other, bias, *earlier)


def attend_whole(place, query, key, value, bias):
    local_heads = query.shape[1] // HEAD_DIM
    column = pl.BlockSpec((CLIP_TOK, HEAD_DIM), lambda i, p: (0, i))
    return pl.pallas_call(
        whole_kernel,
        grid_spec=pltpu.PrefetchScalarGridSpec(
            num_scalar_prefetch=1,
            grid=(local_heads,),
            in_specs=[
                column,
                column,
                column,
                pl.BlockSpec((1, NT, CLIP_TOK), lambda i, p: (p[0] * local_heads + i, 0, 0)),
            ],
            out_specs=column,
            scratch_shapes=[pltpu.VMEM((CLIP_TOK, 2 * HEAD_DIM), jnp.bfloat16)],
        ),
        out_shape=jax.ShapeDtypeStruct(query.shape, jnp.bfloat16),
        compiler_params=pltpu.CompilerParams(vmem_limit_bytes=VMEM_LIMIT),
        cost_estimate=attention_cost(local_heads),
    )(place, query, key, value, bias)


def pack_kernel(place_ref, q_ref, k_ref, v_ref, *rest):
    out_ref = rest[-1]
    out_ref[0] = q_ref[...]
    out_ref[1] = k_ref[...]
    out_ref[2] = v_ref[...]


def pack_partner(place, local_heads, picked, query, key, value, earlier, limit):
    rows = query.shape[0]
    count = len(picked)
    first, step = picked[0], picked[1] - picked[0]

    def head(i, place_ref):
        return (1 - place_ref[0]) * local_heads + first + step * i

    column = pl.BlockSpec((rows, HEAD_DIM), lambda i, p: (0, head(i, p)))
    return pl.pallas_call(
        pack_kernel,
        grid_spec=pltpu.PrefetchScalarGridSpec(
            num_scalar_prefetch=1,
            grid=(count,),
            in_specs=[column, column, column]
            + [pl.BlockSpec(memory_space=pl.ANY)] * len(earlier),
            out_specs=pl.BlockSpec((3, rows, HEAD_DIM), lambda i, p: (0, 0, i)),
        ),
        out_shape=jax.ShapeDtypeStruct((3, rows, count * HEAD_DIM), jnp.bfloat16),
        compiler_params=pltpu.CompilerParams(vmem_limit_bytes=limit),
        cost_estimate=SMALL_COST,
    )(place, query, key, value, *earlier)


def whole_block(shape):
    return pl.BlockSpec(shape, lambda i, p: (0,) * len(shape), pipeline_mode=pl.Buffered(1))


def gradient_kernel(place_ref, *refs, by_call):
    grad_ref = refs[4]
    sent_ref, kept_ref, rows_ref = refs[-3:]
    first_core = place_ref[CORE] == 0
    levels = []
    for n in range(2):
        side = place_ref[SEQ] if n == 0 else 1 - place_ref[SEQ]
        levels += [2 * side, 2 * side + 1] if by_call else [side, 2 + side]

    @pl.when(pl.program_id(0) == 0)
    def _():
        sent, kept = [], []
        for n in range(2):
            for part in range(2):
                if by_call:
                    at = slice(part * HEAD_DIM, (part + 1) * HEAD_DIM)
                    one, two = refs[2 + n][:, at], refs[n][:, at]
                else:
                    one, two = refs[2 * part + n][:, :HEAD_DIM], refs[2 * part + n][:, HEAD_DIM:]
                sent.append(jnp.where(first_core, one, two))
                kept.append(jnp.where(first_core, two, one))
        rows_ref[...] = jnp.concatenate(sent + kept, axis=1).T

    product = jnp.dot(rows_ref[...], grad_ref[...], preferred_element_type=jnp.float32)
    product = product.astype(jnp.bfloat16).reshape(8, HEAD_DIM, grad_ref.shape[1])
    for n, level in enumerate(levels):
        sent_ref[pl.ds(level, 1)] = product[n : n + 1]
        kept_ref[pl.ds(level, 1)] = product[4 + n : 5 + n]


def batch_gradient(place, sources, grad_proj, by_call, earlier=()):
    rows, columns = grad_proj.shape
    step = columns // GRADIENT_STEPS
    out = pl.BlockSpec((4, HEAD_DIM, step), lambda i, p: (0, 0, i))
    result = jax.ShapeDtypeStruct((4, HEAD_DIM, columns), jnp.bfloat16)
    return pl.pallas_call(
        functools.partial(gradient_kernel, by_call=by_call),
        grid_spec=pltpu.PrefetchScalarGridSpec(
            num_scalar_prefetch=1,
            grid=(GRADIENT_STEPS,),
            in_specs=[whole_block(each.shape) for each in sources]
            + [pl.BlockSpec((rows, step), lambda i, p: (0, i))]
            + [pl.BlockSpec(memory_space=pl.ANY)] * len(earlier),
            out_specs=[out, out],
            scratch_shapes=[pltpu.VMEM((8 * HEAD_DIM, rows), jnp.bfloat16)],
        ),
        out_shape=[result, result],
        compiler_params=pltpu.CompilerParams(vmem_limit_bytes=VMEM_GRADIENT),
        cost_estimate=SMALL_COST,
    )(place, *sources, grad_proj, *earlier)


def sum_of(blocks):
    total = blocks[0].astype(jnp.float32)
    for block in blocks[1:]:
        total = total + block.astype(jnp.float32)
    return total


def level_step(place, bit, terms, earlier=()):
    count = len(terms)
    pairs = terms[0].shape[0] // 2
    shape = (pairs,) + terms[0].shape[1:]
    block = (1,) + terms[0].shape[1:]
    keep = pl.BlockSpec(block, lambda i, p: (2 * i + p[bit], 0, 0))
    send = pl.BlockSpec(block, lambda i, p: (2 * i + 1 - p[bit], 0, 0))
    out = pl.BlockSpec(block, lambda i, p: (i, 0, 0))

    def kernel(place_ref, *refs):
        kept_ref, sent_ref = refs[-2:]
        kept_ref[...] = sum_of([ref[...] for ref in refs[:count]])
        sent_ref[...] = sum_of([ref[...] for ref in refs[count : 2 * count]]).astype(jnp.bfloat16)

    return pl.pallas_call(
        kernel,
        grid_spec=pltpu.PrefetchScalarGridSpec(
            num_scalar_prefetch=1,
            grid=(pairs,),
            in_specs=[keep] * count
            + [send] * count
            + [pl.BlockSpec(memory_space=pl.ANY)] * len(earlier),
            out_specs=[out, out],
        ),
        out_shape=[
            jax.ShapeDtypeStruct(shape, jnp.float32),
            jax.ShapeDtypeStruct(shape, jnp.bfloat16),
        ],
        compiler_params=pltpu.CompilerParams(vmem_limit_bytes=VMEM_SMALL),
        cost_estimate=SMALL_COST,
    )(place, *terms, *terms, *earlier)


def total_step(terms, parts=1, earlier=()):
    count = terms[0].shape[0] // parts
    shape = (count,) + terms[0].shape[1:]
    blocks = [
        pl.BlockSpec((1,) + shape[1:], lambda i, part=part: (part * count + i, 0, 0))
        for part in range(parts)
    ]

    def kernel(*refs):
        for part in range(parts):
            mine = refs[part * len(terms) : (part + 1) * len(terms)]
            refs[part - parts][...] = sum_of([ref[...] for ref in mine]).astype(jnp.bfloat16)

    return pl.pallas_call(
        kernel,
        grid=(count,),
        in_specs=[block for block in blocks for _ in terms]
        + [pl.BlockSpec(memory_space=pl.ANY)] * len(earlier),
        out_specs=[blocks[0]] * parts,
        out_shape=[jax.ShapeDtypeStruct(shape, jnp.bfloat16)] * parts,
        compiler_params=pltpu.CompilerParams(vmem_limit_bytes=VMEM_SMALL),
        cost_estimate=SMALL_COST,
    )(*[term for _ in range(parts) for term in terms], *earlier)


def choose_owned(place, batch_a, batch_b, batch_c):
    block = batch_a[0].shape

    def kernel(place_ref, *refs):
        alike = place_ref[CORE] == place_ref[X]
        odd = place_ref[LOW] == 1
        owned = (alike, ~alike & ~odd, ~alike & odd)
        for n, mine in enumerate(owned):

            @pl.when(mine)
            def _():
                refs[-1][...] = refs[2 * n][0] + refs[2 * n + 1][0].astype(jnp.float32)

    return pl.pallas_call(
        kernel,
        grid_spec=pltpu.PrefetchScalarGridSpec(
            num_scalar_prefetch=1,
            grid=(1,),
            in_specs=[whole_block(block)] * 6,
            out_specs=whole_block(block[1:]),
        ),
        out_shape=jax.ShapeDtypeStruct(block[1:], jnp.float32),
        compiler_params=pltpu.CompilerParams(vmem_limit_bytes=VMEM_SMALL),
        cost_estimate=SMALL_COST,
    )(place, *batch_a, *batch_b, *batch_c)


def project_kernel(place_ref, *refs, calls, local_heads, last):
    sources, weight_ref, out_ref, done_ref = refs[:4], refs[4], refs[-2], refs[-1]
    done_ref[...] = jnp.zeros_like(done_ref)
    rows = []
    for n in range(4):
        side = place_ref[0] if n % 2 == 0 else 1 - place_ref[0]
        for head in calls[n // 2]:
            rows.append(weight_ref[side * local_heads + head])
    columns = jnp.concatenate([each[...] for each in sources], axis=1)
    total = jnp.dot(columns, jnp.concatenate(rows, axis=0), preferred_element_type=jnp.float32)
    if last:
        total = (total + refs[5][...]) * refs[6][...]
    out_ref[...] = total.astype(out_ref.dtype)


def project(place, sources, weight, calls, local_heads, last, earlier):
    heads, depth, columns = weight.shape
    rows = sources[0].shape[0]
    step = columns // PROJECT_STEPS
    block = pl.BlockSpec((rows, step), lambda i, p: (0, i))
    return pl.pallas_call(
        functools.partial(project_kernel, calls=calls, local_heads=local_heads, last=bool(last)),
        grid_spec=pltpu.PrefetchScalarGridSpec(
            num_scalar_prefetch=1,
            grid=(PROJECT_STEPS,),
            in_specs=[whole_block(each.shape) for each in sources]
            + [pl.BlockSpec((heads, depth, step), lambda i, p: (0, 0, i))]
            + ([block, pl.BlockSpec((1, step), lambda i, p: (0, i))] if last else [])
            + [pl.BlockSpec(memory_space=pl.ANY)] * len(earlier),
            out_specs=[block, pl.BlockSpec((8, HEAD_DIM), lambda i, p: (0, 0))],
        ),
        out_shape=[
            jax.ShapeDtypeStruct((rows, columns), jnp.bfloat16 if last else jnp.float32),
            jax.ShapeDtypeStruct((8, HEAD_DIM), jnp.float32),
        ],
        compiler_params=pltpu.CompilerParams(vmem_limit_bytes=VMEM_PROJECT),
        cost_estimate=SMALL_COST,
    )(place, *sources, weight, *last, *earlier)


def contract_tokens(columns, grad_proj, kind):
    return lax.dot_general(
        columns, grad_proj, (((0,), (0,)), ((), ())), preferred_element_type=jnp.float32
    ).astype(kind)


def after(value, *earlier):
    return lax.optimization_barrier((value,) + earlier)[0]


def dp_send(value, flip, sender):
    return lax.ppermute(value, "dp", [(i, i ^ flip) for i in range(HEADS) if sender(i)])


def same_bits(i):
    return (i >> 1 ^ i) & 1 == 0


def paired_device(query_rows, key_rows, value_rows, windows, out_weight, gate_scale, out_grad):
    index = lax.axis_index("dp")
    place = jnp.stack([lax.axis_index("seq")] + [index >> bit & 1 for bit in range(4)])
    place = lax.optimization_barrier(place.astype(jnp.int32))
    local_heads = HEADS // 2
    swap = [(0, 1), (1, 0)]
    calls = [(0, 4), (3, 7), (1, 2), (5, 6)]
    bias = window_bias(windows)
    weight = lax.all_gather(out_weight, "dp", axis=0, tiled=True)
    weight = weight.reshape(HEADS, HEAD_DIM, weight.shape[1])
    gate_row = gate_scale[0].astype(jnp.float32)
    grad_proj = (out_grad.astype(jnp.float32) * gate_row).astype(jnp.bfloat16)
    sources = (query_rows, key_rows, value_rows)

    def pack(n, limit, *earlier):
        return pack_partner(place, local_heads, calls[n], *sources, earlier, limit)

    def attention(n, other, *earlier):
        return attend_pair(place, local_heads, calls[n], *sources, other, bias, earlier)

    def exchange(mine):
        return lax.ppermute(mine, "seq", swap)

    def core_step(*operands):
        sent, kept = batch_gradient(place, operands[:4], operands[4], True)
        return total_step([kept, dp_send(sent, 1, lambda i: True)])[0]

    def apart(step, *operands):
        shapes = jax.eval_shape(step, *operands)
        return lax.cond(
            windows[0, 0] > 0,
            step,
            lambda *_: jax.tree.map(lambda leaf: jnp.zeros(leaf.shape, leaf.dtype), shapes),
            *operands,
        )

    packed0 = pack(0, VMEM_WHOLE)
    packed1 = pack(1, VMEM_WHOLE, packed0)
    packed2 = pack(2, VMEM_LIMIT, packed1)
    other0 = exchange(packed0)
    other1 = exchange(packed1)
    other2 = exchange(packed2)
    mine0 = attention(0, other0, packed2)
    theirs0 = exchange(mine0)
    mine1 = attention(1, other1, mine0)
    theirs1 = exchange(mine1)
    packed3 = pack(3, VMEM_LIMIT, mine1)
    other3 = exchange(packed3)
    mine2 = attention(2, other2, mine1, packed3)
    theirs2 = exchange(mine2)

    def unlike(i):
        return not same_bits(i)

    def like_even(i):
        return unlike(i) and i & 4 == 0

    def like_odd(i):
        return unlike(i) and i & 4 != 0

    first = (mine0, theirs0, mine1, theirs1)
    total_a = apart(core_step, after(mine0, mine2, weight), *first[1:], grad_proj)
    across_a = dp_send(total_a, 2, unlike)
    mine3 = attention(3, other3, total_a)
    theirs3 = exchange(mine3)
    projected, done = project(place, first, weight, calls[:2], local_heads, (), (mine3,))
    second = (mine2, theirs2, mine3, theirs3)
    sent, kept = batch_gradient(place, second, grad_proj, False, (done,))
    came = dp_send(sent, 1, lambda i: True)
    kept_a, sent_a = level_step(place, LOW, [total_a, across_a], (sent,))
    low_a = dp_send(sent_a, 4, same_bits)
    total_b, total_c = total_step([kept, came], 2, (sent_a,))
    across_b = dp_send(total_b, 2, same_bits)
    across_c = dp_send(total_c, 2, same_bits)
    block_out, done = project(
        place, second, weight, calls[2:], local_heads, (projected, gate_row[None]), (total_b,)
    )
    kept_a, sent_a = level_step(place, HIGH, [kept_a, low_a], (done,))
    high_a = dp_send(sent_a, 8, same_bits)
    (sent_b,) = total_step([total_b, across_b], 1, (sent_a,))
    low_b = dp_send(sent_b, 4, like_odd)
    (sent_c,) = total_step([total_c, across_c], 1, (sent_b,))
    low_c = dp_send(sent_c, 4, like_even)
    kept_b, sent_b = level_step(place, HIGH, [total_b, across_b, low_b], (sent_c,))
    high_b = dp_send(sent_b, 8, like_even)
    kept_c, sent_c = level_step(place, HIGH, [total_c, across_c, low_c], (high_a, high_b))
    high_c = dp_send(sent_c, 8, like_odd)
    weight_grad = choose_owned(place, (kept_a, high_a), (kept_b, high_b), (kept_c, high_c))
    return (block_out, weight_grad)


def general_device(query_rows, key_rows, value_rows, windows, out_weight, gate_scale, out_grad):
    query, key, value = (
        lax.all_to_all(rows, "seq", split_axis=1, concat_axis=0, tiled=True)
        for rows in (query_rows, key_rows, value_rows)
    )
    place = lax.axis_index("seq").reshape(1).astype(jnp.int32)
    mine = attend_whole(place, query, key, value, window_bias(windows))
    columns = lax.all_gather(mine, "seq", axis=1, tiled=True)
    weight = lax.all_gather(out_weight, "dp", axis=0, tiled=True)
    gate_row = gate_scale[0].astype(jnp.float32)
    projected = jnp.dot(columns, weight, preferred_element_type=jnp.float32)
    block_out = (projected * gate_row).astype(jnp.bfloat16)
    grad_proj = (out_grad.astype(jnp.float32) * gate_row).astype(jnp.bfloat16)
    weight_grad = lax.psum_scatter(
        contract_tokens(columns, grad_proj, jnp.float32), "dp", scatter_dimension=0, tiled=True
    )
    return (block_out, weight_grad)


def solution(mesh):
    paired = mesh.shape["seq"] == 2 and mesh.shape["dp"] == HEADS
    return jax.shard_map(
        paired_device if paired else general_device,
        mesh=mesh,
        in_specs=(
            P(("dp", "seq"), None),
            P(("dp", "seq"), None),
            P(("dp", "seq"), None),
            P(),
            P("dp", "seq"),
            P("dp", "seq"),
            P("dp", "seq"),
        ),
        out_specs=(P("dp", "seq"), P("dp", "seq")),
        check_vma=False,
    )
```

```python
import functools
import math

import jax
import jax.numpy as jnp
import numpy as np
from jax import lax
from jax.experimental import pallas as pl
from jax.experimental.pallas import tpu as pltpu
from jax.sharding import PartitionSpec as P

HEADS = 16
HEAD_DIM = 128
GH = 3
GW = 4
GT = 2
TILE = 48
NT = 24
CLIP_TOK = NT * TILE
Q_ROWS = GW * TILE
LOG2_SCALE = math.log2(math.e) / math.sqrt(HEAD_DIM)
VMEM_LIMIT = 16 * 1024 * 1024
VMEM_GRADIENT = 20 * 1024 * 1024
VMEM_PROJECT = 16 * 1024 * 1024
PROJECT_STEPS = 6
GRADIENT_STEPS = 3
SEQ, CORE, X, LOW, HIGH = range(5)
VMEM_WHOLE = 60 * 1024 * 1024
VMEM_SMALL = 12 * 1024 * 1024
SMALL_COST = pl.CostEstimate(flops=1, bytes_accessed=1, transcendentals=0)
FIRST_PROJECT_COST = pl.CostEstimate(flops=2 * 10**10, bytes_accessed=2 * 10**7, transcendentals=0)


def window_bias(windows):
    tile_id = np.arange(NT)
    coords = np.stack([tile_id // (GH * GW), tile_id // GW % GH, tile_id % GW]).astype(np.int32)
    token_coords = np.repeat(coords, TILE, axis=1)
    inside = None
    for axis_no, limit in enumerate((GT, GH, GW)):
        extent = jnp.minimum(windows[:, axis_no], limit)[:, None]
        start = jnp.clip(coords[axis_no][None, :] - (extent - 1) // 2, 0, limit - extent)
        column = token_coords[axis_no][None, None, :]
        here = (column >= start[:, :, None]) & (column < (start + extent)[:, :, None])
        inside = here if inside is None else inside & here
    return jnp.where(inside, 0.0, -jnp.inf).astype(jnp.float32)


def attend_rows(queries, first_tile, bias_ref, keys, values):
    count = queries.shape[0]
    tiles = count // TILE
    scores = lax.dot_general(
        queries, keys, (((1,), (1,)), ((), ())), preferred_element_type=jnp.float32
    )
    bias = bias_ref[0, first_tile : first_tile + tiles, :]
    scores = (scores.reshape(tiles, TILE, CLIP_TOK) + bias[:, None, :]).reshape(count, CLIP_TOK)
    peak = jnp.max(scores, axis=-1, keepdims=True)
    weights = jnp.exp2((scores - peak) * LOG2_SCALE).astype(jnp.bfloat16)
    blended = jnp.dot(weights, values, preferred_element_type=jnp.float32)
    return (blended[:, :HEAD_DIM] / blended[:, HEAD_DIM:]).astype(jnp.bfloat16)


def fill_values(values_ref, parts):
    at = 0
    for part in parts:
        rows = part.shape[0]
        values_ref[at : at + rows, :HEAD_DIM] = part
        at += rows
    values_ref[:, HEAD_DIM:] = jnp.ones((CLIP_TOK, HEAD_DIM), jnp.bfloat16)


def pair_kernel(place_ref, q_ref, k_ref, v_ref, other_ref, bias_ref, *rest):
    out_ref, keys_ref, values_ref = rest[-3:]
    half = CLIP_TOK // 2
    keys_ref[:half, :] = k_ref[...]
    keys_ref[half:, :] = other_ref[1]
    fill_values(values_ref, (v_ref[...], other_ref[2]))
    keys = keys_ref[...]
    values = values_ref[...]
    for side in range(2):
        base = pl.multiple_of((place_ref[0] if side == 0 else 1 - place_ref[0]) * half, half)
        for at in range(0, half, Q_ROWS):
            queries = q_ref[at : at + Q_ROWS, :] if side == 0 else other_ref[0, at : at + Q_ROWS, :]
            first_tile = (side * half + at) // TILE
            out_ref[pl.ds(base + at, Q_ROWS), :] = attend_rows(
                queries, first_tile, bias_ref, keys, values
            )


def whole_kernel(place_ref, q_ref, k_ref, v_ref, bias_ref, out_ref, values_ref):
    fill_values(values_ref, (v_ref[...],))
    keys = k_ref[...]
    values = values_ref[...]
    for at in range(0, CLIP_TOK, Q_ROWS):
        out_ref[at : at + Q_ROWS, :] = attend_rows(
            q_ref[at : at + Q_ROWS, :], at // TILE, bias_ref, keys, values
        )


def attention_cost(heads):
    pairs = heads * CLIP_TOK * CLIP_TOK
    return pl.CostEstimate(
        flops=pairs * HEAD_DIM * 6,
        bytes_accessed=heads * CLIP_TOK * HEAD_DIM * 8,
        transcendentals=pairs,
    )


def attend_pair(place, local_heads, picked, query, key, value, other, bias, earlier, limit):
    half = CLIP_TOK // 2
    first, step = picked[0], picked[1] - picked[0]

    def head(i, place_ref):
        return place_ref[0] * local_heads + first + step * i

    own = pl.BlockSpec((half, HEAD_DIM), lambda i, p: (0, head(i, p)))
    return pl.pallas_call(
        pair_kernel,
        grid_spec=pltpu.PrefetchScalarGridSpec(
            num_scalar_prefetch=1,
            grid=(len(picked),),
            in_specs=[
                own,
                own,
                own,
                pl.BlockSpec((3, half, HEAD_DIM), lambda i, p: (0, 0, i)),
                pl.BlockSpec((1, NT, CLIP_TOK), lambda i, p: (head(i, p), 0, 0)),
            ]
            + [pl.BlockSpec(memory_space=pl.ANY)] * len(earlier),
            out_specs=pl.BlockSpec((CLIP_TOK, HEAD_DIM), lambda i, p: (0, i)),
            scratch_shapes=[
                pltpu.VMEM((CLIP_TOK, HEAD_DIM), jnp.bfloat16),
                pltpu.VMEM((CLIP_TOK, 2 * HEAD_DIM), jnp.bfloat16),
            ],
        ),
        out_shape=jax.ShapeDtypeStruct((CLIP_TOK, len(picked) * HEAD_DIM), jnp.bfloat16),
        compiler_params=pltpu.CompilerParams(vmem_limit_bytes=limit),
        cost_estimate=SMALL_COST,
    )(place, query, key, value, other, bias, *earlier)


def attend_whole(place, query, key, value, bias):
    local_heads = query.shape[1] // HEAD_DIM
    column = pl.BlockSpec((CLIP_TOK, HEAD_DIM), lambda i, p: (0, i))
    return pl.pallas_call(
        whole_kernel,
        grid_spec=pltpu.PrefetchScalarGridSpec(
            num_scalar_prefetch=1,
            grid=(local_heads,),
            in_specs=[
                column,
                column,
                column,
                pl.BlockSpec((1, NT, CLIP_TOK), lambda i, p: (p[0] * local_heads + i, 0, 0)),
            ],
            out_specs=column,
            scratch_shapes=[pltpu.VMEM((CLIP_TOK, 2 * HEAD_DIM), jnp.bfloat16)],
        ),
        out_shape=jax.ShapeDtypeStruct(query.shape, jnp.bfloat16),
        compiler_params=pltpu.CompilerParams(vmem_limit_bytes=VMEM_LIMIT),
        cost_estimate=attention_cost(local_heads),
    )(place, query, key, value, bias)


def pack_kernel(place_ref, q_ref, k_ref, v_ref, *rest):
    out_ref = rest[-1]
    out_ref[0] = q_ref[...]
    out_ref[1] = k_ref[...]
    out_ref[2] = v_ref[...]


def pack_partner(place, local_heads, picked, query, key, value, earlier, limit):
    rows = query.shape[0]
    count = len(picked)
    first, step = picked[0], picked[1] - picked[0]

    def head(i, place_ref):
        return (1 - place_ref[0]) * local_heads + first + step * i

    column = pl.BlockSpec((rows, HEAD_DIM), lambda i, p: (0, head(i, p)))
    return pl.pallas_call(
        pack_kernel,
        grid_spec=pltpu.PrefetchScalarGridSpec(
            num_scalar_prefetch=1,
            grid=(count,),
            in_specs=[column, column, column]
            + [pl.BlockSpec(memory_space=pl.ANY)] * len(earlier),
            out_specs=pl.BlockSpec((3, rows, HEAD_DIM), lambda i, p: (0, 0, i)),
        ),
        out_shape=jax.ShapeDtypeStruct((3, rows, count * HEAD_DIM), jnp.bfloat16),
        compiler_params=pltpu.CompilerParams(vmem_limit_bytes=limit),
        cost_estimate=SMALL_COST,
    )(place, query, key, value, *earlier)


def whole_block(shape):
    return pl.BlockSpec(shape, lambda i, p: (0,) * len(shape), pipeline_mode=pl.Buffered(1))


def gradient_kernel(place_ref, *refs, by_call):
    count = 4 if by_call else 2
    grad_ref = refs[count]
    sent_ref, kept_ref, rows_ref = refs[-3:]
    first_core = place_ref[CORE] == 0
    sides = (place_ref[SEQ], 1 - place_ref[SEQ])

    @pl.when(pl.program_id(0) == 0)
    def _():
        sent, kept = [], []
        for n in range(2):
            if by_call:
                one, two = refs[2 + n][...], refs[n][...]
            else:
                one, two = refs[n][:, :HEAD_DIM], refs[n][:, HEAD_DIM:]
            sent.append(jnp.where(first_core, one, two))
            kept.append(jnp.where(first_core, two, one))
        rows_ref[...] = jnp.concatenate(sent + kept, axis=1).T

    each = 2 if by_call else 1
    product = jnp.dot(rows_ref[...], grad_ref[...], preferred_element_type=jnp.float32)
    product = product.astype(jnp.bfloat16).reshape(4 * each, HEAD_DIM, grad_ref.shape[1])
    for n, side in enumerate(sides):
        sent_ref[pl.ds(each * side, each)] = product[each * n : each * (n + 1)]
        kept_ref[pl.ds(each * side, each)] = product[each * (2 + n) : each * (3 + n)]


def batch_gradient(place, sources, grad_proj, filled=(), earlier=()):
    by_call = len(sources) == 4
    rows, columns = grad_proj.shape
    step = columns // GRADIENT_STEPS
    half = 1 if filled else 0
    out = pl.BlockSpec((4 if by_call else 2, HEAD_DIM, step), lambda i, p: (half, 0, i))
    result = jax.ShapeDtypeStruct((4, HEAD_DIM, columns), jnp.bfloat16)
    operands = (*sources, grad_proj, *filled, *earlier)
    return pl.pallas_call(
        functools.partial(gradient_kernel, by_call=by_call),
        grid_spec=pltpu.PrefetchScalarGridSpec(
            num_scalar_prefetch=1,
            grid=(GRADIENT_STEPS,),
            in_specs=[whole_block(each.shape) for each in sources]
            + [pl.BlockSpec((rows, step), lambda i, p: (0, i))]
            + [pl.BlockSpec(memory_space=pl.ANY)] * (len(filled) + len(earlier)),
            out_specs=[out, out],
            scratch_shapes=[
                pltpu.VMEM((8 * HEAD_DIM if by_call else 4 * HEAD_DIM, rows), jnp.bfloat16)
            ],
        ),
        out_shape=[result, result],
        input_output_aliases={4: 0, 5: 1} if filled else {},
        compiler_params=pltpu.CompilerParams(vmem_limit_bytes=VMEM_GRADIENT),
        cost_estimate=SMALL_COST,
    )(place, *operands)


def sum_of(blocks):
    total = blocks[0].astype(jnp.float32)
    for block in blocks[1:]:
        total = total + block.astype(jnp.float32)
    return total


def level_step(place, bit, terms, earlier=()):
    count = len(terms)
    pairs = terms[0].shape[0] // 2
    shape = (pairs,) + terms[0].shape[1:]
    block = (1,) + terms[0].shape[1:]
    keep = pl.BlockSpec(block, lambda i, p: (2 * i + p[bit], 0, 0))
    send = pl.BlockSpec(block, lambda i, p: (2 * i + 1 - p[bit], 0, 0))
    out = pl.BlockSpec(block, lambda i, p: (i, 0, 0))

    def kernel(place_ref, *refs):
        kept_ref, sent_ref = refs[-2:]
        kept_ref[...] = sum_of([ref[...] for ref in refs[:count]])
        sent_ref[...] = sum_of([ref[...] for ref in refs[count : 2 * count]]).astype(jnp.bfloat16)

    return pl.pallas_call(
        kernel,
        grid_spec=pltpu.PrefetchScalarGridSpec(
            num_scalar_prefetch=1,
            grid=(pairs,),
            in_specs=[keep] * count
            + [send] * count
            + [pl.BlockSpec(memory_space=pl.ANY)] * len(earlier),
            out_specs=[out, out],
        ),
        out_shape=[
            jax.ShapeDtypeStruct(shape, jnp.float32),
            jax.ShapeDtypeStruct(shape, jnp.bfloat16),
        ],
        compiler_params=pltpu.CompilerParams(vmem_limit_bytes=VMEM_SMALL),
        cost_estimate=SMALL_COST,
    )(place, *terms, *terms, *earlier)


def total_step(terms, parts=1, earlier=()):
    count = terms[0].shape[0] // parts
    shape = (count,) + terms[0].shape[1:]
    blocks = [
        pl.BlockSpec((1,) + shape[1:], lambda i, part=part: (part * count + i, 0, 0))
        for part in range(parts)
    ]

    def kernel(*refs):
        for part in range(parts):
            mine = refs[part * len(terms) : (part + 1) * len(terms)]
            refs[part - parts][...] = sum_of([ref[...] for ref in mine]).astype(jnp.bfloat16)

    return pl.pallas_call(
        kernel,
        grid=(count,),
        in_specs=[block for block in blocks for _ in terms]
        + [pl.BlockSpec(memory_space=pl.ANY)] * len(earlier),
        out_specs=[blocks[0]] * parts,
        out_shape=[jax.ShapeDtypeStruct(shape, jnp.bfloat16)] * parts,
        compiler_params=pltpu.CompilerParams(vmem_limit_bytes=VMEM_SMALL),
        cost_estimate=SMALL_COST,
    )(*[term for _ in range(parts) for term in terms], *earlier)


def choose_owned(place, batch_a, batch_b, batch_c):
    block = batch_a[0].shape

    def kernel(place_ref, *refs):
        alike = place_ref[CORE] == place_ref[X]
        odd = place_ref[LOW] == 1
        owned = (alike, ~alike & ~odd, ~alike & odd)
        for n, mine in enumerate(owned):

            @pl.when(mine)
            def _():
                refs[-1][...] = refs[2 * n][0] + refs[2 * n + 1][0].astype(jnp.float32)

    return pl.pallas_call(
        kernel,
        grid_spec=pltpu.PrefetchScalarGridSpec(
            num_scalar_prefetch=1,
            grid=(1,),
            in_specs=[whole_block(block)] * 6,
            out_specs=whole_block(block[1:]),
        ),
        out_shape=jax.ShapeDtypeStruct(block[1:], jnp.float32),
        compiler_params=pltpu.CompilerParams(vmem_limit_bytes=VMEM_SMALL),
        cost_estimate=SMALL_COST,
    )(place, *batch_a, *batch_b, *batch_c)


def project_kernel(place_ref, *refs, calls, local_heads, last):
    sources, weight_ref, out_ref, done_ref = refs[:4], refs[4], refs[-2], refs[-1]
    done_ref[...] = jnp.zeros_like(done_ref)
    rows = []
    for n in range(4):
        side = place_ref[0] if n % 2 == 0 else 1 - place_ref[0]
        for head in calls[n // 2]:
            rows.append(weight_ref[side * local_heads + head])
    columns = jnp.concatenate([each[...] for each in sources], axis=1)
    total = jnp.dot(columns, jnp.concatenate(rows, axis=0), preferred_element_type=jnp.float32)
    if last:
        total = (total + refs[5][...]) * refs[6][...]
    out_ref[...] = total.astype(out_ref.dtype)


def project(place, sources, weight, calls, local_heads, last, cost, earlier):
    heads, depth, columns = weight.shape
    rows = sources[0].shape[0]
    step = columns // PROJECT_STEPS
    block = pl.BlockSpec((rows, step), lambda i, p: (0, i))
    return pl.pallas_call(
        functools.partial(project_kernel, calls=calls, local_heads=local_heads, last=bool(last)),
        grid_spec=pltpu.PrefetchScalarGridSpec(
            num_scalar_prefetch=1,
            grid=(PROJECT_STEPS,),
            in_specs=[whole_block(each.shape) for each in sources]
            + [pl.BlockSpec((heads, depth, step), lambda i, p: (0, 0, i))]
            + ([block, pl.BlockSpec((1, step), lambda i, p: (0, i))] if last else [])
            + [pl.BlockSpec(memory_space=pl.ANY)] * len(earlier),
            out_specs=[block, pl.BlockSpec((8, HEAD_DIM), lambda i, p: (0, 0))],
        ),
        out_shape=[
            jax.ShapeDtypeStruct((rows, columns), jnp.bfloat16 if last else jnp.float32),
            jax.ShapeDtypeStruct((8, HEAD_DIM), jnp.float32),
        ],
        compiler_params=pltpu.CompilerParams(vmem_limit_bytes=VMEM_PROJECT),
        cost_estimate=cost,
    )(place, *sources, weight, *last, *earlier)


def contract_tokens(columns, grad_proj, kind):
    return lax.dot_general(
        columns, grad_proj, (((0,), (0,)), ((), ())), preferred_element_type=jnp.float32
    ).astype(kind)


def after(value, *earlier):
    return lax.optimization_barrier((value,) + earlier)[0]


def dp_send(value, flip, sender):
    return lax.ppermute(value, "dp", [(i, i ^ flip) for i in range(HEADS) if sender(i)])


def same_bits(i):
    return (i >> 1 ^ i) & 1 == 0


def paired_device(query_rows, key_rows, value_rows, windows, out_weight, gate_scale, out_grad):
    index = lax.axis_index("dp")
    place = jnp.stack([lax.axis_index("seq")] + [index >> bit & 1 for bit in range(4)])
    place = lax.optimization_barrier(place.astype(jnp.int32))
    local_heads = HEADS // 2
    swap = [(0, 1), (1, 0)]
    calls = [(0, 4), (3, 7), (1, 2), (5, 6)]
    bias = window_bias(windows)
    weight = lax.all_gather(out_weight, "dp", axis=0, tiled=True)
    weight = weight.reshape(HEADS, HEAD_DIM, weight.shape[1])
    gate_row = gate_scale[0].astype(jnp.float32)
    grad_proj = (out_grad.astype(jnp.float32) * gate_row).astype(jnp.bfloat16)
    sources = (query_rows, key_rows, value_rows)

    def pack(n, limit, *earlier):
        return pack_partner(place, local_heads, calls[n], *sources, earlier, limit)

    def attention(n, other, *earlier, limit=VMEM_LIMIT):
        return attend_pair(place, local_heads, calls[n], *sources, other, bias, earlier, limit)

    def exchange(mine):
        return lax.ppermute(mine, "seq", swap)

    def core_step(*operands):
        sent, kept = batch_gradient(place, operands[:4], operands[4])
        return total_step([kept, dp_send(sent, 1, lambda i: True)])[0]

    def apart(step, *operands):
        shapes = jax.eval_shape(step, *operands)
        return lax.cond(
            windows[0, 0] > 0,
            step,
            lambda *_: jax.tree.map(lambda leaf: jnp.zeros(leaf.shape, leaf.dtype), shapes),
            *operands,
        )

    packed0 = pack(0, VMEM_WHOLE)
    packed1 = pack(1, VMEM_WHOLE, packed0)
    packed2 = pack(2, VMEM_LIMIT, packed1)
    other0 = exchange(packed0)
    other1 = exchange(packed1)
    other2 = exchange(packed2)
    mine0 = attention(0, other0, packed2)
    theirs0 = exchange(mine0)
    mine1 = attention(1, other1, mine0)
    theirs1 = exchange(mine1)
    packed3 = pack(3, VMEM_LIMIT, mine1)
    other3 = exchange(packed3)
    mine2 = attention(2, other2, mine1, packed3)
    theirs2 = exchange(mine2)

    def unlike(i):
        return not same_bits(i)

    def like_even(i):
        return unlike(i) and i & 4 == 0

    def like_odd(i):
        return unlike(i) and i & 4 != 0

    first = (mine0, theirs0, mine1, theirs1)
    total_a = apart(core_step, after(mine0, mine2, weight), *first[1:], grad_proj)
    across_a = dp_send(total_a, 2, unlike)
    mine3 = attention(3, other3, total_a, limit=VMEM_WHOLE)
    theirs3 = exchange(mine3)
    sent, kept = batch_gradient(place, (mine2, theirs2), grad_proj, (), (mine3,))
    projected, done = project(
        place, first, weight, calls[:2], local_heads, (), FIRST_PROJECT_COST, (sent,)
    )
    kept_a, sent_a = level_step(place, LOW, [total_a, across_a], (done,))
    low_a = dp_send(sent_a, 4, same_bits)
    sent, kept = batch_gradient(place, (mine3, theirs3), grad_proj, (sent, kept), (sent_a,))
    came = dp_send(sent, 1, lambda i: True)
    total_b, total_c = total_step([kept, came], 2)
    across_b = dp_send(total_b, 2, same_bits)
    across_c = dp_send(total_c, 2, same_bits)
    block_out, done = project(
        place,
        (mine2, theirs2, mine3, theirs3),
        weight,
        calls[2:],
        local_heads,
        (projected, gate_row[None]),
        SMALL_COST,
        (total_b,),
    )
    kept_a, sent_a = level_step(place, HIGH, [kept_a, low_a], (done,))
    high_a = dp_send(sent_a, 8, same_bits)
    (sent_b,) = total_step([total_b, across_b], 1, (sent_a,))
    low_b = dp_send(sent_b, 4, like_odd)
    (sent_c,) = total_step([total_c, across_c], 1, (sent_b,))
    low_c = dp_send(sent_c, 4, like_even)
    kept_b, sent_b = level_step(place, HIGH, [total_b, across_b, low_b], (sent_c,))
    high_b = dp_send(sent_b, 8, like_even)
    kept_c, sent_c = level_step(place, HIGH, [total_c, across_c, low_c], (high_a, high_b))
    high_c = dp_send(sent_c, 8, like_odd)
    weight_grad = choose_owned(place, (kept_a, high_a), (kept_b, high_b), (kept_c, high_c))
    return (block_out, weight_grad)


def general_device(query_rows, key_rows, value_rows, windows, out_weight, gate_scale, out_grad):
    query, key, value = (
        lax.all_to_all(rows, "seq", split_axis=1, concat_axis=0, tiled=True)
        for rows in (query_rows, key_rows, value_rows)
    )
    place = lax.axis_index("seq").reshape(1).astype(jnp.int32)
    mine = attend_whole(place, query, key, value, window_bias(windows))
    columns = lax.all_gather(mine, "seq", axis=1, tiled=True)
    weight = lax.all_gather(out_weight, "dp", axis=0, tiled=True)
    gate_row = gate_scale[0].astype(jnp.float32)
    projected = jnp.dot(columns, weight, preferred_element_type=jnp.float32)
    block_out = (projected * gate_row).astype(jnp.bfloat16)
    grad_proj = (out_grad.astype(jnp.float32) * gate_row).astype(jnp.bfloat16)
    weight_grad = lax.psum_scatter(
        contract_tokens(columns, grad_proj, jnp.float32), "dp", scatter_dimension=0, tiled=True
    )
    return (block_out, weight_grad)


def solution(mesh):
    paired = mesh.shape["seq"] == 2 and mesh.shape["dp"] == HEADS
    return jax.shard_map(
        paired_device if paired else general_device,
        mesh=mesh,
        in_specs=(
            P(("dp", "seq"), None),
            P(("dp", "seq"), None),
            P(("dp", "seq"), None),
            P(),
            P("dp", "seq"),
            P("dp", "seq"),
            P("dp", "seq"),
        ),
        out_specs=(P("dp", "seq"), P("dp", "seq")),
        check_vma=False,
    )
```

```python
import functools
import math

import jax
import jax.numpy as jnp
import numpy as np
from jax import lax
from jax.experimental import pallas as pl
from jax.experimental.pallas import tpu as pltpu
from jax.sharding import PartitionSpec as P

HEADS = 16
HEAD_DIM = 128
GH = 3
GW = 4
GT = 2
TILE = 48
NT = 24
CLIP_TOK = NT * TILE
Q_ROWS = GW * TILE
LOG2_SCALE = math.log2(math.e) / math.sqrt(HEAD_DIM)
VMEM_LIMIT = 16 * 1024 * 1024
VMEM_GRADIENT = 20 * 1024 * 1024
VMEM_PROJECT = 24 * 1024 * 1024
PROJECT_STEPS = 6
GRADIENT_STEPS = 3
SEQ, CORE, X, LOW, HIGH = range(5)
VMEM_WHOLE = 60 * 1024 * 1024
VMEM_SMALL = 12 * 1024 * 1024
SMALL_COST = pl.CostEstimate(flops=1, bytes_accessed=1, transcendentals=0)
LONG_COST = pl.CostEstimate(flops=2 * 10**10, bytes_accessed=2 * 10**7, transcendentals=0)


def window_bias(windows):
    tile_id = np.arange(NT)
    coords = np.stack([tile_id // (GH * GW), tile_id // GW % GH, tile_id % GW]).astype(np.int32)
    token_coords = np.repeat(coords, TILE, axis=1)
    inside = None
    for axis_no, limit in enumerate((GT, GH, GW)):
        extent = jnp.minimum(windows[:, axis_no], limit)[:, None]
        start = jnp.clip(coords[axis_no][None, :] - (extent - 1) // 2, 0, limit - extent)
        column = token_coords[axis_no][None, None, :]
        here = (column >= start[:, :, None]) & (column < (start + extent)[:, :, None])
        inside = here if inside is None else inside & here
    return jnp.where(inside, 0.0, -jnp.inf).astype(jnp.float32)


def attend_rows(queries, first_tile, bias_ref, keys, values):
    count = queries.shape[0]
    tiles = count // TILE
    scores = lax.dot_general(
        queries, keys, (((1,), (1,)), ((), ())), preferred_element_type=jnp.float32
    )
    bias = bias_ref[0, first_tile : first_tile + tiles, :]
    scores = (scores.reshape(tiles, TILE, CLIP_TOK) + bias[:, None, :]).reshape(count, CLIP_TOK)
    peak = jnp.max(scores, axis=-1, keepdims=True)
    weights = jnp.exp2((scores - peak) * LOG2_SCALE).astype(jnp.bfloat16)
    blended = jnp.dot(weights, values, preferred_element_type=jnp.float32)
    return (blended[:, :HEAD_DIM] / blended[:, HEAD_DIM:]).astype(jnp.bfloat16)


def fill_values(values_ref, parts):
    at = 0
    for part in parts:
        rows = part.shape[0]
        values_ref[at : at + rows, :HEAD_DIM] = part
        at += rows
    values_ref[:, HEAD_DIM:] = jnp.ones((CLIP_TOK, HEAD_DIM), jnp.bfloat16)


def pair_kernel(place_ref, q_ref, k_ref, v_ref, other_ref, bias_ref, *rest):
    out_ref, keys_ref, values_ref = rest[-3:]
    half = CLIP_TOK // 2
    keys_ref[:half, :] = k_ref[...]
    keys_ref[half:, :] = other_ref[1]
    fill_values(values_ref, (v_ref[...], other_ref[2]))
    keys = keys_ref[...]
    values = values_ref[...]
    for side in range(2):
        base = pl.multiple_of((place_ref[0] if side == 0 else 1 - place_ref[0]) * half, half)
        for at in range(0, half, Q_ROWS):
            queries = q_ref[at : at + Q_ROWS, :] if side == 0 else other_ref[0, at : at + Q_ROWS, :]
            first_tile = (side * half + at) // TILE
            out_ref[pl.ds(base + at, Q_ROWS), :] = attend_rows(
                queries, first_tile, bias_ref, keys, values
            )


def whole_kernel(place_ref, q_ref, k_ref, v_ref, bias_ref, out_ref, values_ref):
    fill_values(values_ref, (v_ref[...],))
    keys = k_ref[...]
    values = values_ref[...]
    for at in range(0, CLIP_TOK, Q_ROWS):
        out_ref[at : at + Q_ROWS, :] = attend_rows(
            q_ref[at : at + Q_ROWS, :], at // TILE, bias_ref, keys, values
        )


def attention_cost(heads):
    pairs = heads * CLIP_TOK * CLIP_TOK
    return pl.CostEstimate(
        flops=pairs * HEAD_DIM * 6,
        bytes_accessed=heads * CLIP_TOK * HEAD_DIM * 8,
        transcendentals=pairs,
    )


def attend_pair(place, local_heads, picked, query, key, value, other, bias, earlier, limit):
    half = CLIP_TOK // 2
    first, step = picked[0], picked[1] - picked[0]

    def head(i, place_ref):
        return place_ref[0] * local_heads + first + step * i

    own = pl.BlockSpec((half, HEAD_DIM), lambda i, p: (0, head(i, p)))
    return pl.pallas_call(
        pair_kernel,
        grid_spec=pltpu.PrefetchScalarGridSpec(
            num_scalar_prefetch=1,
            grid=(len(picked),),
            in_specs=[
                own,
                own,
                own,
                pl.BlockSpec((3, half, HEAD_DIM), lambda i, p: (0, 0, i)),
                pl.BlockSpec((1, NT, CLIP_TOK), lambda i, p: (head(i, p), 0, 0)),
            ]
            + [pl.BlockSpec(memory_space=pl.ANY)] * len(earlier),
            out_specs=pl.BlockSpec((CLIP_TOK, HEAD_DIM), lambda i, p: (0, i)),
            scratch_shapes=[
                pltpu.VMEM((CLIP_TOK, HEAD_DIM), jnp.bfloat16),
                pltpu.VMEM((CLIP_TOK, 2 * HEAD_DIM), jnp.bfloat16),
            ],
        ),
        out_shape=jax.ShapeDtypeStruct((CLIP_TOK, len(picked) * HEAD_DIM), jnp.bfloat16),
        compiler_params=pltpu.CompilerParams(vmem_limit_bytes=limit),
        cost_estimate=SMALL_COST,
    )(place, query, key, value, other, bias, *earlier)


def attend_whole(place, query, key, value, bias):
    local_heads = query.shape[1] // HEAD_DIM
    column = pl.BlockSpec((CLIP_TOK, HEAD_DIM), lambda i, p: (0, i))
    return pl.pallas_call(
        whole_kernel,
        grid_spec=pltpu.PrefetchScalarGridSpec(
            num_scalar_prefetch=1,
            grid=(local_heads,),
            in_specs=[
                column,
                column,
                column,
                pl.BlockSpec((1, NT, CLIP_TOK), lambda i, p: (p[0] * local_heads + i, 0, 0)),
            ],
            out_specs=column,
            scratch_shapes=[pltpu.VMEM((CLIP_TOK, 2 * HEAD_DIM), jnp.bfloat16)],
        ),
        out_shape=jax.ShapeDtypeStruct(query.shape, jnp.bfloat16),
        compiler_params=pltpu.CompilerParams(vmem_limit_bytes=VMEM_LIMIT),
        cost_estimate=attention_cost(local_heads),
    )(place, query, key, value, bias)


def pack_kernel(place_ref, q_ref, k_ref, v_ref, *rest):
    out_ref = rest[-1]
    out_ref[0] = q_ref[...]
    out_ref[1] = k_ref[...]
    out_ref[2] = v_ref[...]


def pack_partner(place, local_heads, picked, query, key, value, earlier, limit):
    rows = query.shape[0]
    count = len(picked)
    first, step = picked[0], picked[1] - picked[0]

    def head(i, place_ref):
        return (1 - place_ref[0]) * local_heads + first + step * i

    column = pl.BlockSpec((rows, HEAD_DIM), lambda i, p: (0, head(i, p)))
    return pl.pallas_call(
        pack_kernel,
        grid_spec=pltpu.PrefetchScalarGridSpec(
            num_scalar_prefetch=1,
            grid=(count,),
            in_specs=[column, column, column]
            + [pl.BlockSpec(memory_space=pl.ANY)] * len(earlier),
            out_specs=pl.BlockSpec((3, rows, HEAD_DIM), lambda i, p: (0, 0, i)),
        ),
        out_shape=jax.ShapeDtypeStruct((3, rows, count * HEAD_DIM), jnp.bfloat16),
        compiler_params=pltpu.CompilerParams(vmem_limit_bytes=limit),
        cost_estimate=SMALL_COST,
    )(place, query, key, value, *earlier)


def whole_block(shape):
    return pl.BlockSpec(shape, lambda i, p: (0,) * len(shape), pipeline_mode=pl.Buffered(1))


def gradient_kernel(place_ref, *refs, by_call):
    count = 4 if by_call else 2
    grad_ref = refs[count]
    sent_ref, kept_ref, rows_ref = refs[-3:]
    first_core = place_ref[CORE] == 0
    sides = (place_ref[SEQ], 1 - place_ref[SEQ])

    @pl.when(pl.program_id(0) == 0)
    def _():
        sent, kept = [], []
        for n in range(2):
            if by_call:
                one, two = refs[2 + n][...], refs[n][...]
            else:
                one, two = refs[n][:, :HEAD_DIM], refs[n][:, HEAD_DIM:]
            sent.append(jnp.where(first_core, one, two))
            kept.append(jnp.where(first_core, two, one))
        rows_ref[...] = jnp.concatenate(sent + kept, axis=1).T

    each = 2 if by_call else 1
    product = jnp.dot(rows_ref[...], grad_ref[...], preferred_element_type=jnp.float32)
    product = product.astype(jnp.bfloat16).reshape(4 * each, HEAD_DIM, grad_ref.shape[1])
    for n, side in enumerate(sides):
        sent_ref[pl.ds(each * side, each)] = product[each * n : each * (n + 1)]
        kept_ref[pl.ds(each * side, each)] = product[each * (2 + n) : each * (3 + n)]


def batch_gradient(place, sources, grad_proj, filled=(), earlier=(), cost=SMALL_COST):
    by_call = len(sources) == 4
    rows, columns = grad_proj.shape
    step = columns // GRADIENT_STEPS
    half = 1 if filled else 0
    out = pl.BlockSpec((4 if by_call else 2, HEAD_DIM, step), lambda i, p: (half, 0, i))
    result = jax.ShapeDtypeStruct((4, HEAD_DIM, columns), jnp.bfloat16)
    operands = (*sources, grad_proj, *filled, *earlier)
    return pl.pallas_call(
        functools.partial(gradient_kernel, by_call=by_call),
        grid_spec=pltpu.PrefetchScalarGridSpec(
            num_scalar_prefetch=1,
            grid=(GRADIENT_STEPS,),
            in_specs=[whole_block(each.shape) for each in sources]
            + [pl.BlockSpec((rows, step), lambda i, p: (0, i))]
            + [pl.BlockSpec(memory_space=pl.ANY)] * (len(filled) + len(earlier)),
            out_specs=[out, out],
            scratch_shapes=[
                pltpu.VMEM((8 * HEAD_DIM if by_call else 4 * HEAD_DIM, rows), jnp.bfloat16)
            ],
        ),
        out_shape=[result, result],
        input_output_aliases={4: 0, 5: 1} if filled else {},
        compiler_params=pltpu.CompilerParams(vmem_limit_bytes=VMEM_GRADIENT),
        cost_estimate=cost,
    )(place, *operands)


def sum_of(blocks):
    total = blocks[0].astype(jnp.float32)
    for block in blocks[1:]:
        total = total + block.astype(jnp.float32)
    return total


def level_step(place, bit, terms, earlier=()):
    count = len(terms)
    pairs = terms[0].shape[0] // 2
    shape = (pairs,) + terms[0].shape[1:]
    block = (1,) + terms[0].shape[1:]
    keep = pl.BlockSpec(block, lambda i, p: (2 * i + p[bit], 0, 0))
    send = pl.BlockSpec(block, lambda i, p: (2 * i + 1 - p[bit], 0, 0))
    out = pl.BlockSpec(block, lambda i, p: (i, 0, 0))

    def kernel(place_ref, *refs):
        kept_ref, sent_ref = refs[-2:]
        kept_ref[...] = sum_of([ref[...] for ref in refs[:count]])
        sent_ref[...] = sum_of([ref[...] for ref in refs[count : 2 * count]]).astype(jnp.bfloat16)

    return pl.pallas_call(
        kernel,
        grid_spec=pltpu.PrefetchScalarGridSpec(
            num_scalar_prefetch=1,
            grid=(pairs,),
            in_specs=[keep] * count
            + [send] * count
            + [pl.BlockSpec(memory_space=pl.ANY)] * len(earlier),
            out_specs=[out, out],
        ),
        out_shape=[
            jax.ShapeDtypeStruct(shape, jnp.float32),
            jax.ShapeDtypeStruct(shape, jnp.bfloat16),
        ],
        compiler_params=pltpu.CompilerParams(vmem_limit_bytes=VMEM_SMALL),
        cost_estimate=SMALL_COST,
    )(place, *terms, *terms, *earlier)


def total_step(terms, parts=1, earlier=()):
    count = terms[0].shape[0] // parts
    shape = (count,) + terms[0].shape[1:]
    blocks = [
        pl.BlockSpec((1,) + shape[1:], lambda i, part=part: (part * count + i, 0, 0))
        for part in range(parts)
    ]

    def kernel(*refs):
        for part in range(parts):
            mine = refs[part * len(terms) : (part + 1) * len(terms)]
            refs[part - parts][...] = sum_of([ref[...] for ref in mine]).astype(jnp.bfloat16)

    return pl.pallas_call(
        kernel,
        grid=(count,),
        in_specs=[block for block in blocks for _ in terms]
        + [pl.BlockSpec(memory_space=pl.ANY)] * len(earlier),
        out_specs=[blocks[0]] * parts,
        out_shape=[jax.ShapeDtypeStruct(shape, jnp.bfloat16)] * parts,
        compiler_params=pltpu.CompilerParams(vmem_limit_bytes=VMEM_SMALL),
        cost_estimate=SMALL_COST,
    )(*[term for _ in range(parts) for term in terms], *earlier)


def choose_owned(place, batch_a, batch_b, batch_c):
    block = batch_a[0].shape

    def kernel(place_ref, *refs):
        alike = place_ref[CORE] == place_ref[X]
        odd = place_ref[LOW] == 1
        owned = (alike, ~alike & ~odd, ~alike & odd)
        for n, mine in enumerate(owned):

            @pl.when(mine)
            def _():
                refs[-1][...] = refs[2 * n][0] + refs[2 * n + 1][0].astype(jnp.float32)

    return pl.pallas_call(
        kernel,
        grid_spec=pltpu.PrefetchScalarGridSpec(
            num_scalar_prefetch=1,
            grid=(1,),
            in_specs=[whole_block(block)] * 6,
            out_specs=whole_block(block[1:]),
        ),
        out_shape=jax.ShapeDtypeStruct(block[1:], jnp.float32),
        compiler_params=pltpu.CompilerParams(vmem_limit_bytes=VMEM_SMALL),
        cost_estimate=SMALL_COST,
    )(place, *batch_a, *batch_b, *batch_c)


def project_kernel(place_ref, *refs, calls, local_heads):
    count = 2 * len(calls)
    weight_ref, gate_ref = refs[count : count + 2]
    out_ref, done_ref, columns_ref = refs[-3:]

    @pl.when(pl.program_id(0) == 0)
    def _():
        done_ref[...] = jnp.zeros_like(done_ref)
        for n in range(count):
            side = place_ref[SEQ] if n % 2 == 0 else 1 - place_ref[SEQ]
            for part, head in enumerate(calls[n // 2]):
                at = pl.multiple_of((side * local_heads + head) * HEAD_DIM, HEAD_DIM)
                columns_ref[:, pl.ds(at, HEAD_DIM)] = refs[n][
                    :, part * HEAD_DIM : (part + 1) * HEAD_DIM
                ]

    total = jnp.dot(columns_ref[...], weight_ref[...], preferred_element_type=jnp.float32)
    out_ref[...] = (total * gate_ref[...]).astype(out_ref.dtype)


def project(place, sources, weight, gate, calls, local_heads, earlier):
    depth, columns = weight.shape
    rows = sources[0].shape[0]
    step = columns // PROJECT_STEPS
    block = pl.BlockSpec((rows, step), lambda i, p: (0, i))
    return pl.pallas_call(
        functools.partial(project_kernel, calls=calls, local_heads=local_heads),
        grid_spec=pltpu.PrefetchScalarGridSpec(
            num_scalar_prefetch=1,
            grid=(PROJECT_STEPS,),
            in_specs=[whole_block(each.shape) for each in sources]
            + [pl.BlockSpec((depth, step), lambda i, p: (0, i))]
            + [pl.BlockSpec((1, step), lambda i, p: (0, i))]
            + [pl.BlockSpec(memory_space=pl.ANY)] * len(earlier),
            out_specs=[block, pl.BlockSpec((8, HEAD_DIM), lambda i, p: (0, 0))],
            scratch_shapes=[pltpu.VMEM((rows, depth), jnp.bfloat16)],
        ),
        out_shape=[
            jax.ShapeDtypeStruct((rows, columns), jnp.bfloat16),
            jax.ShapeDtypeStruct((8, HEAD_DIM), jnp.float32),
        ],
        compiler_params=pltpu.CompilerParams(vmem_limit_bytes=VMEM_PROJECT),
        cost_estimate=SMALL_COST,
    )(place, *sources, weight, gate, *earlier)


def contract_tokens(columns, grad_proj, kind):
    return lax.dot_general(
        columns, grad_proj, (((0,), (0,)), ((), ())), preferred_element_type=jnp.float32
    ).astype(kind)


def after(value, *earlier):
    return lax.optimization_barrier((value,) + earlier)[0]


def dp_send(value, flip, sender):
    return lax.ppermute(value, "dp", [(i, i ^ flip) for i in range(HEADS) if sender(i)])


def same_bits(i):
    return (i >> 1 ^ i) & 1 == 0


def paired_device(query_rows, key_rows, value_rows, windows, out_weight, gate_scale, out_grad):
    index = lax.axis_index("dp")
    place = jnp.stack([lax.axis_index("seq")] + [index >> bit & 1 for bit in range(4)])
    place = lax.optimization_barrier(place.astype(jnp.int32))
    local_heads = HEADS // 2
    swap = [(0, 1), (1, 0)]
    calls = [(0, 4), (3, 7), (1, 2), (5, 6)]
    bias = window_bias(windows)
    weight = lax.all_gather(out_weight, "dp", axis=0, tiled=True)
    gate_row = gate_scale[0].astype(jnp.float32)
    grad_proj = (out_grad.astype(jnp.float32) * gate_row).astype(jnp.bfloat16)
    sources = (query_rows, key_rows, value_rows)

    def pack(n, limit, *earlier):
        return pack_partner(place, local_heads, calls[n], *sources, earlier, limit)

    def attention(n, other, *earlier, limit=VMEM_LIMIT):
        return attend_pair(place, local_heads, calls[n], *sources, other, bias, earlier, limit)

    def exchange(mine):
        return lax.ppermute(mine, "seq", swap)

    def core_step(*operands):
        sent, kept = batch_gradient(place, operands[:4], operands[4])
        return total_step([kept, dp_send(sent, 1, lambda i: True)])[0]

    def apart(step, *operands):
        shapes = jax.eval_shape(step, *operands)
        return lax.cond(
            windows[0, 0] > 0,
            step,
            lambda *_: jax.tree.map(lambda leaf: jnp.zeros(leaf.shape, leaf.dtype), shapes),
            *operands,
        )

    packed0 = pack(0, VMEM_WHOLE)
    packed1 = pack(1, VMEM_WHOLE, packed0)
    packed2 = pack(2, VMEM_LIMIT, packed1)
    other0 = exchange(packed0)
    other1 = exchange(packed1)
    other2 = exchange(packed2)
    mine0 = attention(0, other0, packed2)
    theirs0 = exchange(mine0)
    mine1 = attention(1, other1, mine0)
    theirs1 = exchange(mine1)
    packed3 = pack(3, VMEM_LIMIT, mine1)
    other3 = exchange(packed3)
    mine2 = attention(2, other2, mine1, packed3)
    theirs2 = exchange(mine2)

    def unlike(i):
        return not same_bits(i)

    def like_even(i):
        return unlike(i) and i & 4 == 0

    def like_odd(i):
        return unlike(i) and i & 4 != 0

    first = (mine0, theirs0, mine1, theirs1)
    total_a = apart(core_step, after(mine0, mine2, weight), *first[1:], grad_proj)
    across_a = dp_send(total_a, 2, unlike)
    mine3 = attention(3, other3, total_a, limit=VMEM_WHOLE)
    theirs3 = exchange(mine3)
    sent, kept = batch_gradient(
        place, (mine2, theirs2), grad_proj, earlier=(mine3,), cost=LONG_COST
    )
    kept_a, sent_a = level_step(place, LOW, [total_a, across_a], (sent,))
    low_a = dp_send(sent_a, 4, same_bits)
    sent, kept = batch_gradient(place, (mine3, theirs3), grad_proj, (sent, kept), (sent_a,))
    came = dp_send(sent, 1, lambda i: True)
    total_b, total_c = total_step([kept, came], 2)
    across_b = dp_send(total_b, 2, same_bits)
    across_c = dp_send(total_c, 2, same_bits)
    block_out, done = project(
        place,
        (*first, mine2, theirs2, mine3, theirs3),
        weight,
        gate_row[None],
        calls,
        local_heads,
        (total_b,),
    )
    kept_a, sent_a = level_step(place, HIGH, [kept_a, low_a], (done,))
    high_a = dp_send(sent_a, 8, same_bits)
    (sent_b,) = total_step([total_b, across_b], 1, (sent_a,))
    low_b = dp_send(sent_b, 4, like_odd)
    (sent_c,) = total_step([total_c, across_c], 1, (sent_b, high_a))
    low_c = dp_send(sent_c, 4, like_even)
    kept_b, sent_b = level_step(place, HIGH, [total_b, across_b, low_b], (sent_c,))
    high_b = dp_send(sent_b, 8, like_even)
    kept_c, sent_c = level_step(place, HIGH, [total_c, across_c, low_c], (high_b,))
    high_c = dp_send(sent_c, 8, like_odd)
    weight_grad = choose_owned(place, (kept_a, high_a), (kept_b, high_b), (kept_c, high_c))
    return (block_out, weight_grad)


def general_device(query_rows, key_rows, value_rows, windows, out_weight, gate_scale, out_grad):
    query, key, value = (
        lax.all_to_all(rows, "seq", split_axis=1, concat_axis=0, tiled=True)
        for rows in (query_rows, key_rows, value_rows)
    )
    place = lax.axis_index("seq").reshape(1).astype(jnp.int32)
    mine = attend_whole(place, query, key, value, window_bias(windows))
    columns = lax.all_gather(mine, "seq", axis=1, tiled=True)
    weight = lax.all_gather(out_weight, "dp", axis=0, tiled=True)
    gate_row = gate_scale[0].astype(jnp.float32)
    projected = jnp.dot(columns, weight, preferred_element_type=jnp.float32)
    block_out = (projected * gate_row).astype(jnp.bfloat16)
    grad_proj = (out_grad.astype(jnp.float32) * gate_row).astype(jnp.bfloat16)
    weight_grad = lax.psum_scatter(
        contract_tokens(columns, grad_proj, jnp.float32), "dp", scatter_dimension=0, tiled=True
    )
    return (block_out, weight_grad)


def solution(mesh):
    paired = mesh.shape["seq"] == 2 and mesh.shape["dp"] == HEADS
    return jax.shard_map(
        paired_device if paired else general_device,
        mesh=mesh,
        in_specs=(
            P(("dp", "seq"), None),
            P(("dp", "seq"), None),
            P(("dp", "seq"), None),
            P(),
            P("dp", "seq"),
            P("dp", "seq"),
            P("dp", "seq"),
        ),
        out_specs=(P("dp", "seq"), P("dp", "seq")),
        check_vma=False,
    )
```

```python
import functools
import math

import jax
import jax.numpy as jnp
import numpy as np
from jax import lax
from jax.experimental import pallas as pl
from jax.experimental.pallas import tpu as pltpu
from jax.sharding import PartitionSpec as P

HEADS = 16
HEAD_DIM = 128
GH = 3
GW = 4
GT = 2
TILE = 48
NT = 24
CLIP_TOK = NT * TILE
Q_ROWS = GW * TILE
LOG2_SCALE = math.log2(math.e) / math.sqrt(HEAD_DIM)
VMEM_LIMIT = 16 * 1024 * 1024
VMEM_GRADIENT = 20 * 1024 * 1024
VMEM_PROJECT = 24 * 1024 * 1024
PROJECT_STEPS = 6
GRADIENT_STEPS = 3
SEQ, CORE, X, LOW, HIGH = range(5)
VMEM_WHOLE = 60 * 1024 * 1024
VMEM_SMALL = 12 * 1024 * 1024
SMALL_COST = pl.CostEstimate(flops=1, bytes_accessed=1, transcendentals=0)
LONG_COST = pl.CostEstimate(flops=2 * 10**10, bytes_accessed=2 * 10**7, transcendentals=0)


def window_bias(windows):
    tile_id = np.arange(NT)
    coords = np.stack([tile_id // (GH * GW), tile_id // GW % GH, tile_id % GW]).astype(np.int32)
    token_coords = np.repeat(coords, TILE, axis=1)
    inside = None
    for axis_no, limit in enumerate((GT, GH, GW)):
        extent = jnp.minimum(windows[:, axis_no], limit)[:, None]
        start = jnp.clip(coords[axis_no][None, :] - (extent - 1) // 2, 0, limit - extent)
        column = token_coords[axis_no][None, None, :]
        here = (column >= start[:, :, None]) & (column < (start + extent)[:, :, None])
        inside = here if inside is None else inside & here
    return jnp.where(inside, 0.0, -jnp.inf).astype(jnp.float32)


def attend_rows(queries, first_tile, bias_ref, keys, values):
    count = queries.shape[0]
    tiles = count // TILE
    scores = lax.dot_general(
        queries, keys, (((1,), (1,)), ((), ())), preferred_element_type=jnp.float32
    )
    bias = bias_ref[0, first_tile : first_tile + tiles, :]
    scores = (scores.reshape(tiles, TILE, CLIP_TOK) + bias[:, None, :]).reshape(count, CLIP_TOK)
    peak = jnp.max(scores, axis=-1, keepdims=True)
    weights = jnp.exp2((scores - peak) * LOG2_SCALE).astype(jnp.bfloat16)
    blended = jnp.dot(weights, values, preferred_element_type=jnp.float32)
    return (blended[:, :HEAD_DIM] / blended[:, HEAD_DIM:]).astype(jnp.bfloat16)


def fill_values(values_ref, parts):
    at = 0
    for part in parts:
        rows = part.shape[0]
        values_ref[at : at + rows, :HEAD_DIM] = part
        at += rows
    values_ref[:, HEAD_DIM:] = jnp.ones((CLIP_TOK, HEAD_DIM), jnp.bfloat16)


def pair_kernel(place_ref, q_ref, k_ref, v_ref, other_ref, bias_ref, *rest):
    out_ref, keys_ref, values_ref = rest[-3:]
    half = CLIP_TOK // 2
    keys_ref[:half, :] = k_ref[...]
    keys_ref[half:, :] = other_ref[1]
    fill_values(values_ref, (v_ref[...], other_ref[2]))
    keys = keys_ref[...]
    values = values_ref[...]
    for side in range(2):
        base = pl.multiple_of((place_ref[0] if side == 0 else 1 - place_ref[0]) * half, half)
        for at in range(0, half, Q_ROWS):
            queries = q_ref[at : at + Q_ROWS, :] if side == 0 else other_ref[0, at : at + Q_ROWS, :]
            first_tile = (side * half + at) // TILE
            out_ref[pl.ds(base + at, Q_ROWS), :] = attend_rows(
                queries, first_tile, bias_ref, keys, values
            )


def whole_kernel(place_ref, q_ref, k_ref, v_ref, bias_ref, out_ref, values_ref):
    fill_values(values_ref, (v_ref[...],))
    keys = k_ref[...]
    values = values_ref[...]
    for at in range(0, CLIP_TOK, Q_ROWS):
        out_ref[at : at + Q_ROWS, :] = attend_rows(
            q_ref[at : at + Q_ROWS, :], at // TILE, bias_ref, keys, values
        )


def attention_cost(heads):
    pairs = heads * CLIP_TOK * CLIP_TOK
    return pl.CostEstimate(
        flops=pairs * HEAD_DIM * 6,
        bytes_accessed=heads * CLIP_TOK * HEAD_DIM * 8,
        transcendentals=pairs,
    )


def attend_pair(place, local_heads, picked, query, key, value, other, bias, earlier, limit):
    half = CLIP_TOK // 2
    first, step = picked[0], picked[1] - picked[0]

    def head(i, place_ref):
        return place_ref[0] * local_heads + first + step * i

    own = pl.BlockSpec((half, HEAD_DIM), lambda i, p: (0, head(i, p)))
    return pl.pallas_call(
        pair_kernel,
        grid_spec=pltpu.PrefetchScalarGridSpec(
            num_scalar_prefetch=1,
            grid=(len(picked),),
            in_specs=[
                own,
                own,
                own,
                pl.BlockSpec((3, half, HEAD_DIM), lambda i, p: (0, 0, i)),
                pl.BlockSpec((1, NT, CLIP_TOK), lambda i, p: (head(i, p), 0, 0)),
            ]
            + [pl.BlockSpec(memory_space=pl.ANY)] * len(earlier),
            out_specs=pl.BlockSpec((CLIP_TOK, HEAD_DIM), lambda i, p: (0, i)),
            scratch_shapes=[
                pltpu.VMEM((CLIP_TOK, HEAD_DIM), jnp.bfloat16),
                pltpu.VMEM((CLIP_TOK, 2 * HEAD_DIM), jnp.bfloat16),
            ],
        ),
        out_shape=jax.ShapeDtypeStruct((CLIP_TOK, len(picked) * HEAD_DIM), jnp.bfloat16),
        compiler_params=pltpu.CompilerParams(vmem_limit_bytes=limit),
        cost_estimate=SMALL_COST,
    )(place, query, key, value, other, bias, *earlier)


def attend_whole(place, query, key, value, bias):
    local_heads = query.shape[1] // HEAD_DIM
    column = pl.BlockSpec((CLIP_TOK, HEAD_DIM), lambda i, p: (0, i))
    return pl.pallas_call(
        whole_kernel,
        grid_spec=pltpu.PrefetchScalarGridSpec(
            num_scalar_prefetch=1,
            grid=(local_heads,),
            in_specs=[
                column,
                column,
                column,
                pl.BlockSpec((1, NT, CLIP_TOK), lambda i, p: (p[0] * local_heads + i, 0, 0)),
            ],
            out_specs=column,
            scratch_shapes=[pltpu.VMEM((CLIP_TOK, 2 * HEAD_DIM), jnp.bfloat16)],
        ),
        out_shape=jax.ShapeDtypeStruct(query.shape, jnp.bfloat16),
        compiler_params=pltpu.CompilerParams(vmem_limit_bytes=VMEM_LIMIT),
        cost_estimate=attention_cost(local_heads),
    )(place, query, key, value, bias)


def pack_kernel(place_ref, q_ref, k_ref, v_ref, *rest):
    out_ref = rest[-1]
    out_ref[0] = q_ref[...]
    out_ref[1] = k_ref[...]
    out_ref[2] = v_ref[...]


def pack_partner(place, local_heads, picked, query, key, value, earlier, limit):
    rows = query.shape[0]
    count = len(picked)
    first, step = picked[0], picked[1] - picked[0]

    def head(i, place_ref):
        return (1 - place_ref[0]) * local_heads + first + step * i

    column = pl.BlockSpec((rows, HEAD_DIM), lambda i, p: (0, head(i, p)))
    return pl.pallas_call(
        pack_kernel,
        grid_spec=pltpu.PrefetchScalarGridSpec(
            num_scalar_prefetch=1,
            grid=(count,),
            in_specs=[column, column, column]
            + [pl.BlockSpec(memory_space=pl.ANY)] * len(earlier),
            out_specs=pl.BlockSpec((3, rows, HEAD_DIM), lambda i, p: (0, 0, i)),
        ),
        out_shape=jax.ShapeDtypeStruct((3, rows, count * HEAD_DIM), jnp.bfloat16),
        compiler_params=pltpu.CompilerParams(vmem_limit_bytes=limit),
        cost_estimate=SMALL_COST,
    )(place, query, key, value, *earlier)


def whole_block(shape):
    return pl.BlockSpec(shape, lambda i, p: (0,) * len(shape), pipeline_mode=pl.Buffered(1))


def gradient_kernel(place_ref, *refs, by_call):
    count = 4 if by_call else 2
    grad_ref = refs[count]
    sent_ref, kept_ref, rows_ref = refs[-3:]
    first_core = place_ref[CORE] == 0
    sides = (place_ref[SEQ], 1 - place_ref[SEQ])

    @pl.when(pl.program_id(0) == 0)
    def _():
        sent, kept = [], []
        for n in range(2):
            if by_call:
                one, two = refs[2 + n][...], refs[n][...]
            else:
                one, two = refs[n][:, :HEAD_DIM], refs[n][:, HEAD_DIM:]
            sent.append(jnp.where(first_core, one, two))
            kept.append(jnp.where(first_core, two, one))
        rows_ref[...] = jnp.concatenate(sent + kept, axis=1).T

    each = 2 if by_call else 1
    product = jnp.dot(rows_ref[...], grad_ref[...], preferred_element_type=jnp.float32)
    product = product.astype(jnp.bfloat16).reshape(4 * each, HEAD_DIM, grad_ref.shape[1])
    for n, side in enumerate(sides):
        sent_ref[pl.ds(each * side, each)] = product[each * n : each * (n + 1)]
        kept_ref[pl.ds(each * side, each)] = product[each * (2 + n) : each * (3 + n)]


def batch_gradient(place, sources, grad_proj, earlier=(), cost=SMALL_COST):
    by_call = len(sources) == 4
    heads = len(sources)
    rows, columns = grad_proj.shape
    step = columns // GRADIENT_STEPS
    out = pl.BlockSpec((heads, HEAD_DIM, step), lambda i, p: (0, 0, i))
    result = jax.ShapeDtypeStruct((heads, HEAD_DIM, columns), jnp.bfloat16)
    return pl.pallas_call(
        functools.partial(gradient_kernel, by_call=by_call),
        grid_spec=pltpu.PrefetchScalarGridSpec(
            num_scalar_prefetch=1,
            grid=(GRADIENT_STEPS,),
            in_specs=[whole_block(each.shape) for each in sources]
            + [pl.BlockSpec((rows, step), lambda i, p: (0, i))]
            + [pl.BlockSpec(memory_space=pl.ANY)] * len(earlier),
            out_specs=[out, out],
            scratch_shapes=[pltpu.VMEM((2 * heads * HEAD_DIM, rows), jnp.bfloat16)],
        ),
        out_shape=[result, result],
        compiler_params=pltpu.CompilerParams(vmem_limit_bytes=VMEM_GRADIENT),
        cost_estimate=cost,
    )(place, *sources, grad_proj, *earlier)


def sum_of(blocks):
    total = blocks[0].astype(jnp.float32)
    for block in blocks[1:]:
        total = total + block.astype(jnp.float32)
    return total


def level_step(place, bit, terms, earlier=(), cost=SMALL_COST):
    count = len(terms)
    pairs = terms[0].shape[0] // 2
    shape = (pairs,) + terms[0].shape[1:]
    block = (1,) + terms[0].shape[1:]
    keep = pl.BlockSpec(block, lambda i, p: (2 * i + p[bit], 0, 0))
    send = pl.BlockSpec(block, lambda i, p: (2 * i + 1 - p[bit], 0, 0))
    out = pl.BlockSpec(block, lambda i, p: (i, 0, 0))

    def kernel(place_ref, *refs):
        kept_ref, sent_ref = refs[-2:]
        kept_ref[...] = sum_of([ref[...] for ref in refs[:count]])
        sent_ref[...] = sum_of([ref[...] for ref in refs[count : 2 * count]]).astype(jnp.bfloat16)

    return pl.pallas_call(
        kernel,
        grid_spec=pltpu.PrefetchScalarGridSpec(
            num_scalar_prefetch=1,
            grid=(pairs,),
            in_specs=[keep] * count
            + [send] * count
            + [pl.BlockSpec(memory_space=pl.ANY)] * len(earlier),
            out_specs=[out, out],
        ),
        out_shape=[
            jax.ShapeDtypeStruct(shape, jnp.float32),
            jax.ShapeDtypeStruct(shape, jnp.bfloat16),
        ],
        compiler_params=pltpu.CompilerParams(vmem_limit_bytes=VMEM_SMALL),
        cost_estimate=cost,
    )(place, *terms, *terms, *earlier)


def total_step(terms, earlier=()):
    block = pl.BlockSpec((1,) + terms[0].shape[1:], lambda i: (i, 0, 0))

    def kernel(*refs):
        refs[-1][...] = sum_of([ref[...] for ref in refs[: len(terms)]]).astype(jnp.bfloat16)

    return pl.pallas_call(
        kernel,
        grid=(terms[0].shape[0],),
        in_specs=[block] * len(terms) + [pl.BlockSpec(memory_space=pl.ANY)] * len(earlier),
        out_specs=block,
        out_shape=jax.ShapeDtypeStruct(terms[0].shape, jnp.bfloat16),
        compiler_params=pltpu.CompilerParams(vmem_limit_bytes=VMEM_SMALL),
        cost_estimate=SMALL_COST,
    )(*terms, *earlier)


def choose_owned(place, batch_a, batch_b, batch_c):
    block = batch_a[0].shape

    def kernel(place_ref, *refs):
        alike = place_ref[CORE] == place_ref[X]
        odd = place_ref[LOW] == 1
        owned = (alike, ~alike & ~odd, ~alike & odd)
        for n, mine in enumerate(owned):

            @pl.when(mine)
            def _():
                refs[-1][...] = refs[2 * n][0] + refs[2 * n + 1][0].astype(jnp.float32)

    return pl.pallas_call(
        kernel,
        grid_spec=pltpu.PrefetchScalarGridSpec(
            num_scalar_prefetch=1,
            grid=(1,),
            in_specs=[whole_block(block)] * 6,
            out_specs=whole_block(block[1:]),
        ),
        out_shape=jax.ShapeDtypeStruct(block[1:], jnp.float32),
        compiler_params=pltpu.CompilerParams(vmem_limit_bytes=VMEM_SMALL),
        cost_estimate=SMALL_COST,
    )(place, *batch_a, *batch_b, *batch_c)


def project_kernel(place_ref, *refs, calls, local_heads):
    count = 2 * len(calls)
    weight_ref, gate_ref = refs[count : count + 2]
    out_ref, done_ref, columns_ref = refs[-3:]

    @pl.when(pl.program_id(0) == 0)
    def _():
        done_ref[...] = jnp.zeros_like(done_ref)
        for n in range(count):
            side = place_ref[SEQ] if n % 2 == 0 else 1 - place_ref[SEQ]
            for part, head in enumerate(calls[n // 2]):
                at = pl.multiple_of((side * local_heads + head) * HEAD_DIM, HEAD_DIM)
                columns_ref[:, pl.ds(at, HEAD_DIM)] = refs[n][
                    :, part * HEAD_DIM : (part + 1) * HEAD_DIM
                ]

    total = jnp.dot(columns_ref[...], weight_ref[...], preferred_element_type=jnp.float32)
    out_ref[...] = (total * gate_ref[...]).astype(out_ref.dtype)


def project(place, sources, weight, gate, calls, local_heads, part, filled=(), earlier=()):
    depth, columns = weight.shape
    rows = sources[0].shape[0]
    step = columns // PROJECT_STEPS
    steps = PROJECT_STEPS // 2
    block = pl.BlockSpec((rows, step), lambda i, p: (0, part * steps + i))
    return pl.pallas_call(
        functools.partial(project_kernel, calls=calls, local_heads=local_heads),
        grid_spec=pltpu.PrefetchScalarGridSpec(
            num_scalar_prefetch=1,
            grid=(steps,),
            in_specs=[whole_block(each.shape) for each in sources]
            + [pl.BlockSpec((depth, step), lambda i, p: (0, part * steps + i))]
            + [pl.BlockSpec((1, step), lambda i, p: (0, part * steps + i))]
            + [pl.BlockSpec(memory_space=pl.ANY)] * (len(filled) + len(earlier)),
            out_specs=[block, pl.BlockSpec((8, HEAD_DIM), lambda i, p: (0, 0))],
            scratch_shapes=[pltpu.VMEM((rows, depth), jnp.bfloat16)],
        ),
        out_shape=[
            jax.ShapeDtypeStruct((rows, columns), jnp.bfloat16),
            jax.ShapeDtypeStruct((8, HEAD_DIM), jnp.float32),
        ],
        input_output_aliases={len(sources) + 3: 0} if filled else {},
        compiler_params=pltpu.CompilerParams(vmem_limit_bytes=VMEM_PROJECT),
        cost_estimate=SMALL_COST,
    )(place, *sources, weight, gate, *filled, *earlier)


def contract_tokens(columns, grad_proj, kind):
    return lax.dot_general(
        columns, grad_proj, (((0,), (0,)), ((), ())), preferred_element_type=jnp.float32
    ).astype(kind)


def after(value, *earlier):
    return lax.optimization_barrier((value,) + earlier)[0]


def dp_send(value, flip, sender):
    return lax.ppermute(value, "dp", [(i, i ^ flip) for i in range(HEADS) if sender(i)])


def same_bits(i):
    return (i >> 1 ^ i) & 1 == 0


def paired_device(query_rows, key_rows, value_rows, windows, out_weight, gate_scale, out_grad):
    index = lax.axis_index("dp")
    place = jnp.stack([lax.axis_index("seq")] + [index >> bit & 1 for bit in range(4)])
    place = lax.optimization_barrier(place.astype(jnp.int32))
    local_heads = HEADS // 2
    swap = [(0, 1), (1, 0)]
    calls = [(0, 4), (3, 7), (1, 2), (5, 6)]
    bias = window_bias(windows)
    weight = lax.all_gather(out_weight, "dp", axis=0, tiled=True)
    gate_row = gate_scale[0].astype(jnp.float32)
    grad_proj = (out_grad.astype(jnp.float32) * gate_row).astype(jnp.bfloat16)
    sources = (query_rows, key_rows, value_rows)

    def pack(n, limit, *earlier):
        return pack_partner(place, local_heads, calls[n], *sources, earlier, limit)

    def attention(n, other, *earlier, limit=VMEM_LIMIT):
        return attend_pair(place, local_heads, calls[n], *sources, other, bias, earlier, limit)

    def exchange(mine):
        return lax.ppermute(mine, "seq", swap)

    def core_step(*operands):
        sent, kept = batch_gradient(place, operands[:4], operands[4])
        return total_step([kept, dp_send(sent, 1, lambda i: True)])

    def apart(step, *operands):
        shapes = jax.eval_shape(step, *operands)
        return lax.cond(
            windows[0, 0] > 0,
            step,
            lambda *_: jax.tree.map(lambda leaf: jnp.zeros(leaf.shape, leaf.dtype), shapes),
            *operands,
        )

    packed0 = pack(0, VMEM_WHOLE)
    packed1 = pack(1, VMEM_WHOLE, packed0)
    packed2 = pack(2, VMEM_LIMIT, packed1)
    other0 = exchange(packed0)
    other1 = exchange(packed1)
    other2 = exchange(packed2)
    mine0 = attention(0, other0, packed2)
    theirs0 = exchange(mine0)
    mine1 = attention(1, other1, mine0)
    theirs1 = exchange(mine1)
    packed3 = pack(3, VMEM_LIMIT, mine1)
    other3 = exchange(packed3)
    mine2 = attention(2, other2, mine1, packed3)
    theirs2 = exchange(mine2)

    def unlike(i):
        return not same_bits(i)

    def like_even(i):
        return unlike(i) and i & 4 == 0

    def like_odd(i):
        return unlike(i) and i & 4 != 0

    first = (mine0, theirs0, mine1, theirs1)
    total_a = apart(core_step, after(mine0, mine2, weight), *first[1:], grad_proj)
    across_a = dp_send(total_a, 2, unlike)
    mine3 = attention(3, other3, total_a, limit=VMEM_WHOLE)
    theirs3 = exchange(mine3)
    sent_b, kept_b = batch_gradient(place, (mine2, theirs2), grad_proj, (mine3,), LONG_COST)
    came_b = dp_send(sent_b, 1, lambda i: True)
    kept_a, sent_a = level_step(place, LOW, [total_a, across_a], (sent_b,), LONG_COST)
    low_a = dp_send(sent_a, 4, same_bits)
    total_b = total_step([kept_b, came_b], (sent_a,))
    across_b = dp_send(total_b, 2, same_bits)
    sent_c, kept_c = batch_gradient(place, (mine3, theirs3), grad_proj, (total_b,))
    came_c = dp_send(sent_c, 1, lambda i: True)
    total_c = total_step([kept_c, came_c])
    across_c = dp_send(total_c, 2, same_bits)
    kept_a, sent_a = level_step(place, HIGH, [kept_a, low_a], (total_c,))
    high_a = dp_send(sent_a, 8, same_bits)
    sent_b = total_step([total_b, across_b], (sent_a,))
    low_b = dp_send(sent_b, 4, like_odd)
    to_project = (*first, mine2, theirs2, mine3, theirs3), weight, gate_row[None], calls, local_heads
    half_out, done = project(place, *to_project, 0, (), (sent_b,))
    sent_c = total_step([total_c, across_c], (done, high_a))
    low_c = dp_send(sent_c, 4, like_even)
    kept_b, sent_b = level_step(place, HIGH, [total_b, across_b, low_b], (sent_c,))
    high_b = dp_send(sent_b, 8, like_even)
    block_out, done = project(place, *to_project, 1, (half_out,), (sent_b,))
    kept_c, sent_c = level_step(place, HIGH, [total_c, across_c, low_c], (done,))
    high_c = dp_send(sent_c, 8, like_odd)
    weight_grad = choose_owned(place, (kept_a, high_a), (kept_b, high_b), (kept_c, high_c))
    return (block_out, weight_grad)


def general_device(query_rows, key_rows, value_rows, windows, out_weight, gate_scale, out_grad):
    query, key, value = (
        lax.all_to_all(rows, "seq", split_axis=1, concat_axis=0, tiled=True)
        for rows in (query_rows, key_rows, value_rows)
    )
    place = lax.axis_index("seq").reshape(1).astype(jnp.int32)
    mine = attend_whole(place, query, key, value, window_bias(windows))
    columns = lax.all_gather(mine, "seq", axis=1, tiled=True)
    weight = lax.all_gather(out_weight, "dp", axis=0, tiled=True)
    gate_row = gate_scale[0].astype(jnp.float32)
    projected = jnp.dot(columns, weight, preferred_element_type=jnp.float32)
    block_out = (projected * gate_row).astype(jnp.bfloat16)
    grad_proj = (out_grad.astype(jnp.float32) * gate_row).astype(jnp.bfloat16)
    weight_grad = lax.psum_scatter(
        contract_tokens(columns, grad_proj, jnp.float32), "dp", scatter_dimension=0, tiled=True
    )
    return (block_out, weight_grad)


def solution(mesh):
    paired = mesh.shape["seq"] == 2 and mesh.shape["dp"] == HEADS
    return jax.shard_map(
        paired_device if paired else general_device,
        mesh=mesh,
        in_specs=(
            P(("dp", "seq"), None),
            P(("dp", "seq"), None),
            P(("dp", "seq"), None),
            P(),
            P("dp", "seq"),
            P("dp", "seq"),
            P("dp", "seq"),
        ),
        out_specs=(P("dp", "seq"), P("dp", "seq")),
        check_vma=False,
    )
```

```python
import functools
import math

import jax
import jax.numpy as jnp
import numpy as np
from jax import lax
from jax.experimental import pallas as pl
from jax.experimental.pallas import tpu as pltpu
from jax.sharding import PartitionSpec as P

HEADS = 16
HEAD_DIM = 128
GH = 3
GW = 4
GT = 2
TILE = 48
NT = 24
CLIP_TOK = NT * TILE
Q_ROWS = GW * TILE
LOG2_SCALE = math.log2(math.e) / math.sqrt(HEAD_DIM)
VMEM_LIMIT = 16 * 1024 * 1024
VMEM_GRADIENT = 20 * 1024 * 1024
VMEM_PROJECT = 24 * 1024 * 1024
PROJECT_STEPS = 6
GRADIENT_STEPS = 3
SEQ, CORE, X, LOW, HIGH = range(5)
VMEM_WHOLE = 60 * 1024 * 1024
VMEM_SMALL = 12 * 1024 * 1024
SMALL_COST = pl.CostEstimate(flops=1, bytes_accessed=1, transcendentals=0)
LONG_COST = pl.CostEstimate(flops=2 * 10**10, bytes_accessed=2 * 10**7, transcendentals=0)


def window_bias(windows):
    tile_id = np.arange(NT)
    coords = np.stack([tile_id // (GH * GW), tile_id // GW % GH, tile_id % GW]).astype(np.int32)
    token_coords = np.repeat(coords, TILE, axis=1)
    inside = None
    for axis_no, limit in enumerate((GT, GH, GW)):
        extent = jnp.minimum(windows[:, axis_no], limit)[:, None]
        start = jnp.clip(coords[axis_no][None, :] - (extent - 1) // 2, 0, limit - extent)
        column = token_coords[axis_no][None, None, :]
        here = (column >= start[:, :, None]) & (column < (start + extent)[:, :, None])
        inside = here if inside is None else inside & here
    return jnp.where(inside, 0.0, -jnp.inf).astype(jnp.float32)


def attend_rows(queries, first_tile, bias_ref, keys, values):
    count = queries.shape[0]
    tiles = count // TILE
    scores = lax.dot_general(
        queries, keys, (((1,), (1,)), ((), ())), preferred_element_type=jnp.float32
    )
    bias = bias_ref[0, first_tile : first_tile + tiles, :]
    scores = (scores.reshape(tiles, TILE, CLIP_TOK) + bias[:, None, :]).reshape(count, CLIP_TOK)
    peak = jnp.max(scores, axis=-1, keepdims=True)
    weights = jnp.exp2((scores - peak) * LOG2_SCALE).astype(jnp.bfloat16)
    blended = jnp.dot(weights, values, preferred_element_type=jnp.float32)
    return (blended[:, :HEAD_DIM] / blended[:, HEAD_DIM:]).astype(jnp.bfloat16)


def fill_values(values_ref, parts):
    at = 0
    for part in parts:
        rows = part.shape[0]
        values_ref[at : at + rows, :HEAD_DIM] = part
        at += rows
    values_ref[:, HEAD_DIM:] = jnp.ones((CLIP_TOK, HEAD_DIM), jnp.bfloat16)


def pair_kernel(place_ref, q_ref, k_ref, v_ref, other_ref, bias_ref, *rest):
    out_ref, keys_ref, values_ref = rest[-3:]
    half = CLIP_TOK // 2
    keys_ref[:half, :] = k_ref[...]
    keys_ref[half:, :] = other_ref[1]
    fill_values(values_ref, (v_ref[...], other_ref[2]))
    keys = keys_ref[...]
    values = values_ref[...]
    for side in range(2):
        base = pl.multiple_of((place_ref[0] if side == 0 else 1 - place_ref[0]) * half, half)
        for at in range(0, half, Q_ROWS):
            queries = q_ref[at : at + Q_ROWS, :] if side == 0 else other_ref[0, at : at + Q_ROWS, :]
            first_tile = (side * half + at) // TILE
            out_ref[pl.ds(base + at, Q_ROWS), :] = attend_rows(
                queries, first_tile, bias_ref, keys, values
            )


def whole_kernel(place_ref, q_ref, k_ref, v_ref, bias_ref, out_ref, values_ref):
    fill_values(values_ref, (v_ref[...],))
    keys = k_ref[...]
    values = values_ref[...]
    for at in range(0, CLIP_TOK, Q_ROWS):
        out_ref[at : at + Q_ROWS, :] = attend_rows(
            q_ref[at : at + Q_ROWS, :], at // TILE, bias_ref, keys, values
        )


def attention_cost(heads):
    pairs = heads * CLIP_TOK * CLIP_TOK
    return pl.CostEstimate(
        flops=pairs * HEAD_DIM * 6,
        bytes_accessed=heads * CLIP_TOK * HEAD_DIM * 8,
        transcendentals=pairs,
    )


def attend_pair(place, local_heads, picked, query, key, value, other, bias, earlier, limit):
    half = CLIP_TOK // 2
    first, step = picked[0], picked[1] - picked[0]

    def head(i, place_ref):
        return place_ref[0] * local_heads + first + step * i

    own = pl.BlockSpec((half, HEAD_DIM), lambda i, p: (0, head(i, p)))
    return pl.pallas_call(
        pair_kernel,
        grid_spec=pltpu.PrefetchScalarGridSpec(
            num_scalar_prefetch=1,
            grid=(len(picked),),
            in_specs=[
                own,
                own,
                own,
                pl.BlockSpec((3, half, HEAD_DIM), lambda i, p: (0, 0, i)),
                pl.BlockSpec((1, NT, CLIP_TOK), lambda i, p: (head(i, p), 0, 0)),
            ]
            + [pl.BlockSpec(memory_space=pl.ANY)] * len(earlier),
            out_specs=pl.BlockSpec((CLIP_TOK, HEAD_DIM), lambda i, p: (0, i)),
            scratch_shapes=[
                pltpu.VMEM((CLIP_TOK, HEAD_DIM), jnp.bfloat16),
                pltpu.VMEM((CLIP_TOK, 2 * HEAD_DIM), jnp.bfloat16),
            ],
        ),
        out_shape=jax.ShapeDtypeStruct((CLIP_TOK, len(picked) * HEAD_DIM), jnp.bfloat16),
        compiler_params=pltpu.CompilerParams(vmem_limit_bytes=limit),
        cost_estimate=SMALL_COST,
    )(place, query, key, value, other, bias, *earlier)


def attend_whole(place, query, key, value, bias):
    local_heads = query.shape[1] // HEAD_DIM
    column = pl.BlockSpec((CLIP_TOK, HEAD_DIM), lambda i, p: (0, i))
    return pl.pallas_call(
        whole_kernel,
        grid_spec=pltpu.PrefetchScalarGridSpec(
            num_scalar_prefetch=1,
            grid=(local_heads,),
            in_specs=[
                column,
                column,
                column,
                pl.BlockSpec((1, NT, CLIP_TOK), lambda i, p: (p[0] * local_heads + i, 0, 0)),
            ],
            out_specs=column,
            scratch_shapes=[pltpu.VMEM((CLIP_TOK, 2 * HEAD_DIM), jnp.bfloat16)],
        ),
        out_shape=jax.ShapeDtypeStruct(query.shape, jnp.bfloat16),
        compiler_params=pltpu.CompilerParams(vmem_limit_bytes=VMEM_LIMIT),
        cost_estimate=attention_cost(local_heads),
    )(place, query, key, value, bias)


def pack_kernel(place_ref, q_ref, k_ref, v_ref, *rest):
    out_ref = rest[-1]
    out_ref[0] = q_ref[...]
    out_ref[1] = k_ref[...]
    out_ref[2] = v_ref[...]


def pack_partner(place, local_heads, picked, query, key, value, earlier, limit):
    rows = query.shape[0]
    count = len(picked)
    first, step = picked[0], picked[1] - picked[0]

    def head(i, place_ref):
        return (1 - place_ref[0]) * local_heads + first + step * i

    column = pl.BlockSpec((rows, HEAD_DIM), lambda i, p: (0, head(i, p)))
    return pl.pallas_call(
        pack_kernel,
        grid_spec=pltpu.PrefetchScalarGridSpec(
            num_scalar_prefetch=1,
            grid=(count,),
            in_specs=[column, column, column]
            + [pl.BlockSpec(memory_space=pl.ANY)] * len(earlier),
            out_specs=pl.BlockSpec((3, rows, HEAD_DIM), lambda i, p: (0, 0, i)),
        ),
        out_shape=jax.ShapeDtypeStruct((3, rows, count * HEAD_DIM), jnp.bfloat16),
        compiler_params=pltpu.CompilerParams(vmem_limit_bytes=limit),
        cost_estimate=SMALL_COST,
    )(place, query, key, value, *earlier)


def whole_block(shape):
    return pl.BlockSpec(shape, lambda i, p: (0,) * len(shape), pipeline_mode=pl.Buffered(1))


def gradient_kernel(place_ref, *refs, by_call):
    count = 4 if by_call else 2
    grad_ref = refs[count]
    sent_ref, kept_ref, rows_ref = refs[-3:]
    first_core = place_ref[CORE] == 0
    sides = (place_ref[SEQ], 1 - place_ref[SEQ])

    @pl.when(pl.program_id(0) == 0)
    def _():
        sent, kept = [], []
        for n in range(2):
            if by_call:
                one, two = refs[2 + n][...], refs[n][...]
            else:
                one, two = refs[n][:, :HEAD_DIM], refs[n][:, HEAD_DIM:]
            sent.append(jnp.where(first_core, one, two))
            kept.append(jnp.where(first_core, two, one))
        rows_ref[...] = jnp.concatenate(sent + kept, axis=1).T

    each = 2 if by_call else 1
    product = jnp.dot(rows_ref[...], grad_ref[...], preferred_element_type=jnp.float32)
    product = product.astype(jnp.bfloat16).reshape(4 * each, HEAD_DIM, grad_ref.shape[1])
    for n, side in enumerate(sides):
        sent_ref[pl.ds(each * side, each)] = product[each * n : each * (n + 1)]
        kept_ref[pl.ds(each * side, each)] = product[each * (2 + n) : each * (3 + n)]


def batch_gradient(place, sources, grad_proj, earlier=(), cost=SMALL_COST):
    by_call = len(sources) == 4
    heads = len(sources)
    rows, columns = grad_proj.shape
    step = columns // GRADIENT_STEPS
    out = pl.BlockSpec((heads, HEAD_DIM, step), lambda i, p: (0, 0, i))
    result = jax.ShapeDtypeStruct((heads, HEAD_DIM, columns), jnp.bfloat16)
    return pl.pallas_call(
        functools.partial(gradient_kernel, by_call=by_call),
        grid_spec=pltpu.PrefetchScalarGridSpec(
            num_scalar_prefetch=1,
            grid=(GRADIENT_STEPS,),
            in_specs=[whole_block(each.shape) for each in sources]
            + [pl.BlockSpec((rows, step), lambda i, p: (0, i))]
            + [pl.BlockSpec(memory_space=pl.ANY)] * len(earlier),
            out_specs=[out, out],
            scratch_shapes=[pltpu.VMEM((2 * heads * HEAD_DIM, rows), jnp.bfloat16)],
        ),
        out_shape=[result, result],
        compiler_params=pltpu.CompilerParams(vmem_limit_bytes=VMEM_GRADIENT),
        cost_estimate=cost,
    )(place, *sources, grad_proj, *earlier)


def sum_of(blocks):
    total = blocks[0].astype(jnp.float32)
    for block in blocks[1:]:
        total = total + block.astype(jnp.float32)
    return total


def level_step(place, bit, terms, earlier=(), cost=SMALL_COST):
    count = len(terms)
    pairs = terms[0].shape[0] // 2
    shape = (pairs,) + terms[0].shape[1:]
    block = (1,) + terms[0].shape[1:]
    keep = pl.BlockSpec(block, lambda i, p: (2 * i + p[bit], 0, 0))
    send = pl.BlockSpec(block, lambda i, p: (2 * i + 1 - p[bit], 0, 0))
    out = pl.BlockSpec(block, lambda i, p: (i, 0, 0))

    def kernel(place_ref, *refs):
        kept_ref, sent_ref = refs[-2:]
        kept_ref[...] = sum_of([ref[...] for ref in refs[:count]])
        sent_ref[...] = sum_of([ref[...] for ref in refs[count : 2 * count]]).astype(jnp.bfloat16)

    return pl.pallas_call(
        kernel,
        grid_spec=pltpu.PrefetchScalarGridSpec(
            num_scalar_prefetch=1,
            grid=(pairs,),
            in_specs=[keep] * count
            + [send] * count
            + [pl.BlockSpec(memory_space=pl.ANY)] * len(earlier),
            out_specs=[out, out],
        ),
        out_shape=[
            jax.ShapeDtypeStruct(shape, jnp.float32),
            jax.ShapeDtypeStruct(shape, jnp.bfloat16),
        ],
        compiler_params=pltpu.CompilerParams(vmem_limit_bytes=VMEM_SMALL),
        cost_estimate=cost,
    )(place, *terms, *terms, *earlier)


def total_step(terms, earlier=()):
    block = pl.BlockSpec((1,) + terms[0].shape[1:], lambda i: (i, 0, 0))

    def kernel(*refs):
        refs[-1][...] = sum_of([ref[...] for ref in refs[: len(terms)]]).astype(jnp.bfloat16)

    return pl.pallas_call(
        kernel,
        grid=(terms[0].shape[0],),
        in_specs=[block] * len(terms) + [pl.BlockSpec(memory_space=pl.ANY)] * len(earlier),
        out_specs=block,
        out_shape=jax.ShapeDtypeStruct(terms[0].shape, jnp.bfloat16),
        compiler_params=pltpu.CompilerParams(vmem_limit_bytes=VMEM_SMALL),
        cost_estimate=SMALL_COST,
    )(*terms, *earlier)


def choose_owned(place, batch_a, batch_b, batch_c):
    block = batch_a[0].shape

    def kernel(place_ref, *refs):
        alike = place_ref[CORE] == place_ref[X]
        odd = place_ref[LOW] == 1
        owned = (alike, ~alike & ~odd, ~alike & odd)
        for n, mine in enumerate(owned):

            @pl.when(mine)
            def _():
                refs[-1][...] = refs[2 * n][0] + refs[2 * n + 1][0].astype(jnp.float32)

    return pl.pallas_call(
        kernel,
        grid_spec=pltpu.PrefetchScalarGridSpec(
            num_scalar_prefetch=1,
            grid=(1,),
            in_specs=[whole_block(block)] * 6,
            out_specs=whole_block(block[1:]),
        ),
        out_shape=jax.ShapeDtypeStruct(block[1:], jnp.float32),
        compiler_params=pltpu.CompilerParams(vmem_limit_bytes=VMEM_SMALL),
        cost_estimate=SMALL_COST,
    )(place, *batch_a, *batch_b, *batch_c)


def project_kernel(place_ref, *refs, calls, local_heads):
    count = 2 * len(calls)
    weight_ref, gate_ref = refs[count : count + 2]
    out_ref, done_ref, columns_ref = refs[-3:]

    @pl.when(pl.program_id(0) == 0)
    def _():
        done_ref[...] = jnp.zeros_like(done_ref)
        for n in range(count):
            side = place_ref[SEQ] if n % 2 == 0 else 1 - place_ref[SEQ]
            for part, head in enumerate(calls[n // 2]):
                at = pl.multiple_of((side * local_heads + head) * HEAD_DIM, HEAD_DIM)
                columns_ref[:, pl.ds(at, HEAD_DIM)] = refs[n][
                    :, part * HEAD_DIM : (part + 1) * HEAD_DIM
                ]

    total = jnp.dot(columns_ref[...], weight_ref[...], preferred_element_type=jnp.float32)
    out_ref[...] = (total * gate_ref[...]).astype(out_ref.dtype)


def project(place, sources, weight, gate, calls, local_heads, span, filled=(), earlier=(), cost=SMALL_COST):
    depth, columns = weight.shape
    rows = sources[0].shape[0]
    step = columns // PROJECT_STEPS
    first, steps = span[0], len(span)
    block = pl.BlockSpec((rows, step), lambda i, p: (0, first + i))
    return pl.pallas_call(
        functools.partial(project_kernel, calls=calls, local_heads=local_heads),
        grid_spec=pltpu.PrefetchScalarGridSpec(
            num_scalar_prefetch=1,
            grid=(steps,),
            in_specs=[whole_block(each.shape) for each in sources]
            + [pl.BlockSpec((depth, step), lambda i, p: (0, first + i))]
            + [pl.BlockSpec((1, step), lambda i, p: (0, first + i))]
            + [pl.BlockSpec(memory_space=pl.ANY)] * (len(filled) + len(earlier)),
            out_specs=[block, pl.BlockSpec((8, HEAD_DIM), lambda i, p: (0, 0))],
            scratch_shapes=[pltpu.VMEM((rows, depth), jnp.bfloat16)],
        ),
        out_shape=[
            jax.ShapeDtypeStruct((rows, columns), jnp.bfloat16),
            jax.ShapeDtypeStruct((8, HEAD_DIM), jnp.float32),
        ],
        input_output_aliases={len(sources) + 3: 0} if filled else {},
        compiler_params=pltpu.CompilerParams(vmem_limit_bytes=VMEM_PROJECT),
        cost_estimate=cost,
    )(place, *sources, weight, gate, *filled, *earlier)


def contract_tokens(columns, grad_proj, kind):
    return lax.dot_general(
        columns, grad_proj, (((0,), (0,)), ((), ())), preferred_element_type=jnp.float32
    ).astype(kind)


def after(value, *earlier):
    return lax.optimization_barrier((value,) + earlier)[0]


def dp_send(value, flip, sender):
    return lax.ppermute(value, "dp", [(i, i ^ flip) for i in range(HEADS) if sender(i)])


def same_bits(i):
    return (i >> 1 ^ i) & 1 == 0


def paired_device(query_rows, key_rows, value_rows, windows, out_weight, gate_scale, out_grad):
    index = lax.axis_index("dp")
    place = jnp.stack([lax.axis_index("seq")] + [index >> bit & 1 for bit in range(4)])
    place = lax.optimization_barrier(place.astype(jnp.int32))
    local_heads = HEADS // 2
    swap = [(0, 1), (1, 0)]
    calls = [(0, 4), (3, 7), (1, 2), (5, 6)]
    bias = window_bias(windows)
    weight = lax.all_gather(out_weight, "dp", axis=0, tiled=True)
    gate_row = gate_scale[0].astype(jnp.float32)
    grad_proj = (out_grad.astype(jnp.float32) * gate_row).astype(jnp.bfloat16)
    sources = (query_rows, key_rows, value_rows)

    def pack(n, limit, *earlier):
        return pack_partner(place, local_heads, calls[n], *sources, earlier, limit)

    def attention(n, other, *earlier, limit=VMEM_LIMIT):
        return attend_pair(place, local_heads, calls[n], *sources, other, bias, earlier, limit)

    def exchange(mine):
        return lax.ppermute(mine, "seq", swap)

    def core_step(*operands):
        sent, kept = batch_gradient(place, operands[:4], operands[4])
        return total_step([kept, dp_send(sent, 1, lambda i: True)])

    def apart(step, *operands):
        shapes = jax.eval_shape(step, *operands)
        return lax.cond(
            windows[0, 0] > 0,
            step,
            lambda *_: jax.tree.map(lambda leaf: jnp.zeros(leaf.shape, leaf.dtype), shapes),
            *operands,
        )

    packed0 = pack(0, VMEM_WHOLE)
    packed1 = pack(1, VMEM_WHOLE, packed0)
    packed2 = pack(2, VMEM_LIMIT, packed1)
    other0 = exchange(packed0)
    other1 = exchange(packed1)
    other2 = exchange(packed2)
    mine0 = attention(0, other0, packed2)
    theirs0 = exchange(mine0)
    mine1 = attention(1, other1, mine0)
    theirs1 = exchange(mine1)
    packed3 = pack(3, VMEM_LIMIT, mine1)
    other3 = exchange(packed3)
    mine2 = attention(2, other2, mine1, packed3)
    theirs2 = exchange(mine2)

    def unlike(i):
        return not same_bits(i)

    def like_even(i):
        return unlike(i) and i & 4 == 0

    def like_odd(i):
        return unlike(i) and i & 4 != 0

    first = (mine0, theirs0, mine1, theirs1)
    total_a = apart(core_step, after(mine0, mine2, weight), *first[1:], grad_proj)
    across_a = dp_send(total_a, 2, unlike)
    mine3 = attention(3, other3, total_a, limit=VMEM_WHOLE)
    theirs3 = exchange(mine3)
    sent_b, kept_b = batch_gradient(place, (mine2, theirs2), grad_proj, (mine3,), LONG_COST)
    came_b = dp_send(sent_b, 1, lambda i: True)
    kept_a, sent_a = level_step(place, LOW, [total_a, across_a], (sent_b,), LONG_COST)
    low_a = dp_send(sent_a, 4, same_bits)
    total_b = total_step([kept_b, came_b], (sent_a,))
    across_b = dp_send(total_b, 2, same_bits)
    sent_c, kept_c = batch_gradient(place, (mine3, theirs3), grad_proj, (total_b,))
    came_c = dp_send(sent_c, 1, lambda i: True)
    to_project = (*first, mine2, theirs2, mine3, theirs3), weight, gate_row[None], calls, local_heads
    out, done = project(place, *to_project, range(1), (), (sent_c,), LONG_COST)
    total_c = total_step([kept_c, came_c], (done,))
    across_c = dp_send(total_c, 2, same_bits)
    kept_a, sent_a = level_step(place, HIGH, [kept_a, low_a], (total_c,))
    high_a = dp_send(sent_a, 8, same_bits)
    sent_b = total_step([total_b, across_b], (sent_a,))
    low_b = dp_send(sent_b, 4, like_odd)
    out, done = project(place, *to_project, range(1, 4), (out,), (sent_b,))
    sent_c = total_step([total_c, across_c], (done, high_a))
    low_c = dp_send(sent_c, 4, like_even)
    kept_b, sent_b = level_step(place, HIGH, [total_b, across_b, low_b], (sent_c,))
    high_b = dp_send(sent_b, 8, like_even)
    block_out, done = project(place, *to_project, range(4, PROJECT_STEPS), (out,), (sent_b,))
    kept_c, sent_c = level_step(place, HIGH, [total_c, across_c, low_c], (done,))
    high_c = dp_send(sent_c, 8, like_odd)
    weight_grad = choose_owned(place, (kept_a, high_a), (kept_b, high_b), (kept_c, high_c))
    return (block_out, weight_grad)


def general_device(query_rows, key_rows, value_rows, windows, out_weight, gate_scale, out_grad):
    query, key, value = (
        lax.all_to_all(rows, "seq", split_axis=1, concat_axis=0, tiled=True)
        for rows in (query_rows, key_rows, value_rows)
    )
    place = lax.axis_index("seq").reshape(1).astype(jnp.int32)
    mine = attend_whole(place, query, key, value, window_bias(windows))
    columns = lax.all_gather(mine, "seq", axis=1, tiled=True)
    weight = lax.all_gather(out_weight, "dp", axis=0, tiled=True)
    gate_row = gate_scale[0].astype(jnp.float32)
    projected = jnp.dot(columns, weight, preferred_element_type=jnp.float32)
    block_out = (projected * gate_row).astype(jnp.bfloat16)
    grad_proj = (out_grad.astype(jnp.float32) * gate_row).astype(jnp.bfloat16)
    weight_grad = lax.psum_scatter(
        contract_tokens(columns, grad_proj, jnp.float32), "dp", scatter_dimension=0, tiled=True
    )
    return (block_out, weight_grad)


def solution(mesh):
    paired = mesh.shape["seq"] == 2 and mesh.shape["dp"] == HEADS
    return jax.shard_map(
        paired_device if paired else general_device,
        mesh=mesh,
        in_specs=(
            P(("dp", "seq"), None),
            P(("dp", "seq"), None),
            P(("dp", "seq"), None),
            P(),
            P("dp", "seq"),
            P("dp", "seq"),
            P("dp", "seq"),
        ),
        out_specs=(P("dp", "seq"), P("dp", "seq")),
        check_vma=False,
    )
```

```python
import functools
import math

import jax
import jax.numpy as jnp
import numpy as np
from jax import lax
from jax.experimental import pallas as pl
from jax.experimental.pallas import tpu as pltpu
from jax.sharding import PartitionSpec as P

HEADS = 16
HEAD_DIM = 128
GH = 3
GW = 4
GT = 2
TILE = 48
NT = 24
CLIP_TOK = NT * TILE
Q_ROWS = GW * TILE
LOG2_SCALE = math.log2(math.e) / math.sqrt(HEAD_DIM)
VMEM_LIMIT = 16 * 1024 * 1024
VMEM_GRADIENT = 20 * 1024 * 1024
VMEM_PROJECT = 24 * 1024 * 1024
PROJECT_STEPS = 6
GRADIENT_STEPS = 3
JOIN_STEPS = 4
SEQ, CORE, X, LOW, HIGH = range(5)
VMEM_WHOLE = 60 * 1024 * 1024
VMEM_SMALL = 12 * 1024 * 1024
SMALL_COST = pl.CostEstimate(flops=1, bytes_accessed=1, transcendentals=0)
LONG_COST = pl.CostEstimate(flops=2 * 10**10, bytes_accessed=2 * 10**7, transcendentals=0)


def window_bias(windows):
    tile_id = np.arange(NT)
    coords = np.stack([tile_id // (GH * GW), tile_id // GW % GH, tile_id % GW]).astype(np.int32)
    token_coords = np.repeat(coords, TILE, axis=1)
    inside = None
    for axis_no, limit in enumerate((GT, GH, GW)):
        extent = jnp.minimum(windows[:, axis_no], limit)[:, None]
        start = jnp.clip(coords[axis_no][None, :] - (extent - 1) // 2, 0, limit - extent)
        column = token_coords[axis_no][None, None, :]
        here = (column >= start[:, :, None]) & (column < (start + extent)[:, :, None])
        inside = here if inside is None else inside & here
    return jnp.where(inside, 0.0, -jnp.inf).astype(jnp.float32)


def attend_rows(queries, first_tile, bias_ref, keys, values):
    count = queries.shape[0]
    tiles = count // TILE
    scores = lax.dot_general(
        queries, keys, (((1,), (1,)), ((), ())), preferred_element_type=jnp.float32
    )
    bias = bias_ref[0, first_tile : first_tile + tiles, :]
    scores = (scores.reshape(tiles, TILE, CLIP_TOK) + bias[:, None, :]).reshape(count, CLIP_TOK)
    peak = jnp.max(scores, axis=-1, keepdims=True)
    weights = jnp.exp2((scores - peak) * LOG2_SCALE).astype(jnp.bfloat16)
    blended = jnp.dot(weights, values, preferred_element_type=jnp.float32)
    return (blended[:, :HEAD_DIM] / blended[:, HEAD_DIM:]).astype(jnp.bfloat16)


def fill_values(values_ref, parts):
    at = 0
    for part in parts:
        rows = part.shape[0]
        values_ref[at : at + rows, :HEAD_DIM] = part
        at += rows
    values_ref[:, HEAD_DIM:] = jnp.ones((CLIP_TOK, HEAD_DIM), jnp.bfloat16)


def pair_kernel(place_ref, q_ref, k_ref, v_ref, other_ref, bias_ref, *rest):
    out_ref, keys_ref, values_ref = rest[-3:]
    half = CLIP_TOK // 2
    keys_ref[:half, :] = k_ref[...]
    keys_ref[half:, :] = other_ref[1]
    fill_values(values_ref, (v_ref[...], other_ref[2]))
    keys = keys_ref[...]
    values = values_ref[...]
    for side in range(2):
        base = pl.multiple_of((place_ref[0] if side == 0 else 1 - place_ref[0]) * half, half)
        for at in range(0, half, Q_ROWS):
            queries = q_ref[at : at + Q_ROWS, :] if side == 0 else other_ref[0, at : at + Q_ROWS, :]
            first_tile = (side * half + at) // TILE
            out_ref[pl.ds(base + at, Q_ROWS), :] = attend_rows(
                queries, first_tile, bias_ref, keys, values
            )


def whole_kernel(place_ref, q_ref, k_ref, v_ref, bias_ref, out_ref, values_ref):
    fill_values(values_ref, (v_ref[...],))
    keys = k_ref[...]
    values = values_ref[...]
    for at in range(0, CLIP_TOK, Q_ROWS):
        out_ref[at : at + Q_ROWS, :] = attend_rows(
            q_ref[at : at + Q_ROWS, :], at // TILE, bias_ref, keys, values
        )


def attention_cost(heads):
    pairs = heads * CLIP_TOK * CLIP_TOK
    return pl.CostEstimate(
        flops=pairs * HEAD_DIM * 6,
        bytes_accessed=heads * CLIP_TOK * HEAD_DIM * 8,
        transcendentals=pairs,
    )


def attend_pair(place, local_heads, call, query, key, value, other, bias, earlier, limit):
    half = CLIP_TOK // 2
    count = 2

    def head(i, place_ref):
        return place_ref[SEQ] * local_heads + local_head(call, place_ref[SEQ], i)

    own = pl.BlockSpec((half, HEAD_DIM), lambda i, p: (0, head(i, p)))
    return pl.pallas_call(
        pair_kernel,
        grid_spec=pltpu.PrefetchScalarGridSpec(
            num_scalar_prefetch=1,
            grid=(count,),
            in_specs=[
                own,
                own,
                own,
                pl.BlockSpec((3, half, HEAD_DIM), lambda i, p: (0, 0, i)),
                pl.BlockSpec((1, NT, CLIP_TOK), lambda i, p: (head(i, p), 0, 0)),
            ]
            + [pl.BlockSpec(memory_space=pl.ANY)] * len(earlier),
            out_specs=pl.BlockSpec((CLIP_TOK, HEAD_DIM), lambda i, p: (0, i)),
            scratch_shapes=[
                pltpu.VMEM((CLIP_TOK, HEAD_DIM), jnp.bfloat16),
                pltpu.VMEM((CLIP_TOK, 2 * HEAD_DIM), jnp.bfloat16),
            ],
        ),
        out_shape=jax.ShapeDtypeStruct((CLIP_TOK, count * HEAD_DIM), jnp.bfloat16),
        compiler_params=pltpu.CompilerParams(vmem_limit_bytes=limit),
        cost_estimate=SMALL_COST,
    )(place, query, key, value, other, bias, *earlier)


def attend_whole(place, query, key, value, bias):
    local_heads = query.shape[1] // HEAD_DIM
    column = pl.BlockSpec((CLIP_TOK, HEAD_DIM), lambda i, p: (0, i))
    return pl.pallas_call(
        whole_kernel,
        grid_spec=pltpu.PrefetchScalarGridSpec(
            num_scalar_prefetch=1,
            grid=(local_heads,),
            in_specs=[
                column,
                column,
                column,
                pl.BlockSpec((1, NT, CLIP_TOK), lambda i, p: (p[0] * local_heads + i, 0, 0)),
            ],
            out_specs=column,
            scratch_shapes=[pltpu.VMEM((CLIP_TOK, 2 * HEAD_DIM), jnp.bfloat16)],
        ),
        out_shape=jax.ShapeDtypeStruct(query.shape, jnp.bfloat16),
        compiler_params=pltpu.CompilerParams(vmem_limit_bytes=VMEM_LIMIT),
        cost_estimate=attention_cost(local_heads),
    )(place, query, key, value, bias)


def pack_kernel(place_ref, q_ref, k_ref, v_ref, *rest):
    out_ref = rest[-1]
    out_ref[0] = q_ref[...]
    out_ref[1] = k_ref[...]
    out_ref[2] = v_ref[...]


def local_head(call, side, part):
    first, by_side, step = call
    return first + by_side * side + step * part


def pack_partner(place, local_heads, call, query, key, value, earlier, limit):
    rows = query.shape[0]
    count = 2

    def head(i, place_ref):
        side = 1 - place_ref[SEQ]
        return side * local_heads + local_head(call, side, i)

    column = pl.BlockSpec((rows, HEAD_DIM), lambda i, p: (0, head(i, p)))
    return pl.pallas_call(
        pack_kernel,
        grid_spec=pltpu.PrefetchScalarGridSpec(
            num_scalar_prefetch=1,
            grid=(count,),
            in_specs=[column, column, column]
            + [pl.BlockSpec(memory_space=pl.ANY)] * len(earlier),
            out_specs=pl.BlockSpec((3, rows, HEAD_DIM), lambda i, p: (0, 0, i)),
        ),
        out_shape=jax.ShapeDtypeStruct((3, rows, count * HEAD_DIM), jnp.bfloat16),
        compiler_params=pltpu.CompilerParams(vmem_limit_bytes=limit),
        cost_estimate=SMALL_COST,
    )(place, query, key, value, *earlier)


def whole_block(shape):
    return pl.BlockSpec(shape, lambda i, p: (0,) * len(shape), pipeline_mode=pl.Buffered(1))


def gradient_kernel(place_ref, *refs, by_call):
    count = 4 if by_call else 2
    grad_ref = refs[count]
    sent_ref, kept_ref, rows_ref = refs[-3:]
    first_core = place_ref[CORE] == 0
    sides = (place_ref[SEQ], 1 - place_ref[SEQ])

    @pl.when(pl.program_id(0) == 0)
    def _():
        sent, kept = [], []
        for n in range(2):
            if by_call:
                one, two = refs[2 + n][...], refs[n][...]
            else:
                one, two = refs[n][:, :HEAD_DIM], refs[n][:, HEAD_DIM:]
            sent.append(jnp.where(first_core, one, two))
            kept.append(jnp.where(first_core, two, one))
        rows_ref[...] = jnp.concatenate(sent + kept, axis=1).T

    each = 2 if by_call else 1
    product = jnp.dot(rows_ref[...], grad_ref[...], preferred_element_type=jnp.float32)
    product = product.astype(jnp.bfloat16).reshape(4 * each, HEAD_DIM, grad_ref.shape[1])
    for n, side in enumerate(sides):
        sent_ref[pl.ds(each * side, each)] = product[each * n : each * (n + 1)]
        kept_ref[pl.ds(each * side, each)] = product[each * (2 + n) : each * (3 + n)]


def batch_gradient(place, sources, grad_proj, earlier=(), cost=SMALL_COST):
    by_call = len(sources) == 4
    heads = len(sources)
    rows, columns = grad_proj.shape
    step = columns // GRADIENT_STEPS
    out = pl.BlockSpec((heads, HEAD_DIM, step), lambda i, p: (0, 0, i))
    result = jax.ShapeDtypeStruct((heads, HEAD_DIM, columns), jnp.bfloat16)
    return pl.pallas_call(
        functools.partial(gradient_kernel, by_call=by_call),
        grid_spec=pltpu.PrefetchScalarGridSpec(
            num_scalar_prefetch=1,
            grid=(GRADIENT_STEPS,),
            in_specs=[whole_block(each.shape) for each in sources]
            + [pl.BlockSpec((rows, step), lambda i, p: (0, i))]
            + [pl.BlockSpec(memory_space=pl.ANY)] * len(earlier),
            out_specs=[out, out],
            scratch_shapes=[pltpu.VMEM((2 * heads * HEAD_DIM, rows), jnp.bfloat16)],
        ),
        out_shape=[result, result],
        compiler_params=pltpu.CompilerParams(vmem_limit_bytes=VMEM_GRADIENT),
        cost_estimate=cost,
    )(place, *sources, grad_proj, *earlier)


def sum_of(blocks):
    total = blocks[0].astype(jnp.float32)
    for block in blocks[1:]:
        total = total + block.astype(jnp.float32)
    return total


def level_step(place, bit, terms, earlier=(), cost=SMALL_COST):
    count = len(terms)
    pairs = terms[0].shape[0] // 2
    shape = (pairs,) + terms[0].shape[1:]
    block = (1,) + terms[0].shape[1:]
    keep = pl.BlockSpec(block, lambda i, p: (2 * i + p[bit], 0, 0))
    send = pl.BlockSpec(block, lambda i, p: (2 * i + 1 - p[bit], 0, 0))
    out = pl.BlockSpec(block, lambda i, p: (i, 0, 0))

    def kernel(place_ref, *refs):
        kept_ref, sent_ref = refs[-2:]
        kept_ref[...] = sum_of([ref[...] for ref in refs[:count]])
        sent_ref[...] = sum_of([ref[...] for ref in refs[count : 2 * count]]).astype(jnp.bfloat16)

    return pl.pallas_call(
        kernel,
        grid_spec=pltpu.PrefetchScalarGridSpec(
            num_scalar_prefetch=1,
            grid=(pairs,),
            in_specs=[keep] * count
            + [send] * count
            + [pl.BlockSpec(memory_space=pl.ANY)] * len(earlier),
            out_specs=[out, out],
        ),
        out_shape=[
            jax.ShapeDtypeStruct(shape, jnp.float32),
            jax.ShapeDtypeStruct(shape, jnp.bfloat16),
        ],
        compiler_params=pltpu.CompilerParams(vmem_limit_bytes=VMEM_SMALL),
        cost_estimate=cost,
    )(place, *terms, *terms, *earlier)


def reach_step(place, terms, earlier=()):
    count = len(terms)
    block = (1,) + terms[0].shape[1:]
    near = pl.BlockSpec(block, lambda i, p: (p[HIGH], 0, 0))
    far = pl.BlockSpec(block, lambda i, p: (1 - p[HIGH], 0, 0))

    def kernel(place_ref, *refs):
        kept_ref, near_ref, far_ref = refs[-3:]
        total = sum_of([ref[...] for ref in refs[:count]])
        kept_ref[...] = total
        near_ref[...] = total.astype(jnp.bfloat16)
        far_ref[...] = sum_of([ref[...] for ref in refs[count : 2 * count]]).astype(jnp.bfloat16)

    return pl.pallas_call(
        kernel,
        grid_spec=pltpu.PrefetchScalarGridSpec(
            num_scalar_prefetch=1,
            grid=(1,),
            in_specs=[near] * count
            + [far] * count
            + [pl.BlockSpec(memory_space=pl.ANY)] * len(earlier),
            out_specs=[whole_block(block)] * 3,
        ),
        out_shape=[
            jax.ShapeDtypeStruct(block, kind) for kind in (jnp.float32, jnp.bfloat16, jnp.bfloat16)
        ],
        compiler_params=pltpu.CompilerParams(vmem_limit_bytes=VMEM_SMALL),
        cost_estimate=SMALL_COST,
    )(place, *terms, *terms, *earlier)


def total_step(terms, earlier=()):
    block = pl.BlockSpec((1,) + terms[0].shape[1:], lambda i: (i, 0, 0))

    def kernel(*refs):
        refs[-1][...] = sum_of([ref[...] for ref in refs[: len(terms)]]).astype(jnp.bfloat16)

    return pl.pallas_call(
        kernel,
        grid=(terms[0].shape[0],),
        in_specs=[block] * len(terms) + [pl.BlockSpec(memory_space=pl.ANY)] * len(earlier),
        out_specs=block,
        out_shape=jax.ShapeDtypeStruct(terms[0].shape, jnp.bfloat16),
        compiler_params=pltpu.CompilerParams(vmem_limit_bytes=VMEM_SMALL),
        cost_estimate=SMALL_COST,
    )(*terms, *earlier)


def choose_owned(place, *batches):
    block = batches[0][0].shape
    terms = [term for batch in batches for term in batch]

    def kernel(place_ref, *refs):
        alike = place_ref[CORE] == place_ref[X]
        outer = place_ref[LOW] == place_ref[HIGH]
        owned = (alike, ~alike & outer, ~alike & ~outer)
        at = 0
        for batch, mine in zip(batches, owned):
            chosen = refs[at : at + len(batch)]
            at += len(batch)

            @pl.when(mine)
            def _():
                refs[-1][...] = sum_of([ref[0] for ref in chosen])

    return pl.pallas_call(
        kernel,
        grid_spec=pltpu.PrefetchScalarGridSpec(
            num_scalar_prefetch=1,
            grid=(1,),
            in_specs=[whole_block(block)] * len(terms),
            out_specs=whole_block(block[1:]),
        ),
        out_shape=jax.ShapeDtypeStruct(block[1:], jnp.float32),
        compiler_params=pltpu.CompilerParams(vmem_limit_bytes=VMEM_GRADIENT),
        cost_estimate=SMALL_COST,
    )(place, *terms)


def join_columns(place, sources, calls, local_heads, earlier, cost):
    rows = sources[0].shape[0]
    step = rows // JOIN_STEPS
    shape = (rows, HEADS * HEAD_DIM)

    def kernel(place_ref, *refs):
        out_ref, done_ref = refs[-2:]
        done_ref[...] = jnp.zeros_like(done_ref)
        for n, source in enumerate(refs[: len(sources)]):
            side = place_ref[SEQ] if n % 2 == 0 else 1 - place_ref[SEQ]
            for part in range(2):
                head = side * local_heads + local_head(calls[n // 2], side, part)
                at = pl.multiple_of(head * HEAD_DIM, HEAD_DIM)
                out_ref[:, pl.ds(at, HEAD_DIM)] = source[:, part * HEAD_DIM : (part + 1) * HEAD_DIM]

    return pl.pallas_call(
        kernel,
        grid_spec=pltpu.PrefetchScalarGridSpec(
            num_scalar_prefetch=1,
            grid=(JOIN_STEPS,),
            in_specs=[pl.BlockSpec((step, each.shape[1]), lambda i, p: (i, 0)) for each in sources]
            + [pl.BlockSpec(memory_space=pl.ANY)] * len(earlier),
            out_specs=[
                pl.BlockSpec((step, shape[1]), lambda i, p: (i, 0)),
                pl.BlockSpec((8, HEAD_DIM), lambda i, p: (0, 0)),
            ],
        ),
        out_shape=[
            jax.ShapeDtypeStruct(shape, jnp.bfloat16),
            jax.ShapeDtypeStruct((8, HEAD_DIM), jnp.float32),
        ],
        compiler_params=pltpu.CompilerParams(vmem_limit_bytes=VMEM_SMALL),
        cost_estimate=cost,
    )(place, *sources, *earlier)


def project(attention, weight, gate, span, filled=(), earlier=()):
    rows, depth = attention.shape
    columns = weight.shape[1]
    step = columns // PROJECT_STEPS
    first, steps = span[0], len(span)
    block = pl.BlockSpec((rows, step), lambda i: (0, first + i))

    def kernel(attention_ref, weight_ref, gate_ref, *refs):
        out_ref, done_ref = refs[-2:]
        done_ref[...] = jnp.zeros_like(done_ref)
        total = jnp.dot(attention_ref[...], weight_ref[...], preferred_element_type=jnp.float32)
        out_ref[...] = (total * gate_ref[...]).astype(out_ref.dtype)

    return pl.pallas_call(
        kernel,
        grid=(steps,),
        in_specs=[
            pl.BlockSpec((rows, depth), lambda i: (0, 0), pipeline_mode=pl.Buffered(1)),
            pl.BlockSpec((depth, step), lambda i: (0, first + i)),
            pl.BlockSpec((1, step), lambda i: (0, first + i)),
        ]
        + [pl.BlockSpec(memory_space=pl.ANY)] * (len(filled) + len(earlier)),
        out_specs=[block, pl.BlockSpec((8, HEAD_DIM), lambda i: (0, 0))],
        out_shape=[
            jax.ShapeDtypeStruct((rows, columns), jnp.bfloat16),
            jax.ShapeDtypeStruct((8, HEAD_DIM), jnp.float32),
        ],
        input_output_aliases={3: 0} if filled else {},
        compiler_params=pltpu.CompilerParams(vmem_limit_bytes=VMEM_PROJECT),
        cost_estimate=SMALL_COST,
    )(attention, weight, gate, *filled, *earlier)


def contract_tokens(columns, grad_proj, kind):
    return lax.dot_general(
        columns, grad_proj, (((0,), (0,)), ((), ())), preferred_element_type=jnp.float32
    ).astype(kind)


def after(value, *earlier):
    return lax.optimization_barrier((value,) + earlier)[0]


def dp_send(value, flip, sender):
    return lax.ppermute(value, "dp", [(i, i ^ flip) for i in range(HEADS) if sender(i)])


def same_bits(i):
    return (i >> 1 ^ i) & 1 == 0


def paired_device(query_rows, key_rows, value_rows, windows, out_weight, gate_scale, out_grad):
    index = lax.axis_index("dp")
    place = jnp.stack([lax.axis_index("seq")] + [index >> bit & 1 for bit in range(4)])
    place = lax.optimization_barrier(place.astype(jnp.int32))
    local_heads = HEADS // 2
    swap = [(0, 1), (1, 0)]
    calls = [(0, 0, 4), (3, 0, 4), (1, 4, 1), (5, -4, 1)]
    bias = window_bias(windows)
    weight = lax.all_gather(out_weight, "dp", axis=0, tiled=True)
    gate_row = gate_scale[0].astype(jnp.float32)
    grad_proj = (out_grad.astype(jnp.float32) * gate_row).astype(jnp.bfloat16)
    sources = (query_rows, key_rows, value_rows)

    def pack(n, limit, *earlier):
        return pack_partner(place, local_heads, calls[n], *sources, earlier, limit)

    def attention(n, other, *earlier, limit=VMEM_LIMIT):
        return attend_pair(place, local_heads, calls[n], *sources, other, bias, earlier, limit)

    def exchange(mine):
        return lax.ppermute(mine, "seq", swap)

    def core_step(*operands):
        sent, kept = batch_gradient(place, operands[:4], operands[4])
        return total_step([kept, dp_send(sent, 1, lambda i: True)])

    def apart(step, *operands):
        shapes = jax.eval_shape(step, *operands)
        return lax.cond(
            windows[0, 0] > 0,
            step,
            lambda *_: jax.tree.map(lambda leaf: jnp.zeros(leaf.shape, leaf.dtype), shapes),
            *operands,
        )

    packed0 = pack(0, VMEM_WHOLE)
    packed1 = pack(1, VMEM_WHOLE, packed0)
    packed2 = pack(2, VMEM_LIMIT, packed1)
    other0 = exchange(packed0)
    other1 = exchange(packed1)
    other2 = exchange(packed2)
    mine0 = attention(0, other0, packed2)
    theirs0 = exchange(mine0)
    mine1 = attention(1, other1, mine0)
    theirs1 = exchange(mine1)
    packed3 = pack(3, VMEM_LIMIT, mine1)
    other3 = exchange(packed3)
    mine2 = attention(2, other2, mine1, packed3)
    theirs2 = exchange(mine2)

    def unlike(i):
        return not same_bits(i)

    def outer(i):
        return unlike(i) and (i >> 2 ^ i >> 3) & 1 == 0

    def inner(i):
        return unlike(i) and (i >> 2 ^ i >> 3) & 1 == 1

    def reach(near, far, others, owners):
        return dp_send(near, 4, others), dp_send(far, 12, owners), dp_send(far, 8, others)

    first = (mine0, theirs0, mine1, theirs1)
    total_a = apart(core_step, after(mine0, mine2, weight), *first[1:], grad_proj)
    across_a = dp_send(total_a, 2, unlike)
    mine3 = attention(3, other3, total_a, limit=VMEM_WHOLE)
    theirs3 = exchange(mine3)
    sent_b, kept_b = batch_gradient(place, (mine2, theirs2), grad_proj, (mine3,), LONG_COST)
    came_b = dp_send(sent_b, 1, lambda i: True)
    kept_a, sent_a = level_step(place, LOW, [total_a, across_a], (sent_b,), LONG_COST)
    low_a = dp_send(sent_a, 4, same_bits)
    total_b = total_step([kept_b, came_b], (sent_a,))
    across_b = dp_send(total_b, 2, same_bits)
    sent_c, kept_c = batch_gradient(place, (mine3, theirs3), grad_proj, (total_b,))
    came_c = dp_send(sent_c, 1, lambda i: True)
    results = (*first, mine2, theirs2, mine3, theirs3)
    columns, done = join_columns(place, results, calls, local_heads, (sent_c,), LONG_COST)
    total_c = total_step([kept_c, came_c], (done,))
    across_c = dp_send(total_c, 2, same_bits)
    kept_a, sent_a = level_step(place, HIGH, [kept_a, low_a], (total_c,))
    high_a = dp_send(sent_a, 8, same_bits)
    kept_b, near_b, far_b = reach_step(place, [total_b, across_b], (sent_a,))
    reached_b = reach(near_b, far_b, inner, outer)
    gate = gate_row[None]
    out, done = project(columns, weight, gate, range(3), (), (near_b,))
    kept_c, near_c, far_c = reach_step(place, [total_c, across_c], (done, high_a))
    reached_c = reach(near_c, far_c, outer, inner)
    block_out, done = project(columns, weight, gate, range(3, PROJECT_STEPS), (out,), (near_c,))
    weight_grad = choose_owned(place, (kept_a, high_a), (kept_b, *reached_b), (kept_c, *reached_c))
    return (block_out, weight_grad)


def general_device(query_rows, key_rows, value_rows, windows, out_weight, gate_scale, out_grad):
    query, key, value = (
        lax.all_to_all(rows, "seq", split_axis=1, concat_axis=0, tiled=True)
        for rows in (query_rows, key_rows, value_rows)
    )
    place = lax.axis_index("seq").reshape(1).astype(jnp.int32)
    mine = attend_whole(place, query, key, value, window_bias(windows))
    columns = lax.all_gather(mine, "seq", axis=1, tiled=True)
    weight = lax.all_gather(out_weight, "dp", axis=0, tiled=True)
    gate_row = gate_scale[0].astype(jnp.float32)
    projected = jnp.dot(columns, weight, preferred_element_type=jnp.float32)
    block_out = (projected * gate_row).astype(jnp.bfloat16)
    grad_proj = (out_grad.astype(jnp.float32) * gate_row).astype(jnp.bfloat16)
    weight_grad = lax.psum_scatter(
        contract_tokens(columns, grad_proj, jnp.float32), "dp", scatter_dimension=0, tiled=True
    )
    return (block_out, weight_grad)


def solution(mesh):
    paired = mesh.shape["seq"] == 2 and mesh.shape["dp"] == HEADS
    return jax.shard_map(
        paired_device if paired else general_device,
        mesh=mesh,
        in_specs=(
            P(("dp", "seq"), None),
            P(("dp", "seq"), None),
            P(("dp", "seq"), None),
            P(),
            P("dp", "seq"),
            P("dp", "seq"),
            P("dp", "seq"),
        ),
        out_specs=(P("dp", "seq"), P("dp", "seq")),
        check_vma=False,
    )
```

```python
import functools
import math

import jax
import jax.numpy as jnp
import numpy as np
from jax import lax
from jax.experimental import pallas as pl
from jax.experimental.pallas import tpu as pltpu
from jax.sharding import PartitionSpec as P

HEADS = 16
HEAD_DIM = 128
GH = 3
GW = 4
GT = 2
TILE = 48
NT = 24
CLIP_TOK = NT * TILE
Q_ROWS = GW * TILE
LOG2_SCALE = math.log2(math.e) / math.sqrt(HEAD_DIM)
VMEM_LIMIT = 16 * 1024 * 1024
VMEM_GRADIENT = 20 * 1024 * 1024
VMEM_PROJECT = 24 * 1024 * 1024
PROJECT_STEPS = 6
GRADIENT_STEPS = 3
JOIN_STEPS = 4
SEQ, CORE, X, LOW, HIGH = range(5)
VMEM_WHOLE = 60 * 1024 * 1024
VMEM_SMALL = 12 * 1024 * 1024
SMALL_COST = pl.CostEstimate(flops=1, bytes_accessed=1, transcendentals=0)
LONG_COST = pl.CostEstimate(flops=2 * 10**10, bytes_accessed=2 * 10**7, transcendentals=0)


def window_bias(windows):
    tile_id = np.arange(NT)
    coords = np.stack([tile_id // (GH * GW), tile_id // GW % GH, tile_id % GW]).astype(np.int32)
    token_coords = np.repeat(coords, TILE, axis=1)
    inside = None
    for axis_no, limit in enumerate((GT, GH, GW)):
        extent = jnp.minimum(windows[:, axis_no], limit)[:, None]
        start = jnp.clip(coords[axis_no][None, :] - (extent - 1) // 2, 0, limit - extent)
        column = token_coords[axis_no][None, None, :]
        here = (column >= start[:, :, None]) & (column < (start + extent)[:, :, None])
        inside = here if inside is None else inside & here
    return jnp.where(inside, 0.0, -jnp.inf).astype(jnp.float32)


def attend_rows(queries, first_tile, bias_ref, keys, values):
    count = queries.shape[0]
    tiles = count // TILE
    scores = lax.dot_general(
        queries, keys, (((1,), (1,)), ((), ())), preferred_element_type=jnp.float32
    )
    bias = bias_ref[0, first_tile : first_tile + tiles, :]
    scores = (scores.reshape(tiles, TILE, CLIP_TOK) + bias[:, None, :]).reshape(count, CLIP_TOK)
    peak = jnp.max(scores, axis=-1, keepdims=True)
    weights = jnp.exp2((scores - peak) * LOG2_SCALE).astype(jnp.bfloat16)
    blended = jnp.dot(weights, values, preferred_element_type=jnp.float32)
    return (blended[:, :HEAD_DIM] / blended[:, HEAD_DIM:]).astype(jnp.bfloat16)


def fill_values(values_ref, parts):
    at = 0
    for part in parts:
        rows = part.shape[0]
        values_ref[at : at + rows, :HEAD_DIM] = part
        at += rows
    values_ref[:, HEAD_DIM:] = jnp.ones((CLIP_TOK, HEAD_DIM), jnp.bfloat16)


def pair_kernel(place_ref, q_ref, k_ref, v_ref, other_ref, bias_ref, *rest):
    out_ref, keys_ref, values_ref = rest[-3:]
    half = CLIP_TOK // 2
    keys_ref[:half, :] = k_ref[...]
    keys_ref[half:, :] = other_ref[1]
    fill_values(values_ref, (v_ref[...], other_ref[2]))
    keys = keys_ref[...]
    values = values_ref[...]
    for side in range(2):
        base = pl.multiple_of((place_ref[0] if side == 0 else 1 - place_ref[0]) * half, half)
        for at in range(0, half, Q_ROWS):
            queries = q_ref[at : at + Q_ROWS, :] if side == 0 else other_ref[0, at : at + Q_ROWS, :]
            first_tile = (side * half + at) // TILE
            out_ref[pl.ds(base + at, Q_ROWS), :] = attend_rows(
                queries, first_tile, bias_ref, keys, values
            )


def whole_kernel(place_ref, q_ref, k_ref, v_ref, bias_ref, out_ref, values_ref):
    fill_values(values_ref, (v_ref[...],))
    keys = k_ref[...]
    values = values_ref[...]
    for at in range(0, CLIP_TOK, Q_ROWS):
        out_ref[at : at + Q_ROWS, :] = attend_rows(
            q_ref[at : at + Q_ROWS, :], at // TILE, bias_ref, keys, values
        )


def attention_cost(heads):
    pairs = heads * CLIP_TOK * CLIP_TOK
    return pl.CostEstimate(
        flops=pairs * HEAD_DIM * 6,
        bytes_accessed=heads * CLIP_TOK * HEAD_DIM * 8,
        transcendentals=pairs,
    )


def attend_pair(place, local_heads, call, query, key, value, other, bias, earlier, limit):
    half = CLIP_TOK // 2
    count = 2

    def head(i, place_ref):
        return place_ref[SEQ] * local_heads + local_head(call, place_ref[SEQ], i)

    own = pl.BlockSpec((half, HEAD_DIM), lambda i, p: (0, head(i, p)))
    return pl.pallas_call(
        pair_kernel,
        grid_spec=pltpu.PrefetchScalarGridSpec(
            num_scalar_prefetch=1,
            grid=(count,),
            in_specs=[
                own,
                own,
                own,
                pl.BlockSpec((3, half, HEAD_DIM), lambda i, p: (0, 0, i)),
                pl.BlockSpec((1, NT, CLIP_TOK), lambda i, p: (head(i, p), 0, 0)),
            ]
            + [pl.BlockSpec(memory_space=pl.ANY)] * len(earlier),
            out_specs=pl.BlockSpec((CLIP_TOK, HEAD_DIM), lambda i, p: (0, i)),
            scratch_shapes=[
                pltpu.VMEM((CLIP_TOK, HEAD_DIM), jnp.bfloat16),
                pltpu.VMEM((CLIP_TOK, 2 * HEAD_DIM), jnp.bfloat16),
            ],
        ),
        out_shape=jax.ShapeDtypeStruct((CLIP_TOK, count * HEAD_DIM), jnp.bfloat16),
        compiler_params=pltpu.CompilerParams(vmem_limit_bytes=limit),
        cost_estimate=SMALL_COST,
    )(place, query, key, value, other, bias, *earlier)


def attend_whole(place, query, key, value, bias):
    local_heads = query.shape[1] // HEAD_DIM
    column = pl.BlockSpec((CLIP_TOK, HEAD_DIM), lambda i, p: (0, i))
    return pl.pallas_call(
        whole_kernel,
        grid_spec=pltpu.PrefetchScalarGridSpec(
            num_scalar_prefetch=1,
            grid=(local_heads,),
            in_specs=[
                column,
                column,
                column,
                pl.BlockSpec((1, NT, CLIP_TOK), lambda i, p: (p[0] * local_heads + i, 0, 0)),
            ],
            out_specs=column,
            scratch_shapes=[pltpu.VMEM((CLIP_TOK, 2 * HEAD_DIM), jnp.bfloat16)],
        ),
        out_shape=jax.ShapeDtypeStruct(query.shape, jnp.bfloat16),
        compiler_params=pltpu.CompilerParams(vmem_limit_bytes=VMEM_LIMIT),
        cost_estimate=attention_cost(local_heads),
    )(place, query, key, value, bias)


def pack_kernel(place_ref, q_ref, k_ref, v_ref, *rest):
    out_ref = rest[-1]
    out_ref[0] = q_ref[...]
    out_ref[1] = k_ref[...]
    out_ref[2] = v_ref[...]


def local_head(call, side, part):
    first, by_side, step = call
    return first + by_side * side + step * part


def pack_partner(place, local_heads, call, query, key, value, earlier, limit):
    rows = query.shape[0]
    count = 2

    def head(i, place_ref):
        side = 1 - place_ref[SEQ]
        return side * local_heads + local_head(call, side, i)

    column = pl.BlockSpec((rows, HEAD_DIM), lambda i, p: (0, head(i, p)))
    return pl.pallas_call(
        pack_kernel,
        grid_spec=pltpu.PrefetchScalarGridSpec(
            num_scalar_prefetch=1,
            grid=(count,),
            in_specs=[column, column, column]
            + [pl.BlockSpec(memory_space=pl.ANY)] * len(earlier),
            out_specs=pl.BlockSpec((3, rows, HEAD_DIM), lambda i, p: (0, 0, i)),
        ),
        out_shape=jax.ShapeDtypeStruct((3, rows, count * HEAD_DIM), jnp.bfloat16),
        compiler_params=pltpu.CompilerParams(vmem_limit_bytes=limit),
        cost_estimate=SMALL_COST,
    )(place, query, key, value, *earlier)


def whole_block(shape):
    return pl.BlockSpec(shape, lambda i, p: (0,) * len(shape), pipeline_mode=pl.Buffered(1))


def gradient_kernel(place_ref, *refs, by_call):
    count = 4 if by_call else 2
    grad_ref = refs[count]
    sent_ref, kept_ref, rows_ref = refs[-3:]
    first_core = place_ref[CORE] == 0
    sides = (place_ref[SEQ], 1 - place_ref[SEQ])

    @pl.when(pl.program_id(0) == 0)
    def _():
        sent, kept = [], []
        for n in range(2):
            if by_call:
                one, two = refs[2 + n][...], refs[n][...]
            else:
                one, two = refs[n][:, :HEAD_DIM], refs[n][:, HEAD_DIM:]
            sent.append(jnp.where(first_core, one, two))
            kept.append(jnp.where(first_core, two, one))
        rows_ref[...] = jnp.concatenate(sent + kept, axis=1).T

    each = 2 if by_call else 1
    product = jnp.dot(rows_ref[...], grad_ref[...], preferred_element_type=jnp.float32)
    product = product.astype(jnp.bfloat16).reshape(4 * each, HEAD_DIM, grad_ref.shape[1])
    for n, side in enumerate(sides):
        sent_ref[pl.ds(each * side, each)] = product[each * n : each * (n + 1)]
        kept_ref[pl.ds(each * side, each)] = product[each * (2 + n) : each * (3 + n)]


def batch_gradient(place, sources, grad_proj, earlier=(), cost=SMALL_COST):
    by_call = len(sources) == 4
    heads = len(sources)
    rows, columns = grad_proj.shape
    step = columns // GRADIENT_STEPS
    out = pl.BlockSpec((heads, HEAD_DIM, step), lambda i, p: (0, 0, i))
    result = jax.ShapeDtypeStruct((heads, HEAD_DIM, columns), jnp.bfloat16)
    return pl.pallas_call(
        functools.partial(gradient_kernel, by_call=by_call),
        grid_spec=pltpu.PrefetchScalarGridSpec(
            num_scalar_prefetch=1,
            grid=(GRADIENT_STEPS,),
            in_specs=[whole_block(each.shape) for each in sources]
            + [pl.BlockSpec((rows, step), lambda i, p: (0, i))]
            + [pl.BlockSpec(memory_space=pl.ANY)] * len(earlier),
            out_specs=[out, out],
            scratch_shapes=[pltpu.VMEM((2 * heads * HEAD_DIM, rows), jnp.bfloat16)],
        ),
        out_shape=[result, result],
        compiler_params=pltpu.CompilerParams(vmem_limit_bytes=VMEM_GRADIENT),
        cost_estimate=cost,
    )(place, *sources, grad_proj, *earlier)


def sum_of(blocks):
    total = blocks[0].astype(jnp.float32)
    for block in blocks[1:]:
        total = total + block.astype(jnp.float32)
    return total


def level_step(place, bit, terms, earlier=(), cost=SMALL_COST):
    count = len(terms)
    pairs = terms[0].shape[0] // 2
    shape = (pairs,) + terms[0].shape[1:]
    block = (1,) + terms[0].shape[1:]
    keep = pl.BlockSpec(block, lambda i, p: (2 * i + p[bit], 0, 0))
    send = pl.BlockSpec(block, lambda i, p: (2 * i + 1 - p[bit], 0, 0))
    out = pl.BlockSpec(block, lambda i, p: (i, 0, 0))

    def kernel(place_ref, *refs):
        kept_ref, sent_ref = refs[-2:]
        kept_ref[...] = sum_of([ref[...] for ref in refs[:count]])
        sent_ref[...] = sum_of([ref[...] for ref in refs[count : 2 * count]]).astype(jnp.bfloat16)

    return pl.pallas_call(
        kernel,
        grid_spec=pltpu.PrefetchScalarGridSpec(
            num_scalar_prefetch=1,
            grid=(pairs,),
            in_specs=[keep] * count
            + [send] * count
            + [pl.BlockSpec(memory_space=pl.ANY)] * len(earlier),
            out_specs=[out, out],
        ),
        out_shape=[
            jax.ShapeDtypeStruct(shape, jnp.float32),
            jax.ShapeDtypeStruct(shape, jnp.bfloat16),
        ],
        compiler_params=pltpu.CompilerParams(vmem_limit_bytes=VMEM_SMALL),
        cost_estimate=cost,
    )(place, *terms, *terms, *earlier)


def reach_step(place, terms, earlier=()):
    count = len(terms)
    block = (1,) + terms[0].shape[1:]
    near = pl.BlockSpec(block, lambda i, p: (p[HIGH], 0, 0))
    far = pl.BlockSpec(block, lambda i, p: (1 - p[HIGH], 0, 0))

    def kernel(place_ref, *refs):
        kept_ref, near_ref, far_ref = refs[-3:]
        total = sum_of([ref[...] for ref in refs[:count]])
        kept_ref[...] = total
        near_ref[...] = total.astype(jnp.bfloat16)
        far_ref[...] = sum_of([ref[...] for ref in refs[count : 2 * count]]).astype(jnp.bfloat16)

    return pl.pallas_call(
        kernel,
        grid_spec=pltpu.PrefetchScalarGridSpec(
            num_scalar_prefetch=1,
            grid=(1,),
            in_specs=[near] * count
            + [far] * count
            + [pl.BlockSpec(memory_space=pl.ANY)] * len(earlier),
            out_specs=[whole_block(block)] * 3,
        ),
        out_shape=[
            jax.ShapeDtypeStruct(block, kind) for kind in (jnp.float32, jnp.bfloat16, jnp.bfloat16)
        ],
        compiler_params=pltpu.CompilerParams(vmem_limit_bytes=VMEM_SMALL),
        cost_estimate=SMALL_COST,
    )(place, *terms, *terms, *earlier)


def total_step(terms, earlier=(), kind=jnp.bfloat16):
    block = pl.BlockSpec((1,) + terms[0].shape[1:], lambda i: (i, 0, 0))

    def kernel(*refs):
        refs[-1][...] = sum_of([ref[...] for ref in refs[: len(terms)]]).astype(kind)

    return pl.pallas_call(
        kernel,
        grid=(terms[0].shape[0],),
        in_specs=[block] * len(terms) + [pl.BlockSpec(memory_space=pl.ANY)] * len(earlier),
        out_specs=block,
        out_shape=jax.ShapeDtypeStruct(terms[0].shape, kind),
        compiler_params=pltpu.CompilerParams(vmem_limit_bytes=VMEM_SMALL),
        cost_estimate=SMALL_COST,
    )(*terms, *earlier)


def choose_owned(place, *batches):
    block = batches[0][0].shape
    terms = [term for batch in batches for term in batch]

    def kernel(place_ref, *refs):
        alike = place_ref[CORE] == place_ref[X]
        outer = place_ref[LOW] == place_ref[HIGH]
        owned = (alike, ~alike & outer, ~alike & ~outer)
        at = 0
        for batch, mine in zip(batches, owned):
            chosen = refs[at : at + len(batch)]
            at += len(batch)

            @pl.when(mine)
            def _():
                refs[-1][...] = sum_of([ref[0] for ref in chosen])

    return pl.pallas_call(
        kernel,
        grid_spec=pltpu.PrefetchScalarGridSpec(
            num_scalar_prefetch=1,
            grid=(1,),
            in_specs=[whole_block(block)] * len(terms),
            out_specs=whole_block(block[1:]),
        ),
        out_shape=jax.ShapeDtypeStruct(block[1:], jnp.float32),
        compiler_params=pltpu.CompilerParams(vmem_limit_bytes=VMEM_GRADIENT),
        cost_estimate=SMALL_COST,
    )(place, *terms)


def join_columns(place, sources, calls, local_heads, earlier, cost):
    rows = sources[0].shape[0]
    step = rows // JOIN_STEPS
    shape = (rows, HEADS * HEAD_DIM)

    def kernel(place_ref, *refs):
        out_ref, done_ref = refs[-2:]
        done_ref[...] = jnp.zeros_like(done_ref)
        for n, source in enumerate(refs[: len(sources)]):
            side = place_ref[SEQ] if n % 2 == 0 else 1 - place_ref[SEQ]
            for part in range(2):
                head = side * local_heads + local_head(calls[n // 2], side, part)
                at = pl.multiple_of(head * HEAD_DIM, HEAD_DIM)
                out_ref[:, pl.ds(at, HEAD_DIM)] = source[:, part * HEAD_DIM : (part + 1) * HEAD_DIM]

    return pl.pallas_call(
        kernel,
        grid_spec=pltpu.PrefetchScalarGridSpec(
            num_scalar_prefetch=1,
            grid=(JOIN_STEPS,),
            in_specs=[pl.BlockSpec((step, each.shape[1]), lambda i, p: (i, 0)) for each in sources]
            + [pl.BlockSpec(memory_space=pl.ANY)] * len(earlier),
            out_specs=[
                pl.BlockSpec((step, shape[1]), lambda i, p: (i, 0)),
                pl.BlockSpec((8, HEAD_DIM), lambda i, p: (0, 0)),
            ],
        ),
        out_shape=[
            jax.ShapeDtypeStruct(shape, jnp.bfloat16),
            jax.ShapeDtypeStruct((8, HEAD_DIM), jnp.float32),
        ],
        compiler_params=pltpu.CompilerParams(vmem_limit_bytes=VMEM_SMALL),
        cost_estimate=cost,
    )(place, *sources, *earlier)


def project(attention, weight, gate, span, filled=(), earlier=(), cost=SMALL_COST):
    rows, depth = attention.shape
    columns = weight.shape[1]
    step = columns // PROJECT_STEPS
    first, steps = span[0], len(span)

    def kernel(attention_ref, weight_ref, gate_ref, *refs):
        out_ref, done_ref = refs[-2:]
        done_ref[...] = jnp.zeros_like(done_ref)
        total = jnp.dot(attention_ref[...], weight_ref[...], preferred_element_type=jnp.float32)
        out_ref[...] = (total * gate_ref[...]).astype(out_ref.dtype)

    return pl.pallas_call(
        kernel,
        grid=(steps,),
        in_specs=[
            pl.BlockSpec((rows, depth), lambda i: (0, 0), pipeline_mode=pl.Buffered(1)),
            pl.BlockSpec((depth, step), lambda i: (0, first + i)),
            pl.BlockSpec((1, step), lambda i: (0, first + i)),
        ]
        + [pl.BlockSpec(memory_space=pl.ANY)] * (len(filled) + len(earlier)),
        out_specs=[
            pl.BlockSpec((rows, step), lambda i: (0, first + i)),
            pl.BlockSpec((8, HEAD_DIM), lambda i: (0, 0)),
        ],
        out_shape=[
            jax.ShapeDtypeStruct((rows, columns), jnp.bfloat16),
            jax.ShapeDtypeStruct((8, HEAD_DIM), jnp.float32),
        ],
        input_output_aliases={3: 0} if filled else {},
        compiler_params=pltpu.CompilerParams(vmem_limit_bytes=VMEM_PROJECT),
        cost_estimate=cost,
    )(attention, weight, gate, *filled, *earlier)


def contract_tokens(columns, grad_proj, kind):
    return lax.dot_general(
        columns, grad_proj, (((0,), (0,)), ((), ())), preferred_element_type=jnp.float32
    ).astype(kind)


def after(value, *earlier):
    return lax.optimization_barrier((value,) + earlier)[0]


def dp_send(value, flip, sender):
    return lax.ppermute(value, "dp", [(i, i ^ flip) for i in range(HEADS) if sender(i)])


def same_bits(i):
    return (i >> 1 ^ i) & 1 == 0


def paired_device(query_rows, key_rows, value_rows, windows, out_weight, gate_scale, out_grad):
    index = lax.axis_index("dp")
    place = jnp.stack([lax.axis_index("seq")] + [index >> bit & 1 for bit in range(4)])
    place = lax.optimization_barrier(place.astype(jnp.int32))
    local_heads = HEADS // 2
    swap = [(0, 1), (1, 0)]
    calls = [(0, 0, 4), (3, 0, 4), (1, 4, 1), (5, -4, 1)]
    bias = window_bias(windows)
    weight = lax.all_gather(out_weight, "dp", axis=0, tiled=True)
    gate_row = gate_scale[0].astype(jnp.float32)
    grad_proj = (out_grad.astype(jnp.float32) * gate_row).astype(jnp.bfloat16)
    sources = (query_rows, key_rows, value_rows)

    def pack(n, limit, *earlier):
        return pack_partner(place, local_heads, calls[n], *sources, earlier, limit)

    def attention(n, other, *earlier, limit=VMEM_LIMIT):
        return attend_pair(place, local_heads, calls[n], *sources, other, bias, earlier, limit)

    def exchange(mine):
        return lax.ppermute(mine, "seq", swap)

    def core_step(*operands):
        sent, kept = batch_gradient(place, operands[:4], operands[4])
        return total_step([kept, dp_send(sent, 1, lambda i: True)])

    def apart(step, *operands):
        shapes = jax.eval_shape(step, *operands)
        return lax.cond(
            windows[0, 0] > 0,
            step,
            lambda *_: jax.tree.map(lambda leaf: jnp.zeros(leaf.shape, leaf.dtype), shapes),
            *operands,
        )

    packed0 = pack(0, VMEM_WHOLE)
    packed1 = pack(1, VMEM_WHOLE, packed0)
    packed2 = pack(2, VMEM_LIMIT, packed1)
    other0 = exchange(packed0)
    other1 = exchange(packed1)
    other2 = exchange(packed2)
    mine0 = attention(0, other0, packed2)
    theirs0 = exchange(mine0)
    mine1 = attention(1, other1, mine0)
    theirs1 = exchange(mine1)
    packed3 = pack(3, VMEM_LIMIT, mine1)
    other3 = exchange(packed3)
    mine2 = attention(2, other2, mine1, packed3)
    theirs2 = exchange(mine2)

    def unlike(i):
        return not same_bits(i)

    def outer(i):
        return unlike(i) and (i >> 2 ^ i >> 3) & 1 == 0

    def inner(i):
        return unlike(i) and (i >> 2 ^ i >> 3) & 1 == 1

    first = (mine0, theirs0, mine1, theirs1)
    total_a = apart(core_step, after(mine0, mine2, weight), *first[1:], grad_proj)
    across_a = dp_send(total_a, 2, unlike)
    mine3 = attention(3, other3, total_a, limit=VMEM_WHOLE)
    theirs3 = exchange(mine3)
    sent_b, kept_b = batch_gradient(place, (mine2, theirs2), grad_proj, (mine3,), LONG_COST)
    came_b = dp_send(sent_b, 1, lambda i: True)
    kept_a, sent_a = level_step(place, LOW, [total_a, across_a], (sent_b,), LONG_COST)
    low_a = dp_send(sent_a, 4, same_bits)
    total_b = total_step([kept_b, came_b], (sent_a,))
    across_b = dp_send(total_b, 2, same_bits)
    sent_c, kept_c = batch_gradient(place, (mine3, theirs3), grad_proj, (total_b,))
    came_c = dp_send(sent_c, 1, lambda i: True)
    results = (*first, mine2, theirs2, mine3, theirs3)
    columns, done = join_columns(place, results, calls, local_heads, (sent_c,), LONG_COST)
    total_c = total_step([kept_c, came_c], (done,))
    across_c = dp_send(total_c, 2, same_bits)
    kept_a, sent_a = level_step(place, HIGH, [kept_a, low_a], (total_c,))
    high_a = dp_send(sent_a, 8, same_bits)
    sent_b = total_step([total_b, across_b], (sent_a,))
    low_b = dp_send(sent_b, 4, inner)
    kept_c, near_c, far_c = reach_step(place, [total_c, across_c], (sent_b,))
    reached_c = dp_send(far_c, 8, outer), dp_send(far_c, 12, inner), dp_send(near_c, 4, outer)
    out, done = project(columns, weight, gate_row[None], range(3), (), (near_c,))
    kept_b, sent_b = level_step(place, HIGH, [total_b, across_b, low_b], (done,))
    high_b = dp_send(sent_b, 12, outer)
    block_out, done = project(
        columns, weight, gate_row[None], range(3, PROJECT_STEPS), (out,), (sent_b,), LONG_COST
    )
    final_a = total_step([kept_a, high_a], (done,), jnp.float32)
    weight_grad = choose_owned(place, (final_a,), (kept_b, high_b), (kept_c, *reached_c))
    return (block_out, weight_grad)


def general_device(query_rows, key_rows, value_rows, windows, out_weight, gate_scale, out_grad):
    query, key, value = (
        lax.all_to_all(rows, "seq", split_axis=1, concat_axis=0, tiled=True)
        for rows in (query_rows, key_rows, value_rows)
    )
    place = lax.axis_index("seq").reshape(1).astype(jnp.int32)
    mine = attend_whole(place, query, key, value, window_bias(windows))
    columns = lax.all_gather(mine, "seq", axis=1, tiled=True)
    weight = lax.all_gather(out_weight, "dp", axis=0, tiled=True)
    gate_row = gate_scale[0].astype(jnp.float32)
    projected = jnp.dot(columns, weight, preferred_element_type=jnp.float32)
    block_out = (projected * gate_row).astype(jnp.bfloat16)
    grad_proj = (out_grad.astype(jnp.float32) * gate_row).astype(jnp.bfloat16)
    weight_grad = lax.psum_scatter(
        contract_tokens(columns, grad_proj, jnp.float32), "dp", scatter_dimension=0, tiled=True
    )
    return (block_out, weight_grad)


def solution(mesh):
    paired = mesh.shape["seq"] == 2 and mesh.shape["dp"] == HEADS
    return jax.shard_map(
        paired_device if paired else general_device,
        mesh=mesh,
        in_specs=(
            P(("dp", "seq"), None),
            P(("dp", "seq"), None),
            P(("dp", "seq"), None),
            P(),
            P("dp", "seq"),
            P("dp", "seq"),
            P("dp", "seq"),
        ),
        out_specs=(P("dp", "seq"), P("dp", "seq")),
        check_vma=False,
    )
```

```python
import functools
import math

import jax
import jax.numpy as jnp
import numpy as np
from jax import lax
from jax.experimental import pallas as pl
from jax.experimental.pallas import tpu as pltpu
from jax.sharding import PartitionSpec as P

HEADS = 16
HEAD_DIM = 128
GH = 3
GW = 4
GT = 2
TILE = 48
NT = 24
CLIP_TOK = NT * TILE
Q_ROWS = GW * TILE
LOG2_SCALE = math.log2(math.e) / math.sqrt(HEAD_DIM)
VMEM_LIMIT = 16 * 1024 * 1024
VMEM_GRADIENT = 20 * 1024 * 1024
VMEM_PROJECT = 24 * 1024 * 1024
PROJECT_STEPS = 6
GRADIENT_STEPS = 3
JOIN_STEPS = 4
SEQ, CORE, X, LOW, HIGH = range(5)
VMEM_WHOLE = 60 * 1024 * 1024
VMEM_SMALL = 12 * 1024 * 1024
SMALL_COST = pl.CostEstimate(flops=1, bytes_accessed=1, transcendentals=0)
LONG_COST = pl.CostEstimate(flops=2 * 10**10, bytes_accessed=2 * 10**7, transcendentals=0)


def window_bias(windows):
    tile_id = np.arange(NT)
    coords = np.stack([tile_id // (GH * GW), tile_id // GW % GH, tile_id % GW]).astype(np.int32)
    token_coords = np.repeat(coords, TILE, axis=1)
    inside = None
    for axis_no, limit in enumerate((GT, GH, GW)):
        extent = jnp.minimum(windows[:, axis_no], limit)[:, None]
        start = jnp.clip(coords[axis_no][None, :] - (extent - 1) // 2, 0, limit - extent)
        column = token_coords[axis_no][None, None, :]
        here = (column >= start[:, :, None]) & (column < (start + extent)[:, :, None])
        inside = here if inside is None else inside & here
    return jnp.where(inside, 0.0, -jnp.inf).astype(jnp.float32)


def attend_rows(queries, first_tile, bias_ref, keys, values):
    count = queries.shape[0]
    tiles = count // TILE
    scores = lax.dot_general(
        queries, keys, (((1,), (1,)), ((), ())), preferred_element_type=jnp.float32
    )
    bias = bias_ref[0, first_tile : first_tile + tiles, :]
    scores = (scores.reshape(tiles, TILE, CLIP_TOK) + bias[:, None, :]).reshape(count, CLIP_TOK)
    peak = jnp.max(scores, axis=-1, keepdims=True)
    weights = jnp.exp2((scores - peak) * LOG2_SCALE).astype(jnp.bfloat16)
    blended = jnp.dot(weights, values, preferred_element_type=jnp.float32)
    return (blended[:, :HEAD_DIM] / blended[:, HEAD_DIM:]).astype(jnp.bfloat16)


def fill_values(values_ref, parts):
    at = 0
    for part in parts:
        rows = part.shape[0]
        values_ref[at : at + rows, :HEAD_DIM] = part
        at += rows
    values_ref[:, HEAD_DIM:] = jnp.ones((CLIP_TOK, HEAD_DIM), jnp.bfloat16)


def pair_kernel(place_ref, q_ref, k_ref, v_ref, other_ref, bias_ref, *rest):
    out_ref, keys_ref, values_ref = rest[-3:]
    half = CLIP_TOK // 2
    keys_ref[:half, :] = k_ref[...]
    keys_ref[half:, :] = other_ref[1]
    fill_values(values_ref, (v_ref[...], other_ref[2]))
    keys = keys_ref[...]
    values = values_ref[...]
    for side in range(2):
        base = pl.multiple_of((place_ref[0] if side == 0 else 1 - place_ref[0]) * half, half)
        for at in range(0, half, Q_ROWS):
            queries = q_ref[at : at + Q_ROWS, :] if side == 0 else other_ref[0, at : at + Q_ROWS, :]
            first_tile = (side * half + at) // TILE
            out_ref[pl.ds(base + at, Q_ROWS), :] = attend_rows(
                queries, first_tile, bias_ref, keys, values
            )


def whole_kernel(place_ref, q_ref, k_ref, v_ref, bias_ref, out_ref, values_ref):
    fill_values(values_ref, (v_ref[...],))
    keys = k_ref[...]
    values = values_ref[...]
    for at in range(0, CLIP_TOK, Q_ROWS):
        out_ref[at : at + Q_ROWS, :] = attend_rows(
            q_ref[at : at + Q_ROWS, :], at // TILE, bias_ref, keys, values
        )


def attention_cost(heads):
    pairs = heads * CLIP_TOK * CLIP_TOK
    return pl.CostEstimate(
        flops=pairs * HEAD_DIM * 6,
        bytes_accessed=heads * CLIP_TOK * HEAD_DIM * 8,
        transcendentals=pairs,
    )


def attend_pair(place, local_heads, call, query, key, value, other, bias, earlier, limit):
    half = CLIP_TOK // 2
    count = 2

    def head(i, place_ref):
        return place_ref[SEQ] * local_heads + local_head(call, place_ref[SEQ], i)

    own = pl.BlockSpec((half, HEAD_DIM), lambda i, p: (0, head(i, p)))
    return pl.pallas_call(
        pair_kernel,
        grid_spec=pltpu.PrefetchScalarGridSpec(
            num_scalar_prefetch=1,
            grid=(count,),
            in_specs=[
                own,
                own,
                own,
                pl.BlockSpec((3, half, HEAD_DIM), lambda i, p: (0, 0, i)),
                pl.BlockSpec((1, NT, CLIP_TOK), lambda i, p: (head(i, p), 0, 0)),
            ]
            + [pl.BlockSpec(memory_space=pl.ANY)] * len(earlier),
            out_specs=pl.BlockSpec((CLIP_TOK, HEAD_DIM), lambda i, p: (0, i)),
            scratch_shapes=[
                pltpu.VMEM((CLIP_TOK, HEAD_DIM), jnp.bfloat16),
                pltpu.VMEM((CLIP_TOK, 2 * HEAD_DIM), jnp.bfloat16),
            ],
        ),
        out_shape=jax.ShapeDtypeStruct((CLIP_TOK, count * HEAD_DIM), jnp.bfloat16),
        compiler_params=pltpu.CompilerParams(vmem_limit_bytes=limit),
        cost_estimate=SMALL_COST,
    )(place, query, key, value, other, bias, *earlier)


def attend_whole(place, query, key, value, bias):
    local_heads = query.shape[1] // HEAD_DIM
    column = pl.BlockSpec((CLIP_TOK, HEAD_DIM), lambda i, p: (0, i))
    return pl.pallas_call(
        whole_kernel,
        grid_spec=pltpu.PrefetchScalarGridSpec(
            num_scalar_prefetch=1,
            grid=(local_heads,),
            in_specs=[
                column,
                column,
                column,
                pl.BlockSpec((1, NT, CLIP_TOK), lambda i, p: (p[0] * local_heads + i, 0, 0)),
            ],
            out_specs=column,
            scratch_shapes=[pltpu.VMEM((CLIP_TOK, 2 * HEAD_DIM), jnp.bfloat16)],
        ),
        out_shape=jax.ShapeDtypeStruct(query.shape, jnp.bfloat16),
        compiler_params=pltpu.CompilerParams(vmem_limit_bytes=VMEM_LIMIT),
        cost_estimate=attention_cost(local_heads),
    )(place, query, key, value, bias)


def pack_kernel(place_ref, q_ref, k_ref, v_ref, *rest):
    out_ref = rest[-1]
    out_ref[0] = q_ref[...]
    out_ref[1] = k_ref[...]
    out_ref[2] = v_ref[...]


def local_head(call, side, part):
    first, by_side, step = call
    return first + by_side * side + step * part


def pack_partner(place, local_heads, call, query, key, value, earlier, limit):
    rows = query.shape[0]
    count = 2

    def head(i, place_ref):
        side = 1 - place_ref[SEQ]
        return side * local_heads + local_head(call, side, i)

    column = pl.BlockSpec((rows, HEAD_DIM), lambda i, p: (0, head(i, p)))
    return pl.pallas_call(
        pack_kernel,
        grid_spec=pltpu.PrefetchScalarGridSpec(
            num_scalar_prefetch=1,
            grid=(count,),
            in_specs=[column, column, column]
            + [pl.BlockSpec(memory_space=pl.ANY)] * len(earlier),
            out_specs=pl.BlockSpec((3, rows, HEAD_DIM), lambda i, p: (0, 0, i)),
        ),
        out_shape=jax.ShapeDtypeStruct((3, rows, count * HEAD_DIM), jnp.bfloat16),
        compiler_params=pltpu.CompilerParams(vmem_limit_bytes=limit),
        cost_estimate=SMALL_COST,
    )(place, query, key, value, *earlier)


def whole_block(shape):
    return pl.BlockSpec(shape, lambda i, p: (0,) * len(shape), pipeline_mode=pl.Buffered(1))


def gradient_kernel(place_ref, *refs, by_call):
    count = 4 if by_call else 2
    grad_ref = refs[count]
    sent_ref, kept_ref, rows_ref = refs[-3:]
    first_core = place_ref[CORE] == 0
    sides = (place_ref[SEQ], 1 - place_ref[SEQ])

    @pl.when(pl.program_id(0) == 0)
    def _():
        sent, kept = [], []
        for n in range(2):
            if by_call:
                one, two = refs[2 + n][...], refs[n][...]
            else:
                one, two = refs[n][:, :HEAD_DIM], refs[n][:, HEAD_DIM:]
            sent.append(jnp.where(first_core, one, two))
            kept.append(jnp.where(first_core, two, one))
        rows_ref[...] = jnp.concatenate(sent + kept, axis=1).T

    each = 2 if by_call else 1
    product = jnp.dot(rows_ref[...], grad_ref[...], preferred_element_type=jnp.float32)
    product = product.astype(jnp.bfloat16).reshape(4 * each, HEAD_DIM, grad_ref.shape[1])
    for n, side in enumerate(sides):
        sent_ref[pl.ds(each * side, each)] = product[each * n : each * (n + 1)]
        kept_ref[pl.ds(each * side, each)] = product[each * (2 + n) : each * (3 + n)]


def batch_gradient(place, sources, grad_proj, earlier=(), cost=SMALL_COST):
    by_call = len(sources) == 4
    heads = len(sources)
    rows, columns = grad_proj.shape
    step = columns // GRADIENT_STEPS
    out = pl.BlockSpec((heads, HEAD_DIM, step), lambda i, p: (0, 0, i))
    result = jax.ShapeDtypeStruct((heads, HEAD_DIM, columns), jnp.bfloat16)
    return pl.pallas_call(
        functools.partial(gradient_kernel, by_call=by_call),
        grid_spec=pltpu.PrefetchScalarGridSpec(
            num_scalar_prefetch=1,
            grid=(GRADIENT_STEPS,),
            in_specs=[whole_block(each.shape) for each in sources]
            + [pl.BlockSpec((rows, step), lambda i, p: (0, i))]
            + [pl.BlockSpec(memory_space=pl.ANY)] * len(earlier),
            out_specs=[out, out],
            scratch_shapes=[pltpu.VMEM((2 * heads * HEAD_DIM, rows), jnp.bfloat16)],
        ),
        out_shape=[result, result],
        compiler_params=pltpu.CompilerParams(vmem_limit_bytes=VMEM_GRADIENT),
        cost_estimate=cost,
    )(place, *sources, grad_proj, *earlier)


def sum_of(blocks):
    total = blocks[0].astype(jnp.float32)
    for block in blocks[1:]:
        total = total + block.astype(jnp.float32)
    return total


def level_step(place, bit, terms, earlier=(), cost=SMALL_COST):
    count = len(terms)
    pairs = terms[0].shape[0] // 2
    shape = (pairs,) + terms[0].shape[1:]
    block = (1,) + terms[0].shape[1:]
    keep = pl.BlockSpec(block, lambda i, p: (2 * i + p[bit], 0, 0))
    send = pl.BlockSpec(block, lambda i, p: (2 * i + 1 - p[bit], 0, 0))
    out = pl.BlockSpec(block, lambda i, p: (i, 0, 0))

    def kernel(place_ref, *refs):
        kept_ref, sent_ref = refs[-2:]
        kept_ref[...] = sum_of([ref[...] for ref in refs[:count]])
        sent_ref[...] = sum_of([ref[...] for ref in refs[count : 2 * count]]).astype(jnp.bfloat16)

    return pl.pallas_call(
        kernel,
        grid_spec=pltpu.PrefetchScalarGridSpec(
            num_scalar_prefetch=1,
            grid=(pairs,),
            in_specs=[keep] * count
            + [send] * count
            + [pl.BlockSpec(memory_space=pl.ANY)] * len(earlier),
            out_specs=[out, out],
        ),
        out_shape=[
            jax.ShapeDtypeStruct(shape, jnp.float32),
            jax.ShapeDtypeStruct(shape, jnp.bfloat16),
        ],
        compiler_params=pltpu.CompilerParams(vmem_limit_bytes=VMEM_SMALL),
        cost_estimate=cost,
    )(place, *terms, *terms, *earlier)


def reach_step(place, terms, earlier=()):
    count = len(terms)
    block = (1,) + terms[0].shape[1:]
    near = pl.BlockSpec(block, lambda i, p: (p[HIGH], 0, 0))
    far = pl.BlockSpec(block, lambda i, p: (1 - p[HIGH], 0, 0))

    def kernel(place_ref, *refs):
        kept_ref, near_ref, far_ref = refs[-3:]
        total = sum_of([ref[...] for ref in refs[:count]])
        kept_ref[...] = total
        near_ref[...] = total.astype(jnp.bfloat16)
        far_ref[...] = sum_of([ref[...] for ref in refs[count : 2 * count]]).astype(jnp.bfloat16)

    return pl.pallas_call(
        kernel,
        grid_spec=pltpu.PrefetchScalarGridSpec(
            num_scalar_prefetch=1,
            grid=(1,),
            in_specs=[near] * count
            + [far] * count
            + [pl.BlockSpec(memory_space=pl.ANY)] * len(earlier),
            out_specs=[whole_block(block)] * 3,
        ),
        out_shape=[
            jax.ShapeDtypeStruct(block, kind) for kind in (jnp.float32, jnp.bfloat16, jnp.bfloat16)
        ],
        compiler_params=pltpu.CompilerParams(vmem_limit_bytes=VMEM_SMALL),
        cost_estimate=SMALL_COST,
    )(place, *terms, *terms, *earlier)


def total_step(terms, earlier=(), kind=jnp.bfloat16):
    block = pl.BlockSpec((1,) + terms[0].shape[1:], lambda i: (i, 0, 0))

    def kernel(*refs):
        refs[-1][...] = sum_of([ref[...] for ref in refs[: len(terms)]]).astype(kind)

    return pl.pallas_call(
        kernel,
        grid=(terms[0].shape[0],),
        in_specs=[block] * len(terms) + [pl.BlockSpec(memory_space=pl.ANY)] * len(earlier),
        out_specs=block,
        out_shape=jax.ShapeDtypeStruct(terms[0].shape, kind),
        compiler_params=pltpu.CompilerParams(vmem_limit_bytes=VMEM_SMALL),
        cost_estimate=SMALL_COST,
    )(*terms, *earlier)


def choose_owned(place, *batches):
    block = batches[0][0].shape
    terms = [term for batch in batches for term in batch]

    def kernel(place_ref, *refs):
        alike = place_ref[CORE] == place_ref[X]
        outer = place_ref[LOW] == place_ref[HIGH]
        owned = (alike, ~alike & outer, ~alike & ~outer)
        at = 0
        for batch, mine in zip(batches, owned):
            chosen = refs[at : at + len(batch)]
            at += len(batch)

            @pl.when(mine)
            def _():
                refs[-1][...] = sum_of([ref[0] for ref in chosen])

    return pl.pallas_call(
        kernel,
        grid_spec=pltpu.PrefetchScalarGridSpec(
            num_scalar_prefetch=1,
            grid=(1,),
            in_specs=[whole_block(block)] * len(terms),
            out_specs=whole_block(block[1:]),
        ),
        out_shape=jax.ShapeDtypeStruct(block[1:], jnp.float32),
        compiler_params=pltpu.CompilerParams(vmem_limit_bytes=VMEM_GRADIENT),
        cost_estimate=SMALL_COST,
    )(place, *terms)


def join_columns(place, sources, calls, local_heads, earlier, cost):
    rows = sources[0].shape[0]
    step = rows // JOIN_STEPS
    shape = (rows, HEADS * HEAD_DIM)

    def kernel(place_ref, *refs):
        out_ref, done_ref = refs[-2:]
        done_ref[...] = jnp.zeros_like(done_ref)
        for n, source in enumerate(refs[: len(sources)]):
            side = place_ref[SEQ] if n % 2 == 0 else 1 - place_ref[SEQ]
            for part in range(2):
                head = side * local_heads + local_head(calls[n // 2], side, part)
                at = pl.multiple_of(head * HEAD_DIM, HEAD_DIM)
                out_ref[:, pl.ds(at, HEAD_DIM)] = source[:, part * HEAD_DIM : (part + 1) * HEAD_DIM]

    return pl.pallas_call(
        kernel,
        grid_spec=pltpu.PrefetchScalarGridSpec(
            num_scalar_prefetch=1,
            grid=(JOIN_STEPS,),
            in_specs=[pl.BlockSpec((step, each.shape[1]), lambda i, p: (i, 0)) for each in sources]
            + [pl.BlockSpec(memory_space=pl.ANY)] * len(earlier),
            out_specs=[
                pl.BlockSpec((step, shape[1]), lambda i, p: (i, 0)),
                pl.BlockSpec((8, HEAD_DIM), lambda i, p: (0, 0)),
            ],
        ),
        out_shape=[
            jax.ShapeDtypeStruct(shape, jnp.bfloat16),
            jax.ShapeDtypeStruct((8, HEAD_DIM), jnp.float32),
        ],
        compiler_params=pltpu.CompilerParams(vmem_limit_bytes=VMEM_SMALL),
        cost_estimate=cost,
    )(place, *sources, *earlier)


def project(attention, weight, gate, span, filled=(), earlier=(), cost=SMALL_COST):
    rows, depth = attention.shape
    columns = weight.shape[1]
    step = columns // PROJECT_STEPS
    first, steps = span[0], len(span)

    def kernel(attention_ref, weight_ref, gate_ref, *refs):
        out_ref, done_ref = refs[-2:]
        done_ref[...] = jnp.zeros_like(done_ref)
        total = jnp.dot(attention_ref[...], weight_ref[...], preferred_element_type=jnp.float32)
        out_ref[...] = (total * gate_ref[...]).astype(out_ref.dtype)

    return pl.pallas_call(
        kernel,
        grid=(steps,),
        in_specs=[
            pl.BlockSpec((rows, depth), lambda i: (0, 0), pipeline_mode=pl.Buffered(1)),
            pl.BlockSpec((depth, step), lambda i: (0, first + i)),
            pl.BlockSpec((1, step), lambda i: (0, first + i)),
        ]
        + [pl.BlockSpec(memory_space=pl.ANY)] * (len(filled) + len(earlier)),
        out_specs=[
            pl.BlockSpec((rows, step), lambda i: (0, first + i)),
            pl.BlockSpec((8, HEAD_DIM), lambda i: (0, 0)),
        ],
        out_shape=[
            jax.ShapeDtypeStruct((rows, columns), jnp.bfloat16),
            jax.ShapeDtypeStruct((8, HEAD_DIM), jnp.float32),
        ],
        input_output_aliases={3: 0} if filled else {},
        compiler_params=pltpu.CompilerParams(vmem_limit_bytes=VMEM_PROJECT),
        cost_estimate=cost,
    )(attention, weight, gate, *filled, *earlier)


def contract_tokens(columns, grad_proj, kind):
    return lax.dot_general(
        columns, grad_proj, (((0,), (0,)), ((), ())), preferred_element_type=jnp.float32
    ).astype(kind)


def after(value, *earlier):
    return lax.optimization_barrier((value,) + earlier)[0]


def dp_send(value, flip, sender):
    return lax.ppermute(value, "dp", [(i, i ^ flip) for i in range(HEADS) if sender(i)])


def same_bits(i):
    return (i >> 1 ^ i) & 1 == 0


def paired_device(query_rows, key_rows, value_rows, windows, out_weight, gate_scale, out_grad):
    index = lax.axis_index("dp")
    place = jnp.stack([lax.axis_index("seq")] + [index >> bit & 1 for bit in range(4)])
    place = lax.optimization_barrier(place.astype(jnp.int32))
    local_heads = HEADS // 2
    swap = [(0, 1), (1, 0)]
    calls = [(0, 0, 4), (3, 0, 4), (1, 4, 1), (5, -4, 1)]
    bias = window_bias(windows)
    weight = lax.all_gather(out_weight, "dp", axis=0, tiled=True)
    gate_row = gate_scale[0].astype(jnp.float32)
    grad_proj = (out_grad.astype(jnp.float32) * gate_row).astype(jnp.bfloat16)
    sources = (query_rows, key_rows, value_rows)

    def pack(n, limit, *earlier):
        return pack_partner(place, local_heads, calls[n], *sources, earlier, limit)

    def attention(n, other, *earlier, limit=VMEM_LIMIT):
        return attend_pair(place, local_heads, calls[n], *sources, other, bias, earlier, limit)

    def exchange(mine):
        return lax.ppermute(mine, "seq", swap)

    def core_step(*operands):
        sent, kept = batch_gradient(place, operands[:4], operands[4])
        return total_step([kept, dp_send(sent, 1, lambda i: True)])

    def apart(step, *operands):
        shapes = jax.eval_shape(step, *operands)
        return lax.cond(
            windows[0, 0] > 0,
            step,
            lambda *_: jax.tree.map(lambda leaf: jnp.zeros(leaf.shape, leaf.dtype), shapes),
            *operands,
        )

    packed0 = pack(0, VMEM_WHOLE)
    packed1 = pack(1, VMEM_WHOLE, packed0)
    packed2 = pack(2, VMEM_LIMIT, packed1)
    other0 = exchange(packed0)
    other1 = exchange(packed1)
    other2 = exchange(packed2)
    mine0 = attention(0, other0, packed2)
    theirs0 = exchange(mine0)
    mine1 = attention(1, other1, mine0)
    theirs1 = exchange(mine1)
    packed3 = pack(3, VMEM_LIMIT, mine1)
    other3 = exchange(packed3)
    mine2 = attention(2, other2, mine1, packed3)
    theirs2 = exchange(mine2)

    def unlike(i):
        return not same_bits(i)

    def outer(i):
        return unlike(i) and (i >> 2 ^ i >> 3) & 1 == 0

    def inner(i):
        return unlike(i) and (i >> 2 ^ i >> 3) & 1 == 1

    first = (mine0, theirs0, mine1, theirs1)
    total_a = apart(core_step, after(mine0, mine2, weight), *first[1:], grad_proj)
    across_a = dp_send(total_a, 2, unlike)
    mine3 = attention(3, other3, total_a, limit=VMEM_WHOLE)
    theirs3 = exchange(mine3)
    sent_b, kept_b = batch_gradient(place, (mine2, theirs2), grad_proj, (mine3,), LONG_COST)
    came_b = dp_send(sent_b, 1, lambda i: True)
    kept_a, sent_a = level_step(place, LOW, [total_a, across_a], (sent_b,), LONG_COST)
    low_a = dp_send(sent_a, 4, same_bits)
    total_b = total_step([kept_b, came_b], (sent_a,))
    across_b = dp_send(total_b, 2, same_bits)
    sent_c, kept_c = batch_gradient(place, (mine3, theirs3), grad_proj, (total_b,))
    came_c = dp_send(sent_c, 1, lambda i: True)
    results = (*first, mine2, theirs2, mine3, theirs3)
    columns, done = join_columns(place, results, calls, local_heads, (sent_c,), LONG_COST)
    total_c = total_step([kept_c, came_c], (done,))
    across_c = dp_send(total_c, 2, same_bits)
    kept_a, sent_a = level_step(place, HIGH, [kept_a, low_a], (total_c,))
    high_a = dp_send(sent_a, 8, same_bits)
    sent_b = total_step([total_b, across_b], (sent_a,))
    low_b = dp_send(sent_b, 4, inner)
    gate = gate_row[None]
    out, done = project(columns, weight, gate, range(3), (), (sent_b,))
    kept_c, near_c, far_c = reach_step(place, [total_c, across_c], (done,))
    reached_c = dp_send(far_c, 8, outer), dp_send(far_c, 12, inner), dp_send(near_c, 4, outer)
    kept_b, sent_b = level_step(place, HIGH, [total_b, across_b, low_b], (near_c,))
    high_b = dp_send(sent_b, 12, outer)
    block_out, done = project(columns, weight, gate, range(3, PROJECT_STEPS), (out,), (sent_b,))
    final_a = total_step([kept_a, high_a], (done,), jnp.float32)
    weight_grad = choose_owned(place, (final_a,), (kept_b, high_b), (kept_c, *reached_c))
    return (block_out, weight_grad)


def general_device(query_rows, key_rows, value_rows, windows, out_weight, gate_scale, out_grad):
    query, key, value = (
        lax.all_to_all(rows, "seq", split_axis=1, concat_axis=0, tiled=True)
        for rows in (query_rows, key_rows, value_rows)
    )
    place = lax.axis_index("seq").reshape(1).astype(jnp.int32)
    mine = attend_whole(place, query, key, value, window_bias(windows))
    columns = lax.all_gather(mine, "seq", axis=1, tiled=True)
    weight = lax.all_gather(out_weight, "dp", axis=0, tiled=True)
    gate_row = gate_scale[0].astype(jnp.float32)
    projected = jnp.dot(columns, weight, preferred_element_type=jnp.float32)
    block_out = (projected * gate_row).astype(jnp.bfloat16)
    grad_proj = (out_grad.astype(jnp.float32) * gate_row).astype(jnp.bfloat16)
    weight_grad = lax.psum_scatter(
        contract_tokens(columns, grad_proj, jnp.float32), "dp", scatter_dimension=0, tiled=True
    )
    return (block_out, weight_grad)


def solution(mesh):
    paired = mesh.shape["seq"] == 2 and mesh.shape["dp"] == HEADS
    return jax.shard_map(
        paired_device if paired else general_device,
        mesh=mesh,
        in_specs=(
            P(("dp", "seq"), None),
            P(("dp", "seq"), None),
            P(("dp", "seq"), None),
            P(),
            P("dp", "seq"),
            P("dp", "seq"),
            P("dp", "seq"),
        ),
        out_specs=(P("dp", "seq"), P("dp", "seq")),
        check_vma=False,
    )
```

```python
import functools
import math

import jax
import jax.numpy as jnp
import numpy as np
from jax import lax
from jax.experimental import pallas as pl
from jax.experimental.pallas import tpu as pltpu
from jax.sharding import PartitionSpec as P

HEADS = 16
HEAD_DIM = 128
GH = 3
GW = 4
GT = 2
TILE = 48
NT = 24
CLIP_TOK = NT * TILE
Q_ROWS = GW * TILE
LOG2_SCALE = math.log2(math.e) / math.sqrt(HEAD_DIM)
VMEM_LIMIT = 16 * 1024 * 1024
VMEM_GRADIENT = 20 * 1024 * 1024
VMEM_PROJECT = 24 * 1024 * 1024
PROJECT_STEPS = 6
GRADIENT_STEPS = 3
JOIN_STEPS = 4
SEQ, CORE, X, LOW, HIGH = range(5)
VMEM_WHOLE = 60 * 1024 * 1024
VMEM_SMALL = 12 * 1024 * 1024
SMALL_COST = pl.CostEstimate(flops=1, bytes_accessed=1, transcendentals=0)
LONG_COST = pl.CostEstimate(flops=2 * 10**10, bytes_accessed=2 * 10**7, transcendentals=0)


def window_bias(windows):
    tile_id = np.arange(NT)
    coords = np.stack([tile_id // (GH * GW), tile_id // GW % GH, tile_id % GW]).astype(np.int32)
    token_coords = np.repeat(coords, TILE, axis=1)
    inside = None
    for axis_no, limit in enumerate((GT, GH, GW)):
        extent = jnp.minimum(windows[:, axis_no], limit)[:, None]
        start = jnp.clip(coords[axis_no][None, :] - (extent - 1) // 2, 0, limit - extent)
        column = token_coords[axis_no][None, None, :]
        here = (column >= start[:, :, None]) & (column < (start + extent)[:, :, None])
        inside = here if inside is None else inside & here
    return jnp.where(inside, 0.0, -jnp.inf).astype(jnp.float32)


def attend_rows(queries, first_tile, bias_ref, keys, values):
    count = queries.shape[0]
    tiles = count // TILE
    scores = lax.dot_general(
        queries, keys, (((1,), (1,)), ((), ())), preferred_element_type=jnp.float32
    )
    bias = bias_ref[0, first_tile : first_tile + tiles, :]
    scores = (scores.reshape(tiles, TILE, CLIP_TOK) + bias[:, None, :]).reshape(count, CLIP_TOK)
    peak = jnp.max(scores, axis=-1, keepdims=True)
    weights = jnp.exp2((scores - peak) * LOG2_SCALE).astype(jnp.bfloat16)
    blended = jnp.dot(weights, values, preferred_element_type=jnp.float32)
    return (blended[:, :HEAD_DIM] / blended[:, HEAD_DIM:]).astype(jnp.bfloat16)


def fill_values(values_ref, parts):
    at = 0
    for part in parts:
        rows = part.shape[0]
        values_ref[at : at + rows, :HEAD_DIM] = part
        at += rows
    values_ref[:, HEAD_DIM:] = jnp.ones((CLIP_TOK, HEAD_DIM), jnp.bfloat16)


def pair_kernel(place_ref, q_ref, k_ref, v_ref, other_ref, bias_ref, *rest):
    out_ref, keys_ref, values_ref = rest[-3:]
    half = CLIP_TOK // 2
    keys_ref[:half, :] = k_ref[...]
    keys_ref[half:, :] = other_ref[1]
    fill_values(values_ref, (v_ref[...], other_ref[2]))
    keys = keys_ref[...]
    values = values_ref[...]
    for side in range(2):
        base = pl.multiple_of((place_ref[0] if side == 0 else 1 - place_ref[0]) * half, half)
        for at in range(0, half, Q_ROWS):
            queries = q_ref[at : at + Q_ROWS, :] if side == 0 else other_ref[0, at : at + Q_ROWS, :]
            first_tile = (side * half + at) // TILE
            out_ref[pl.ds(base + at, Q_ROWS), :] = attend_rows(
                queries, first_tile, bias_ref, keys, values
            )


def whole_kernel(place_ref, q_ref, k_ref, v_ref, bias_ref, out_ref, values_ref):
    fill_values(values_ref, (v_ref[...],))
    keys = k_ref[...]
    values = values_ref[...]
    for at in range(0, CLIP_TOK, Q_ROWS):
        out_ref[at : at + Q_ROWS, :] = attend_rows(
            q_ref[at : at + Q_ROWS, :], at // TILE, bias_ref, keys, values
        )


def attention_cost(heads):
    pairs = heads * CLIP_TOK * CLIP_TOK
    return pl.CostEstimate(
        flops=pairs * HEAD_DIM * 6,
        bytes_accessed=heads * CLIP_TOK * HEAD_DIM * 8,
        transcendentals=pairs,
    )


def attend_pair(place, local_heads, call, query, key, value, other, bias, earlier, limit):
    half = CLIP_TOK // 2
    count = 2

    def head(i, place_ref):
        return place_ref[SEQ] * local_heads + local_head(call, place_ref[SEQ], i)

    own = pl.BlockSpec((half, HEAD_DIM), lambda i, p: (0, head(i, p)))
    return pl.pallas_call(
        pair_kernel,
        grid_spec=pltpu.PrefetchScalarGridSpec(
            num_scalar_prefetch=1,
            grid=(count,),
            in_specs=[
                own,
                own,
                own,
                pl.BlockSpec((3, half, HEAD_DIM), lambda i, p: (0, 0, i)),
                pl.BlockSpec((1, NT, CLIP_TOK), lambda i, p: (head(i, p), 0, 0)),
            ]
            + [pl.BlockSpec(memory_space=pl.ANY)] * len(earlier),
            out_specs=pl.BlockSpec((CLIP_TOK, HEAD_DIM), lambda i, p: (0, i)),
            scratch_shapes=[
                pltpu.VMEM((CLIP_TOK, HEAD_DIM), jnp.bfloat16),
                pltpu.VMEM((CLIP_TOK, 2 * HEAD_DIM), jnp.bfloat16),
            ],
        ),
        out_shape=jax.ShapeDtypeStruct((CLIP_TOK, count * HEAD_DIM), jnp.bfloat16),
        compiler_params=pltpu.CompilerParams(vmem_limit_bytes=limit),
        cost_estimate=SMALL_COST,
    )(place, query, key, value, other, bias, *earlier)


def attend_whole(place, query, key, value, bias):
    local_heads = query.shape[1] // HEAD_DIM
    column = pl.BlockSpec((CLIP_TOK, HEAD_DIM), lambda i, p: (0, i))
    return pl.pallas_call(
        whole_kernel,
        grid_spec=pltpu.PrefetchScalarGridSpec(
            num_scalar_prefetch=1,
            grid=(local_heads,),
            in_specs=[
                column,
                column,
                column,
                pl.BlockSpec((1, NT, CLIP_TOK), lambda i, p: (p[0] * local_heads + i, 0, 0)),
            ],
            out_specs=column,
            scratch_shapes=[pltpu.VMEM((CLIP_TOK, 2 * HEAD_DIM), jnp.bfloat16)],
        ),
        out_shape=jax.ShapeDtypeStruct(query.shape, jnp.bfloat16),
        compiler_params=pltpu.CompilerParams(vmem_limit_bytes=VMEM_LIMIT),
        cost_estimate=attention_cost(local_heads),
    )(place, query, key, value, bias)


def pack_kernel(place_ref, q_ref, k_ref, v_ref, *rest):
    out_ref = rest[-1]
    out_ref[0] = q_ref[...]
    out_ref[1] = k_ref[...]
    out_ref[2] = v_ref[...]


def local_head(call, side, part):
    first, by_side, step = call
    return first + by_side * side + step * part


def pack_partner(place, local_heads, call, query, key, value, earlier, limit):
    rows = query.shape[0]
    count = 2

    def head(i, place_ref):
        side = 1 - place_ref[SEQ]
        return side * local_heads + local_head(call, side, i)

    column = pl.BlockSpec((rows, HEAD_DIM), lambda i, p: (0, head(i, p)))
    return pl.pallas_call(
        pack_kernel,
        grid_spec=pltpu.PrefetchScalarGridSpec(
            num_scalar_prefetch=1,
            grid=(count,),
            in_specs=[column, column, column]
            + [pl.BlockSpec(memory_space=pl.ANY)] * len(earlier),
            out_specs=pl.BlockSpec((3, rows, HEAD_DIM), lambda i, p: (0, 0, i)),
        ),
        out_shape=jax.ShapeDtypeStruct((3, rows, count * HEAD_DIM), jnp.bfloat16),
        compiler_params=pltpu.CompilerParams(vmem_limit_bytes=limit),
        cost_estimate=SMALL_COST,
    )(place, query, key, value, *earlier)


def whole_block(shape):
    return pl.BlockSpec(shape, lambda i, p: (0,) * len(shape), pipeline_mode=pl.Buffered(1))


def gradient_kernel(place_ref, *refs, by_call):
    count = 4 if by_call else 2
    grad_ref = refs[count]
    sent_ref, kept_ref, rows_ref = refs[-3:]
    first_core = place_ref[CORE] == 0
    sides = (place_ref[SEQ], 1 - place_ref[SEQ])

    @pl.when(pl.program_id(0) == 0)
    def _():
        sent, kept = [], []
        for n in range(2):
            if by_call:
                one, two = refs[2 + n][...], refs[n][...]
            else:
                one, two = refs[n][:, :HEAD_DIM], refs[n][:, HEAD_DIM:]
            sent.append(jnp.where(first_core, one, two))
            kept.append(jnp.where(first_core, two, one))
        rows_ref[...] = jnp.concatenate(sent + kept, axis=1).T

    each = 2 if by_call else 1
    product = jnp.dot(rows_ref[...], grad_ref[...], preferred_element_type=jnp.float32)
    product = product.astype(jnp.bfloat16).reshape(4 * each, HEAD_DIM, grad_ref.shape[1])
    for n, side in enumerate(sides):
        sent_ref[pl.ds(each * side, each)] = product[each * n : each * (n + 1)]
        kept_ref[pl.ds(each * side, each)] = product[each * (2 + n) : each * (3 + n)]


def batch_gradient(place, sources, grad_proj, earlier=(), cost=SMALL_COST):
    by_call = len(sources) == 4
    heads = len(sources)
    rows, columns = grad_proj.shape
    step = columns // GRADIENT_STEPS
    out = pl.BlockSpec((heads, HEAD_DIM, step), lambda i, p: (0, 0, i))
    result = jax.ShapeDtypeStruct((heads, HEAD_DIM, columns), jnp.bfloat16)
    return pl.pallas_call(
        functools.partial(gradient_kernel, by_call=by_call),
        grid_spec=pltpu.PrefetchScalarGridSpec(
            num_scalar_prefetch=1,
            grid=(GRADIENT_STEPS,),
            in_specs=[whole_block(each.shape) for each in sources]
            + [pl.BlockSpec((rows, step), lambda i, p: (0, i))]
            + [pl.BlockSpec(memory_space=pl.ANY)] * len(earlier),
            out_specs=[out, out],
            scratch_shapes=[pltpu.VMEM((2 * heads * HEAD_DIM, rows), jnp.bfloat16)],
        ),
        out_shape=[result, result],
        compiler_params=pltpu.CompilerParams(vmem_limit_bytes=VMEM_GRADIENT),
        cost_estimate=cost,
    )(place, *sources, grad_proj, *earlier)


def sum_of(blocks):
    total = blocks[0].astype(jnp.float32)
    for block in blocks[1:]:
        total = total + block.astype(jnp.float32)
    return total


def level_step(place, bit, terms, earlier=(), cost=SMALL_COST):
    count = len(terms)
    pairs = terms[0].shape[0] // 2
    shape = (pairs,) + terms[0].shape[1:]
    block = (1,) + terms[0].shape[1:]
    keep = pl.BlockSpec(block, lambda i, p: (2 * i + p[bit], 0, 0))
    send = pl.BlockSpec(block, lambda i, p: (2 * i + 1 - p[bit], 0, 0))
    out = pl.BlockSpec(block, lambda i, p: (i, 0, 0))

    def kernel(place_ref, *refs):
        kept_ref, sent_ref = refs[-2:]
        kept_ref[...] = sum_of([ref[...] for ref in refs[:count]])
        sent_ref[...] = sum_of([ref[...] for ref in refs[count : 2 * count]]).astype(jnp.bfloat16)

    return pl.pallas_call(
        kernel,
        grid_spec=pltpu.PrefetchScalarGridSpec(
            num_scalar_prefetch=1,
            grid=(pairs,),
            in_specs=[keep] * count
            + [send] * count
            + [pl.BlockSpec(memory_space=pl.ANY)] * len(earlier),
            out_specs=[out, out],
        ),
        out_shape=[
            jax.ShapeDtypeStruct(shape, jnp.float32),
            jax.ShapeDtypeStruct(shape, jnp.bfloat16),
        ],
        compiler_params=pltpu.CompilerParams(vmem_limit_bytes=VMEM_SMALL),
        cost_estimate=cost,
    )(place, *terms, *terms, *earlier)


def reach_step(place, terms, earlier=()):
    count = len(terms)
    block = (1,) + terms[0].shape[1:]
    near = pl.BlockSpec(block, lambda i, p: (p[HIGH], 0, 0))
    far = pl.BlockSpec(block, lambda i, p: (1 - p[HIGH], 0, 0))

    def kernel(place_ref, *refs):
        kept_ref, near_ref, far_ref = refs[-3:]
        total = sum_of([ref[...] for ref in refs[:count]])
        kept_ref[...] = total
        near_ref[...] = total.astype(jnp.bfloat16)
        far_ref[...] = sum_of([ref[...] for ref in refs[count : 2 * count]]).astype(jnp.bfloat16)

    return pl.pallas_call(
        kernel,
        grid_spec=pltpu.PrefetchScalarGridSpec(
            num_scalar_prefetch=1,
            grid=(1,),
            in_specs=[near] * count
            + [far] * count
            + [pl.BlockSpec(memory_space=pl.ANY)] * len(earlier),
            out_specs=[whole_block(block)] * 3,
        ),
        out_shape=[
            jax.ShapeDtypeStruct(block, kind) for kind in (jnp.float32, jnp.bfloat16, jnp.bfloat16)
        ],
        compiler_params=pltpu.CompilerParams(vmem_limit_bytes=VMEM_SMALL),
        cost_estimate=SMALL_COST,
    )(place, *terms, *terms, *earlier)


def total_step(terms, earlier=(), kind=jnp.bfloat16):
    block = pl.BlockSpec((1,) + terms[0].shape[1:], lambda i: (i, 0, 0))

    def kernel(*refs):
        refs[-1][...] = sum_of([ref[...] for ref in refs[: len(terms)]]).astype(kind)

    return pl.pallas_call(
        kernel,
        grid=(terms[0].shape[0],),
        in_specs=[block] * len(terms) + [pl.BlockSpec(memory_space=pl.ANY)] * len(earlier),
        out_specs=block,
        out_shape=jax.ShapeDtypeStruct(terms[0].shape, kind),
        compiler_params=pltpu.CompilerParams(vmem_limit_bytes=VMEM_SMALL),
        cost_estimate=SMALL_COST,
    )(*terms, *earlier)


def choose_owned(place, *batches):
    block = batches[0][0].shape
    terms = [term for batch in batches for term in batch]

    def kernel(place_ref, *refs):
        alike = place_ref[CORE] == place_ref[X]
        outer = place_ref[LOW] == place_ref[HIGH]
        owned = (alike, ~alike & outer, ~alike & ~outer)
        at = 0
        for batch, mine in zip(batches, owned):
            chosen = refs[at : at + len(batch)]
            at += len(batch)

            @pl.when(mine)
            def _():
                refs[-1][...] = sum_of([ref[0] for ref in chosen])

    return pl.pallas_call(
        kernel,
        grid_spec=pltpu.PrefetchScalarGridSpec(
            num_scalar_prefetch=1,
            grid=(1,),
            in_specs=[whole_block(block)] * len(terms),
            out_specs=whole_block(block[1:]),
        ),
        out_shape=jax.ShapeDtypeStruct(block[1:], jnp.float32),
        compiler_params=pltpu.CompilerParams(vmem_limit_bytes=VMEM_GRADIENT),
        cost_estimate=SMALL_COST,
    )(place, *terms)


def join_columns(place, sources, calls, local_heads, earlier, cost):
    rows = sources[0].shape[0]
    step = rows // JOIN_STEPS
    shape = (rows, HEADS * HEAD_DIM)

    def kernel(place_ref, *refs):
        out_ref, done_ref = refs[-2:]
        done_ref[...] = jnp.zeros_like(done_ref)
        for n, source in enumerate(refs[: len(sources)]):
            side = place_ref[SEQ] if n % 2 == 0 else 1 - place_ref[SEQ]
            for part in range(2):
                head = side * local_heads + local_head(calls[n // 2], side, part)
                at = pl.multiple_of(head * HEAD_DIM, HEAD_DIM)
                out_ref[:, pl.ds(at, HEAD_DIM)] = source[:, part * HEAD_DIM : (part + 1) * HEAD_DIM]

    return pl.pallas_call(
        kernel,
        grid_spec=pltpu.PrefetchScalarGridSpec(
            num_scalar_prefetch=1,
            grid=(JOIN_STEPS,),
            in_specs=[pl.BlockSpec((step, each.shape[1]), lambda i, p: (i, 0)) for each in sources]
            + [pl.BlockSpec(memory_space=pl.ANY)] * len(earlier),
            out_specs=[
                pl.BlockSpec((step, shape[1]), lambda i, p: (i, 0)),
                pl.BlockSpec((8, HEAD_DIM), lambda i, p: (0, 0)),
            ],
        ),
        out_shape=[
            jax.ShapeDtypeStruct(shape, jnp.bfloat16),
            jax.ShapeDtypeStruct((8, HEAD_DIM), jnp.float32),
        ],
        compiler_params=pltpu.CompilerParams(vmem_limit_bytes=VMEM_SMALL),
        cost_estimate=cost,
    )(place, *sources, *earlier)


def project(attention, weight, gate, span, filled=(), earlier=(), cost=SMALL_COST):
    rows, depth = attention.shape
    columns = weight.shape[1]
    step = columns // PROJECT_STEPS
    first, steps = span[0], len(span)

    def kernel(attention_ref, weight_ref, gate_ref, *refs):
        out_ref, done_ref = refs[-2:]
        done_ref[...] = jnp.zeros_like(done_ref)
        total = jnp.dot(attention_ref[...], weight_ref[...], preferred_element_type=jnp.float32)
        out_ref[...] = (total * gate_ref[...]).astype(out_ref.dtype)

    return pl.pallas_call(
        kernel,
        grid=(steps,),
        in_specs=[
            pl.BlockSpec((rows, depth), lambda i: (0, 0), pipeline_mode=pl.Buffered(1)),
            pl.BlockSpec((depth, step), lambda i: (0, first + i)),
            pl.BlockSpec((1, step), lambda i: (0, first + i)),
        ]
        + [pl.BlockSpec(memory_space=pl.ANY)] * (len(filled) + len(earlier)),
        out_specs=[
            pl.BlockSpec((rows, step), lambda i: (0, first + i)),
            pl.BlockSpec((8, HEAD_DIM), lambda i: (0, 0)),
        ],
        out_shape=[
            jax.ShapeDtypeStruct((rows, columns), jnp.bfloat16),
            jax.ShapeDtypeStruct((8, HEAD_DIM), jnp.float32),
        ],
        input_output_aliases={3: 0} if filled else {},
        compiler_params=pltpu.CompilerParams(vmem_limit_bytes=VMEM_PROJECT),
        cost_estimate=cost,
    )(attention, weight, gate, *filled, *earlier)


def contract_tokens(columns, grad_proj, kind):
    return lax.dot_general(
        columns, grad_proj, (((0,), (0,)), ((), ())), preferred_element_type=jnp.float32
    ).astype(kind)


def after(value, *earlier):
    return lax.optimization_barrier((value,) + earlier)[0]


def dp_send(value, flip, sender):
    return lax.ppermute(value, "dp", [(i, i ^ flip) for i in range(HEADS) if sender(i)])


def same_bits(i):
    return (i >> 1 ^ i) & 1 == 0


def paired_device(query_rows, key_rows, value_rows, windows, out_weight, gate_scale, out_grad):
    index = lax.axis_index("dp")
    place = jnp.stack([lax.axis_index("seq")] + [index >> bit & 1 for bit in range(4)])
    place = lax.optimization_barrier(place.astype(jnp.int32))
    local_heads = HEADS // 2
    swap = [(0, 1), (1, 0)]
    calls = [(0, 0, 4), (3, 0, 4), (1, 4, 1), (5, -4, 1)]
    bias = window_bias(windows)
    weight = lax.all_gather(out_weight, "dp", axis=0, tiled=True)
    gate_row = gate_scale[0].astype(jnp.float32)
    grad_proj = (out_grad.astype(jnp.float32) * gate_row).astype(jnp.bfloat16)
    sources = (query_rows, key_rows, value_rows)

    def pack(n, limit, *earlier):
        return pack_partner(place, local_heads, calls[n], *sources, earlier, limit)

    def attention(n, other, *earlier, limit=VMEM_LIMIT):
        return attend_pair(place, local_heads, calls[n], *sources, other, bias, earlier, limit)

    def exchange(mine):
        return lax.ppermute(mine, "seq", swap)

    def core_step(*operands):
        sent, kept = batch_gradient(place, operands[:4], operands[4])
        return total_step([kept, dp_send(sent, 1, lambda i: True)])

    def apart(step, *operands):
        shapes = jax.eval_shape(step, *operands)
        return lax.cond(
            windows[0, 0] > 0,
            step,
            lambda *_: jax.tree.map(lambda leaf: jnp.zeros(leaf.shape, leaf.dtype), shapes),
            *operands,
        )

    packed0 = pack(0, VMEM_WHOLE)
    packed1 = pack(1, VMEM_WHOLE, packed0)
    packed2 = pack(2, VMEM_LIMIT, packed1)
    other0 = exchange(packed0)
    other1 = exchange(packed1)
    other2 = exchange(packed2)
    mine0 = attention(0, other0, packed2)
    theirs0 = exchange(mine0)
    mine1 = attention(1, other1, mine0)
    theirs1 = exchange(mine1)
    packed3 = pack(3, VMEM_LIMIT, mine1)
    other3 = exchange(packed3)
    mine2 = attention(2, other2, mine1, packed3)
    theirs2 = exchange(mine2)

    def unlike(i):
        return not same_bits(i)

    def outer(i):
        return unlike(i) and (i >> 2 ^ i >> 3) & 1 == 0

    def inner(i):
        return unlike(i) and (i >> 2 ^ i >> 3) & 1 == 1

    first = (mine0, theirs0, mine1, theirs1)
    total_a = apart(core_step, after(mine0, mine2, weight), *first[1:], grad_proj)
    across_a = dp_send(total_a, 2, unlike)
    mine3 = attention(3, other3, total_a, limit=VMEM_WHOLE)
    theirs3 = exchange(mine3)
    sent_b, kept_b = batch_gradient(place, (mine2, theirs2), grad_proj, (mine3,), LONG_COST)
    came_b = dp_send(sent_b, 1, lambda i: True)
    kept_a, sent_a = level_step(place, LOW, [total_a, across_a], (sent_b,), LONG_COST)
    low_a = dp_send(sent_a, 4, same_bits)
    total_b = total_step([kept_b, came_b], (sent_a,))
    across_b = dp_send(total_b, 2, same_bits)
    sent_c, kept_c = batch_gradient(place, (mine3, theirs3), grad_proj, (total_b,))
    came_c = dp_send(sent_c, 1, lambda i: True)
    results = (*first, mine2, theirs2, mine3, theirs3)
    columns, done = join_columns(place, results, calls, local_heads, (sent_c,), LONG_COST)
    total_c = total_step([kept_c, came_c], (done,))
    across_c = dp_send(total_c, 2, same_bits)
    kept_a, sent_a = level_step(place, HIGH, [kept_a, low_a], (total_c,))
    high_a = dp_send(sent_a, 8, same_bits)
    sent_b = total_step([total_b, across_b], (sent_a,))
    low_b = dp_send(sent_b, 4, inner)
    gate = gate_row[None]
    out, done = project(columns, weight, gate, range(3), (), (sent_b,))
    kept_c, near_c, far_c = reach_step(place, [total_c, across_c], (done,))
    reached_c = dp_send(far_c, 8, outer), dp_send(far_c, 12, inner), dp_send(near_c, 4, outer)
    kept_b, sent_b = level_step(place, HIGH, [total_b, across_b, low_b], (near_c,))
    high_b = dp_send(sent_b, 12, outer)
    last = range(3, PROJECT_STEPS)
    block_out, done = project(columns, weight, gate, last, (out,), (sent_b,), LONG_COST)
    final_a = total_step([kept_a, high_a], (done,), jnp.float32)
    weight_grad = choose_owned(place, (final_a,), (kept_b, high_b), (kept_c, *reached_c))
    return (block_out, weight_grad)


def general_device(query_rows, key_rows, value_rows, windows, out_weight, gate_scale, out_grad):
    query, key, value = (
        lax.all_to_all(rows, "seq", split_axis=1, concat_axis=0, tiled=True)
        for rows in (query_rows, key_rows, value_rows)
    )
    place = lax.axis_index("seq").reshape(1).astype(jnp.int32)
    mine = attend_whole(place, query, key, value, window_bias(windows))
    columns = lax.all_gather(mine, "seq", axis=1, tiled=True)
    weight = lax.all_gather(out_weight, "dp", axis=0, tiled=True)
    gate_row = gate_scale[0].astype(jnp.float32)
    projected = jnp.dot(columns, weight, preferred_element_type=jnp.float32)
    block_out = (projected * gate_row).astype(jnp.bfloat16)
    grad_proj = (out_grad.astype(jnp.float32) * gate_row).astype(jnp.bfloat16)
    weight_grad = lax.psum_scatter(
        contract_tokens(columns, grad_proj, jnp.float32), "dp", scatter_dimension=0, tiled=True
    )
    return (block_out, weight_grad)


def solution(mesh):
    paired = mesh.shape["seq"] == 2 and mesh.shape["dp"] == HEADS
    return jax.shard_map(
        paired_device if paired else general_device,
        mesh=mesh,
        in_specs=(
            P(("dp", "seq"), None),
            P(("dp", "seq"), None),
            P(("dp", "seq"), None),
            P(),
            P("dp", "seq"),
            P("dp", "seq"),
            P("dp", "seq"),
        ),
        out_specs=(P("dp", "seq"), P("dp", "seq")),
        check_vma=False,
    )
```

```python
import functools
import math

import jax
import jax.numpy as jnp
import numpy as np
from jax import lax
from jax.experimental import pallas as pl
from jax.experimental.pallas import tpu as pltpu
from jax.sharding import PartitionSpec as P

HEADS = 16
HEAD_DIM = 128
GH = 3
GW = 4
GT = 2
TILE = 48
NT = 24
CLIP_TOK = NT * TILE
Q_ROWS = GW * TILE
LOG2_SCALE = math.log2(math.e) / math.sqrt(HEAD_DIM)
VMEM_LIMIT = 16 * 1024 * 1024
VMEM_GRADIENT = 20 * 1024 * 1024
VMEM_PROJECT = 24 * 1024 * 1024
PROJECT_STEPS = 6
GRADIENT_STEPS = 3
JOIN_STEPS = 4
SEQ, CORE, X, LOW, HIGH = range(5)
VMEM_WHOLE = 60 * 1024 * 1024
VMEM_SMALL = 12 * 1024 * 1024
SMALL_COST = pl.CostEstimate(flops=1, bytes_accessed=1, transcendentals=0)
LONG_COST = pl.CostEstimate(flops=2 * 10**10, bytes_accessed=2 * 10**7, transcendentals=0)


def window_bias(windows):
    tile_id = np.arange(NT)
    coords = np.stack([tile_id // (GH * GW), tile_id // GW % GH, tile_id % GW]).astype(np.int32)
    token_coords = np.repeat(coords, TILE, axis=1)
    inside = None
    for axis_no, limit in enumerate((GT, GH, GW)):
        extent = jnp.minimum(windows[:, axis_no], limit)[:, None]
        start = jnp.clip(coords[axis_no][None, :] - (extent - 1) // 2, 0, limit - extent)
        column = token_coords[axis_no][None, None, :]
        here = (column >= start[:, :, None]) & (column < (start + extent)[:, :, None])
        inside = here if inside is None else inside & here
    return jnp.where(inside, 0.0, -jnp.inf).astype(jnp.float32)


def attend_rows(queries, first_tile, bias_ref, keys, values):
    count = queries.shape[0]
    tiles = count // TILE
    scores = lax.dot_general(
        queries, keys, (((1,), (1,)), ((), ())), preferred_element_type=jnp.float32
    )
    bias = bias_ref[0, first_tile : first_tile + tiles, :]
    scores = (scores.reshape(tiles, TILE, CLIP_TOK) + bias[:, None, :]).reshape(count, CLIP_TOK)
    peak = jnp.max(scores, axis=-1, keepdims=True)
    weights = jnp.exp2((scores - peak) * LOG2_SCALE).astype(jnp.bfloat16)
    blended = jnp.dot(weights, values, preferred_element_type=jnp.float32)
    return (blended[:, :HEAD_DIM] / blended[:, HEAD_DIM:]).astype(jnp.bfloat16)


def fill_values(values_ref, parts):
    at = 0
    for part in parts:
        rows = part.shape[0]
        values_ref[at : at + rows, :HEAD_DIM] = part
        at += rows
    values_ref[:, HEAD_DIM:] = jnp.ones((CLIP_TOK, HEAD_DIM), jnp.bfloat16)


def pair_kernel(place_ref, q_ref, k_ref, v_ref, other_ref, bias_ref, *rest):
    out_ref, keys_ref, values_ref = rest[-3:]
    half = CLIP_TOK // 2
    keys_ref[:half, :] = k_ref[...]
    keys_ref[half:, :] = other_ref[1]
    fill_values(values_ref, (v_ref[...], other_ref[2]))
    keys = keys_ref[...]
    values = values_ref[...]
    for side in range(2):
        base = pl.multiple_of((place_ref[0] if side == 0 else 1 - place_ref[0]) * half, half)
        for at in range(0, half, Q_ROWS):
            queries = q_ref[at : at + Q_ROWS, :] if side == 0 else other_ref[0, at : at + Q_ROWS, :]
            first_tile = (side * half + at) // TILE
            out_ref[pl.ds(base + at, Q_ROWS), :] = attend_rows(
                queries, first_tile, bias_ref, keys, values
            )


def whole_kernel(place_ref, q_ref, k_ref, v_ref, bias_ref, out_ref, values_ref):
    fill_values(values_ref, (v_ref[...],))
    keys = k_ref[...]
    values = values_ref[...]
    for at in range(0, CLIP_TOK, Q_ROWS):
        out_ref[at : at + Q_ROWS, :] = attend_rows(
            q_ref[at : at + Q_ROWS, :], at // TILE, bias_ref, keys, values
        )


def attention_cost(heads):
    pairs = heads * CLIP_TOK * CLIP_TOK
    return pl.CostEstimate(
        flops=pairs * HEAD_DIM * 6,
        bytes_accessed=heads * CLIP_TOK * HEAD_DIM * 8,
        transcendentals=pairs,
    )


def attend_pair(place, local_heads, call, query, key, value, other, bias, earlier, limit):
    half = CLIP_TOK // 2
    count = 2

    def head(i, place_ref):
        return place_ref[SEQ] * local_heads + local_head(call, place_ref[SEQ], i)

    own = pl.BlockSpec((half, HEAD_DIM), lambda i, p: (0, head(i, p)))
    return pl.pallas_call(
        pair_kernel,
        grid_spec=pltpu.PrefetchScalarGridSpec(
            num_scalar_prefetch=1,
            grid=(count,),
            in_specs=[
                own,
                own,
                own,
                pl.BlockSpec((3, half, HEAD_DIM), lambda i, p: (0, 0, i)),
                pl.BlockSpec((1, NT, CLIP_TOK), lambda i, p: (head(i, p), 0, 0)),
            ]
            + [pl.BlockSpec(memory_space=pl.ANY)] * len(earlier),
            out_specs=pl.BlockSpec((CLIP_TOK, HEAD_DIM), lambda i, p: (0, i)),
            scratch_shapes=[
                pltpu.VMEM((CLIP_TOK, HEAD_DIM), jnp.bfloat16),
                pltpu.VMEM((CLIP_TOK, 2 * HEAD_DIM), jnp.bfloat16),
            ],
        ),
        out_shape=jax.ShapeDtypeStruct((CLIP_TOK, count * HEAD_DIM), jnp.bfloat16),
        compiler_params=pltpu.CompilerParams(vmem_limit_bytes=limit),
        cost_estimate=SMALL_COST,
    )(place, query, key, value, other, bias, *earlier)


def attend_whole(place, query, key, value, bias):
    local_heads = query.shape[1] // HEAD_DIM
    column = pl.BlockSpec((CLIP_TOK, HEAD_DIM), lambda i, p: (0, i))
    return pl.pallas_call(
        whole_kernel,
        grid_spec=pltpu.PrefetchScalarGridSpec(
            num_scalar_prefetch=1,
            grid=(local_heads,),
            in_specs=[
                column,
                column,
                column,
                pl.BlockSpec((1, NT, CLIP_TOK), lambda i, p: (p[0] * local_heads + i, 0, 0)),
            ],
            out_specs=column,
            scratch_shapes=[pltpu.VMEM((CLIP_TOK, 2 * HEAD_DIM), jnp.bfloat16)],
        ),
        out_shape=jax.ShapeDtypeStruct(query.shape, jnp.bfloat16),
        compiler_params=pltpu.CompilerParams(vmem_limit_bytes=VMEM_LIMIT),
        cost_estimate=attention_cost(local_heads),
    )(place, query, key, value, bias)


def pack_kernel(place_ref, q_ref, k_ref, v_ref, *rest):
    out_ref = rest[-1]
    out_ref[0] = q_ref[...]
    out_ref[1] = k_ref[...]
    out_ref[2] = v_ref[...]


def local_head(call, side, part):
    first, by_side, step = call
    return first + by_side * side + step * part


def pack_partner(place, local_heads, call, query, key, value, earlier, limit):
    rows = query.shape[0]
    count = 2

    def head(i, place_ref):
        side = 1 - place_ref[SEQ]
        return side * local_heads + local_head(call, side, i)

    column = pl.BlockSpec((rows, HEAD_DIM), lambda i, p: (0, head(i, p)))
    return pl.pallas_call(
        pack_kernel,
        grid_spec=pltpu.PrefetchScalarGridSpec(
            num_scalar_prefetch=1,
            grid=(count,),
            in_specs=[column, column, column]
            + [pl.BlockSpec(memory_space=pl.ANY)] * len(earlier),
            out_specs=pl.BlockSpec((3, rows, HEAD_DIM), lambda i, p: (0, 0, i)),
        ),
        out_shape=jax.ShapeDtypeStruct((3, rows, count * HEAD_DIM), jnp.bfloat16),
        compiler_params=pltpu.CompilerParams(vmem_limit_bytes=limit),
        cost_estimate=SMALL_COST,
    )(place, query, key, value, *earlier)


def whole_block(shape):
    return pl.BlockSpec(shape, lambda i, p: (0,) * len(shape), pipeline_mode=pl.Buffered(1))


def gradient_kernel(place_ref, *refs, by_call):
    count = 4 if by_call else 2
    grad_ref = refs[count]
    sent_ref, kept_ref, rows_ref = refs[-3:]
    first_core = place_ref[CORE] == 0
    sides = (place_ref[SEQ], 1 - place_ref[SEQ])

    @pl.when(pl.program_id(0) == 0)
    def _():
        sent, kept = [], []
        for n in range(2):
            if by_call:
                one, two = refs[2 + n][...], refs[n][...]
            else:
                one, two = refs[n][:, :HEAD_DIM], refs[n][:, HEAD_DIM:]
            sent.append(jnp.where(first_core, one, two))
            kept.append(jnp.where(first_core, two, one))
        rows_ref[...] = jnp.concatenate(sent + kept, axis=1).T

    each = 2 if by_call else 1
    product = jnp.dot(rows_ref[...], grad_ref[...], preferred_element_type=jnp.float32)
    product = product.astype(jnp.bfloat16).reshape(4 * each, HEAD_DIM, grad_ref.shape[1])
    for n, side in enumerate(sides):
        sent_ref[pl.ds(each * side, each)] = product[each * n : each * (n + 1)]
        kept_ref[pl.ds(each * side, each)] = product[each * (2 + n) : each * (3 + n)]


def batch_gradient(place, sources, grad_proj, earlier=(), cost=SMALL_COST):
    by_call = len(sources) == 4
    heads = len(sources)
    rows, columns = grad_proj.shape
    step = columns // GRADIENT_STEPS
    out = pl.BlockSpec((heads, HEAD_DIM, step), lambda i, p: (0, 0, i))
    result = jax.ShapeDtypeStruct((heads, HEAD_DIM, columns), jnp.bfloat16)
    return pl.pallas_call(
        functools.partial(gradient_kernel, by_call=by_call),
        grid_spec=pltpu.PrefetchScalarGridSpec(
            num_scalar_prefetch=1,
            grid=(GRADIENT_STEPS,),
            in_specs=[whole_block(each.shape) for each in sources]
            + [pl.BlockSpec((rows, step), lambda i, p: (0, i))]
            + [pl.BlockSpec(memory_space=pl.ANY)] * len(earlier),
            out_specs=[out, out],
            scratch_shapes=[pltpu.VMEM((2 * heads * HEAD_DIM, rows), jnp.bfloat16)],
        ),
        out_shape=[result, result],
        compiler_params=pltpu.CompilerParams(vmem_limit_bytes=VMEM_GRADIENT),
        cost_estimate=cost,
    )(place, *sources, grad_proj, *earlier)


def sum_of(blocks):
    total = blocks[0].astype(jnp.float32)
    for block in blocks[1:]:
        total = total + block.astype(jnp.float32)
    return total


def level_step(place, bit, terms, earlier=(), cost=SMALL_COST):
    count = len(terms)
    pairs = terms[0].shape[0] // 2
    shape = (pairs,) + terms[0].shape[1:]
    block = (1,) + terms[0].shape[1:]
    keep = pl.BlockSpec(block, lambda i, p: (2 * i + p[bit], 0, 0))
    send = pl.BlockSpec(block, lambda i, p: (2 * i + 1 - p[bit], 0, 0))
    out = pl.BlockSpec(block, lambda i, p: (i, 0, 0))

    def kernel(place_ref, *refs):
        kept_ref, sent_ref = refs[-2:]
        kept_ref[...] = sum_of([ref[...] for ref in refs[:count]])
        sent_ref[...] = sum_of([ref[...] for ref in refs[count : 2 * count]]).astype(jnp.bfloat16)

    return pl.pallas_call(
        kernel,
        grid_spec=pltpu.PrefetchScalarGridSpec(
            num_scalar_prefetch=1,
            grid=(pairs,),
            in_specs=[keep] * count
            + [send] * count
            + [pl.BlockSpec(memory_space=pl.ANY)] * len(earlier),
            out_specs=[out, out],
        ),
        out_shape=[
            jax.ShapeDtypeStruct(shape, jnp.float32),
            jax.ShapeDtypeStruct(shape, jnp.bfloat16),
        ],
        compiler_params=pltpu.CompilerParams(vmem_limit_bytes=VMEM_SMALL),
        cost_estimate=cost,
    )(place, *terms, *terms, *earlier)


def reach_step(place, terms, earlier=()):
    count = len(terms)
    block = (1,) + terms[0].shape[1:]
    near = pl.BlockSpec(block, lambda i, p: (p[HIGH], 0, 0))
    far = pl.BlockSpec(block, lambda i, p: (1 - p[HIGH], 0, 0))

    def kernel(place_ref, *refs):
        kept_ref, near_ref, far_ref = refs[-3:]
        total = sum_of([ref[...] for ref in refs[:count]])
        kept_ref[...] = total
        near_ref[...] = total.astype(jnp.bfloat16)
        far_ref[...] = sum_of([ref[...] for ref in refs[count : 2 * count]]).astype(jnp.bfloat16)

    return pl.pallas_call(
        kernel,
        grid_spec=pltpu.PrefetchScalarGridSpec(
            num_scalar_prefetch=1,
            grid=(1,),
            in_specs=[near] * count
            + [far] * count
            + [pl.BlockSpec(memory_space=pl.ANY)] * len(earlier),
            out_specs=[whole_block(block)] * 3,
        ),
        out_shape=[
            jax.ShapeDtypeStruct(block, kind) for kind in (jnp.float32, jnp.bfloat16, jnp.bfloat16)
        ],
        compiler_params=pltpu.CompilerParams(vmem_limit_bytes=VMEM_SMALL),
        cost_estimate=SMALL_COST,
    )(place, *terms, *terms, *earlier)


def total_step(terms, earlier=(), kind=jnp.bfloat16):
    block = pl.BlockSpec((1,) + terms[0].shape[1:], lambda i: (i, 0, 0))

    def kernel(*refs):
        refs[-1][...] = sum_of([ref[...] for ref in refs[: len(terms)]]).astype(kind)

    return pl.pallas_call(
        kernel,
        grid=(terms[0].shape[0],),
        in_specs=[block] * len(terms) + [pl.BlockSpec(memory_space=pl.ANY)] * len(earlier),
        out_specs=block,
        out_shape=jax.ShapeDtypeStruct(terms[0].shape, kind),
        compiler_params=pltpu.CompilerParams(vmem_limit_bytes=VMEM_SMALL),
        cost_estimate=SMALL_COST,
    )(*terms, *earlier)


def choose_owned(place, *batches):
    block = batches[0][0].shape
    terms = [term for batch in batches for term in batch]

    def kernel(place_ref, *refs):
        alike = place_ref[CORE] == place_ref[X]
        outer = place_ref[LOW] == place_ref[HIGH]
        owned = (alike, ~alike & outer, ~alike & ~outer)
        at = 0
        for batch, mine in zip(batches, owned):
            chosen = refs[at : at + len(batch)]
            at += len(batch)

            @pl.when(mine)
            def _():
                refs[-1][...] = sum_of([ref[0] for ref in chosen])

    return pl.pallas_call(
        kernel,
        grid_spec=pltpu.PrefetchScalarGridSpec(
            num_scalar_prefetch=1,
            grid=(1,),
            in_specs=[whole_block(block)] * len(terms),
            out_specs=whole_block(block[1:]),
        ),
        out_shape=jax.ShapeDtypeStruct(block[1:], jnp.float32),
        compiler_params=pltpu.CompilerParams(vmem_limit_bytes=VMEM_GRADIENT),
        cost_estimate=SMALL_COST,
    )(place, *terms)


def join_columns(place, sources, calls, local_heads, earlier, cost):
    rows = sources[0].shape[0]
    step = rows // JOIN_STEPS
    shape = (rows, HEADS * HEAD_DIM)

    def kernel(place_ref, *refs):
        out_ref, done_ref = refs[-2:]
        done_ref[...] = jnp.zeros_like(done_ref)
        for n, source in enumerate(refs[: len(sources)]):
            side = place_ref[SEQ] if n % 2 == 0 else 1 - place_ref[SEQ]
            for part in range(2):
                head = side * local_heads + local_head(calls[n // 2], side, part)
                at = pl.multiple_of(head * HEAD_DIM, HEAD_DIM)
                out_ref[:, pl.ds(at, HEAD_DIM)] = source[:, part * HEAD_DIM : (part + 1) * HEAD_DIM]

    return pl.pallas_call(
        kernel,
        grid_spec=pltpu.PrefetchScalarGridSpec(
            num_scalar_prefetch=1,
            grid=(JOIN_STEPS,),
            in_specs=[pl.BlockSpec((step, each.shape[1]), lambda i, p: (i, 0)) for each in sources]
            + [pl.BlockSpec(memory_space=pl.ANY)] * len(earlier),
            out_specs=[
                pl.BlockSpec((step, shape[1]), lambda i, p: (i, 0)),
                pl.BlockSpec((8, HEAD_DIM), lambda i, p: (0, 0)),
            ],
        ),
        out_shape=[
            jax.ShapeDtypeStruct(shape, jnp.bfloat16),
            jax.ShapeDtypeStruct((8, HEAD_DIM), jnp.float32),
        ],
        compiler_params=pltpu.CompilerParams(vmem_limit_bytes=VMEM_SMALL),
        cost_estimate=cost,
    )(place, *sources, *earlier)


def project(attention, weight, gate, span, filled=(), earlier=(), cost=SMALL_COST):
    rows, depth = attention.shape
    columns = weight.shape[1]
    step = columns // PROJECT_STEPS
    first, steps = span[0], len(span)

    def kernel(attention_ref, weight_ref, gate_ref, *refs):
        out_ref, done_ref = refs[-2:]
        done_ref[...] = jnp.zeros_like(done_ref)
        total = jnp.dot(attention_ref[...], weight_ref[...], preferred_element_type=jnp.float32)
        out_ref[...] = (total * gate_ref[...]).astype(out_ref.dtype)

    return pl.pallas_call(
        kernel,
        grid=(steps,),
        in_specs=[
            pl.BlockSpec((rows, depth), lambda i: (0, 0), pipeline_mode=pl.Buffered(1)),
            pl.BlockSpec((depth, step), lambda i: (0, first + i)),
            pl.BlockSpec((1, step), lambda i: (0, first + i)),
        ]
        + [pl.BlockSpec(memory_space=pl.ANY)] * (len(filled) + len(earlier)),
        out_specs=[
            pl.BlockSpec((rows, step), lambda i: (0, first + i)),
            pl.BlockSpec((8, HEAD_DIM), lambda i: (0, 0)),
        ],
        out_shape=[
            jax.ShapeDtypeStruct((rows, columns), jnp.bfloat16),
            jax.ShapeDtypeStruct((8, HEAD_DIM), jnp.float32),
        ],
        input_output_aliases={3: 0} if filled else {},
        compiler_params=pltpu.CompilerParams(vmem_limit_bytes=VMEM_PROJECT),
        cost_estimate=cost,
    )(attention, weight, gate, *filled, *earlier)


def contract_tokens(columns, grad_proj, kind):
    return lax.dot_general(
        columns, grad_proj, (((0,), (0,)), ((), ())), preferred_element_type=jnp.float32
    ).astype(kind)


def after(value, *earlier):
    return lax.optimization_barrier((value,) + earlier)[0]


def dp_send(value, flip, sender):
    return lax.ppermute(value, "dp", [(i, i ^ flip) for i in range(HEADS) if sender(i)])


def same_bits(i):
    return (i >> 1 ^ i) & 1 == 0


def paired_device(query_rows, key_rows, value_rows, windows, out_weight, gate_scale, out_grad):
    index = lax.axis_index("dp")
    place = jnp.stack([lax.axis_index("seq")] + [index >> bit & 1 for bit in range(4)])
    place = lax.optimization_barrier(place.astype(jnp.int32))
    local_heads = HEADS // 2
    swap = [(0, 1), (1, 0)]
    calls = [(0, 0, 4), (3, 0, 4), (1, 4, 1), (5, -4, 1)]
    bias = window_bias(windows)
    weight = lax.all_gather(out_weight, "dp", axis=0, tiled=True)
    gate_row = gate_scale[0].astype(jnp.float32)
    grad_proj = (out_grad.astype(jnp.float32) * gate_row).astype(jnp.bfloat16)
    sources = (query_rows, key_rows, value_rows)

    def pack(n, limit, *earlier):
        return pack_partner(place, local_heads, calls[n], *sources, earlier, limit)

    def attention(n, other, *earlier, limit=VMEM_LIMIT):
        return attend_pair(place, local_heads, calls[n], *sources, other, bias, earlier, limit)

    def exchange(mine):
        return lax.ppermute(mine, "seq", swap)

    def core_step(*operands):
        sent, kept = batch_gradient(place, operands[:4], operands[4])
        return total_step([kept, dp_send(sent, 1, lambda i: True)])

    def apart(step, *operands):
        shapes = jax.eval_shape(step, *operands)
        return lax.cond(
            windows[0, 0] > 0,
            step,
            lambda *_: jax.tree.map(lambda leaf: jnp.zeros(leaf.shape, leaf.dtype), shapes),
            *operands,
        )

    packed0 = pack(0, VMEM_WHOLE)
    packed1 = pack(1, VMEM_WHOLE, packed0)
    packed2 = pack(2, VMEM_LIMIT, packed1)
    other0 = exchange(packed0)
    other1 = exchange(packed1)
    other2 = exchange(packed2)
    mine0 = attention(0, other0, packed2)
    theirs0 = exchange(mine0)
    mine1 = attention(1, other1, mine0)
    theirs1 = exchange(mine1)
    packed3 = pack(3, VMEM_LIMIT, mine1)
    other3 = exchange(packed3)
    mine2 = attention(2, other2, mine1, packed3)
    theirs2 = exchange(mine2)

    def unlike(i):
        return not same_bits(i)

    def outer(i):
        return unlike(i) and (i >> 2 ^ i >> 3) & 1 == 0

    def inner(i):
        return unlike(i) and (i >> 2 ^ i >> 3) & 1 == 1

    first = (mine0, theirs0, mine1, theirs1)
    total_a = apart(core_step, after(mine0, mine2, weight), *first[1:], grad_proj)
    across_a = dp_send(total_a, 2, unlike)
    mine3 = attention(3, other3, total_a, limit=VMEM_WHOLE)
    theirs3 = exchange(mine3)
    sent_b, kept_b = batch_gradient(place, (mine2, theirs2), grad_proj, (mine3,), LONG_COST)
    came_b = dp_send(sent_b, 1, lambda i: True)
    kept_a, sent_a = level_step(place, LOW, [total_a, across_a], (sent_b,), LONG_COST)
    low_a = dp_send(sent_a, 4, same_bits)
    total_b = total_step([kept_b, came_b], (sent_a,))
    across_b = dp_send(total_b, 2, same_bits)
    sent_c, kept_c = batch_gradient(place, (mine3, theirs3), grad_proj, (total_b,))
    came_c = dp_send(sent_c, 1, lambda i: True)
    results = (*first, mine2, theirs2, mine3, theirs3)
    columns, done = join_columns(place, results, calls, local_heads, (sent_c,), LONG_COST)
    total_c = total_step([kept_c, came_c], (done,))
    across_c = dp_send(total_c, 2, same_bits)
    kept_a, sent_a = level_step(place, HIGH, [kept_a, low_a], (total_c,))
    high_a = dp_send(sent_a, 8, same_bits)
    sent_b = total_step([total_b, across_b], (sent_a,))
    low_b = dp_send(sent_b, 4, inner)
    gate = gate_row[None]
    out, done = project(columns, weight, gate, range(3), (), (sent_b,))
    kept_c, near_c, far_c = reach_step(place, [total_c, across_c], (done,))
    reached_c = dp_send(far_c, 8, outer), dp_send(far_c, 12, inner)
    kept_b, sent_b = level_step(place, HIGH, [total_b, across_b, low_b], (far_c,))
    high_b = dp_send(sent_b, 12, outer)
    reached_c += (dp_send(after(near_c, sent_b), 4, outer),)
    last = range(3, PROJECT_STEPS)
    block_out, done = project(columns, weight, gate, last, (out,), (sent_b,), LONG_COST)
    final_a = total_step([kept_a, high_a], (done,), jnp.float32)
    weight_grad = choose_owned(place, (final_a,), (kept_b, high_b), (kept_c, *reached_c))
    return (block_out, weight_grad)


def general_device(query_rows, key_rows, value_rows, windows, out_weight, gate_scale, out_grad):
    query, key, value = (
        lax.all_to_all(rows, "seq", split_axis=1, concat_axis=0, tiled=True)
        for rows in (query_rows, key_rows, value_rows)
    )
    place = lax.axis_index("seq").reshape(1).astype(jnp.int32)
    mine = attend_whole(place, query, key, value, window_bias(windows))
    columns = lax.all_gather(mine, "seq", axis=1, tiled=True)
    weight = lax.all_gather(out_weight, "dp", axis=0, tiled=True)
    gate_row = gate_scale[0].astype(jnp.float32)
    projected = jnp.dot(columns, weight, preferred_element_type=jnp.float32)
    block_out = (projected * gate_row).astype(jnp.bfloat16)
    grad_proj = (out_grad.astype(jnp.float32) * gate_row).astype(jnp.bfloat16)
    weight_grad = lax.psum_scatter(
        contract_tokens(columns, grad_proj, jnp.float32), "dp", scatter_dimension=0, tiled=True
    )
    return (block_out, weight_grad)


def solution(mesh):
    paired = mesh.shape["seq"] == 2 and mesh.shape["dp"] == HEADS
    return jax.shard_map(
        paired_device if paired else general_device,
        mesh=mesh,
        in_specs=(
            P(("dp", "seq"), None),
            P(("dp", "seq"), None),
            P(("dp", "seq"), None),
            P(),
            P("dp", "seq"),
            P("dp", "seq"),
            P("dp", "seq"),
        ),
        out_specs=(P("dp", "seq"), P("dp", "seq")),
        check_vma=False,
    )
```

```python
import functools
import math

import jax
import jax.numpy as jnp
import numpy as np
from jax import lax
from jax.experimental import pallas as pl
from jax.experimental.pallas import tpu as pltpu
from jax.sharding import PartitionSpec as P

HEADS = 16
HEAD_DIM = 128
GH = 3
GW = 4
GT = 2
TILE = 48
NT = 24
CLIP_TOK = NT * TILE
Q_ROWS = GW * TILE
LOG2_SCALE = math.log2(math.e) / math.sqrt(HEAD_DIM)
VMEM_LIMIT = 16 * 1024 * 1024
VMEM_GRADIENT = 20 * 1024 * 1024
VMEM_PROJECT = 24 * 1024 * 1024
PROJECT_STEPS = 6
GRADIENT_STEPS = 3
JOIN_STEPS = 4
SEQ, CORE, X, LOW, HIGH = range(5)
VMEM_WHOLE = 60 * 1024 * 1024
VMEM_SMALL = 12 * 1024 * 1024
SMALL_COST = pl.CostEstimate(flops=1, bytes_accessed=1, transcendentals=0)
LONG_COST = pl.CostEstimate(flops=2 * 10**10, bytes_accessed=2 * 10**7, transcendentals=0)


def window_bias(windows):
    tile_id = np.arange(NT)
    coords = np.stack([tile_id // (GH * GW), tile_id // GW % GH, tile_id % GW]).astype(np.int32)
    token_coords = np.repeat(coords, TILE, axis=1)
    inside = None
    for axis_no, limit in enumerate((GT, GH, GW)):
        extent = jnp.minimum(windows[:, axis_no], limit)[:, None]
        start = jnp.clip(coords[axis_no][None, :] - (extent - 1) // 2, 0, limit - extent)
        column = token_coords[axis_no][None, None, :]
        here = (column >= start[:, :, None]) & (column < (start + extent)[:, :, None])
        inside = here if inside is None else inside & here
    return jnp.where(inside, 0.0, -jnp.inf).astype(jnp.float32)


def attend_rows(queries, first_tile, bias_ref, keys, values):
    count = queries.shape[0]
    tiles = count // TILE
    scores = lax.dot_general(
        queries, keys, (((1,), (1,)), ((), ())), preferred_element_type=jnp.float32
    )
    bias = bias_ref[0, first_tile : first_tile + tiles, :]
    scores = (scores.reshape(tiles, TILE, CLIP_TOK) + bias[:, None, :]).reshape(count, CLIP_TOK)
    peak = jnp.max(scores, axis=-1, keepdims=True)
    weights = jnp.exp2((scores - peak) * LOG2_SCALE).astype(jnp.bfloat16)
    blended = jnp.dot(weights, values, preferred_element_type=jnp.float32)
    return (blended[:, :HEAD_DIM] / blended[:, HEAD_DIM:]).astype(jnp.bfloat16)


def fill_values(values_ref, parts):
    at = 0
    for part in parts:
        rows = part.shape[0]
        values_ref[at : at + rows, :HEAD_DIM] = part
        at += rows
    values_ref[:, HEAD_DIM:] = jnp.ones((CLIP_TOK, HEAD_DIM), jnp.bfloat16)


def pair_kernel(place_ref, q_ref, k_ref, v_ref, other_ref, bias_ref, *rest):
    out_ref, keys_ref, values_ref = rest[-3:]
    half = CLIP_TOK // 2
    keys_ref[:half, :] = k_ref[...]
    keys_ref[half:, :] = other_ref[1]
    fill_values(values_ref, (v_ref[...], other_ref[2]))
    keys = keys_ref[...]
    values = values_ref[...]
    for side in range(2):
        base = pl.multiple_of((place_ref[0] if side == 0 else 1 - place_ref[0]) * half, half)
        for at in range(0, half, Q_ROWS):
            queries = q_ref[at : at + Q_ROWS, :] if side == 0 else other_ref[0, at : at + Q_ROWS, :]
            first_tile = (side * half + at) // TILE
            out_ref[pl.ds(base + at, Q_ROWS), :] = attend_rows(
                queries, first_tile, bias_ref, keys, values
            )


def whole_kernel(place_ref, q_ref, k_ref, v_ref, bias_ref, out_ref, values_ref):
    fill_values(values_ref, (v_ref[...],))
    keys = k_ref[...]
    values = values_ref[...]
    for at in range(0, CLIP_TOK, Q_ROWS):
        out_ref[at : at + Q_ROWS, :] = attend_rows(
            q_ref[at : at + Q_ROWS, :], at // TILE, bias_ref, keys, values
        )


def attention_cost(heads):
    pairs = heads * CLIP_TOK * CLIP_TOK
    return pl.CostEstimate(
        flops=pairs * HEAD_DIM * 6,
        bytes_accessed=heads * CLIP_TOK * HEAD_DIM * 8,
        transcendentals=pairs,
    )


def attend_pair(place, local_heads, call, query, key, value, other, bias, earlier, limit):
    half = CLIP_TOK // 2
    count = 2

    def head(i, place_ref):
        return place_ref[SEQ] * local_heads + local_head(call, place_ref[SEQ], i)

    own = pl.BlockSpec((half, HEAD_DIM), lambda i, p: (0, head(i, p)))
    return pl.pallas_call(
        pair_kernel,
        grid_spec=pltpu.PrefetchScalarGridSpec(
            num_scalar_prefetch=1,
            grid=(count,),
            in_specs=[
                own,
                own,
                own,
                pl.BlockSpec((3, half, HEAD_DIM), lambda i, p: (0, 0, i)),
                pl.BlockSpec((1, NT, CLIP_TOK), lambda i, p: (head(i, p), 0, 0)),
            ]
            + [pl.BlockSpec(memory_space=pl.ANY)] * len(earlier),
            out_specs=pl.BlockSpec((CLIP_TOK, HEAD_DIM), lambda i, p: (0, i)),
            scratch_shapes=[
                pltpu.VMEM((CLIP_TOK, HEAD_DIM), jnp.bfloat16),
                pltpu.VMEM((CLIP_TOK, 2 * HEAD_DIM), jnp.bfloat16),
            ],
        ),
        out_shape=jax.ShapeDtypeStruct((CLIP_TOK, count * HEAD_DIM), jnp.bfloat16),
        compiler_params=pltpu.CompilerParams(vmem_limit_bytes=limit),
        cost_estimate=SMALL_COST,
    )(place, query, key, value, other, bias, *earlier)


def attend_whole(place, query, key, value, bias):
    local_heads = query.shape[1] // HEAD_DIM
    column = pl.BlockSpec((CLIP_TOK, HEAD_DIM), lambda i, p: (0, i))
    return pl.pallas_call(
        whole_kernel,
        grid_spec=pltpu.PrefetchScalarGridSpec(
            num_scalar_prefetch=1,
            grid=(local_heads,),
            in_specs=[
                column,
                column,
                column,
                pl.BlockSpec((1, NT, CLIP_TOK), lambda i, p: (p[0] * local_heads + i, 0, 0)),
            ],
            out_specs=column,
            scratch_shapes=[pltpu.VMEM((CLIP_TOK, 2 * HEAD_DIM), jnp.bfloat16)],
        ),
        out_shape=jax.ShapeDtypeStruct(query.shape, jnp.bfloat16),
        compiler_params=pltpu.CompilerParams(vmem_limit_bytes=VMEM_LIMIT),
        cost_estimate=attention_cost(local_heads),
    )(place, query, key, value, bias)


def pack_kernel(place_ref, q_ref, k_ref, v_ref, *rest):
    out_ref = rest[-1]
    out_ref[0] = q_ref[...]
    out_ref[1] = k_ref[...]
    out_ref[2] = v_ref[...]


def local_head(call, side, part):
    first, by_side, step = call
    return first + by_side * side + step * part


def pack_partner(place, local_heads, call, query, key, value, earlier, limit):
    rows = query.shape[0]
    count = 2

    def head(i, place_ref):
        side = 1 - place_ref[SEQ]
        return side * local_heads + local_head(call, side, i)

    column = pl.BlockSpec((rows, HEAD_DIM), lambda i, p: (0, head(i, p)))
    return pl.pallas_call(
        pack_kernel,
        grid_spec=pltpu.PrefetchScalarGridSpec(
            num_scalar_prefetch=1,
            grid=(count,),
            in_specs=[column, column, column]
            + [pl.BlockSpec(memory_space=pl.ANY)] * len(earlier),
            out_specs=pl.BlockSpec((3, rows, HEAD_DIM), lambda i, p: (0, 0, i)),
        ),
        out_shape=jax.ShapeDtypeStruct((3, rows, count * HEAD_DIM), jnp.bfloat16),
        compiler_params=pltpu.CompilerParams(vmem_limit_bytes=limit),
        cost_estimate=SMALL_COST,
    )(place, query, key, value, *earlier)


def whole_block(shape):
    return pl.BlockSpec(shape, lambda i, p: (0,) * len(shape), pipeline_mode=pl.Buffered(1))


def gradient_kernel(place_ref, *refs, by_call):
    count = 4 if by_call else 2
    grad_ref = refs[count]
    sent_ref, kept_ref, rows_ref = refs[-3:]
    first_core = place_ref[CORE] == 0
    sides = (place_ref[SEQ], 1 - place_ref[SEQ])

    @pl.when(pl.program_id(0) == 0)
    def _():
        sent, kept = [], []
        for n in range(2):
            if by_call:
                one, two = refs[2 + n][...], refs[n][...]
            else:
                one, two = refs[n][:, :HEAD_DIM], refs[n][:, HEAD_DIM:]
            sent.append(jnp.where(first_core, one, two))
            kept.append(jnp.where(first_core, two, one))
        rows_ref[...] = jnp.concatenate(sent + kept, axis=1).T

    each = 2 if by_call else 1
    product = jnp.dot(rows_ref[...], grad_ref[...], preferred_element_type=jnp.float32)
    product = product.astype(jnp.bfloat16).reshape(4 * each, HEAD_DIM, grad_ref.shape[1])
    for n, side in enumerate(sides):
        sent_ref[pl.ds(each * side, each)] = product[each * n : each * (n + 1)]
        kept_ref[pl.ds(each * side, each)] = product[each * (2 + n) : each * (3 + n)]


def batch_gradient(place, sources, grad_proj, earlier=(), cost=SMALL_COST):
    by_call = len(sources) == 4
    heads = len(sources)
    rows, columns = grad_proj.shape
    step = columns // GRADIENT_STEPS
    out = pl.BlockSpec((heads, HEAD_DIM, step), lambda i, p: (0, 0, i))
    result = jax.ShapeDtypeStruct((heads, HEAD_DIM, columns), jnp.bfloat16)
    return pl.pallas_call(
        functools.partial(gradient_kernel, by_call=by_call),
        grid_spec=pltpu.PrefetchScalarGridSpec(
            num_scalar_prefetch=1,
            grid=(GRADIENT_STEPS,),
            in_specs=[whole_block(each.shape) for each in sources]
            + [pl.BlockSpec((rows, step), lambda i, p: (0, i))]
            + [pl.BlockSpec(memory_space=pl.ANY)] * len(earlier),
            out_specs=[out, out],
            scratch_shapes=[pltpu.VMEM((2 * heads * HEAD_DIM, rows), jnp.bfloat16)],
        ),
        out_shape=[result, result],
        compiler_params=pltpu.CompilerParams(vmem_limit_bytes=VMEM_GRADIENT),
        cost_estimate=cost,
    )(place, *sources, grad_proj, *earlier)


def sum_of(blocks):
    total = blocks[0].astype(jnp.float32)
    for block in blocks[1:]:
        total = total + block.astype(jnp.float32)
    return total


def level_step(place, bit, terms, earlier=(), cost=SMALL_COST):
    count = len(terms)
    pairs = terms[0].shape[0] // 2
    shape = (pairs,) + terms[0].shape[1:]
    block = (1,) + terms[0].shape[1:]
    keep = pl.BlockSpec(block, lambda i, p: (2 * i + p[bit], 0, 0))
    send = pl.BlockSpec(block, lambda i, p: (2 * i + 1 - p[bit], 0, 0))
    out = pl.BlockSpec(block, lambda i, p: (i, 0, 0))

    def kernel(place_ref, *refs):
        kept_ref, sent_ref = refs[-2:]
        kept_ref[...] = sum_of([ref[...] for ref in refs[:count]])
        sent_ref[...] = sum_of([ref[...] for ref in refs[count : 2 * count]]).astype(jnp.bfloat16)

    return pl.pallas_call(
        kernel,
        grid_spec=pltpu.PrefetchScalarGridSpec(
            num_scalar_prefetch=1,
            grid=(pairs,),
            in_specs=[keep] * count
            + [send] * count
            + [pl.BlockSpec(memory_space=pl.ANY)] * len(earlier),
            out_specs=[out, out],
        ),
        out_shape=[
            jax.ShapeDtypeStruct(shape, jnp.float32),
            jax.ShapeDtypeStruct(shape, jnp.bfloat16),
        ],
        compiler_params=pltpu.CompilerParams(vmem_limit_bytes=VMEM_SMALL),
        cost_estimate=cost,
    )(place, *terms, *terms, *earlier)


def reach_step(place, terms, earlier=()):
    count = len(terms)
    block = (1,) + terms[0].shape[1:]
    near = pl.BlockSpec(block, lambda i, p: (p[HIGH], 0, 0))
    far = pl.BlockSpec(block, lambda i, p: (1 - p[HIGH], 0, 0))

    def kernel(place_ref, *refs):
        kept_ref, near_ref, far_ref = refs[-3:]
        total = sum_of([ref[...] for ref in refs[:count]])
        kept_ref[...] = total
        near_ref[...] = total.astype(jnp.bfloat16)
        far_ref[...] = sum_of([ref[...] for ref in refs[count : 2 * count]]).astype(jnp.bfloat16)

    return pl.pallas_call(
        kernel,
        grid_spec=pltpu.PrefetchScalarGridSpec(
            num_scalar_prefetch=1,
            grid=(1,),
            in_specs=[near] * count
            + [far] * count
            + [pl.BlockSpec(memory_space=pl.ANY)] * len(earlier),
            out_specs=[whole_block(block)] * 3,
        ),
        out_shape=[
            jax.ShapeDtypeStruct(block, kind) for kind in (jnp.float32, jnp.bfloat16, jnp.bfloat16)
        ],
        compiler_params=pltpu.CompilerParams(vmem_limit_bytes=VMEM_SMALL),
        cost_estimate=SMALL_COST,
    )(place, *terms, *terms, *earlier)


def total_step(terms, earlier=(), kind=jnp.bfloat16):
    block = pl.BlockSpec((1,) + terms[0].shape[1:], lambda i: (i, 0, 0))

    def kernel(*refs):
        refs[-1][...] = sum_of([ref[...] for ref in refs[: len(terms)]]).astype(kind)

    return pl.pallas_call(
        kernel,
        grid=(terms[0].shape[0],),
        in_specs=[block] * len(terms) + [pl.BlockSpec(memory_space=pl.ANY)] * len(earlier),
        out_specs=block,
        out_shape=jax.ShapeDtypeStruct(terms[0].shape, kind),
        compiler_params=pltpu.CompilerParams(vmem_limit_bytes=VMEM_SMALL),
        cost_estimate=SMALL_COST,
    )(*terms, *earlier)


def choose_owned(place, *batches):
    block = batches[0][0].shape
    terms = [term for batch in batches for term in batch]

    def kernel(place_ref, *refs):
        alike = place_ref[CORE] == place_ref[X]
        outer = place_ref[LOW] == place_ref[HIGH]
        owned = (alike, ~alike & ~outer, ~alike & outer)
        at = 0
        for batch, mine in zip(batches, owned):
            chosen = refs[at : at + len(batch)]
            at += len(batch)

            @pl.when(mine)
            def _():
                refs[-1][...] = sum_of([ref[0] for ref in chosen])

    return pl.pallas_call(
        kernel,
        grid_spec=pltpu.PrefetchScalarGridSpec(
            num_scalar_prefetch=1,
            grid=(1,),
            in_specs=[whole_block(block)] * len(terms),
            out_specs=whole_block(block[1:]),
        ),
        out_shape=jax.ShapeDtypeStruct(block[1:], jnp.float32),
        compiler_params=pltpu.CompilerParams(vmem_limit_bytes=VMEM_GRADIENT),
        cost_estimate=SMALL_COST,
    )(place, *terms)


def join_columns(place, sources, calls, local_heads, earlier, cost):
    rows = sources[0].shape[0]
    step = rows // JOIN_STEPS
    shape = (rows, HEADS * HEAD_DIM)

    def kernel(place_ref, *refs):
        out_ref, done_ref = refs[-2:]
        done_ref[...] = jnp.zeros_like(done_ref)
        for n, source in enumerate(refs[: len(sources)]):
            side = place_ref[SEQ] if n % 2 == 0 else 1 - place_ref[SEQ]
            for part in range(2):
                head = side * local_heads + local_head(calls[n // 2], side, part)
                at = pl.multiple_of(head * HEAD_DIM, HEAD_DIM)
                out_ref[:, pl.ds(at, HEAD_DIM)] = source[:, part * HEAD_DIM : (part + 1) * HEAD_DIM]

    return pl.pallas_call(
        kernel,
        grid_spec=pltpu.PrefetchScalarGridSpec(
            num_scalar_prefetch=1,
            grid=(JOIN_STEPS,),
            in_specs=[pl.BlockSpec((step, each.shape[1]), lambda i, p: (i, 0)) for each in sources]
            + [pl.BlockSpec(memory_space=pl.ANY)] * len(earlier),
            out_specs=[
                pl.BlockSpec((step, shape[1]), lambda i, p: (i, 0)),
                pl.BlockSpec((8, HEAD_DIM), lambda i, p: (0, 0)),
            ],
        ),
        out_shape=[
            jax.ShapeDtypeStruct(shape, jnp.bfloat16),
            jax.ShapeDtypeStruct((8, HEAD_DIM), jnp.float32),
        ],
        compiler_params=pltpu.CompilerParams(vmem_limit_bytes=VMEM_SMALL),
        cost_estimate=cost,
    )(place, *sources, *earlier)


def project(attention, weight, gate, span, filled=(), earlier=(), cost=SMALL_COST):
    rows, depth = attention.shape
    columns = weight.shape[1]
    step = columns // PROJECT_STEPS
    first, steps = span[0], len(span)

    def kernel(attention_ref, weight_ref, gate_ref, *refs):
        out_ref, done_ref = refs[-2:]
        done_ref[...] = jnp.zeros_like(done_ref)
        total = jnp.dot(attention_ref[...], weight_ref[...], preferred_element_type=jnp.float32)
        out_ref[...] = (total * gate_ref[...]).astype(out_ref.dtype)

    return pl.pallas_call(
        kernel,
        grid=(steps,),
        in_specs=[
            pl.BlockSpec((rows, depth), lambda i: (0, 0), pipeline_mode=pl.Buffered(1)),
            pl.BlockSpec((depth, step), lambda i: (0, first + i)),
            pl.BlockSpec((1, step), lambda i: (0, first + i)),
        ]
        + [pl.BlockSpec(memory_space=pl.ANY)] * (len(filled) + len(earlier)),
        out_specs=[
            pl.BlockSpec((rows, step), lambda i: (0, first + i)),
            pl.BlockSpec((8, HEAD_DIM), lambda i: (0, 0)),
        ],
        out_shape=[
            jax.ShapeDtypeStruct((rows, columns), jnp.bfloat16),
            jax.ShapeDtypeStruct((8, HEAD_DIM), jnp.float32),
        ],
        input_output_aliases={3: 0} if filled else {},
        compiler_params=pltpu.CompilerParams(vmem_limit_bytes=VMEM_PROJECT),
        cost_estimate=cost,
    )(attention, weight, gate, *filled, *earlier)


def contract_tokens(columns, grad_proj, kind):
    return lax.dot_general(
        columns, grad_proj, (((0,), (0,)), ((), ())), preferred_element_type=jnp.float32
    ).astype(kind)


def after(value, *earlier):
    return lax.optimization_barrier((value,) + earlier)[0]


def dp_send(value, flip, sender):
    return lax.ppermute(value, "dp", [(i, i ^ flip) for i in range(HEADS) if sender(i)])


def same_bits(i):
    return (i >> 1 ^ i) & 1 == 0


def paired_device(query_rows, key_rows, value_rows, windows, out_weight, gate_scale, out_grad):
    index = lax.axis_index("dp")
    place = jnp.stack([lax.axis_index("seq")] + [index >> bit & 1 for bit in range(4)])
    place = lax.optimization_barrier(place.astype(jnp.int32))
    local_heads = HEADS // 2
    swap = [(0, 1), (1, 0)]
    calls = [(0, 0, 4), (3, 0, 4), (5, -4, 1), (1, 4, 1)]
    bias = window_bias(windows)
    weight = lax.all_gather(out_weight, "dp", axis=0, tiled=True)
    gate_row = gate_scale[0].astype(jnp.float32)
    grad_proj = (out_grad.astype(jnp.float32) * gate_row).astype(jnp.bfloat16)
    sources = (query_rows, key_rows, value_rows)

    def pack(n, limit, *earlier):
        return pack_partner(place, local_heads, calls[n], *sources, earlier, limit)

    def attention(n, other, *earlier, limit=VMEM_LIMIT):
        return attend_pair(place, local_heads, calls[n], *sources, other, bias, earlier, limit)

    def exchange(mine):
        return lax.ppermute(mine, "seq", swap)

    def core_step(*operands):
        sent, kept = batch_gradient(place, operands[:4], operands[4])
        return total_step([kept, dp_send(sent, 1, lambda i: True)])

    def apart(step, *operands):
        shapes = jax.eval_shape(step, *operands)
        return lax.cond(
            windows[0, 0] > 0,
            step,
            lambda *_: jax.tree.map(lambda leaf: jnp.zeros(leaf.shape, leaf.dtype), shapes),
            *operands,
        )

    packed0 = pack(0, VMEM_WHOLE)
    packed1 = pack(1, VMEM_WHOLE, packed0)
    packed2 = pack(2, VMEM_LIMIT, packed1)
    other0 = exchange(packed0)
    other1 = exchange(packed1)
    other2 = exchange(packed2)
    mine0 = attention(0, other0, packed2)
    theirs0 = exchange(mine0)
    mine1 = attention(1, other1, mine0)
    theirs1 = exchange(mine1)
    packed3 = pack(3, VMEM_LIMIT, mine1)
    other3 = exchange(packed3)
    mine2 = attention(2, other2, mine1, packed3)
    theirs2 = exchange(mine2)

    def unlike(i):
        return not same_bits(i)

    def outer(i):
        return unlike(i) and (i >> 2 ^ i >> 3) & 1 == 0

    def inner(i):
        return unlike(i) and (i >> 2 ^ i >> 3) & 1 == 1

    first = (mine0, theirs0, mine1, theirs1)
    total_a = apart(core_step, after(mine0, mine2, weight), *first[1:], grad_proj)
    across_a = dp_send(total_a, 2, unlike)
    mine3 = attention(3, other3, total_a, limit=VMEM_WHOLE)
    theirs3 = exchange(mine3)
    sent_b, kept_b = batch_gradient(place, (mine2, theirs2), grad_proj, (mine3,), LONG_COST)
    came_b = dp_send(sent_b, 1, lambda i: True)
    kept_a, sent_a = level_step(place, LOW, [total_a, across_a], (sent_b,), LONG_COST)
    low_a = dp_send(sent_a, 4, same_bits)
    total_b = total_step([kept_b, came_b], (sent_a,))
    across_b = dp_send(total_b, 2, same_bits)
    sent_c, kept_c = batch_gradient(place, (mine3, theirs3), grad_proj, (total_b,))
    came_c = dp_send(sent_c, 1, lambda i: True)
    results = (*first, mine2, theirs2, mine3, theirs3)
    columns, done = join_columns(place, results, calls, local_heads, (sent_c,), LONG_COST)
    total_c = total_step([kept_c, came_c], (done,))
    across_c = dp_send(total_c, 2, same_bits)
    kept_a, sent_a = level_step(place, HIGH, [kept_a, low_a], (total_c,))
    high_a = dp_send(sent_a, 8, same_bits)
    sent_b = total_step([total_b, across_b], (sent_a,))
    low_b = dp_send(sent_b, 4, outer)
    gate = gate_row[None]
    out, done = project(columns, weight, gate, range(3), (), (sent_b,))
    kept_c, near_c, far_c = reach_step(place, [total_c, across_c], (done,))
    reached_c = dp_send(far_c, 8, inner), dp_send(far_c, 12, outer), dp_send(near_c, 4, inner)
    kept_b, sent_b = level_step(place, HIGH, [total_b, across_b, low_b], (near_c,))
    high_b = dp_send(sent_b, 12, inner)
    last = range(3, PROJECT_STEPS)
    block_out, done = project(columns, weight, gate, last, (out,), (sent_b,), LONG_COST)
    final_a = total_step([kept_a, high_a], (done,), jnp.float32)
    weight_grad = choose_owned(place, (final_a,), (kept_b, high_b), (kept_c, *reached_c))
    return (block_out, weight_grad)


def general_device(query_rows, key_rows, value_rows, windows, out_weight, gate_scale, out_grad):
    query, key, value = (
        lax.all_to_all(rows, "seq", split_axis=1, concat_axis=0, tiled=True)
        for rows in (query_rows, key_rows, value_rows)
    )
    place = lax.axis_index("seq").reshape(1).astype(jnp.int32)
    mine = attend_whole(place, query, key, value, window_bias(windows))
    columns = lax.all_gather(mine, "seq", axis=1, tiled=True)
    weight = lax.all_gather(out_weight, "dp", axis=0, tiled=True)
    gate_row = gate_scale[0].astype(jnp.float32)
    projected = jnp.dot(columns, weight, preferred_element_type=jnp.float32)
    block_out = (projected * gate_row).astype(jnp.bfloat16)
    grad_proj = (out_grad.astype(jnp.float32) * gate_row).astype(jnp.bfloat16)
    weight_grad = lax.psum_scatter(
        contract_tokens(columns, grad_proj, jnp.float32), "dp", scatter_dimension=0, tiled=True
    )
    return (block_out, weight_grad)


def solution(mesh):
    paired = mesh.shape["seq"] == 2 and mesh.shape["dp"] == HEADS
    return jax.shard_map(
        paired_device if paired else general_device,
        mesh=mesh,
        in_specs=(
            P(("dp", "seq"), None),
            P(("dp", "seq"), None),
            P(("dp", "seq"), None),
            P(),
            P("dp", "seq"),
            P("dp", "seq"),
            P("dp", "seq"),
        ),
        out_specs=(P("dp", "seq"), P("dp", "seq")),
        check_vma=False,
    )
```

```python
import functools
import math

import jax
import jax.numpy as jnp
import numpy as np
from jax import lax
from jax.experimental import pallas as pl
from jax.experimental.pallas import tpu as pltpu
from jax.sharding import PartitionSpec as P

HEADS = 16
HEAD_DIM = 128
GH = 3
GW = 4
GT = 2
TILE = 48
NT = 24
CLIP_TOK = NT * TILE
Q_ROWS = GW * TILE
LOG2_SCALE = math.log2(math.e) / math.sqrt(HEAD_DIM)
VMEM_LIMIT = 16 * 1024 * 1024
VMEM_GRADIENT = 20 * 1024 * 1024
VMEM_PROJECT = 24 * 1024 * 1024
PROJECT_STEPS = 6
GRADIENT_STEPS = 3
JOIN_STEPS = 4
SEQ, CORE, X, LOW, HIGH = range(5)
VMEM_WHOLE = 60 * 1024 * 1024
VMEM_SMALL = 12 * 1024 * 1024
SMALL_COST = pl.CostEstimate(flops=1, bytes_accessed=1, transcendentals=0)
LONG_COST = pl.CostEstimate(flops=2 * 10**10, bytes_accessed=2 * 10**7, transcendentals=0)


def window_bias(windows):
    tile_id = np.arange(NT)
    coords = np.stack([tile_id // (GH * GW), tile_id // GW % GH, tile_id % GW]).astype(np.int32)
    token_coords = np.repeat(coords, TILE, axis=1)
    inside = None
    for axis_no, limit in enumerate((GT, GH, GW)):
        extent = jnp.minimum(windows[:, axis_no], limit)[:, None]
        start = jnp.clip(coords[axis_no][None, :] - (extent - 1) // 2, 0, limit - extent)
        column = token_coords[axis_no][None, None, :]
        here = (column >= start[:, :, None]) & (column < (start + extent)[:, :, None])
        inside = here if inside is None else inside & here
    return jnp.where(inside, 0.0, -jnp.inf).astype(jnp.float32)


def attend_rows(queries, first_tile, bias_ref, keys, values):
    count = queries.shape[0]
    tiles = count // TILE
    scores = lax.dot_general(
        queries, keys, (((1,), (1,)), ((), ())), preferred_element_type=jnp.float32
    )
    bias = bias_ref[0, first_tile : first_tile + tiles, :]
    scores = (scores.reshape(tiles, TILE, CLIP_TOK) + bias[:, None, :]).reshape(count, CLIP_TOK)
    peak = jnp.max(scores, axis=-1, keepdims=True)
    weights = jnp.exp2((scores - peak) * LOG2_SCALE).astype(jnp.bfloat16)
    blended = jnp.dot(weights, values, preferred_element_type=jnp.float32)
    return (blended[:, :HEAD_DIM] / blended[:, HEAD_DIM:]).astype(jnp.bfloat16)


def fill_values(values_ref, parts):
    at = 0
    for part in parts:
        rows = part.shape[0]
        values_ref[at : at + rows, :HEAD_DIM] = part
        at += rows
    values_ref[:, HEAD_DIM:] = jnp.ones((CLIP_TOK, HEAD_DIM), jnp.bfloat16)


def pair_kernel(place_ref, q_ref, k_ref, v_ref, other_ref, bias_ref, *rest):
    out_ref, keys_ref, values_ref = rest[-3:]
    half = CLIP_TOK // 2
    keys_ref[:half, :] = k_ref[...]
    keys_ref[half:, :] = other_ref[1]
    fill_values(values_ref, (v_ref[...], other_ref[2]))
    keys = keys_ref[...]
    values = values_ref[...]
    for side in range(2):
        base = pl.multiple_of((place_ref[0] if side == 0 else 1 - place_ref[0]) * half, half)
        for at in range(0, half, Q_ROWS):
            queries = q_ref[at : at + Q_ROWS, :] if side == 0 else other_ref[0, at : at + Q_ROWS, :]
            first_tile = (side * half + at) // TILE
            out_ref[pl.ds(base + at, Q_ROWS), :] = attend_rows(
                queries, first_tile, bias_ref, keys, values
            )


def whole_kernel(place_ref, q_ref, k_ref, v_ref, bias_ref, out_ref, values_ref):
    fill_values(values_ref, (v_ref[...],))
    keys = k_ref[...]
    values = values_ref[...]
    for at in range(0, CLIP_TOK, Q_ROWS):
        out_ref[at : at + Q_ROWS, :] = attend_rows(
            q_ref[at : at + Q_ROWS, :], at // TILE, bias_ref, keys, values
        )


def attention_cost(heads):
    pairs = heads * CLIP_TOK * CLIP_TOK
    return pl.CostEstimate(
        flops=pairs * HEAD_DIM * 6,
        bytes_accessed=heads * CLIP_TOK * HEAD_DIM * 8,
        transcendentals=pairs,
    )


def attend_pair(place, local_heads, call, query, key, value, other, bias, earlier, limit):
    half = CLIP_TOK // 2
    count = 2

    def head(i, place_ref):
        return place_ref[SEQ] * local_heads + local_head(call, place_ref[SEQ], i)

    own = pl.BlockSpec((half, HEAD_DIM), lambda i, p: (0, head(i, p)))
    return pl.pallas_call(
        pair_kernel,
        grid_spec=pltpu.PrefetchScalarGridSpec(
            num_scalar_prefetch=1,
            grid=(count,),
            in_specs=[
                own,
                own,
                own,
                pl.BlockSpec((3, half, HEAD_DIM), lambda i, p: (0, 0, i)),
                pl.BlockSpec((1, NT, CLIP_TOK), lambda i, p: (head(i, p), 0, 0)),
            ]
            + [pl.BlockSpec(memory_space=pl.ANY)] * len(earlier),
            out_specs=pl.BlockSpec((CLIP_TOK, HEAD_DIM), lambda i, p: (0, i)),
            scratch_shapes=[
                pltpu.VMEM((CLIP_TOK, HEAD_DIM), jnp.bfloat16),
                pltpu.VMEM((CLIP_TOK, 2 * HEAD_DIM), jnp.bfloat16),
            ],
        ),
        out_shape=jax.ShapeDtypeStruct((CLIP_TOK, count * HEAD_DIM), jnp.bfloat16),
        compiler_params=pltpu.CompilerParams(vmem_limit_bytes=limit),
        cost_estimate=SMALL_COST,
    )(place, query, key, value, other, bias, *earlier)


def attend_whole(place, query, key, value, bias):
    local_heads = query.shape[1] // HEAD_DIM
    column = pl.BlockSpec((CLIP_TOK, HEAD_DIM), lambda i, p: (0, i))
    return pl.pallas_call(
        whole_kernel,
        grid_spec=pltpu.PrefetchScalarGridSpec(
            num_scalar_prefetch=1,
            grid=(local_heads,),
            in_specs=[
                column,
                column,
                column,
                pl.BlockSpec((1, NT, CLIP_TOK), lambda i, p: (p[0] * local_heads + i, 0, 0)),
            ],
            out_specs=column,
            scratch_shapes=[pltpu.VMEM((CLIP_TOK, 2 * HEAD_DIM), jnp.bfloat16)],
        ),
        out_shape=jax.ShapeDtypeStruct(query.shape, jnp.bfloat16),
        compiler_params=pltpu.CompilerParams(vmem_limit_bytes=VMEM_LIMIT),
        cost_estimate=attention_cost(local_heads),
    )(place, query, key, value, bias)


def pack_kernel(place_ref, q_ref, k_ref, v_ref, *rest):
    out_ref = rest[-1]
    out_ref[0] = q_ref[...]
    out_ref[1] = k_ref[...]
    out_ref[2] = v_ref[...]


def local_head(call, side, part):
    first, by_side, step = call
    return first + by_side * side + step * part


def pack_partner(place, local_heads, call, query, key, value, earlier, limit):
    rows = query.shape[0]
    count = 2

    def head(i, place_ref):
        side = 1 - place_ref[SEQ]
        return side * local_heads + local_head(call, side, i)

    column = pl.BlockSpec((rows, HEAD_DIM), lambda i, p: (0, head(i, p)))
    return pl.pallas_call(
        pack_kernel,
        grid_spec=pltpu.PrefetchScalarGridSpec(
            num_scalar_prefetch=1,
            grid=(count,),
            in_specs=[column, column, column]
            + [pl.BlockSpec(memory_space=pl.ANY)] * len(earlier),
            out_specs=pl.BlockSpec((3, rows, HEAD_DIM), lambda i, p: (0, 0, i)),
        ),
        out_shape=jax.ShapeDtypeStruct((3, rows, count * HEAD_DIM), jnp.bfloat16),
        compiler_params=pltpu.CompilerParams(vmem_limit_bytes=limit),
        cost_estimate=SMALL_COST,
    )(place, query, key, value, *earlier)


def whole_block(shape):
    return pl.BlockSpec(shape, lambda i, p: (0,) * len(shape), pipeline_mode=pl.Buffered(1))


def gradient_kernel(place_ref, *refs, by_call):
    count = 4 if by_call else 2
    grad_ref = refs[count]
    sent_ref, kept_ref, rows_ref = refs[-3:]
    first_core = place_ref[CORE] == 0
    sides = (place_ref[SEQ], 1 - place_ref[SEQ])

    @pl.when(pl.program_id(0) == 0)
    def _():
        sent, kept = [], []
        for n in range(2):
            if by_call:
                one, two = refs[2 + n][...], refs[n][...]
            else:
                one, two = refs[n][:, :HEAD_DIM], refs[n][:, HEAD_DIM:]
            sent.append(jnp.where(first_core, one, two))
            kept.append(jnp.where(first_core, two, one))
        rows_ref[...] = jnp.concatenate(sent + kept, axis=1).T

    each = 2 if by_call else 1
    product = jnp.dot(rows_ref[...], grad_ref[...], preferred_element_type=jnp.float32)
    product = product.astype(jnp.bfloat16).reshape(4 * each, HEAD_DIM, grad_ref.shape[1])
    for n, side in enumerate(sides):
        sent_ref[pl.ds(each * side, each)] = product[each * n : each * (n + 1)]
        kept_ref[pl.ds(each * side, each)] = product[each * (2 + n) : each * (3 + n)]


def batch_gradient(place, sources, grad_proj, earlier=(), cost=SMALL_COST):
    by_call = len(sources) == 4
    heads = len(sources)
    rows, columns = grad_proj.shape
    step = columns // GRADIENT_STEPS
    out = pl.BlockSpec((heads, HEAD_DIM, step), lambda i, p: (0, 0, i))
    result = jax.ShapeDtypeStruct((heads, HEAD_DIM, columns), jnp.bfloat16)
    return pl.pallas_call(
        functools.partial(gradient_kernel, by_call=by_call),
        grid_spec=pltpu.PrefetchScalarGridSpec(
            num_scalar_prefetch=1,
            grid=(GRADIENT_STEPS,),
            in_specs=[whole_block(each.shape) for each in sources]
            + [pl.BlockSpec((rows, step), lambda i, p: (0, i))]
            + [pl.BlockSpec(memory_space=pl.ANY)] * len(earlier),
            out_specs=[out, out],
            scratch_shapes=[pltpu.VMEM((2 * heads * HEAD_DIM, rows), jnp.bfloat16)],
        ),
        out_shape=[result, result],
        compiler_params=pltpu.CompilerParams(vmem_limit_bytes=VMEM_GRADIENT),
        cost_estimate=cost,
    )(place, *sources, grad_proj, *earlier)


def sum_of(blocks):
    total = blocks[0].astype(jnp.float32)
    for block in blocks[1:]:
        total = total + block.astype(jnp.float32)
    return total


def level_step(place, bit, terms, earlier=(), cost=SMALL_COST):
    count = len(terms)
    pairs = terms[0].shape[0] // 2
    shape = (pairs,) + terms[0].shape[1:]
    block = (1,) + terms[0].shape[1:]
    keep = pl.BlockSpec(block, lambda i, p: (2 * i + p[bit], 0, 0))
    send = pl.BlockSpec(block, lambda i, p: (2 * i + 1 - p[bit], 0, 0))
    out = pl.BlockSpec(block, lambda i, p: (i, 0, 0))

    def kernel(place_ref, *refs):
        kept_ref, sent_ref = refs[-2:]
        kept_ref[...] = sum_of([ref[...] for ref in refs[:count]])
        sent_ref[...] = sum_of([ref[...] for ref in refs[count : 2 * count]]).astype(jnp.bfloat16)

    return pl.pallas_call(
        kernel,
        grid_spec=pltpu.PrefetchScalarGridSpec(
            num_scalar_prefetch=1,
            grid=(pairs,),
            in_specs=[keep] * count
            + [send] * count
            + [pl.BlockSpec(memory_space=pl.ANY)] * len(earlier),
            out_specs=[out, out],
        ),
        out_shape=[
            jax.ShapeDtypeStruct(shape, jnp.float32),
            jax.ShapeDtypeStruct(shape, jnp.bfloat16),
        ],
        compiler_params=pltpu.CompilerParams(vmem_limit_bytes=VMEM_SMALL),
        cost_estimate=cost,
    )(place, *terms, *terms, *earlier)


def reach_step(place, terms, earlier=()):
    count = len(terms)
    block = (1,) + terms[0].shape[1:]
    near = pl.BlockSpec(block, lambda i, p: (p[HIGH], 0, 0))
    far = pl.BlockSpec(block, lambda i, p: (1 - p[HIGH], 0, 0))

    def kernel(place_ref, *refs):
        kept_ref, near_ref, far_ref = refs[-3:]
        total = sum_of([ref[...] for ref in refs[:count]])
        kept_ref[...] = total
        near_ref[...] = total.astype(jnp.bfloat16)
        far_ref[...] = sum_of([ref[...] for ref in refs[count : 2 * count]]).astype(jnp.bfloat16)

    return pl.pallas_call(
        kernel,
        grid_spec=pltpu.PrefetchScalarGridSpec(
            num_scalar_prefetch=1,
            grid=(1,),
            in_specs=[near] * count
            + [far] * count
            + [pl.BlockSpec(memory_space=pl.ANY)] * len(earlier),
            out_specs=[whole_block(block)] * 3,
        ),
        out_shape=[
            jax.ShapeDtypeStruct(block, kind) for kind in (jnp.float32, jnp.bfloat16, jnp.bfloat16)
        ],
        compiler_params=pltpu.CompilerParams(vmem_limit_bytes=VMEM_SMALL),
        cost_estimate=SMALL_COST,
    )(place, *terms, *terms, *earlier)


def total_step(terms, earlier=(), kind=jnp.bfloat16):
    block = pl.BlockSpec((1,) + terms[0].shape[1:], lambda i: (i, 0, 0))

    def kernel(*refs):
        refs[-1][...] = sum_of([ref[...] for ref in refs[: len(terms)]]).astype(kind)

    return pl.pallas_call(
        kernel,
        grid=(terms[0].shape[0],),
        in_specs=[block] * len(terms) + [pl.BlockSpec(memory_space=pl.ANY)] * len(earlier),
        out_specs=block,
        out_shape=jax.ShapeDtypeStruct(terms[0].shape, kind),
        compiler_params=pltpu.CompilerParams(vmem_limit_bytes=VMEM_SMALL),
        cost_estimate=SMALL_COST,
    )(*terms, *earlier)


def choose_owned(place, *batches):
    block = batches[0][0].shape
    terms = [term for batch in batches for term in batch]

    def kernel(place_ref, *refs):
        alike = place_ref[CORE] == place_ref[X]
        outer = place_ref[LOW] == place_ref[HIGH]
        owned = (alike, ~alike & ~outer, ~alike & outer)
        at = 0
        for batch, mine in zip(batches, owned):
            chosen = refs[at : at + len(batch)]
            at += len(batch)

            @pl.when(mine)
            def _():
                refs[-1][...] = sum_of([ref[0] for ref in chosen])

    return pl.pallas_call(
        kernel,
        grid_spec=pltpu.PrefetchScalarGridSpec(
            num_scalar_prefetch=1,
            grid=(1,),
            in_specs=[whole_block(block)] * len(terms),
            out_specs=whole_block(block[1:]),
        ),
        out_shape=jax.ShapeDtypeStruct(block[1:], jnp.float32),
        compiler_params=pltpu.CompilerParams(vmem_limit_bytes=VMEM_GRADIENT),
        cost_estimate=SMALL_COST,
    )(place, *terms)


def join_columns(place, sources, calls, local_heads, earlier, cost):
    rows = sources[0].shape[0]
    step = rows // JOIN_STEPS
    shape = (rows, HEADS * HEAD_DIM)

    def kernel(place_ref, *refs):
        out_ref, done_ref = refs[-2:]
        done_ref[...] = jnp.zeros_like(done_ref)
        for n, source in enumerate(refs[: len(sources)]):
            side = place_ref[SEQ] if n % 2 == 0 else 1 - place_ref[SEQ]
            for part in range(2):
                head = side * local_heads + local_head(calls[n // 2], side, part)
                at = pl.multiple_of(head * HEAD_DIM, HEAD_DIM)
                out_ref[:, pl.ds(at, HEAD_DIM)] = source[:, part * HEAD_DIM : (part + 1) * HEAD_DIM]

    return pl.pallas_call(
        kernel,
        grid_spec=pltpu.PrefetchScalarGridSpec(
            num_scalar_prefetch=1,
            grid=(JOIN_STEPS,),
            in_specs=[pl.BlockSpec((step, each.shape[1]), lambda i, p: (i, 0)) for each in sources]
            + [pl.BlockSpec(memory_space=pl.ANY)] * len(earlier),
            out_specs=[
                pl.BlockSpec((step, shape[1]), lambda i, p: (i, 0)),
                pl.BlockSpec((8, HEAD_DIM), lambda i, p: (0, 0)),
            ],
        ),
        out_shape=[
            jax.ShapeDtypeStruct(shape, jnp.bfloat16),
            jax.ShapeDtypeStruct((8, HEAD_DIM), jnp.float32),
        ],
        compiler_params=pltpu.CompilerParams(vmem_limit_bytes=VMEM_SMALL),
        cost_estimate=cost,
    )(place, *sources, *earlier)


def project(attention, weight, gate, span, filled=(), earlier=(), cost=SMALL_COST):
    rows, depth = attention.shape
    columns = weight.shape[1]
    step = columns // PROJECT_STEPS
    first, steps = span[0], len(span)

    def kernel(attention_ref, weight_ref, gate_ref, *refs):
        out_ref, done_ref = refs[-2:]
        done_ref[...] = jnp.zeros_like(done_ref)
        total = jnp.dot(attention_ref[...], weight_ref[...], preferred_element_type=jnp.float32)
        out_ref[...] = (total * gate_ref[...]).astype(out_ref.dtype)

    return pl.pallas_call(
        kernel,
        grid=(steps,),
        in_specs=[
            pl.BlockSpec((rows, depth), lambda i: (0, 0), pipeline_mode=pl.Buffered(1)),
            pl.BlockSpec((depth, step), lambda i: (0, first + i)),
            pl.BlockSpec((1, step), lambda i: (0, first + i)),
        ]
        + [pl.BlockSpec(memory_space=pl.ANY)] * (len(filled) + len(earlier)),
        out_specs=[
            pl.BlockSpec((rows, step), lambda i: (0, first + i)),
            pl.BlockSpec((8, HEAD_DIM), lambda i: (0, 0)),
        ],
        out_shape=[
            jax.ShapeDtypeStruct((rows, columns), jnp.bfloat16),
            jax.ShapeDtypeStruct((8, HEAD_DIM), jnp.float32),
        ],
        input_output_aliases={3: 0} if filled else {},
        compiler_params=pltpu.CompilerParams(vmem_limit_bytes=VMEM_PROJECT),
        cost_estimate=cost,
    )(attention, weight, gate, *filled, *earlier)


def contract_tokens(columns, grad_proj, kind):
    return lax.dot_general(
        columns, grad_proj, (((0,), (0,)), ((), ())), preferred_element_type=jnp.float32
    ).astype(kind)


def after(value, *earlier):
    return lax.optimization_barrier((value,) + earlier)[0]


def dp_send(value, flip, sender):
    return lax.ppermute(value, "dp", [(i, i ^ flip) for i in range(HEADS) if sender(i)])


def same_bits(i):
    return (i >> 1 ^ i) & 1 == 0


def paired_device(query_rows, key_rows, value_rows, windows, out_weight, gate_scale, out_grad):
    index = lax.axis_index("dp")
    place = jnp.stack([lax.axis_index("seq")] + [index >> bit & 1 for bit in range(4)])
    place = lax.optimization_barrier(place.astype(jnp.int32))
    local_heads = HEADS // 2
    swap = [(0, 1), (1, 0)]
    calls = [(0, 0, 4), (3, 0, 4), (5, -4, 1), (1, 4, 1)]
    bias = window_bias(windows)
    weight = lax.all_gather(out_weight, "dp", axis=0, tiled=True)
    gate_row = gate_scale[0].astype(jnp.float32)
    grad_proj = (out_grad.astype(jnp.float32) * gate_row).astype(jnp.bfloat16)
    sources = (query_rows, key_rows, value_rows)

    def pack(n, limit, *earlier):
        return pack_partner(place, local_heads, calls[n], *sources, earlier, limit)

    def attention(n, other, *earlier, limit=VMEM_LIMIT):
        return attend_pair(place, local_heads, calls[n], *sources, other, bias, earlier, limit)

    def exchange(mine):
        return lax.ppermute(mine, "seq", swap)

    def core_step(*operands):
        sent, kept = batch_gradient(place, operands[:4], operands[4])
        return total_step([kept, dp_send(sent, 1, lambda i: True)])

    def apart(step, *operands):
        shapes = jax.eval_shape(step, *operands)
        return lax.cond(
            windows[0, 0] > 0,
            step,
            lambda *_: jax.tree.map(lambda leaf: jnp.zeros(leaf.shape, leaf.dtype), shapes),
            *operands,
        )

    packed0 = pack(0, VMEM_WHOLE)
    packed1 = pack(1, VMEM_WHOLE, packed0)
    packed2 = pack(2, VMEM_LIMIT, packed1)
    other0 = exchange(packed0)
    other1 = exchange(packed1)
    other2 = exchange(packed2)
    mine0 = attention(0, other0, packed2)
    theirs0 = exchange(mine0)
    mine1 = attention(1, other1, mine0)
    theirs1 = exchange(mine1)
    packed3 = pack(3, VMEM_LIMIT, mine1)
    other3 = exchange(packed3)
    mine2 = attention(2, other2, mine1, packed3)
    theirs2 = exchange(mine2)

    def unlike(i):
        return not same_bits(i)

    def outer(i):
        return unlike(i) and (i >> 2 ^ i >> 3) & 1 == 0

    def inner(i):
        return unlike(i) and (i >> 2 ^ i >> 3) & 1 == 1

    first = (mine0, theirs0, mine1, theirs1)
    total_a = apart(core_step, after(mine0, mine2, weight), *first[1:], grad_proj)
    across_a = dp_send(total_a, 2, unlike)
    mine3 = attention(3, other3, total_a, limit=VMEM_WHOLE)
    theirs3 = exchange(mine3)
    sent_b, kept_b = batch_gradient(place, (mine2, theirs2), grad_proj, (mine3,), LONG_COST)
    came_b = dp_send(sent_b, 1, lambda i: True)
    kept_a, sent_a = level_step(place, LOW, [total_a, across_a], (sent_b,), LONG_COST)
    low_a = dp_send(sent_a, 4, same_bits)
    total_b = total_step([kept_b, came_b], (sent_a,))
    across_b = dp_send(total_b, 2, same_bits)
    sent_c, kept_c = batch_gradient(place, (mine3, theirs3), grad_proj, (total_b,))
    came_c = dp_send(sent_c, 1, lambda i: True)
    results = (*first, mine2, theirs2, mine3, theirs3)
    columns, done = join_columns(place, results, calls, local_heads, (sent_c,), LONG_COST)
    total_c = total_step([kept_c, came_c], (done,))
    across_c = dp_send(total_c, 2, same_bits)
    kept_a, sent_a = level_step(place, HIGH, [kept_a, low_a], (total_c,))
    high_a = dp_send(sent_a, 8, same_bits)
    sent_b = total_step([total_b, across_b], (sent_a,))
    low_b = dp_send(sent_b, 4, outer)
    gate = gate_row[None]
    out, done = project(columns, weight, gate, range(3), (), (sent_b,))
    kept_c, near_c, far_c = reach_step(place, [total_c, across_c], (done,))
    reached_c = dp_send(near_c, 4, inner), dp_send(far_c, 8, inner), dp_send(far_c, 12, outer)
    kept_b, sent_b = level_step(place, HIGH, [total_b, across_b, low_b], (near_c,))
    high_b = dp_send(sent_b, 12, inner)
    last = range(3, PROJECT_STEPS)
    block_out, done = project(columns, weight, gate, last, (out,), (sent_b,), LONG_COST)
    final_a = total_step([kept_a, high_a], (done,), jnp.float32)
    weight_grad = choose_owned(place, (final_a,), (kept_b, high_b), (kept_c, *reached_c))
    return (block_out, weight_grad)


def general_device(query_rows, key_rows, value_rows, windows, out_weight, gate_scale, out_grad):
    query, key, value = (
        lax.all_to_all(rows, "seq", split_axis=1, concat_axis=0, tiled=True)
        for rows in (query_rows, key_rows, value_rows)
    )
    place = lax.axis_index("seq").reshape(1).astype(jnp.int32)
    mine = attend_whole(place, query, key, value, window_bias(windows))
    columns = lax.all_gather(mine, "seq", axis=1, tiled=True)
    weight = lax.all_gather(out_weight, "dp", axis=0, tiled=True)
    gate_row = gate_scale[0].astype(jnp.float32)
    projected = jnp.dot(columns, weight, preferred_element_type=jnp.float32)
    block_out = (projected * gate_row).astype(jnp.bfloat16)
    grad_proj = (out_grad.astype(jnp.float32) * gate_row).astype(jnp.bfloat16)
    weight_grad = lax.psum_scatter(
        contract_tokens(columns, grad_proj, jnp.float32), "dp", scatter_dimension=0, tiled=True
    )
    return (block_out, weight_grad)


def solution(mesh):
    paired = mesh.shape["seq"] == 2 and mesh.shape["dp"] == HEADS
    return jax.shard_map(
        paired_device if paired else general_device,
        mesh=mesh,
        in_specs=(
            P(("dp", "seq"), None),
            P(("dp", "seq"), None),
            P(("dp", "seq"), None),
            P(),
            P("dp", "seq"),
            P("dp", "seq"),
            P("dp", "seq"),
        ),
        out_specs=(P("dp", "seq"), P("dp", "seq")),
        check_vma=False,
    )
```

```python
import functools
import math

import jax
import jax.numpy as jnp
import numpy as np
from jax import lax
from jax.experimental import pallas as pl
from jax.experimental.pallas import tpu as pltpu
from jax.sharding import PartitionSpec as P

HEADS = 16
HEAD_DIM = 128
GH = 3
GW = 4
GT = 2
TILE = 48
NT = 24
CLIP_TOK = NT * TILE
Q_ROWS = GW * TILE
LOG2_SCALE = math.log2(math.e) / math.sqrt(HEAD_DIM)
VMEM_LIMIT = 16 * 1024 * 1024
VMEM_GRADIENT = 20 * 1024 * 1024
VMEM_PROJECT = 24 * 1024 * 1024
PROJECT_STEPS = 6
GRADIENT_STEPS = 3
JOIN_STEPS = 8
SEQ, CORE, X, LOW, HIGH = range(5)
VMEM_WHOLE = 60 * 1024 * 1024
VMEM_SMALL = 12 * 1024 * 1024
SMALL_COST = pl.CostEstimate(flops=1, bytes_accessed=1, transcendentals=0)
LONG_COST = pl.CostEstimate(flops=2 * 10**10, bytes_accessed=2 * 10**7, transcendentals=0)


def window_bias(windows):
    tile_id = np.arange(NT)
    coords = np.stack([tile_id // (GH * GW), tile_id // GW % GH, tile_id % GW]).astype(np.int32)
    token_coords = np.repeat(coords, TILE, axis=1)
    inside = None
    for axis_no, limit in enumerate((GT, GH, GW)):
        extent = jnp.minimum(windows[:, axis_no], limit)[:, None]
        start = jnp.clip(coords[axis_no][None, :] - (extent - 1) // 2, 0, limit - extent)
        column = token_coords[axis_no][None, None, :]
        here = (column >= start[:, :, None]) & (column < (start + extent)[:, :, None])
        inside = here if inside is None else inside & here
    return jnp.where(inside, 0.0, -jnp.inf).astype(jnp.float32)


def attend_rows(queries, first_tile, bias_ref, keys, values):
    count = queries.shape[0]
    tiles = count // TILE
    scores = lax.dot_general(
        queries, keys, (((1,), (1,)), ((), ())), preferred_element_type=jnp.float32
    )
    bias = bias_ref[0, first_tile : first_tile + tiles, :]
    scores = (scores.reshape(tiles, TILE, CLIP_TOK) + bias[:, None, :]).reshape(count, CLIP_TOK)
    peak = jnp.max(scores, axis=-1, keepdims=True)
    weights = jnp.exp2((scores - peak) * LOG2_SCALE).astype(jnp.bfloat16)
    blended = jnp.dot(weights, values, preferred_element_type=jnp.float32)
    return (blended[:, :HEAD_DIM] / blended[:, HEAD_DIM:]).astype(jnp.bfloat16)


def fill_values(values_ref, parts):
    at = 0
    for part in parts:
        rows = part.shape[0]
        values_ref[at : at + rows, :HEAD_DIM] = part
        at += rows
    values_ref[:, HEAD_DIM:] = jnp.ones((CLIP_TOK, HEAD_DIM), jnp.bfloat16)


def pair_kernel(place_ref, q_ref, k_ref, v_ref, other_ref, bias_ref, *rest):
    out_ref, keys_ref, values_ref = rest[-3:]
    half = CLIP_TOK // 2
    keys_ref[:half, :] = k_ref[...]
    keys_ref[half:, :] = other_ref[1]
    fill_values(values_ref, (v_ref[...], other_ref[2]))
    keys = keys_ref[...]
    values = values_ref[...]
    for side in range(2):
        base = pl.multiple_of((place_ref[0] if side == 0 else 1 - place_ref[0]) * half, half)
        for at in range(0, half, Q_ROWS):
            queries = q_ref[at : at + Q_ROWS, :] if side == 0 else other_ref[0, at : at + Q_ROWS, :]
            first_tile = (side * half + at) // TILE
            out_ref[pl.ds(base + at, Q_ROWS), :] = attend_rows(
                queries, first_tile, bias_ref, keys, values
            )


def whole_kernel(place_ref, q_ref, k_ref, v_ref, bias_ref, out_ref, values_ref):
    fill_values(values_ref, (v_ref[...],))
    keys = k_ref[...]
    values = values_ref[...]
    for at in range(0, CLIP_TOK, Q_ROWS):
        out_ref[at : at + Q_ROWS, :] = attend_rows(
            q_ref[at : at + Q_ROWS, :], at // TILE, bias_ref, keys, values
        )


def attention_cost(heads):
    pairs = heads * CLIP_TOK * CLIP_TOK
    return pl.CostEstimate(
        flops=pairs * HEAD_DIM * 6,
        bytes_accessed=heads * CLIP_TOK * HEAD_DIM * 8,
        transcendentals=pairs,
    )


def attend_pair(place, local_heads, call, query, key, value, other, bias, earlier, limit):
    half = CLIP_TOK // 2
    count = 2

    def head(i, place_ref):
        return place_ref[SEQ] * local_heads + local_head(call, place_ref[SEQ], i)

    own = pl.BlockSpec((half, HEAD_DIM), lambda i, p: (0, head(i, p)))
    return pl.pallas_call(
        pair_kernel,
        grid_spec=pltpu.PrefetchScalarGridSpec(
            num_scalar_prefetch=1,
            grid=(count,),
            in_specs=[
                own,
                own,
                own,
                pl.BlockSpec((3, half, HEAD_DIM), lambda i, p: (0, 0, i)),
                pl.BlockSpec((1, NT, CLIP_TOK), lambda i, p: (head(i, p), 0, 0)),
            ]
            + [pl.BlockSpec(memory_space=pl.ANY)] * len(earlier),
            out_specs=pl.BlockSpec((CLIP_TOK, HEAD_DIM), lambda i, p: (0, i)),
            scratch_shapes=[
                pltpu.VMEM((CLIP_TOK, HEAD_DIM), jnp.bfloat16),
                pltpu.VMEM((CLIP_TOK, 2 * HEAD_DIM), jnp.bfloat16),
            ],
        ),
        out_shape=jax.ShapeDtypeStruct((CLIP_TOK, count * HEAD_DIM), jnp.bfloat16),
        compiler_params=pltpu.CompilerParams(vmem_limit_bytes=limit),
        cost_estimate=SMALL_COST,
    )(place, query, key, value, other, bias, *earlier)


def attend_whole(place, query, key, value, bias):
    local_heads = query.shape[1] // HEAD_DIM
    column = pl.BlockSpec((CLIP_TOK, HEAD_DIM), lambda i, p: (0, i))
    return pl.pallas_call(
        whole_kernel,
        grid_spec=pltpu.PrefetchScalarGridSpec(
            num_scalar_prefetch=1,
            grid=(local_heads,),
            in_specs=[
                column,
                column,
                column,
                pl.BlockSpec((1, NT, CLIP_TOK), lambda i, p: (p[0] * local_heads + i, 0, 0)),
            ],
            out_specs=column,
            scratch_shapes=[pltpu.VMEM((CLIP_TOK, 2 * HEAD_DIM), jnp.bfloat16)],
        ),
        out_shape=jax.ShapeDtypeStruct(query.shape, jnp.bfloat16),
        compiler_params=pltpu.CompilerParams(vmem_limit_bytes=VMEM_LIMIT),
        cost_estimate=attention_cost(local_heads),
    )(place, query, key, value, bias)


def pack_kernel(place_ref, q_ref, k_ref, v_ref, *rest):
    out_ref = rest[-1]
    out_ref[0] = q_ref[...]
    out_ref[1] = k_ref[...]
    out_ref[2] = v_ref[...]


def local_head(call, side, part):
    first, by_side, step = call
    return first + by_side * side + step * part


def pack_partner(place, local_heads, call, query, key, value, earlier, limit):
    rows = query.shape[0]
    count = 2

    def head(i, place_ref):
        side = 1 - place_ref[SEQ]
        return side * local_heads + local_head(call, side, i)

    column = pl.BlockSpec((rows, HEAD_DIM), lambda i, p: (0, head(i, p)))
    return pl.pallas_call(
        pack_kernel,
        grid_spec=pltpu.PrefetchScalarGridSpec(
            num_scalar_prefetch=1,
            grid=(count,),
            in_specs=[column, column, column]
            + [pl.BlockSpec(memory_space=pl.ANY)] * len(earlier),
            out_specs=pl.BlockSpec((3, rows, HEAD_DIM), lambda i, p: (0, 0, i)),
        ),
        out_shape=jax.ShapeDtypeStruct((3, rows, count * HEAD_DIM), jnp.bfloat16),
        compiler_params=pltpu.CompilerParams(vmem_limit_bytes=limit),
        cost_estimate=SMALL_COST,
    )(place, query, key, value, *earlier)


def whole_block(shape):
    return pl.BlockSpec(shape, lambda i, p: (0,) * len(shape), pipeline_mode=pl.Buffered(1))


def gradient_kernel(place_ref, *refs, by_call):
    count = 4 if by_call else 2
    grad_ref = refs[count]
    sent_ref, kept_ref, rows_ref = refs[-3:]
    first_core = place_ref[CORE] == 0
    sides = (place_ref[SEQ], 1 - place_ref[SEQ])

    @pl.when(pl.program_id(0) == 0)
    def _():
        sent, kept = [], []
        for n in range(2):
            if by_call:
                one, two = refs[2 + n][...], refs[n][...]
            else:
                one, two = refs[n][:, :HEAD_DIM], refs[n][:, HEAD_DIM:]
            sent.append(jnp.where(first_core, one, two))
            kept.append(jnp.where(first_core, two, one))
        rows_ref[...] = jnp.concatenate(sent + kept, axis=1).T

    each = 2 if by_call else 1
    product = jnp.dot(rows_ref[...], grad_ref[...], preferred_element_type=jnp.float32)
    product = product.astype(jnp.bfloat16).reshape(4 * each, HEAD_DIM, grad_ref.shape[1])
    for n, side in enumerate(sides):
        sent_ref[pl.ds(each * side, each)] = product[each * n : each * (n + 1)]
        kept_ref[pl.ds(each * side, each)] = product[each * (2 + n) : each * (3 + n)]


def batch_gradient(place, sources, grad_proj, earlier=(), cost=SMALL_COST):
    by_call = len(sources) == 4
    heads = len(sources)
    rows, columns = grad_proj.shape
    step = columns // GRADIENT_STEPS
    out = pl.BlockSpec((heads, HEAD_DIM, step), lambda i, p: (0, 0, i))
    result = jax.ShapeDtypeStruct((heads, HEAD_DIM, columns), jnp.bfloat16)
    return pl.pallas_call(
        functools.partial(gradient_kernel, by_call=by_call),
        grid_spec=pltpu.PrefetchScalarGridSpec(
            num_scalar_prefetch=1,
            grid=(GRADIENT_STEPS,),
            in_specs=[whole_block(each.shape) for each in sources]
            + [pl.BlockSpec((rows, step), lambda i, p: (0, i))]
            + [pl.BlockSpec(memory_space=pl.ANY)] * len(earlier),
            out_specs=[out, out],
            scratch_shapes=[pltpu.VMEM((2 * heads * HEAD_DIM, rows), jnp.bfloat16)],
        ),
        out_shape=[result, result],
        compiler_params=pltpu.CompilerParams(vmem_limit_bytes=VMEM_GRADIENT),
        cost_estimate=cost,
    )(place, *sources, grad_proj, *earlier)


def sum_of(blocks):
    total = blocks[0].astype(jnp.float32)
    for block in blocks[1:]:
        total = total + block.astype(jnp.float32)
    return total


def level_step(place, bit, terms, earlier=(), cost=SMALL_COST):
    count = len(terms)
    pairs = terms[0].shape[0] // 2
    shape = (pairs,) + terms[0].shape[1:]
    block = (1,) + terms[0].shape[1:]
    keep = pl.BlockSpec(block, lambda i, p: (2 * i + p[bit], 0, 0))
    send = pl.BlockSpec(block, lambda i, p: (2 * i + 1 - p[bit], 0, 0))
    out = pl.BlockSpec(block, lambda i, p: (i, 0, 0))

    def kernel(place_ref, *refs):
        kept_ref, sent_ref = refs[-2:]
        kept_ref[...] = sum_of([ref[...] for ref in refs[:count]])
        sent_ref[...] = sum_of([ref[...] for ref in refs[count : 2 * count]]).astype(jnp.bfloat16)

    return pl.pallas_call(
        kernel,
        grid_spec=pltpu.PrefetchScalarGridSpec(
            num_scalar_prefetch=1,
            grid=(pairs,),
            in_specs=[keep] * count
            + [send] * count
            + [pl.BlockSpec(memory_space=pl.ANY)] * len(earlier),
            out_specs=[out, out],
        ),
        out_shape=[
            jax.ShapeDtypeStruct(shape, jnp.float32),
            jax.ShapeDtypeStruct(shape, jnp.bfloat16),
        ],
        compiler_params=pltpu.CompilerParams(vmem_limit_bytes=VMEM_SMALL),
        cost_estimate=cost,
    )(place, *terms, *terms, *earlier)


def reach_step(place, terms, earlier=()):
    count = len(terms)
    block = (1,) + terms[0].shape[1:]
    near = pl.BlockSpec(block, lambda i, p: (p[HIGH], 0, 0))
    far = pl.BlockSpec(block, lambda i, p: (1 - p[HIGH], 0, 0))

    def kernel(place_ref, *refs):
        kept_ref, near_ref, far_ref = refs[-3:]
        total = sum_of([ref[...] for ref in refs[:count]])
        kept_ref[...] = total
        near_ref[...] = total.astype(jnp.bfloat16)
        far_ref[...] = sum_of([ref[...] for ref in refs[count : 2 * count]]).astype(jnp.bfloat16)

    return pl.pallas_call(
        kernel,
        grid_spec=pltpu.PrefetchScalarGridSpec(
            num_scalar_prefetch=1,
            grid=(1,),
            in_specs=[near] * count
            + [far] * count
            + [pl.BlockSpec(memory_space=pl.ANY)] * len(earlier),
            out_specs=[whole_block(block)] * 3,
        ),
        out_shape=[
            jax.ShapeDtypeStruct(block, kind) for kind in (jnp.float32, jnp.bfloat16, jnp.bfloat16)
        ],
        compiler_params=pltpu.CompilerParams(vmem_limit_bytes=VMEM_SMALL),
        cost_estimate=SMALL_COST,
    )(place, *terms, *terms, *earlier)


def total_step(terms, earlier=(), kind=jnp.bfloat16):
    block = pl.BlockSpec((1,) + terms[0].shape[1:], lambda i: (i, 0, 0))

    def kernel(*refs):
        refs[-1][...] = sum_of([ref[...] for ref in refs[: len(terms)]]).astype(kind)

    return pl.pallas_call(
        kernel,
        grid=(terms[0].shape[0],),
        in_specs=[block] * len(terms) + [pl.BlockSpec(memory_space=pl.ANY)] * len(earlier),
        out_specs=block,
        out_shape=jax.ShapeDtypeStruct(terms[0].shape, kind),
        compiler_params=pltpu.CompilerParams(vmem_limit_bytes=VMEM_SMALL),
        cost_estimate=SMALL_COST,
    )(*terms, *earlier)


def choose_owned(place, *batches):
    block = batches[0][0].shape
    terms = [term for batch in batches for term in batch]

    def kernel(place_ref, *refs):
        alike = place_ref[CORE] == place_ref[X]
        outer = place_ref[LOW] == place_ref[HIGH]
        owned = (alike, ~alike & ~outer, ~alike & outer)
        at = 0
        for batch, mine in zip(batches, owned):
            chosen = refs[at : at + len(batch)]
            at += len(batch)

            @pl.when(mine)
            def _():
                refs[-1][...] = sum_of([ref[0] for ref in chosen])

    return pl.pallas_call(
        kernel,
        grid_spec=pltpu.PrefetchScalarGridSpec(
            num_scalar_prefetch=1,
            grid=(1,),
            in_specs=[whole_block(block)] * len(terms),
            out_specs=whole_block(block[1:]),
        ),
        out_shape=jax.ShapeDtypeStruct(block[1:], jnp.float32),
        compiler_params=pltpu.CompilerParams(vmem_limit_bytes=VMEM_GRADIENT),
        cost_estimate=SMALL_COST,
    )(place, *terms)


def join_columns(place, sources, calls, local_heads, earlier, cost):
    rows = sources[0].shape[0]
    step = rows // JOIN_STEPS
    shape = (rows, HEADS * HEAD_DIM)

    def kernel(place_ref, *refs):
        out_ref, done_ref = refs[-2:]
        done_ref[...] = jnp.zeros_like(done_ref)
        for n, source in enumerate(refs[: len(sources)]):
            side = place_ref[SEQ] if n % 2 == 0 else 1 - place_ref[SEQ]
            for part in range(2):
                head = side * local_heads + local_head(calls[n // 2], side, part)
                at = pl.multiple_of(head * HEAD_DIM, HEAD_DIM)
                out_ref[:, pl.ds(at, HEAD_DIM)] = source[:, part * HEAD_DIM : (part + 1) * HEAD_DIM]

    return pl.pallas_call(
        kernel,
        grid_spec=pltpu.PrefetchScalarGridSpec(
            num_scalar_prefetch=1,
            grid=(JOIN_STEPS,),
            in_specs=[pl.BlockSpec((step, each.shape[1]), lambda i, p: (i, 0)) for each in sources]
            + [pl.BlockSpec(memory_space=pl.ANY)] * len(earlier),
            out_specs=[
                pl.BlockSpec((step, shape[1]), lambda i, p: (i, 0)),
                pl.BlockSpec((8, HEAD_DIM), lambda i, p: (0, 0)),
            ],
        ),
        out_shape=[
            jax.ShapeDtypeStruct(shape, jnp.bfloat16),
            jax.ShapeDtypeStruct((8, HEAD_DIM), jnp.float32),
        ],
        compiler_params=pltpu.CompilerParams(vmem_limit_bytes=VMEM_SMALL),
        cost_estimate=cost,
    )(place, *sources, *earlier)


def project(attention, weight, gate, span, filled=(), earlier=(), cost=SMALL_COST):
    rows, depth = attention.shape
    columns = weight.shape[1]
    step = columns // PROJECT_STEPS
    first, steps = span[0], len(span)

    def kernel(attention_ref, weight_ref, gate_ref, *refs):
        out_ref, done_ref = refs[-2:]
        done_ref[...] = jnp.zeros_like(done_ref)
        total = jnp.dot(attention_ref[...], weight_ref[...], preferred_element_type=jnp.float32)
        out_ref[...] = (total * gate_ref[...]).astype(out_ref.dtype)

    return pl.pallas_call(
        kernel,
        grid=(steps,),
        in_specs=[
            pl.BlockSpec((rows, depth), lambda i: (0, 0), pipeline_mode=pl.Buffered(1)),
            pl.BlockSpec((depth, step), lambda i: (0, first + i)),
            pl.BlockSpec((1, step), lambda i: (0, first + i)),
        ]
        + [pl.BlockSpec(memory_space=pl.ANY)] * (len(filled) + len(earlier)),
        out_specs=[
            pl.BlockSpec((rows, step), lambda i: (0, first + i)),
            pl.BlockSpec((8, HEAD_DIM), lambda i: (0, 0)),
        ],
        out_shape=[
            jax.ShapeDtypeStruct((rows, columns), jnp.bfloat16),
            jax.ShapeDtypeStruct((8, HEAD_DIM), jnp.float32),
        ],
        input_output_aliases={3: 0} if filled else {},
        compiler_params=pltpu.CompilerParams(vmem_limit_bytes=VMEM_PROJECT),
        cost_estimate=cost,
    )(attention, weight, gate, *filled, *earlier)


def contract_tokens(columns, grad_proj, kind):
    return lax.dot_general(
        columns, grad_proj, (((0,), (0,)), ((), ())), preferred_element_type=jnp.float32
    ).astype(kind)


def after(value, *earlier):
    return lax.optimization_barrier((value,) + earlier)[0]


def dp_send(value, flip, sender):
    return lax.ppermute(value, "dp", [(i, i ^ flip) for i in range(HEADS) if sender(i)])


def same_bits(i):
    return (i >> 1 ^ i) & 1 == 0


def paired_device(query_rows, key_rows, value_rows, windows, out_weight, gate_scale, out_grad):
    index = lax.axis_index("dp")
    place = jnp.stack([lax.axis_index("seq")] + [index >> bit & 1 for bit in range(4)])
    place = lax.optimization_barrier(place.astype(jnp.int32))
    local_heads = HEADS // 2
    swap = [(0, 1), (1, 0)]
    calls = [(0, 0, 4), (3, 0, 4), (5, -4, 1), (1, 4, 1)]
    bias = window_bias(windows)
    weight = lax.all_gather(out_weight, "dp", axis=0, tiled=True)
    gate_row = gate_scale[0].astype(jnp.float32)
    grad_proj = (out_grad.astype(jnp.float32) * gate_row).astype(jnp.bfloat16)
    sources = (query_rows, key_rows, value_rows)

    def pack(n, limit, *earlier):
        return pack_partner(place, local_heads, calls[n], *sources, earlier, limit)

    def attention(n, other, *earlier, limit=VMEM_LIMIT):
        return attend_pair(place, local_heads, calls[n], *sources, other, bias, earlier, limit)

    def exchange(mine):
        return lax.ppermute(mine, "seq", swap)

    def core_step(*operands):
        sent, kept = batch_gradient(place, operands[:4], operands[4])
        return total_step([kept, dp_send(sent, 1, lambda i: True)])

    def apart(step, *operands):
        shapes = jax.eval_shape(step, *operands)
        return lax.cond(
            windows[0, 0] > 0,
            step,
            lambda *_: jax.tree.map(lambda leaf: jnp.zeros(leaf.shape, leaf.dtype), shapes),
            *operands,
        )

    packed0 = pack(0, VMEM_WHOLE)
    packed1 = pack(1, VMEM_WHOLE, packed0)
    packed2 = pack(2, VMEM_LIMIT, packed1)
    other0 = exchange(packed0)
    other1 = exchange(packed1)
    other2 = exchange(packed2)
    mine0 = attention(0, other0, packed2)
    theirs0 = exchange(mine0)
    mine1 = attention(1, other1, mine0)
    theirs1 = exchange(mine1)
    packed3 = pack(3, VMEM_LIMIT, mine1)
    other3 = exchange(packed3)
    mine2 = attention(2, other2, mine1, packed3)
    theirs2 = exchange(mine2)

    def unlike(i):
        return not same_bits(i)

    def outer(i):
        return unlike(i) and (i >> 2 ^ i >> 3) & 1 == 0

    def inner(i):
        return unlike(i) and (i >> 2 ^ i >> 3) & 1 == 1

    first = (mine0, theirs0, mine1, theirs1)
    total_a = apart(core_step, after(mine0, mine2, weight), *first[1:], grad_proj)
    across_a = dp_send(total_a, 2, unlike)
    mine3 = attention(3, other3, total_a, limit=VMEM_WHOLE)
    theirs3 = exchange(mine3)
    sent_b, kept_b = batch_gradient(place, (mine2, theirs2), grad_proj, (mine3,), LONG_COST)
    came_b = dp_send(sent_b, 1, lambda i: True)
    kept_a, sent_a = level_step(place, LOW, [total_a, across_a], (sent_b,), LONG_COST)
    low_a = dp_send(sent_a, 4, same_bits)
    total_b = total_step([kept_b, came_b], (sent_a,))
    across_b = dp_send(total_b, 2, same_bits)
    sent_c, kept_c = batch_gradient(place, (mine3, theirs3), grad_proj, (total_b,))
    came_c = dp_send(sent_c, 1, lambda i: True)
    results = (*first, mine2, theirs2, mine3, theirs3)
    columns, done = join_columns(place, results, calls, local_heads, (sent_c,), LONG_COST)
    total_c = total_step([kept_c, came_c], (done,))
    across_c = dp_send(total_c, 2, same_bits)
    kept_a, sent_a = level_step(place, HIGH, [kept_a, low_a], (total_c,))
    high_a = dp_send(sent_a, 8, same_bits)
    sent_b = total_step([total_b, across_b], (sent_a,))
    low_b = dp_send(sent_b, 4, outer)
    gate = gate_row[None]
    out, done = project(columns, weight, gate, range(3), (), (sent_b,))
    kept_c, near_c, far_c = reach_step(place, [total_c, across_c], (done,))
    reached_c = dp_send(far_c, 8, inner), dp_send(far_c, 12, outer), dp_send(near_c, 4, inner)
    kept_b, sent_b = level_step(place, HIGH, [total_b, across_b, low_b], (near_c,))
    high_b = dp_send(sent_b, 12, inner)
    last = range(3, PROJECT_STEPS)
    block_out, done = project(columns, weight, gate, last, (out,), (sent_b,), LONG_COST)
    final_a = total_step([kept_a, high_a], (done,), jnp.float32)
    weight_grad = choose_owned(place, (final_a,), (kept_b, high_b), (kept_c, *reached_c))
    return (block_out, weight_grad)


def general_device(query_rows, key_rows, value_rows, windows, out_weight, gate_scale, out_grad):
    query, key, value = (
        lax.all_to_all(rows, "seq", split_axis=1, concat_axis=0, tiled=True)
        for rows in (query_rows, key_rows, value_rows)
    )
    place = lax.axis_index("seq").reshape(1).astype(jnp.int32)
    mine = attend_whole(place, query, key, value, window_bias(windows))
    columns = lax.all_gather(mine, "seq", axis=1, tiled=True)
    weight = lax.all_gather(out_weight, "dp", axis=0, tiled=True)
    gate_row = gate_scale[0].astype(jnp.float32)
    projected = jnp.dot(columns, weight, preferred_element_type=jnp.float32)
    block_out = (projected * gate_row).astype(jnp.bfloat16)
    grad_proj = (out_grad.astype(jnp.float32) * gate_row).astype(jnp.bfloat16)
    weight_grad = lax.psum_scatter(
        contract_tokens(columns, grad_proj, jnp.float32), "dp", scatter_dimension=0, tiled=True
    )
    return (block_out, weight_grad)


def solution(mesh):
    paired = mesh.shape["seq"] == 2 and mesh.shape["dp"] == HEADS
    return jax.shard_map(
        paired_device if paired else general_device,
        mesh=mesh,
        in_specs=(
            P(("dp", "seq"), None),
            P(("dp", "seq"), None),
            P(("dp", "seq"), None),
            P(),
            P("dp", "seq"),
            P("dp", "seq"),
            P("dp", "seq"),
        ),
        out_specs=(P("dp", "seq"), P("dp", "seq")),
        check_vma=False,
    )
```
